32 devices in a mesh: groups: 2 (over y), plane: 4 (over z), span: 2 (over x), wall: 2 (over core).
Axes of the slice: x: 2, y: 2, z: 4, core: 2. Of those that a mesh axis runs over, the one named last changes fastest.
Arguments:
- velocity: float32 [6, 32, 128, 512], P('groups', 'wall', 'plane', 'span'), parts along dimension 0, may hold values from -5 to 5
- levels: int32 [256, 512], P(('groups', 'plane'), 'span'), parts along dimension 0, may hold values from 1 to 30
- fraction: float32 [256, 512], P(('groups', 'plane'), 'span'), parts along dimension 0, may hold values from 0.2 to 1
- bed_height: float32 [256, 512], P(('groups', 'plane', 'span', 'wall')), parts along dimension 0, may hold values from -4 to 4
Outputs:
- velocity_next: float32 [6, 32, 128, 512], P('groups', 'wall', 'plane', 'span'), parts along dimension 0
- bed_next: float32 [256, 512], P(('groups', 'plane'), 'span'), parts along dimension 0
The draws below stay inside these ranges and needn't reach their ends.
There are 2 independent parts, one for each index of `groups`. The reference program is written for one: setup_inputs(seed, part) draws one part's arguments, and reference() takes and returns one part's arrays. A program takes and returns all parts, laid end to end along the dimension named above; each array names one. Nothing has to cross between parts.
All inputs are finite; a program needn't handle non-finite values.
Results may differ from the reference program's by a relative error of at most 0.00002.
Values sent between devices are 32-bit elements; how exact they have to be, the bound alone decides.
No kernel may reach another device: no remote copies, remote signals or barrier semaphores. Data moves between devices by JAX's collectives and lax.ppermute only.
A program may use at most 64 MiB of HBM per device.

```python
import jax
import jax.numpy as jnp
from jax import lax

NX = 512
NY = 128
NZ = 32


def place_ends(drawn, own_key, smallest, largest):
    longest = drawn.shape.index(max(drawn.shape))
    spots = []
    for shift in (0, 1):
        where = [jax.random.randint(jax.random.fold_in(own_key, axis), (), 0, length) for axis, length in enumerate(drawn.shape)]
        where[longest] = (where[longest] + shift) % drawn.shape[longest]
        spots.append(tuple(where))
    return drawn.at[spots[0]].set(smallest).at[spots[1]].set(largest)


def block_scale(key, extent, pieces, low, largest):
    gain = 1.0
    for axis_at, parts in pieces:
        heights = jax.random.uniform(jax.random.fold_in(jax.random.fold_in(key, 6), axis_at), (parts,), jnp.float32, low / len(pieces), largest / len(pieces))
        gain = gain * jnp.repeat(jnp.exp(heights), extent[axis_at] // parts).reshape((-1,) + (1,) * (len(extent) - 1 - axis_at))
    return gain


def normal_values(key, dims, width, bound, split=(), held_as=jnp.bfloat16):
    factor_of = block_scale(key, dims, split, -0.22, 0.18) if split else 1.0
    array = jax.random.normal(key, dims, jnp.float32) * width * factor_of
    return jnp.minimum(jnp.maximum(array, -bound), bound).astype(held_as)


def setup_inputs(seed: int = 0, part: int = 0) -> dict:
    key_of = jax.random.split(jax.random.key(seed), 5)
    own_keys = jax.random.split(jax.random.fold_in(key_of[4], part), 5)
    return {
        "velocity": normal_values(own_keys[0], (3, NZ, NY, NX), 1.0, 5.0, ((1, 2), (2, 4), (3, 2)), jnp.float32),
        "levels": place_ends(jax.random.randint(own_keys[1], (NY, NX), 1, NZ - 1), jax.random.fold_in(own_keys[1], 1), 1, (NZ - 1) - 1).astype(jnp.int32),
        "fraction": jnp.clip(0.2 + 0.8 * jax.random.uniform(own_keys[2], (NY, NX), jnp.float32) ** block_scale(own_keys[2], (NY, NX), ((0, 4), (1, 2)), -0.2, 0.2), 0.2, 1.0),
        "bed_height": normal_values(own_keys[3], (NY, NX), 1.0, 4.0, ((0, 16),), jnp.float32),
    }


time_step = 0.1
viscosity = 0.5
bed_step = 0.4
slope_rate = 0.25
threshold_sq = 0.25


def shifted(field, axis, offset):
    widths = [(2, 2) if number == axis else (0, 0) for number in range(field.ndim)]
    padded = jnp.pad(field, widths)
    return lax.slice_in_dim(padded, 2 + offset, 2 + offset + field.shape[axis], axis=axis)


def fourth(field, axis):
    near = shifted(field, axis, 1) - shifted(field, axis, -1)
    far = shifted(field, axis, 2) - shifted(field, axis, -2)
    return (8.0 * near - far) / 12.0


def laplace(field):
    total = -2.0 * field.ndim * field
    for axis in range(field.ndim):
        total = total + shifted(field, axis, 1) + shifted(field, axis, -1)
    return total


def openness(levels, fraction, layers):
    return jnp.where(layers == levels[None], fraction[None], jnp.where(layers > levels[None], 1.0, 0.0))


def reference(velocity, levels, fraction, bed_height):
    layers = jnp.arange(velocity.shape[1], dtype=jnp.int32)[:, None, None]
    opened = openness(levels, fraction, layers)
    along = (2, 1, 0)
    updated = []
    for component in range(3):
        carried = opened * velocity[component]
        advect = fourth(velocity[0] * carried, along[0])
        advect = advect + fourth(velocity[1] * carried, along[1])
        advect = advect + fourth(velocity[2] * carried, along[2])
        change = -advect + viscosity * laplace(carried)
        updated.append(velocity[component] + time_step * opened * change)
    velocity_next = jnp.stack(updated)
    cutting = jnp.where(layers == levels[None], 1.0, 0.0)
    scale = 1.0 / (0.5 + fraction)
    shear_x = jnp.sum(cutting * velocity_next[0], axis=0) * scale
    shear_y = jnp.sum(cutting * velocity_next[1], axis=0) * scale
    square = shear_x * shear_x + shear_y * shear_y
    factor = jnp.maximum(square - threshold_sq, 0.0) / (square + threshold_sq)
    load_x = shear_x * factor
    load_y = shear_y * factor
    divergence = 0.5 * (shifted(load_x, 1, 1) - shifted(load_x, 1, -1))
    divergence = divergence + 0.5 * (shifted(load_y, 0, 1) - shifted(load_y, 0, -1))
    height = bed_height
    for turn in range(2):
        height = height - bed_step * divergence + bed_step * slope_rate * laplace(height)
    return velocity_next, height
```

```python
import functools

import jax
import jax.numpy as jnp
from jax import lax
from jax.experimental import pallas as pl
from jax.experimental.pallas import tpu as pltpu
from jax.sharding import PartitionSpec as P

time_step = 0.1
bed_step = 0.4
slope_rate = 0.25
threshold_sq = 0.25
gain = time_step / 12.0
EDGE = 4
SUB = 8
LANE = 128
VMEM = pltpu.VMEM
MIB = 1024 * 1024


def call(kernel, outs, ins, scratch=(), any_inputs=(), flops=0, moved=0, limit=20, aliases=None):
    specs = [pl.BlockSpec(memory_space=pl.ANY if i in any_inputs else VMEM) for i in range(len(ins))]
    shapes = [jax.ShapeDtypeStruct(s, jnp.float32) for s in outs]
    return pl.pallas_call(
        kernel,
        out_shape=shapes,
        in_specs=specs,
        out_specs=[pl.BlockSpec(memory_space=VMEM) for _ in outs],
        scratch_shapes=list(scratch),
        input_output_aliases=aliases or {},
        cost_estimate=pl.CostEstimate(flops=flops, bytes_accessed=moved, transcendentals=0),
        compiler_params=pltpu.CompilerParams(vmem_limit_bytes=limit * MIB),
    )(*ins)


def iota(shape, dim):
    return lax.broadcasted_iota(jnp.int32, shape, dim)


def ahead(x, step, axis):
    return pltpu.roll(x, (-step) % x.shape[axis], axis)


def sweep(flux, b, axis):
    a = 8.0 * flux
    return ahead((b - a) + ahead(flux, 1, axis), 1, axis) + ahead((b + a) - ahead(flux, -1, axis), -1, axis)


def opened_at(level, fraction, layer):
    return jnp.where(level == layer, fraction, jnp.where(layer > level, 1.0, 0.0))


def even(axis):
    return lax.rem(lax.axis_index(axis), 2) == 0


def brick(read, level, fraction, base, layers, q_ref, f_ref, write):
    rows, cols = level.shape
    blank = jnp.zeros((rows, cols), jnp.float32)
    for c in range(3):
        for z in (0, 1, layers + 2, layers + 3):
            q_ref[c, z] = blank
            f_ref[c, z] = blank
    cut_gain = fraction * (gain / 1.0)
    scale = 1.0 / (0.5 + fraction)

    def prepare(z, carry):
        vel = [read(c, z) for c in range(3)]
        opened = opened_at(level, fraction, (base + z).astype(jnp.float32))
        for c in range(3):
            q = opened * vel[c]
            q_ref[c, z + 2] = q
            f_ref[c, z + 2] = vel[2] * q
        return carry

    lax.fori_loop(0, layers, prepare, 0, unroll=2)

    def vertical(c, z):
        near = f_ref[c, z + 3] - f_ref[c, z + 1]
        both = q_ref[c, z + 3] + q_ref[c, z + 1]
        return 6.0 * both - 8.0 * near + (f_ref[c, z + 4] - f_ref[c, z])

    def outside(z):
        hit = level == (base + z).astype(jnp.float32)
        found = []
        for c in range(2):
            total = blank
            if z + 3 <= layers + 3 and z + 1 >= 0:
                low, high = (z + 1, z + 3)
            for offset, weight_f, weight_q in ((1, -8.0, 6.0), (-1, 8.0, 6.0), (2, 1.0, 0.0), (-2, -1.0, 0.0)):
                at = z + offset
                if 0 <= at < layers:
                    total = total + weight_f * f_ref[c, at + 2]
                    if weight_q:
                        total = total + weight_q * q_ref[c, at + 2]
            found.append(jnp.where(hit, cut_gain * total, 0.0))
        return found

    sums = [blank, blank]
    for z in (-2, -1, layers, layers + 1):
        found = outside(z)
        sums = [s + f for s, f in zip(sums, found)]

    def update(z, sums):
        vel = [read(c, z) for c in range(3)]
        q = [q_ref[c, z + 2] for c in range(3)]
        layer = (base + z).astype(jnp.float32)
        opened = opened_at(level, fraction, layer)
        hit = level == layer
        weight = gain * opened
        cross = vel[0] * q[1]
        along_x = (vel[0] * q[0], cross, f_ref[0, z + 2])
        along_y = (cross, vel[1] * q[1], f_ref[1, z + 2])
        sums = list(sums)
        for c in range(3):
            b = 6.0 * q[c]
            total = vertical(c, z) - 6.0 * b
            total = total + sweep(along_x[c], b, 1) + sweep(along_y[c], b, 0)
            fresh = vel[c] + weight * total
            write(c, z, fresh)
            if c < 2:
                sums[c] = sums[c] + jnp.where(hit, fresh, 0.0)
        return tuple(sums)

    sums = lax.fori_loop(0, layers, update, tuple(sums))
    return [s * scale for s in sums]


def pack_kernel(layers, bed_in, vel, lev, frac, bed, a_ref, b_ref, z_ref, top, bottom, sems):
    rows = lev.shape[0]
    wall = lax.axis_index("wall")
    start = jnp.where(wall == 0, layers - 2, 0)
    copies = [
        pltpu.make_async_copy(vel.at[:, :, pl.ds(0, SUB), :], top, sems.at[0]),
        pltpu.make_async_copy(vel.at[:, :, pl.ds(rows - SUB, SUB), :], bottom, sems.at[1]),
        pltpu.make_async_copy(vel.at[:, pl.ds(start, 2)], z_ref, sems.at[2]),
    ]
    for copy in copies:
        copy.start()
    cols = lev.shape[1]
    half = iota((SUB, cols), 0) < EDGE
    is_even = even("plane")

    def put(n, low, high):
        a_ref[n] = jnp.where(is_even, low, high)
        b_ref[n] = jnp.where(is_even, high, low)

    levels = lev[...].astype(jnp.float32)
    count = 3 * layers // 2
    put(
        count,
        jnp.where(half, pltpu.roll(levels[-SUB:], EDGE, 0), frac[-SUB:]),
        jnp.where(half, levels[:SUB], pltpu.roll(frac[:SUB], EDGE, 0)),
    )
    if bed_in:
        for i in range(bed.shape[1] // cols):
            tile = bed[:, i * cols : (i + 1) * cols]
            put(count + 1 + i, tile, tile)
    for copy in copies:
        copy.wait()
    for c in range(3):
        for k in range(layers // 2):
            low = jnp.where(half, pltpu.roll(bottom[c, 2 * k], EDGE, 0), bottom[c, 2 * k + 1])
            high = jnp.where(half, top[c, 2 * k], pltpu.roll(top[c, 2 * k + 1], EDGE, 0))
            put(c * (layers // 2) + k, low, high)


def gather_edges(read, layers, rows, cols, put):
    lane = iota((rows, LANE), 1)
    column = lax.rem(lane, 2 * EDGE)
    for c in range(3):
        right = jnp.zeros((rows, LANE), jnp.float32)
        left = right
        for z in range(layers):
            group = (lane // (2 * EDGE)) == z
            field = read(c, z)
            last = field[:, cols - LANE :]
            first = field[:, :LANE]
            at = 2 * EDGE * z
            right = jnp.where(group, pltpu.roll(last, (at - (LANE - EDGE)) % LANE, 1), right)
            left = jnp.where(group, pltpu.roll(first, (at + EDGE) % LANE, 1), left)
        put(0, c, jnp.where(column < EDGE, right, 0.0))
        put(1, c, jnp.where(column >= EDGE, left, 0.0))


def repeat_edges(field, rows, cols):
    lane = iota((rows, LANE), 1)
    right = jnp.where(lane < EDGE, pltpu.roll(field[:, cols - LANE :], EDGE, 1), 0.0)
    left = pltpu.roll(jnp.where(lane < EDGE, field[:, :LANE], 0.0), EDGE, 1)
    step = 2 * EDGE
    while step < LANE:
        right = right + pltpu.roll(right, step, 1)
        left = left + pltpu.roll(left, step, 1)
        step *= 2
    return right, left


def inner_kernel(layers, vel, lev, frac, new_ref, shear_ref, edge_ref, q_ref, f_ref):
    rows, cols = lev.shape
    base = lax.axis_index("wall") * layers
    levels = lev[...].astype(jnp.float32)
    fraction = frac[...]

    def write(c, z, value):
        new_ref[c, z] = value

    sums = brick(lambda c, z: vel[c, z], levels, fraction, base, layers, q_ref, f_ref, write)
    shear_ref[0] = sums[0]
    shear_ref[1] = sums[1]

    def put(side, n, value):
        edge_ref[side, n] = value.reshape(rows // SUB, SUB, LANE)

    gather_edges(lambda c, z: vel[c, z], layers, rows, cols, put)
    for n, field in ((3, levels), (4, fraction)):
        right, left = repeat_edges(field, rows, cols)
        put(0, n, right)
        put(1, n, left)


def unpack_kernel(layers, count, bed_in, got_a, got_b, edge, bed, halo_ref, flat_ref, full_ref, *messages):
    cols = halo_ref.shape[3]
    tiles = edge.shape[2]
    half = iota((SUB, cols), 0) < EDGE
    is_even = even("plane")

    def sides(n):
        one, two = got_a[n], got_b[n]
        return jnp.where(is_even, one, two), jnp.where(is_even, two, one)

    for c in range(3):
        for k in range(layers // 2):
            low, high = sides(c * (layers // 2) + k)
            halo_ref[c, 2 * k] = jnp.where(half, low, pltpu.roll(high, EDGE, 0))
            halo_ref[c, 2 * k + 1] = jnp.where(half, pltpu.roll(low, EDGE, 0), high)
    low, high = sides(3 * layers // 2)
    levels = jnp.where(half, low, pltpu.roll(high, EDGE, 0))
    fraction = jnp.where(half, pltpu.roll(low, EDGE, 0), high)
    flat_ref[0] = levels
    flat_ref[1] = fraction

    def put(side, n, value):
        full_ref[side, n * (tiles + 1) + tiles] = value

    gather_edges(lambda c, z: halo_ref[c, z], layers, SUB, cols, put)
    for n, field in ((3, levels), (4, fraction)):
        right, left = repeat_edges(field, SUB, cols)
        put(0, n, right)
        put(1, n, left)
    for side in range(2):
        for n in range(5):
            for t in range(tiles):
                full_ref[side, n * (tiles + 1) + t] = edge[side, n, t]
    used = 5 * (tiles + 1)
    right_first = even("span")
    for i, message in enumerate(messages):
        is_right = right_first if i == 0 else jnp.logical_not(right_first)
        for n in range(used):
            message[n] = jnp.where(is_right, full_ref[0, n], full_ref[1, n])
    if bed_in:
        parts = bed.shape[1] // LANE
        for i in range(parts):
            messages[0][used + i] = bed[:, i * LANE : (i + 1) * LANE]
        per = cols // LANE
        for i in range(bed.shape[1] // cols):
            low, high = sides(3 * layers // 2 + 1 + i)
            tile = jnp.where(half, low, high)
            for j in range(per):
                messages[0][used + parts + i * per + j] = tile[:, j * LANE : (j + 1) * LANE]


def strip_kernel(layers, vel, lev, frac, halo, flat, top_ref, bottom_ref, shear_ref, top, bottom, q_ref, f_ref, sems):
    rows, cols = lev.shape
    copies = [
        pltpu.make_async_copy(vel.at[:, :, pl.ds(0, SUB), :], top, sems.at[0]),
        pltpu.make_async_copy(vel.at[:, :, pl.ds(rows - SUB, SUB), :], bottom, sems.at[1]),
    ]
    for copy in copies:
        copy.start()
    base = lax.axis_index("wall") * layers
    half = iota((SUB, cols), 0) < EDGE
    for copy in copies:
        copy.wait()
    for side, own, new in ((0, top, top_ref), (1, bottom, bottom_ref)):
        inside = half if side == 0 else jnp.logical_not(half)
        first = 0 if side == 0 else rows - SUB
        levels = jnp.where(inside, lev[first : first + SUB].astype(jnp.float32), flat[0])
        fraction = jnp.where(inside, frac[first : first + SUB], flat[1])

        def read(c, z):
            return jnp.where(inside, own[c, z], halo[c, z])

        def write(c, z, value):
            new[c, z] = value

        sums = brick(read, levels, fraction, base, layers, q_ref, f_ref, write)
        shear_ref[side, 0] = sums[0]
        shear_ref[side, 1] = sums[1]


def column_strip(vel, levels, fraction, base, layers):
    shape = levels.shape
    width = 2 * EDGE
    here = iota(shape, 1) // width
    layer = (here + base).astype(jnp.float32)
    opened = opened_at(levels, fraction, layer)
    hit = levels == layer
    hit_down = levels == layer - layers
    hit_up = levels == layer + layers
    scale = 1.0 / (0.5 + fraction)
    fresh, shear = [], []
    for c in range(3):
        q = opened * vel[c]
        b = 6.0 * q
        total = sweep(vel[0] * q, b, 1) + sweep(vel[1] * q, b, 0) - 6.0 * b
        flux = vel[2] * q
        plus = ahead(b - 8.0 * flux, width, 1)
        minus = ahead(b + 8.0 * flux, -width, 1)
        plus_far = ahead(flux, 2 * width, 1)
        minus_far = ahead(flux, -2 * width, 1)
        total = total + jnp.where(here <= layers - 2, plus, 0.0) + jnp.where(here <= layers - 3, plus_far, 0.0)
        total = total + jnp.where(here >= 1, minus, 0.0) - jnp.where(here >= 2, minus_far, 0.0)
        value = vel[c] + gain * opened * total
        fresh.append(value)
        if c < 2:
            down = jnp.where(here > layers - 2, plus, 0.0) + jnp.where(here > layers - 3, plus_far, 0.0)
            up = jnp.where(here < 1, minus, 0.0) - jnp.where(here < 2, minus_far, 0.0)
            part = jnp.where(hit, value, 0.0)
            part = part + gain * fraction * (jnp.where(hit_down, down, 0.0) + jnp.where(hit_up, up, 0.0))
            step = LANE // 2
            while step >= width:
                part = part + pltpu.roll(part, step, 1)
                step //= 2
            shear.append(part * scale)
    return fresh, shear


def side_kernel(layers, spans, bed_in, full, shear, strips, *rest):
    got = rest[:spans]
    rest = rest[spans:]
    own_message = rest[0]
    fresh_ref, out_ref = rest[1:]
    _, rows, cols = shear.shape
    tiles = rows // SUB
    tall = tiles + 1
    base = lax.axis_index("wall") * layers
    right_first = even("span")
    results = []
    for side in range(2):
        fields = []
        for n in range(5):
            at = slice(n * tall, (n + 1) * tall)
            own = full[side, at]
            first = right_first if side == 0 else jnp.logical_not(right_first)
            other = jnp.where(first, got[0][at], got[1][at] if spans > 1 else 0.0)
            fields.append((own + other).reshape(tall * SUB, LANE))
        fresh, edge_shear = column_strip(fields[:3], fields[3], fields[4], base, layers)
        for c in range(3):
            fresh_ref[side, c] = fresh[c]
        results.append(edge_shear)
    lane = iota((SUB, LANE), 1)
    sub = iota((SUB, LANE), 0)
    lanes = cols // LANE
    for c in range(2):
        right, left = results[0][c], results[1][c]
        for t in range(tall):
            at = slice(t * SUB, (t + 1) * SUB)
            for k in range(lanes):
                cut = slice(k * LANE, (k + 1) * LANE)
                if t == tiles:
                    piece = jnp.where(sub < EDGE, strips[1, c, :, cut], strips[0, c, :, cut])
                    piece = jnp.where((sub < 2) | (sub >= SUB - 2), piece, 0.0)
                else:
                    piece = shear[c, at, cut]
                    if t == 0:
                        piece = jnp.where(sub < 2, strips[0, c, :, cut], piece)
                    if t == tiles - 1:
                        piece = jnp.where(sub >= SUB - 2, strips[1, c, :, cut], piece)
                if k == 0:
                    piece = jnp.where(lane < 2, pltpu.roll(left[at], LANE - EDGE, 1), piece)
                if k == lanes - 1:
                    piece = jnp.where(lane >= LANE - 2, pltpu.roll(right[at], LANE - EDGE, 1), piece)
                out_ref[(c * tall + t) * (lanes + 1) + k] = piece
            beyond = jnp.where(lane < 2, pltpu.roll(right[at], LANE - EDGE, 1), 0.0)
            beyond = jnp.where(lane >= LANE - 2, pltpu.roll(left[at], LANE - EDGE, 1), beyond)
            out_ref[(c * tall + t) * (lanes + 1) + lanes] = beyond
    if bed_in:
        used = 2 * tall * (lanes + 1)
        start = 5 * tall
        count = own_message.shape[0] - start
        for i in range(count):
            out_ref[used + i] = own_message[start + i]
            out_ref[used + count + i] = got[0][start + i]


def merge_kernel(layers, new, strip_top, strip_bottom, fresh, far, lev, frac, out_ref):
    rows, cols = lev.shape
    tiles = rows // SUB
    lanes = cols // LANE
    wall = lax.axis_index("wall")
    lower = wall == 0
    sub = iota((SUB, cols), 0)
    lane = iota((rows, LANE), 1)
    levels = lev[...].astype(jnp.float32)
    fraction = frac[...]
    for c in range(3):
        right, left = fresh[0, c, :rows], fresh[1, c, :rows]

        def layer_step(z, carry):
            shift = 2 * EDGE * z
            block = new[c, z]
            first = jnp.where(sub < 2, strip_top[c, z], block[:SUB])
            last = jnp.where(sub >= SUB - 2, strip_bottom[c, z], block[rows - SUB :])
            block = jnp.concatenate([first, block[SUB : rows - SUB], last], axis=0)
            pieces = [block[:, k * LANE : (k + 1) * LANE] for k in range(lanes)]
            at_left = pltpu.roll(left, lax.rem(2 * LANE - EDGE - shift, LANE), 1)
            at_right = pltpu.roll(right, lax.rem(2 * LANE - EDGE - shift, LANE), 1)
            pieces[0] = jnp.where(lane < 2, at_left, pieces[0])
            pieces[-1] = jnp.where(lane >= LANE - 2, at_right, pieces[-1])
            for k in range(lanes):
                out_ref[c, z, :, k * LANE : (k + 1) * LANE] = pieces[k]
            return carry

        lax.fori_loop(0, layers, layer_step, 0, unroll=4)
    base = wall * layers
    near_from = jnp.where(lower, 0, 1)
    far_from = 1 - near_from
    near_to = jnp.where(lower, layers - 1, 0)
    far_to = jnp.where(lower, layers - 2, 1)
    sign = jnp.where(lower, -1.0, 1.0)
    other = jnp.where(lower, layers, 0)
    near_open = opened_at(levels, fraction, (other + jnp.where(lower, 0, layers - 1)).astype(jnp.float32))
    far_open = opened_at(levels, fraction, (other + jnp.where(lower, 1, layers - 2)).astype(jnp.float32))
    near_gain = gain * opened_at(levels, fraction, (base + near_to).astype(jnp.float32))
    far_gain = gain * opened_at(levels, fraction, (base + far_to).astype(jnp.float32))
    near_w, far_w = far[2, near_from], far[2, far_from]
    for c in range(3):
        near_q = near_open * far[c, near_from]
        near_f = sign * (near_w * near_q)
        far_f = sign * (far_w * (far_open * far[c, far_from]))
        out_ref[c, near_to] = out_ref[c, near_to] + near_gain * (6.0 * near_q + 8.0 * near_f - far_f)
        out_ref[c, far_to] = out_ref[c, far_to] - far_gain * near_f


def bed_kernel(tall, lanes, bed_in, mine, theirs, *rest):
    out_ref = rest[-1]
    rows = (tall - 1) * SUB
    wide = (lanes + 1) * LANE
    span = lax.axis_index("span")
    wall = lax.axis_index("wall")
    plane = lax.axis_index("plane")

    def sheared(c):
        whole = []
        for t in range(tall):
            first = (c * tall + t) * (lanes + 1)
            whole.append(
                jnp.concatenate([mine[first + k] + theirs[first + k] for k in range(lanes + 1)], axis=1)
            )
        return jnp.concatenate(whole, axis=0)

    shear_x, shear_y = sheared(0), sheared(1)
    if bed_in:
        used = 2 * tall * (lanes + 1)
        parts = 2 * lanes

        def tile_of(s, w, which):
            pieces = []
            for k in range(parts):
                own = used + which * parts + k
                across = own + 2 * parts
                from_mine = jnp.where(span == s, mine[own], mine[across])
                from_theirs = jnp.where(span == s, theirs[own], theirs[across])
                pieces.append(jnp.where(wall == w, from_mine, from_theirs))
            return pieces

        def window(pieces):
            lane = iota((SUB, LANE), 1)
            low = span == 0
            inside = [jnp.where(low, pieces[k], pieces[lanes + k]) for k in range(lanes)]
            beyond = jnp.where(
                low,
                jnp.where(lane < LANE // 2, pieces[lanes], 0.0),
                jnp.where(lane < LANE // 2, 0.0, pieces[lanes - 1]),
            )
            return jnp.concatenate(inside + [beyond], axis=1)

        sub = iota((SUB, LANE), 0)
        whole = [window(tile_of(s, w, 0)) for s in range(2) for w in range(2)]
        after = tile_of(0, 0, 1)
        before = tile_of(1, 1, 1)
        whole.append(window([jnp.where(sub < EDGE, a, b) for a, b in zip(after, before)]))
        bed = jnp.concatenate(whole, axis=0)
    else:
        bed = rest[0][...]
    square = shear_x * shear_x + shear_y * shear_y
    factor = jnp.maximum(square - threshold_sq, 0.0) / (square + threshold_sq)
    load_x = shear_x * factor
    load_y = shear_y * factor
    divergence = 0.5 * (ahead(load_x, 1, 1) - ahead(load_x, -1, 1)) + 0.5 * (
        ahead(load_y, 1, 0) - ahead(load_y, -1, 0)
    )
    row = iota((tall * SUB, wide), 0)
    col = iota((tall * SUB, wide), 1)
    last_plane = plane == lax.axis_size("plane") - 1
    last_span = span == lax.axis_size("span") - 1
    row_low = jnp.where(last_plane, rows, rows + EDGE)
    row_high = jnp.where(plane == 0, rows + SUB, rows + EDGE)
    col_low = jnp.where(last_span, wide - LANE, wide - LANE // 2)
    col_high = jnp.where(span == 0, wide, wide - LANE // 2)
    valid = ((row < row_low) | (row >= row_high)) & ((col < col_low) | (col >= col_high))

    def step(height):
        around = ahead(height, 1, 0) + ahead(height, -1, 0) + ahead(height, 1, 1) + ahead(height, -1, 1)
        return height - bed_step * divergence + bed_step * slope_rate * (around - 4.0 * height)

    first = jnp.where(valid, step(bed), 0.0)
    out_ref[...] = step(first)[:rows, : lanes * LANE]


def pairings(axis):
    size = lax.axis_size(axis)
    lists = []
    for start in (0, 1):
        found = []
        for i in range(start, size - 1, 2):
            found += [(i, i + 1), (i + 1, i)]
        lists.append(found)
    return lists


def bed_around(bed_height, rows, cols):
    spans = lax.axis_size("span")
    whole = lax.all_gather(bed_height, ("span", "wall"), axis=0, tiled=True)
    padded = jnp.pad(whole, ((0, 0), (EDGE, EDGE)))
    piece = lax.dynamic_slice_in_dim(padded, lax.axis_index("span") * cols, cols + 2 * EDGE, axis=1)
    size = lax.axis_size("plane")
    up = [(i, i + 1) for i in range(size - 1)]
    before = lax.ppermute(piece[-EDGE:], "plane", up)
    after = lax.ppermute(piece[:EDGE], "plane", [(j, i) for i, j in up])
    tall = jnp.concatenate([piece, after, before], axis=0)
    gap = jnp.zeros((tall.shape[0], LANE - 2 * EDGE), jnp.float32)
    return jnp.concatenate([tall[:, EDGE:], gap, tall[:, :EDGE]], axis=1)


def body(velocity, levels, fraction, bed_height):
    _, layers, rows, cols = velocity.shape
    tiles = rows // SUB
    tall = tiles + 1
    lanes = cols // LANE
    spans = lax.axis_size("span")
    walls = lax.axis_size("wall")
    assert walls == 2 and layers * 2 * EDGE == LANE
    bed_in = spans == 2 and bed_height.shape == (SUB, 2 * cols)
    count = 3 * layers // 2 + 1 + (bed_height.shape[1] // cols if bed_in else 0)
    dma = pltpu.SemaphoreType.DMA
    sheet = (3, layers, SUB, cols)
    send_a, send_b, send_z = call(
        functools.partial(pack_kernel, layers, bed_in),
        [(count, SUB, cols), (count, SUB, cols), (3, 2, rows, cols)],
        [velocity, levels, fraction, bed_height],
        [pltpu.VMEM(sheet, jnp.float32), pltpu.VMEM(sheet, jnp.float32), dma((3,))],
        any_inputs=(0,),
        flops=1,
        moved=1_000_000,
        limit=10,
    )
    plane_a, plane_b = pairings("plane")
    got_a = lax.ppermute(send_a, "plane", plane_a)
    got_b = lax.ppermute(send_b, "plane", plane_b)
    got_z = lax.ppermute(send_z, "wall", pairings("wall")[0])
    deep = (3, layers + 4, rows, cols)
    new, shear, edge = call(
        functools.partial(inner_kernel, layers),
        [velocity.shape, (2, rows, cols), (2, 5, tiles, SUB, LANE)],
        [velocity, levels, fraction],
        [pltpu.VMEM(deep, jnp.float32), pltpu.VMEM(deep, jnp.float32)],
        flops=20_000_000,
        moved=3_000_000,
    )
    span_lists = [p for p in pairings("span") if p]
    message = (5 * tall + (4 * lanes if bed_in else 0), SUB, LANE)
    unpacked = call(
        functools.partial(unpack_kernel, layers, count, bed_in),
        [sheet, (2, SUB, cols), (2, 5 * tall, SUB, LANE)] + [message] * len(span_lists),
        [got_a, got_b, edge, bed_height],
        moved=1_000_000,
        limit=10,
    )
    halo, flat, full = unpacked[:3]
    messages = unpacked[3:]
    got = [lax.ppermute(m, "span", pairs) for m, pairs in zip(messages, span_lists)]
    shallow = (3, layers + 4, SUB, cols)
    new_top, new_bottom, strip_shear = call(
        functools.partial(strip_kernel, layers),
        [sheet, sheet, (2, 2, SUB, cols)],
        [velocity, levels, fraction, halo, flat],
        [pltpu.VMEM(sheet, jnp.float32)] * 2 + [pltpu.VMEM(shallow, jnp.float32)] * 2 + [dma((2,))],
        any_inputs=(0,),
        flops=10_000_000,
        moved=2_000_000,
    )
    shear_count = 2 * tall * (lanes + 1)
    out_count = shear_count + (8 * lanes if bed_in else 0)
    fresh, mine = call(
        functools.partial(side_kernel, layers, len(got), bed_in),
        [(2, 3, tall * SUB, LANE), (out_count, SUB, LANE)],
        [full, shear, strip_shear] + got + [messages[0]],
        moved=1_000_000,
        limit=10,
    )
    theirs = lax.ppermute(mine, "wall", pairings("wall")[0])
    (velocity_next,) = call(
        functools.partial(merge_kernel, layers),
        [velocity.shape],
        [new, new_top, new_bottom, fresh, got_z, levels, fraction],
        flops=2_000_000,
        moved=4_000_000,
    )
    extra = [] if bed_in else [bed_around(bed_height, rows, cols)]
    (bed_next,) = call(
        functools.partial(bed_kernel, tall, lanes, bed_in),
        [(rows, cols)],
        [mine, theirs] + extra,
        moved=1_000_000,
        limit=10,
    )
    return velocity_next, bed_next


def solution(mesh):
    return jax.shard_map(
        body,
        mesh=mesh,
        in_specs=(
            P("groups", "wall", "plane", "span"),
            P(("groups", "plane"), "span"),
            P(("groups", "plane"), "span"),
            P(("groups", "plane", "span", "wall"), None),
        ),
        out_specs=(P("groups", "wall", "plane", "span"), P(("groups", "plane"), "span")),
        check_vma=False,
    )
```

```python
import functools

import jax
import jax.numpy as jnp
from jax import lax
from jax.experimental import pallas as pl
from jax.experimental.pallas import tpu as pltpu
from jax.sharding import PartitionSpec as P

time_step = 0.1
bed_step = 0.4
slope_rate = 0.25
threshold_sq = 0.25
gain = time_step / 12.0
EDGE = 4
SUB = 8
LANE = 128
VMEM = pltpu.VMEM
MIB = 1024 * 1024


def call(kernel, outs, ins, scratch=(), any_inputs=(), any_outputs=(), flops=0, moved=0, limit=20, aliases=None):
    specs = [pl.BlockSpec(memory_space=pl.ANY if i in any_inputs else VMEM) for i in range(len(ins))]
    shapes = [jax.ShapeDtypeStruct(s, jnp.float32) for s in outs]
    return pl.pallas_call(
        kernel,
        out_shape=shapes,
        in_specs=specs,
        out_specs=[pl.BlockSpec(memory_space=pl.ANY if i in any_outputs else VMEM) for i in range(len(outs))],
        scratch_shapes=list(scratch),
        input_output_aliases=aliases or {},
        cost_estimate=pl.CostEstimate(flops=flops, bytes_accessed=moved, transcendentals=0),
        compiler_params=pltpu.CompilerParams(vmem_limit_bytes=limit * MIB),
    )(*ins)


def iota(shape, dim):
    return lax.broadcasted_iota(jnp.int32, shape, dim)


def ahead(x, step, axis):
    return pltpu.roll(x, (-step) % x.shape[axis], axis)


def sweep(flux, b, axis):
    a = 8.0 * flux
    return ahead((b - a) + ahead(flux, 1, axis), 1, axis) + ahead((b + a) - ahead(flux, -1, axis), -1, axis)


def opened_at(level, fraction, layer):
    return jnp.where(level == layer, fraction, jnp.where(layer > level, 1.0, 0.0))


def even(axis):
    return lax.rem(lax.axis_index(axis), 2) == 0


def brick(read, level, fraction, base, layers, q_ref, f_ref, write, extra, unroll):
    rows, cols = level.shape
    blank = jnp.zeros((rows, cols), jnp.float32)
    for c in range(3):
        for z in (0, 1, layers + 2, layers + 3):
            q_ref[c, z] = blank
            f_ref[c, z] = blank
    cut_gain = fraction * gain
    scale = 1.0 / (0.5 + fraction)

    def prepare(z, carry):
        vel = [read(c, z) for c in range(3)]
        opened = opened_at(level, fraction, (base + z).astype(jnp.float32))
        for c in range(3):
            q = opened * vel[c]
            q_ref[c, z + 2] = q
            f_ref[c, z + 2] = vel[2] * q
        return carry

    lax.fori_loop(0, layers, prepare, 0, unroll=4)

    def vertical(c, z):
        near = f_ref[c, z + 3] - f_ref[c, z + 1]
        both = q_ref[c, z + 3] + q_ref[c, z + 1]
        return 6.0 * both - 8.0 * near + (f_ref[c, z + 4] - f_ref[c, z])

    def outside(z):
        hit = level == (base + z).astype(jnp.float32)
        found = []
        for c in range(2):
            total = blank
            for offset, weight_f, weight_q in ((1, -8.0, 6.0), (-1, 8.0, 6.0), (2, 1.0, 0.0), (-2, -1.0, 0.0)):
                at = z + offset
                if 0 <= at < layers:
                    total = total + weight_f * f_ref[c, at + 2]
                    if weight_q:
                        total = total + weight_q * q_ref[c, at + 2]
            found.append(jnp.where(hit, cut_gain * total, 0.0))
        return found

    sums = extra
    for z in (-2, -1, layers, layers + 1):
        found = outside(z)
        sums = [s + f for s, f in zip(sums, found)]

    def update(z, sums):
        vel = [read(c, z) for c in range(3)]
        q = [q_ref[c, z + 2] for c in range(3)]
        layer = (base + z).astype(jnp.float32)
        opened = opened_at(level, fraction, layer)
        hit = level == layer
        weight = gain * opened
        cross = vel[0] * q[1]
        along_x = (vel[0] * q[0], cross, f_ref[0, z + 2])
        along_y = (cross, vel[1] * q[1], f_ref[1, z + 2])
        sums = list(sums)
        for c in range(3):
            b = 6.0 * q[c]
            total = vertical(c, z) - 6.0 * b
            total = total + sweep(along_x[c], b, 1) + sweep(along_y[c], b, 0)
            fresh = vel[c] + weight * total
            write(c, z, fresh)
            if c < 2:
                sums[c] = sums[c] + jnp.where(hit, fresh, 0.0)
        return tuple(sums)

    sums = lax.fori_loop(0, layers, update, tuple(sums), unroll=unroll)
    return [s * scale for s in sums]


def beyond_terms(tile, level, fraction, base, layers, forward):
    near = pltpu.roll(level, SUB - 1, 0) if forward else pltpu.roll(level, 1, 0)
    far = pltpu.roll(level, SUB - 2, 0) if forward else pltpu.roll(level, 2, 0)
    sign = 1.0 if forward else -1.0
    one = [jnp.zeros(level.shape, jnp.float32)] * 2
    two = list(one)
    for z in range(layers):
        layer = (base + z).astype(jnp.float32)
        opened = opened_at(level, fraction, layer)
        near_hit, far_hit = near == layer, far == layer
        for c in range(2):
            q = opened * tile[c, z]
            flux = sign * (tile[1, z] * q)
            one[c] = one[c] + jnp.where(near_hit, 6.0 * q + 8.0 * flux, 0.0)
            two[c] = two[c] - jnp.where(far_hit, flux, 0.0)
    sub = iota(level.shape, 0)
    source = SUB - 3 if forward else 2
    past = source - 1 if forward else source + 1
    shift = 1 if forward else SUB - 1
    shift_two = 2 if forward else SUB - 2
    found = []
    for c in range(2):
        a = pltpu.roll(jnp.where(sub == source, one[c], 0.0), shift, 0)
        b = pltpu.roll(jnp.where((sub == source) | (sub == past), two[c], 0.0), shift_two, 0)
        found.append(a + b)
    return found


def pack_kernel(layers, bed_in, vel_in, lev_in, frac_in, bed_from, a_ref, b_ref, z_ref, vel, flat, bed, lev, sems):
    _, rows, cols = flat.shape
    wall = lax.axis_index("wall")
    base = wall * layers
    small = [
        pltpu.make_async_copy(lev_in, lev, sems.at[0]),
        pltpu.make_async_copy(frac_in, flat.at[1], sems.at[1]),
        pltpu.make_async_copy(bed_from, bed, sems.at[2]),
    ]
    pieces = []
    for i, (start, size) in enumerate(((0, SUB), (rows - SUB, SUB), (SUB, rows - 2 * SUB))):
        at = pl.ds(start, size)
        pieces.append(pltpu.make_async_copy(vel_in.at[:, :, at, :], vel.at[:, :, at, :], sems.at[3 + i]))
    for copy in small + pieces:
        copy.start()
    sub = iota((SUB, cols), 0)
    pair = sub // 2
    is_even = even("plane")

    def put(n, low, high):
        a_ref[n] = jnp.where(is_even, low, high)
        b_ref[n] = jnp.where(is_even, high, low)

    def stack(fields, place):
        tile = jnp.zeros((SUB, cols), jnp.float32)
        for i, field in enumerate(fields):
            tile = jnp.where(pair == i, pltpu.roll(field, (2 * i + place) % SUB, 0), tile)
        return tile

    for copy in small:
        copy.wait()
    flat[0] = lev[...].astype(jnp.float32)
    low_lev, low_frac = flat[0, rows - SUB :], flat[1, rows - SUB :]
    high_lev, high_frac = flat[0, :SUB], flat[1, :SUB]
    count = 3 * layers // 4
    if bed_in:
        halves = [bed[:, i * cols : (i + 1) * cols] for i in range(bed.shape[1] // cols)]
        put(count + 1, stack(halves, 2), stack(halves, 0))
    for copy in pieces[:2]:
        copy.wait()
    top = vel.at[:, :, pl.ds(0, SUB), :]
    bottom = vel.at[:, :, pl.ds(rows - SUB, SUB), :]
    for c in range(3):
        for k in range(layers // 4):
            low = stack([bottom[c, 4 * k + i] for i in range(4)], 2)
            high = stack([top[c, 4 * k + i] for i in range(4)], 0)
            put(c * (layers // 4) + k, low, high)
    low_far = beyond_terms(bottom, low_lev, low_frac, base, layers, True)
    high_far = beyond_terms(top, high_lev, high_frac, base, layers, False)
    put(count, stack([low_lev, low_frac] + low_far, 2), stack([high_lev, high_frac] + high_far, 0))
    pieces[2].wait()
    start = jnp.where(wall == 0, layers - 2, 0)
    for c in range(3):
        for z in range(2):
            z_ref[c, z] = vel[c, start + z]


def gather_edges(read, layers, rows, cols, put):
    lane = iota((rows, LANE), 1)
    column = lax.rem(lane, 2 * EDGE)
    for c in range(3):
        right = jnp.zeros((rows, LANE), jnp.float32)
        left = right
        for z in range(layers):
            group = (lane // (2 * EDGE)) == z
            field = read(c, z)
            last = field[:, cols - LANE :]
            first = field[:, :LANE]
            at = 2 * EDGE * z
            right = jnp.where(group, pltpu.roll(last, (at - (LANE - EDGE)) % LANE, 1), right)
            left = jnp.where(group, pltpu.roll(first, (at + EDGE) % LANE, 1), left)
        put(0, c, jnp.where(column < EDGE, right, 0.0))
        put(1, c, jnp.where(column >= EDGE, left, 0.0))


def repeat_edges(field, rows, cols):
    lane = iota((rows, LANE), 1)
    right = jnp.where(lane < EDGE, pltpu.roll(field[:, cols - LANE :], EDGE, 1), 0.0)
    left = pltpu.roll(jnp.where(lane < EDGE, field[:, :LANE], 0.0), EDGE, 1)
    step = 2 * EDGE
    while step < LANE:
        right = right + pltpu.roll(right, step, 1)
        left = left + pltpu.roll(left, step, 1)
        step *= 2
    return right, left


def inner_kernel(layers, vel, flat, new_ref, shear_ref, edge_ref, q_ref, f_ref, split_ref, band_ref, x_ref):
    _, rows, cols = flat.shape
    base = lax.axis_index("wall") * layers
    lanes = cols // LANE
    tall = iota((cols, cols), 0) - iota((cols, cols), 1)
    flux_band = jnp.where(tall == 1, -8.0, jnp.where(tall == -1, 8.0, 0.0))
    flux_band = flux_band + jnp.where(tall == 2, 1.0, jnp.where(tall == -2, -1.0, 0.0))
    field_band = jnp.where(jnp.abs(tall) == 1, 6.0, jnp.where(tall == 0, -36.0, 0.0))
    for i, band in enumerate((flux_band, flux_band, field_band, field_band)):
        band_ref[i * cols : (i + 1) * cols] = band.astype(jnp.bfloat16)
    blank = jnp.zeros((rows, cols), jnp.float32)
    for c in range(3):
        for z in (0, 1, layers + 2, layers + 3):
            q_ref[c, z] = blank
            f_ref[c, z] = blank

    def halves(x):
        high = x.astype(jnp.bfloat16)
        return high, (x - high.astype(jnp.float32)).astype(jnp.bfloat16)

    def prepare(z, carry):
        layer = (base + z).astype(jnp.float32)
        at = pl.ds(pl.multiple_of(z * rows, rows), rows)
        for k in range(lanes):
            cut = slice(k * LANE, (k + 1) * LANE)
            opened = opened_at(flat[0, :, cut], flat[1, :, cut], layer)
            vel_x, vel_z = vel[0, z, :, cut], vel[2, z, :, cut]
            for c in range(3):
                q = opened * vel[c, z, :, cut]
                q_ref[c, z + 2, :, cut] = q
                f_ref[c, z + 2, :, cut] = vel_z * q
                parts = halves(vel_x * q) + halves(q)
                for i, part in enumerate(parts):
                    split_ref[c, at, i * cols + k * LANE : i * cols + (k + 1) * LANE] = part
        return carry

    lax.fori_loop(0, layers, prepare, 0)
    for c in range(3):
        x_ref[c] = jnp.dot(split_ref[c], band_ref[...], preferred_element_type=jnp.float32)

    def outside(z, c, cut):
        total = jnp.zeros((rows, LANE), jnp.float32)
        for offset, weight in ((1, -8.0), (-1, 8.0), (2, 1.0), (-2, -1.0)):
            at = z + offset
            if 0 <= at < layers:
                total = total + weight * f_ref[c, at + 2, :, cut]
                if abs(offset) == 1:
                    total = total + 6.0 * q_ref[c, at + 2, :, cut]
        hit = flat[0, :, cut] == (base + z).astype(jnp.float32)
        return jnp.where(hit, gain * flat[1, :, cut] * total, 0.0)

    sums = []
    for k in range(lanes):
        for c in range(2):
            sums.append(sum(outside(z, c, slice(k * LANE, (k + 1) * LANE)) for z in (-2, -1, layers, layers + 1)))

    def update(z, sums):
        sums = list(sums)
        layer = (base + z).astype(jnp.float32)
        at = pl.ds(pl.multiple_of(z * rows, rows), rows)
        for k in range(lanes):
            cut = slice(k * LANE, (k + 1) * LANE)
            level = flat[0, :, cut]
            weight = gain * opened_at(level, flat[1, :, cut], layer)
            hit = level == layer
            vel_y = vel[1, z, :, cut]
            for c in range(3):
                q = q_ref[c, z + 2, :, cut]
                flux = f_ref[1, z + 2, :, cut] if c == 2 else vel_y * q
                total = x_ref[c, at, cut] + sweep(flux, 6.0 * q, 0)
                near = f_ref[c, z + 3, :, cut] - f_ref[c, z + 1, :, cut]
                both = q_ref[c, z + 3, :, cut] + q_ref[c, z + 1, :, cut]
                total = total + (6.0 * both - 8.0 * near + (f_ref[c, z + 4, :, cut] - f_ref[c, z, :, cut]))
                fresh = vel[c, z, :, cut] + weight * total
                new_ref[c, z, :, cut] = fresh
                if c < 2:
                    sums[2 * k + c] = sums[2 * k + c] + jnp.where(hit, fresh, 0.0)
        return tuple(sums)

    sums = lax.fori_loop(0, layers, update, tuple(sums))
    for k in range(lanes):
        cut = slice(k * LANE, (k + 1) * LANE)
        scale = 1.0 / (0.5 + flat[1, :, cut])
        for c in range(2):
            shear_ref[c, :, cut] = sums[2 * k + c] * scale

    def put(side, n, value):
        edge_ref[side, n] = value.reshape(rows // SUB, SUB, LANE)

    gather_edges(lambda c, z: vel[c, z], layers, rows, cols, put)
    for n in range(2):
        right, left = repeat_edges(flat[n], rows, cols)
        put(0, 3 + n, right)
        put(1, 3 + n, left)


def unpack_kernel(layers, bed_in, got_a, got_b, edge, bed, got_z, halo_ref, beside_ref, full_ref, far_ref, *messages):
    cols = halo_ref.shape[3]
    tiles = edge.shape[2]
    tall = tiles + 1
    sub = iota((SUB, cols), 0)
    is_even = even("plane")

    def sides(n):
        one, two = got_a[n], got_b[n]
        return jnp.where(is_even, one, two), jnp.where(is_even, two, one)

    def spread(n, fields):
        low, high = sides(n)
        found = []
        for i in range(fields):
            above = pltpu.roll(high, (SUB - 2 - 2 * i) % SUB, 0)
            below = pltpu.roll(low, (-2 * i) % SUB, 0)
            found.append(jnp.where(sub < 2, below, jnp.where(sub >= SUB - 2, above, 0.0)))
        return found

    for c in range(3):
        for k in range(layers // 4):
            for i, tile in enumerate(spread(c * (layers // 4) + k, 4)):
                halo_ref[c, 4 * k + i] = tile
    count = 3 * layers // 4
    beside = spread(count, 4)
    for i, tile in enumerate(beside):
        beside_ref[i] = tile

    def put(side, n, value):
        full_ref[side, n * tall + tiles] = value

    gather_edges(lambda c, z: halo_ref[c, z], layers, SUB, cols, put)
    for n in range(2):
        right, left = repeat_edges(beside[n], SUB, cols)
        put(0, 3 + n, right)
        put(1, 3 + n, left)
    for side in range(2):
        for n in range(5):
            for t in range(tiles):
                full_ref[side, n * tall + t] = edge[side, n, t]
    lane = iota((SUB, LANE), 1)
    group = lane // (2 * EDGE)
    far_right = [repeat_edges(tile, SUB, cols) for tile in beside[2:]]
    for side in range(2):
        far_ref[side] = jnp.where(group == 0, far_right[0][side], jnp.where(group == 1, far_right[1][side], 0.0))
    right_first = even("span")
    packed = []
    for side, shift in ((0, EDGE), (1, LANE - EDGE)):
        for t in range(tall):
            u, v, w, level, fraction = [full_ref[side, n * tall + t] for n in range(5)]
            last = jnp.where(group == 0, level, jnp.where(group == 1, fraction, 0.0))
            packed.append(u + pltpu.roll(v, shift, 1))
            packed.append(w + pltpu.roll(last, shift, 1))
    for i, message in enumerate(messages):
        is_right = right_first if i == 0 else jnp.logical_not(right_first)
        for n in range(2 * tall):
            message[n] = jnp.where(is_right, packed[n], packed[2 * tall + n])
        message[2 * tall] = jnp.where(is_right, far_ref[0], far_ref[1])
    if bed_in:
        used = 2 * tall + 1
        parts = bed.shape[1] // LANE
        for i in range(parts):
            messages[0][used + i] = bed[:, i * LANE : (i + 1) * LANE]
        per = cols // LANE
        for i, tile in enumerate(spread(count + 1, bed.shape[1] // cols)):
            for j in range(per):
                messages[0][used + parts + i * per + j] = tile[:, j * LANE : (j + 1) * LANE]


def strip_kernel(layers, vel, flat, halo, beside, top_ref, bottom_ref, shear_ref, q_ref, f_ref):
    _, rows, cols = flat.shape
    base = lax.axis_index("wall") * layers
    sub = iota((SUB, cols), 0)
    for side, new in ((0, top_ref), (1, bottom_ref)):
        inside = sub < EDGE if side == 0 else sub >= EDGE
        outer = sub >= SUB - 2 if side == 0 else sub < 2
        first = 0 if side == 0 else rows - SUB
        at = slice(first, first + SUB)
        levels = jnp.where(inside, flat[0, at], beside[0])
        fraction = jnp.where(inside, flat[1, at], beside[1])
        extra = [jnp.where(outer, gain * fraction * beside[2 + c], 0.0) for c in range(2)]

        def read(c, z):
            return jnp.where(inside, vel[c, z, at], halo[c, z])

        def write(c, z, value):
            new[c, z] = value

        sums = brick(read, levels, fraction, base, layers, q_ref, f_ref, write, extra, 4)
        shear_ref[side, 0] = sums[0]
        shear_ref[side, 1] = sums[1]


def column_strip(vel, levels, fraction, extra, base, layers):
    shape = levels.shape
    width = 2 * EDGE
    here = iota(shape, 1) // width
    layer = (here + base).astype(jnp.float32)
    opened = opened_at(levels, fraction, layer)
    hit = levels == layer
    hit_down = levels == layer - layers
    hit_up = levels == layer + layers
    scale = 1.0 / (0.5 + fraction)
    fresh, shear = [], []
    for c in range(3):
        q = opened * vel[c]
        b = 6.0 * q
        total = sweep(vel[0] * q, b, 1) + sweep(vel[1] * q, b, 0) - 6.0 * b
        flux = vel[2] * q
        plus = ahead(b - 8.0 * flux, width, 1)
        minus = ahead(b + 8.0 * flux, -width, 1)
        plus_far = ahead(flux, 2 * width, 1)
        minus_far = ahead(flux, -2 * width, 1)
        total = total + jnp.where(here <= layers - 2, plus, 0.0) + jnp.where(here <= layers - 3, plus_far, 0.0)
        total = total + jnp.where(here >= 1, minus, 0.0) - jnp.where(here >= 2, minus_far, 0.0)
        value = vel[c] + gain * opened * total
        fresh.append(value)
        if c < 2:
            down = jnp.where(here > layers - 2, plus, 0.0) + jnp.where(here > layers - 3, plus_far, 0.0)
            up = jnp.where(here < 1, minus, 0.0) - jnp.where(here < 2, minus_far, 0.0)
            part = jnp.where(hit, value, 0.0)
            part = part + gain * fraction * (jnp.where(hit_down, down, 0.0) + jnp.where(hit_up, up, 0.0))
            step = LANE // 2
            while step >= width:
                part = part + pltpu.roll(part, step, 1)
                step //= 2
            more = extra if c == 0 else ahead(extra, width, 1)
            more = jnp.concatenate([jnp.zeros((shape[0] - SUB, LANE), jnp.float32), more], axis=0)
            shear.append((part + gain * fraction * more) * scale)
    return fresh, shear


def everywhere(x):
    step = 2 * EDGE
    x = jnp.where(iota(x.shape, 1) < step, x, 0.0)
    while step < LANE:
        x = x + pltpu.roll(x, step, 1)
        step *= 2
    return x


def side_kernel(layers, spans, bed_in, full, far, shear, strips, *rest):
    got = rest[:spans]
    rest = rest[spans:]
    own_message = rest[0]
    fresh_ref, out_ref = rest[1:]
    _, rows, cols = shear.shape
    tiles = rows // SUB
    tall = tiles + 1
    base = lax.axis_index("wall") * layers
    right_first = even("span")
    results = []
    column = lax.rem(iota((tall * SUB, LANE), 1), 2 * EDGE)
    fresh_sides = []
    for side in range(2):
        first = right_first if side == 0 else jnp.logical_not(right_first)

        def other(n):
            return jnp.where(first, got[0][n], got[1][n] if spans > 1 else 0.0)

        given = column >= EDGE if side == 0 else column < EDGE
        back = EDGE if side == 0 else LANE - EDGE
        both = [jnp.concatenate([other(2 * t + i) for t in range(tall)], axis=0) for i in range(2)]
        turned = [jnp.where(given, pltpu.roll(b, back, 1), 0.0) for b in both]
        theirs = [jnp.where(given, both[0], 0.0), turned[0], jnp.where(given, both[1], 0.0)]
        theirs += [everywhere(turned[1]), everywhere(ahead(turned[1], 2 * EDGE, 1))]
        fields = []
        for n in range(5):
            own = full[side, n * tall : (n + 1) * tall].reshape(tall * SUB, LANE)
            fields.append(own + theirs[n])
        extra = far[side] + other(2 * tall)
        fresh, edge_shear = column_strip(fields[:3], fields[3], fields[4], extra, base, layers)
        fresh_sides.append(fresh)
        results.append(edge_shear)
    for c in range(3):
        fresh_ref[c] = jnp.where(column < EDGE, fresh_sides[0][c], fresh_sides[1][c])[:rows]
    lane = iota((SUB, LANE), 1)
    sub = iota((SUB, LANE), 0)
    lanes = cols // LANE
    for c in range(2):
        right, left = results[0][c], results[1][c]
        for t in range(tall):
            at = slice(t * SUB, (t + 1) * SUB)
            for k in range(lanes):
                cut = slice(k * LANE, (k + 1) * LANE)
                if t == tiles:
                    piece = jnp.where(sub < EDGE, strips[1, c, :, cut], strips[0, c, :, cut])
                    piece = jnp.where((sub < 2) | (sub >= SUB - 2), piece, 0.0)
                else:
                    piece = shear[c, at, cut]
                    if t == 0:
                        piece = jnp.where(sub < 2, strips[0, c, :, cut], piece)
                    if t == tiles - 1:
                        piece = jnp.where(sub >= SUB - 2, strips[1, c, :, cut], piece)
                if k == 0:
                    piece = jnp.where(lane < 2, pltpu.roll(left[at], LANE - EDGE, 1), piece)
                if k == lanes - 1:
                    piece = jnp.where(lane >= LANE - 2, pltpu.roll(right[at], LANE - EDGE, 1), piece)
                out_ref[(c * tall + t) * (lanes + 1) + k] = piece
            beyond = jnp.where(lane < 2, pltpu.roll(right[at], LANE - EDGE, 1), 0.0)
            beyond = jnp.where(lane >= LANE - 2, pltpu.roll(left[at], LANE - EDGE, 1), beyond)
            out_ref[(c * tall + t) * (lanes + 1) + lanes] = beyond
    if bed_in:
        used = 2 * tall * (lanes + 1)
        start = 2 * tall + 1
        count = own_message.shape[0] - start
        for i in range(count):
            out_ref[used + i] = own_message[start + i]
            out_ref[used + count + i] = got[0][start + i]


def merge_kernel(layers, new, strip_top, strip_bottom, fresh, far, flat, final, out_ref, sems):
    _, rows, cols = flat.shape
    lanes = cols // LANE
    wall = lax.axis_index("wall")
    lower = wall == 0
    sub = iota((SUB, LANE), 0)
    lane = iota((SUB, LANE), 1)
    levels = flat[0]
    fraction = flat[1]
    base = wall * layers
    near_from = jnp.where(lower, 0, 1)
    far_from = 1 - near_from
    near_to = jnp.where(lower, layers - 1, 0)
    far_to = jnp.where(lower, layers - 2, 1)
    sign = jnp.where(lower, -1.0, 1.0)
    other = jnp.where(lower, layers, 0)
    near_open = opened_at(levels, fraction, (other + jnp.where(lower, 0, layers - 1)).astype(jnp.float32))
    far_open = opened_at(levels, fraction, (other + jnp.where(lower, 1, layers - 2)).astype(jnp.float32))
    near_gain = gain * opened_at(levels, fraction, (base + near_to).astype(jnp.float32))
    far_gain = gain * opened_at(levels, fraction, (base + far_to).astype(jnp.float32))
    near_w, far_w = far[2, near_from], far[2, far_from]
    copies = []
    for c in range(3):
        for z in range(layers):
            for t in range(rows // SUB):
                at = slice(t * SUB, (t + 1) * SUB)
                side = pltpu.roll(fresh[c, at], (LANE - EDGE - 2 * EDGE * z) % LANE, 1)
                for k in range(lanes):
                    cut = slice(k * LANE, (k + 1) * LANE)
                    piece = new[c, z, at, cut]
                    if t == 0:
                        piece = jnp.where(sub < 2, strip_top[c, z, :, cut], piece)
                    if t == rows // SUB - 1:
                        piece = jnp.where(sub >= SUB - 2, strip_bottom[c, z, :, cut], piece)
                    if k == 0:
                        piece = jnp.where(lane < 2, side, piece)
                    if k == lanes - 1:
                        piece = jnp.where(lane >= LANE - 2, side, piece)
                    out_ref[c, z, at, cut] = piece
        near_q = near_open * far[c, near_from]
        near_f = sign * (near_w * near_q)
        far_f = sign * (far_w * (far_open * far[c, far_from]))
        out_ref[c, near_to] = out_ref[c, near_to] + near_gain * (6.0 * near_q + 8.0 * near_f - far_f)
        out_ref[c, far_to] = out_ref[c, far_to] - far_gain * near_f
        part = layers // 4
        for i in range(4):
            at = pl.ds(i * part, part)
            copies.append(pltpu.make_async_copy(out_ref.at[c, at], final.at[c, at], sems.at[4 * c + i]))
            copies[-1].start()
    for copy in copies:
        copy.wait()


def bed_kernel(tall, lanes, bed_in, mine, theirs, *rest):
    out_ref = rest[-1]
    rows = (tall - 1) * SUB
    wide = (lanes + 1) * LANE
    span = lax.axis_index("span")
    wall = lax.axis_index("wall")
    plane = lax.axis_index("plane")

    def sheared(c):
        whole = []
        for t in range(tall):
            first = (c * tall + t) * (lanes + 1)
            whole.append(
                jnp.concatenate([mine[first + k] + theirs[first + k] for k in range(lanes + 1)], axis=1)
            )
        return jnp.concatenate(whole, axis=0)

    shear_x, shear_y = sheared(0), sheared(1)
    if bed_in:
        used = 2 * tall * (lanes + 1)
        parts = 2 * lanes

        def tile_of(s, w, which):
            pieces = []
            for k in range(parts):
                own = used + which * parts + k
                across = own + 2 * parts
                from_mine = jnp.where(span == s, mine[own], mine[across])
                from_theirs = jnp.where(span == s, theirs[own], theirs[across])
                pieces.append(jnp.where(wall == w, from_mine, from_theirs))
            return pieces

        def window(pieces):
            lane = iota((SUB, LANE), 1)
            low = span == 0
            inside = [jnp.where(low, pieces[k], pieces[lanes + k]) for k in range(lanes)]
            beyond = jnp.where(
                low,
                jnp.where(lane < LANE // 2, pieces[lanes], 0.0),
                jnp.where(lane < LANE // 2, 0.0, pieces[lanes - 1]),
            )
            return jnp.concatenate(inside + [beyond], axis=1)

        sub = iota((SUB, LANE), 0)
        whole = [window(tile_of(s, w, 0)) for s in range(2) for w in range(2)]
        after = tile_of(0, 0, 1)
        before = tile_of(1, 1, 1)
        whole.append(window([jnp.where(sub < EDGE, a, b) for a, b in zip(after, before)]))
        bed = jnp.concatenate(whole, axis=0)
    else:
        bed = rest[0][...]
    square = shear_x * shear_x + shear_y * shear_y
    factor = jnp.maximum(square - threshold_sq, 0.0) / (square + threshold_sq)
    load_x = shear_x * factor
    load_y = shear_y * factor
    divergence = 0.5 * (ahead(load_x, 1, 1) - ahead(load_x, -1, 1)) + 0.5 * (
        ahead(load_y, 1, 0) - ahead(load_y, -1, 0)
    )
    row = iota((tall * SUB, wide), 0)
    col = iota((tall * SUB, wide), 1)
    last_plane = plane == lax.axis_size("plane") - 1
    last_span = span == lax.axis_size("span") - 1
    row_low = jnp.where(last_plane, rows, rows + EDGE)
    row_high = jnp.where(plane == 0, rows + SUB, rows + EDGE)
    col_low = jnp.where(last_span, wide - LANE, wide - LANE // 2)
    col_high = jnp.where(span == 0, wide, wide - LANE // 2)
    valid = ((row < row_low) | (row >= row_high)) & ((col < col_low) | (col >= col_high))

    def step(height):
        around = ahead(height, 1, 0) + ahead(height, -1, 0) + ahead(height, 1, 1) + ahead(height, -1, 1)
        return height - bed_step * divergence + bed_step * slope_rate * (around - 4.0 * height)

    first = jnp.where(valid, step(bed), 0.0)
    out_ref[...] = step(first)[:rows, : lanes * LANE]


def pairings(axis):
    size = lax.axis_size(axis)
    lists = []
    for start in (0, 1):
        found = []
        for i in range(start, size - 1, 2):
            found += [(i, i + 1), (i + 1, i)]
        lists.append(found)
    return lists


def bed_around(bed_height, rows, cols):
    spans = lax.axis_size("span")
    whole = lax.all_gather(bed_height, ("span", "wall"), axis=0, tiled=True)
    padded = jnp.pad(whole, ((0, 0), (EDGE, EDGE)))
    piece = lax.dynamic_slice_in_dim(padded, lax.axis_index("span") * cols, cols + 2 * EDGE, axis=1)
    size = lax.axis_size("plane")
    up = [(i, i + 1) for i in range(size - 1)]
    before = lax.ppermute(piece[-EDGE:], "plane", up)
    after = lax.ppermute(piece[:EDGE], "plane", [(j, i) for i, j in up])
    tall = jnp.concatenate([piece, after, before], axis=0)
    gap = jnp.zeros((tall.shape[0], LANE - 2 * EDGE), jnp.float32)
    return jnp.concatenate([tall[:, EDGE:], gap, tall[:, :EDGE]], axis=1)


def body(velocity, levels, fraction, bed_height):
    _, layers, rows, cols = velocity.shape
    tiles = rows // SUB
    tall = tiles + 1
    lanes = cols // LANE
    spans = lax.axis_size("span")
    walls = lax.axis_size("wall")
    assert walls == 2 and layers * 2 * EDGE == LANE
    bed_in = spans == 2 and bed_height.shape == (SUB, 2 * cols)
    count = 3 * layers // 4 + (2 if bed_in else 1)
    dma = pltpu.SemaphoreType.DMA
    sheet = (3, layers, SUB, cols)
    send_a, send_b, send_z, vel, flat, bed = call(
        functools.partial(pack_kernel, layers, bed_in),
        [(count, SUB, cols), (count, SUB, cols), (3, 2, rows, cols), velocity.shape, (2, rows, cols), bed_height.shape],
        [pltpu.with_memory_space_constraint(x, pltpu.HBM) for x in (velocity, levels, fraction, bed_height)],
        [pltpu.VMEM(levels.shape, jnp.int32), dma((6,))],
        any_inputs=(0, 1, 2, 3),
        moved=1_000_000,
        limit=10,
    )
    plane_a, plane_b = pairings("plane")
    got_a = lax.ppermute(send_a, "plane", plane_a)
    got_b = lax.ppermute(send_b, "plane", plane_b)
    got_z = lax.ppermute(send_z, "wall", pairings("wall")[0])
    deep = pltpu.VMEM((3, layers + 4, rows, cols), jnp.float32)
    new, shear, edge = call(
        functools.partial(inner_kernel, layers),
        [velocity.shape, (2, rows, cols), (2, 5, tiles, SUB, LANE)],
        [vel, flat],
        [deep, deep, pltpu.VMEM((3, layers * rows, 4 * cols), jnp.bfloat16), pltpu.VMEM((4 * cols, cols), jnp.bfloat16)]
        + [pltpu.VMEM((3, layers * rows, cols), jnp.float32)],
        flops=20_000_000,
        moved=3_000_000,
    )
    span_lists = [p for p in pairings("span") if p]
    message = (2 * tall + 1 + (4 * lanes if bed_in else 0), SUB, LANE)
    unpacked = call(
        functools.partial(unpack_kernel, layers, bed_in),
        [sheet, (4, SUB, cols), (2, 5 * tall, SUB, LANE), (2, SUB, LANE)] + [message] * len(span_lists),
        [got_a, got_b, edge, bed, got_z],
        any_inputs=(4,),
        moved=1_000_000,
        limit=10,
    )
    halo, beside, full, far = unpacked[:4]
    messages = unpacked[4:]
    got = [lax.ppermute(m, "span", pairs) for m, pairs in zip(messages, span_lists)]
    shallow = pltpu.VMEM((3, layers + 4, SUB, cols), jnp.float32)
    new_top, new_bottom, strip_shear = call(
        functools.partial(strip_kernel, layers),
        [sheet, sheet, (2, 2, SUB, cols)],
        [vel, flat, halo, beside],
        [shallow, shallow],
        flops=10_000_000,
        moved=2_000_000,
    )
    shear_count = 2 * tall * (lanes + 1)
    out_count = shear_count + (8 * lanes if bed_in else 0)
    fresh, mine = call(
        functools.partial(side_kernel, layers, len(got), bed_in),
        [(3, rows, LANE), (out_count, SUB, LANE)],
        [full, far, shear, strip_shear] + got + [messages[0]],
        moved=1_000_000,
        limit=10,
    )
    theirs = lax.ppermute(mine, "wall", pairings("wall")[0])
    (velocity_next,) = call(
        functools.partial(merge_kernel, layers),
        [velocity.shape],
        [new, new_top, new_bottom, fresh, got_z, flat],
        [pltpu.VMEM(velocity.shape, jnp.float32), dma((12,))],
        any_outputs=(0,),
        flops=2_000_000,
        moved=4_000_000,
    )
    extra = [] if bed_in else [bed_around(bed_height, rows, cols)]
    (bed_next,) = call(
        functools.partial(bed_kernel, tall, lanes, bed_in),
        [(rows, cols)],
        [mine, theirs] + extra,
        moved=1_000_000,
        limit=10,
    )
    return velocity_next, bed_next


def solution(mesh):
    return jax.shard_map(
        body,
        mesh=mesh,
        in_specs=(
            P("groups", "wall", "plane", "span"),
            P(("groups", "plane"), "span"),
            P(("groups", "plane"), "span"),
            P(("groups", "plane", "span", "wall"), None),
        ),
        out_specs=(P("groups", "wall", "plane", "span"), P(("groups", "plane"), "span")),
        check_vma=False,
    )
```

```python
import functools

import jax
import jax.numpy as jnp
from jax import lax
from jax.experimental import pallas as pl
from jax.experimental.pallas import tpu as pltpu
from jax.sharding import PartitionSpec as P

time_step = 0.1
bed_step = 0.4
slope_rate = 0.25
threshold_sq = 0.25
gain = time_step / 12.0
EDGE = 4
SUB = 8
LANE = 128
VMEM = pltpu.VMEM
MIB = 1024 * 1024


def call(kernel, outs, ins, scratch=(), any_inputs=(), any_outputs=(), flops=0, moved=0, limit=20, aliases=None):
    specs = [pl.BlockSpec(memory_space=pl.ANY if i in any_inputs else VMEM) for i in range(len(ins))]
    shapes = [jax.ShapeDtypeStruct(s, jnp.float32) for s in outs]
    return pl.pallas_call(
        kernel,
        out_shape=shapes,
        in_specs=specs,
        out_specs=[pl.BlockSpec(memory_space=pl.ANY if i in any_outputs else VMEM) for i in range(len(outs))],
        scratch_shapes=list(scratch),
        input_output_aliases=aliases or {},
        cost_estimate=pl.CostEstimate(flops=flops, bytes_accessed=moved, transcendentals=0),
        compiler_params=pltpu.CompilerParams(vmem_limit_bytes=limit * MIB),
    )(*ins)


def iota(shape, dim):
    return lax.broadcasted_iota(jnp.int32, shape, dim)


def ahead(x, step, axis):
    return pltpu.roll(x, (-step) % x.shape[axis], axis)


def sweep(flux, b, axis):
    a = 8.0 * flux
    return ahead((b - a) + ahead(flux, 1, axis), 1, axis) + ahead((b + a) - ahead(flux, -1, axis), -1, axis)


def opened_at(level, fraction, layer):
    return jnp.where(level == layer, fraction, jnp.where(layer > level, 1.0, 0.0))


def even(axis):
    return lax.rem(lax.axis_index(axis), 2) == 0


def brick(read, level, fraction, base, layers, q_ref, f_ref, write, extra, unroll):
    rows, cols = level.shape
    blank = jnp.zeros((rows, cols), jnp.float32)
    for c in range(3):
        for z in (0, 1, layers + 2, layers + 3):
            q_ref[c, z] = blank
            f_ref[c, z] = blank
    cut_gain = fraction * gain
    scale = 1.0 / (0.5 + fraction)

    def prepare(z, carry):
        vel = [read(c, z) for c in range(3)]
        opened = opened_at(level, fraction, (base + z).astype(jnp.float32))
        for c in range(3):
            q = opened * vel[c]
            q_ref[c, z + 2] = q
            f_ref[c, z + 2] = vel[2] * q
        return carry

    lax.fori_loop(0, layers, prepare, 0, unroll=4)

    def vertical(c, z):
        near = f_ref[c, z + 3] - f_ref[c, z + 1]
        both = q_ref[c, z + 3] + q_ref[c, z + 1]
        return 6.0 * both - 8.0 * near + (f_ref[c, z + 4] - f_ref[c, z])

    def outside(z):
        hit = level == (base + z).astype(jnp.float32)
        found = []
        for c in range(2):
            total = blank
            for offset, weight_f, weight_q in ((1, -8.0, 6.0), (-1, 8.0, 6.0), (2, 1.0, 0.0), (-2, -1.0, 0.0)):
                at = z + offset
                if 0 <= at < layers:
                    total = total + weight_f * f_ref[c, at + 2]
                    if weight_q:
                        total = total + weight_q * q_ref[c, at + 2]
            found.append(jnp.where(hit, cut_gain * total, 0.0))
        return found

    sums = extra
    for z in (-2, -1, layers, layers + 1):
        found = outside(z)
        sums = [s + f for s, f in zip(sums, found)]

    def update(z, sums):
        vel = [read(c, z) for c in range(3)]
        q = [q_ref[c, z + 2] for c in range(3)]
        layer = (base + z).astype(jnp.float32)
        opened = opened_at(level, fraction, layer)
        hit = level == layer
        weight = gain * opened
        cross = vel[0] * q[1]
        along_x = (vel[0] * q[0], cross, f_ref[0, z + 2])
        along_y = (cross, vel[1] * q[1], f_ref[1, z + 2])
        sums = list(sums)
        for c in range(3):
            b = 6.0 * q[c]
            total = vertical(c, z) - 6.0 * b
            total = total + sweep(along_x[c], b, 1) + sweep(along_y[c], b, 0)
            fresh = vel[c] + weight * total
            write(c, z, fresh)
            if c < 2:
                sums[c] = sums[c] + jnp.where(hit, fresh, 0.0)
        return tuple(sums)

    sums = lax.fori_loop(0, layers, update, tuple(sums), unroll=unroll)
    return [s * scale for s in sums]


def beyond_terms(tile, level, fraction, base, layers, forward):
    near = pltpu.roll(level, SUB - 1, 0) if forward else pltpu.roll(level, 1, 0)
    far = pltpu.roll(level, SUB - 2, 0) if forward else pltpu.roll(level, 2, 0)
    sign = 1.0 if forward else -1.0
    one = [jnp.zeros(level.shape, jnp.float32)] * 2
    two = list(one)
    for z in range(layers):
        layer = (base + z).astype(jnp.float32)
        opened = opened_at(level, fraction, layer)
        near_hit, far_hit = near == layer, far == layer
        for c in range(2):
            q = opened * tile[c, z]
            flux = sign * (tile[1, z] * q)
            one[c] = one[c] + jnp.where(near_hit, 6.0 * q + 8.0 * flux, 0.0)
            two[c] = two[c] - jnp.where(far_hit, flux, 0.0)
    sub = iota(level.shape, 0)
    source = SUB - 3 if forward else 2
    past = source - 1 if forward else source + 1
    shift = 1 if forward else SUB - 1
    shift_two = 2 if forward else SUB - 2
    found = []
    for c in range(2):
        a = pltpu.roll(jnp.where(sub == source, one[c], 0.0), shift, 0)
        b = pltpu.roll(jnp.where((sub == source) | (sub == past), two[c], 0.0), shift_two, 0)
        found.append(a + b)
    return found


def pack_kernel(layers, bed_in, vel_in, lev_in, frac_in, bed_from, a_ref, b_ref, vel, flat, bed, lev, sems):
    _, rows, cols = flat.shape
    wall = lax.axis_index("wall")
    base = wall * layers
    small = [
        pltpu.make_async_copy(lev_in, lev, sems.at[0]),
        pltpu.make_async_copy(frac_in, flat.at[1], sems.at[1]),
        pltpu.make_async_copy(bed_from, bed, sems.at[2]),
    ]
    pieces = []
    for i, (start, size) in enumerate(((0, SUB), (rows - SUB, SUB), (SUB, rows - 2 * SUB))):
        at = pl.ds(start, size)
        pieces.append(pltpu.make_async_copy(vel_in.at[:, :, at, :], vel.at[:, :, at, :], sems.at[3 + i]))
    for copy in small + pieces:
        copy.start()
    sub = iota((SUB, cols), 0)
    pair = sub // 2
    is_even = even("plane")

    def put(n, low, high):
        a_ref[n] = jnp.where(is_even, low, high)
        b_ref[n] = jnp.where(is_even, high, low)

    def stack(fields, place):
        tile = jnp.zeros((SUB, cols), jnp.float32)
        for i, field in enumerate(fields):
            tile = jnp.where(pair == i, pltpu.roll(field, (2 * i + place) % SUB, 0), tile)
        return tile

    for copy in small:
        copy.wait()
    flat[0] = lev[...].astype(jnp.float32)
    low_lev, low_frac = flat[0, rows - SUB :], flat[1, rows - SUB :]
    high_lev, high_frac = flat[0, :SUB], flat[1, :SUB]
    count = 3 * layers // 4
    if bed_in:
        halves = [bed[:, i * cols : (i + 1) * cols] for i in range(bed.shape[1] // cols)]
        put(count + 1, stack(halves, 2), stack(halves, 0))
    for copy in pieces[:2]:
        copy.wait()
    top = vel.at[:, :, pl.ds(0, SUB), :]
    bottom = vel.at[:, :, pl.ds(rows - SUB, SUB), :]
    for c in range(3):
        for k in range(layers // 4):
            low = stack([bottom[c, 4 * k + i] for i in range(4)], 2)
            high = stack([top[c, 4 * k + i] for i in range(4)], 0)
            put(c * (layers // 4) + k, low, high)
    low_far = beyond_terms(bottom, low_lev, low_frac, base, layers, True)
    high_far = beyond_terms(top, high_lev, high_frac, base, layers, False)
    put(count, stack([low_lev, low_frac] + low_far, 2), stack([high_lev, high_frac] + high_far, 0))
    pieces[2].wait()


def gather_edges(read, layers, rows, cols, put):
    lane = iota((rows, LANE), 1)
    column = lax.rem(lane, 2 * EDGE)
    for c in range(3):
        right = jnp.zeros((rows, LANE), jnp.float32)
        left = right
        for z in range(layers):
            group = (lane // (2 * EDGE)) == z
            field = read(c, z)
            last = field[:, cols - LANE :]
            first = field[:, :LANE]
            at = 2 * EDGE * z
            right = jnp.where(group, pltpu.roll(last, (at - (LANE - EDGE)) % LANE, 1), right)
            left = jnp.where(group, pltpu.roll(first, (at + EDGE) % LANE, 1), left)
        put(0, c, jnp.where(column < EDGE, right, 0.0))
        put(1, c, jnp.where(column >= EDGE, left, 0.0))


def repeat_edges(field, rows, cols):
    lane = iota((rows, LANE), 1)
    right = jnp.where(lane < EDGE, pltpu.roll(field[:, cols - LANE :], EDGE, 1), 0.0)
    left = pltpu.roll(jnp.where(lane < EDGE, field[:, :LANE], 0.0), EDGE, 1)
    step = 2 * EDGE
    while step < LANE:
        right = right + pltpu.roll(right, step, 1)
        left = left + pltpu.roll(left, step, 1)
        step *= 2
    return right, left


def inner_kernel(layers, comps, vel, flat, *refs):
    with_shear = 0 in comps
    new_ref = refs[0]
    q_ref, f_ref, split_ref, band_ref, x_ref = refs[-5:]
    _, rows, cols = flat.shape
    base = lax.axis_index("wall") * layers
    lanes = cols // LANE
    tall = iota((cols, cols), 0) - iota((cols, cols), 1)
    flux_band = jnp.where(tall == 1, -8.0, jnp.where(tall == -1, 8.0, 0.0))
    flux_band = flux_band + jnp.where(tall == 2, 1.0, jnp.where(tall == -2, -1.0, 0.0))
    field_band = jnp.where(jnp.abs(tall) == 1, 6.0, jnp.where(tall == 0, -36.0, 0.0))
    for i, band in enumerate((flux_band, flux_band, field_band, field_band)):
        band_ref[i * cols : (i + 1) * cols] = band.astype(jnp.bfloat16)
    blank = jnp.zeros((rows, cols), jnp.float32)
    for n in range(len(comps)):
        for z in (0, 1, layers + 2, layers + 3):
            q_ref[n, z] = blank
            f_ref[n, z] = blank

    def halves(x):
        high = x.astype(jnp.bfloat16)
        return high, (x - high.astype(jnp.float32)).astype(jnp.bfloat16)

    def prepare(z, carry):
        layer = (base + z).astype(jnp.float32)
        at = pl.ds(pl.multiple_of(z * rows, rows), rows)
        for k in range(lanes):
            cut = slice(k * LANE, (k + 1) * LANE)
            opened = opened_at(flat[0, :, cut], flat[1, :, cut], layer)
            vel_x, vel_z = vel[0, z, :, cut], vel[2, z, :, cut]
            for n, c in enumerate(comps):
                q = opened * vel[c, z, :, cut]
                q_ref[n, z + 2, :, cut] = q
                f_ref[n, z + 2, :, cut] = vel_z * q
                parts = halves(vel_x * q) + halves(q)
                for i, part in enumerate(parts):
                    split_ref[n, at, i * cols + k * LANE : i * cols + (k + 1) * LANE] = part
        return carry

    lax.fori_loop(0, layers, prepare, 0)
    for n in range(len(comps)):
        x_ref[n] = jnp.dot(split_ref[n], band_ref[...], preferred_element_type=jnp.float32)

    def outside(z, c, cut):
        total = jnp.zeros((rows, LANE), jnp.float32)
        for offset, weight in ((1, -8.0), (-1, 8.0), (2, 1.0), (-2, -1.0)):
            at = z + offset
            if 0 <= at < layers:
                total = total + weight * f_ref[c, at + 2, :, cut]
                if abs(offset) == 1:
                    total = total + 6.0 * q_ref[c, at + 2, :, cut]
        hit = flat[0, :, cut] == (base + z).astype(jnp.float32)
        return jnp.where(hit, gain * flat[1, :, cut] * total, 0.0)

    sums = []
    if with_shear:
        for k in range(lanes):
            cut = slice(k * LANE, (k + 1) * LANE)
            for c in range(2):
                sums.append(sum(outside(z, c, cut) for z in (-2, -1, layers, layers + 1)))

    def update(z, sums):
        sums = list(sums)
        layer = (base + z).astype(jnp.float32)
        at = pl.ds(pl.multiple_of(z * rows, rows), rows)
        for k in range(lanes):
            cut = slice(k * LANE, (k + 1) * LANE)
            level = flat[0, :, cut]
            weight = gain * opened_at(level, flat[1, :, cut], layer)
            hit = level == layer
            vel_y = vel[1, z, :, cut]
            for n, c in enumerate(comps):
                q = q_ref[n, z + 2, :, cut]
                total = x_ref[n, at, cut] + sweep(vel_y * q, 6.0 * q, 0)
                near = f_ref[n, z + 3, :, cut] - f_ref[n, z + 1, :, cut]
                both = q_ref[n, z + 3, :, cut] + q_ref[n, z + 1, :, cut]
                total = total + (6.0 * both - 8.0 * near + (f_ref[n, z + 4, :, cut] - f_ref[n, z, :, cut]))
                fresh = vel[c, z, :, cut] + weight * total
                new_ref[n, z, :, cut] = fresh
                if with_shear:
                    sums[2 * k + c] = sums[2 * k + c] + jnp.where(hit, fresh, 0.0)
        return tuple(sums)

    sums = lax.fori_loop(0, layers, update, tuple(sums))
    if not with_shear:
        return
    shear_ref, edge_ref = refs[1:3]
    for k in range(lanes):
        cut = slice(k * LANE, (k + 1) * LANE)
        scale = 1.0 / (0.5 + flat[1, :, cut])
        for c in range(2):
            shear_ref[c, :, cut] = sums[2 * k + c] * scale

    def put(side, n, value):
        edge_ref[side, n] = value.reshape(rows // SUB, SUB, LANE)

    gather_edges(lambda c, z: vel[c, z], layers, rows, cols, put)
    for n in range(2):
        right, left = repeat_edges(flat[n], rows, cols)
        put(0, 3 + n, right)
        put(1, 3 + n, left)


def unpack_kernel(layers, bed_in, got_a, got_b, edge, bed, halo_ref, beside_ref, full_ref, far_ref, *messages):
    cols = halo_ref.shape[3]
    tiles = edge.shape[2]
    tall = tiles + 1
    sub = iota((SUB, cols), 0)
    is_even = even("plane")

    def sides(n):
        one, two = got_a[n], got_b[n]
        return jnp.where(is_even, one, two), jnp.where(is_even, two, one)

    def spread(n, fields):
        low, high = sides(n)
        found = []
        for i in range(fields):
            above = pltpu.roll(high, (SUB - 2 - 2 * i) % SUB, 0)
            below = pltpu.roll(low, (-2 * i) % SUB, 0)
            found.append(jnp.where(sub < 2, below, jnp.where(sub >= SUB - 2, above, 0.0)))
        return found

    for c in range(3):
        for k in range(layers // 4):
            for i, tile in enumerate(spread(c * (layers // 4) + k, 4)):
                halo_ref[c, 4 * k + i] = tile
    count = 3 * layers // 4
    beside = spread(count, 4)
    for i, tile in enumerate(beside):
        beside_ref[i] = tile

    def put(side, n, value):
        full_ref[side, n * tall + tiles] = value

    gather_edges(lambda c, z: halo_ref[c, z], layers, SUB, cols, put)
    for n in range(2):
        right, left = repeat_edges(beside[n], SUB, cols)
        put(0, 3 + n, right)
        put(1, 3 + n, left)
    for side in range(2):
        for n in range(5):
            for t in range(tiles):
                full_ref[side, n * tall + t] = edge[side, n, t]
    lane = iota((SUB, LANE), 1)
    group = lane // (2 * EDGE)
    far_right = [repeat_edges(tile, SUB, cols) for tile in beside[2:]]
    for side in range(2):
        far_ref[side] = jnp.where(group == 0, far_right[0][side], jnp.where(group == 1, far_right[1][side], 0.0))
    right_first = even("span")
    packed = []
    for side, shift in ((0, EDGE), (1, LANE - EDGE)):
        for t in range(tall):
            u, v, w, level, fraction = [full_ref[side, n * tall + t] for n in range(5)]
            last = jnp.where(group == 0, level, jnp.where(group == 1, fraction, 0.0))
            packed.append(u + pltpu.roll(v, shift, 1))
            packed.append(w + pltpu.roll(last, shift, 1))
    for i, message in enumerate(messages):
        is_right = right_first if i == 0 else jnp.logical_not(right_first)
        for n in range(2 * tall):
            message[n] = jnp.where(is_right, packed[n], packed[2 * tall + n])
        message[2 * tall] = jnp.where(is_right, far_ref[0], far_ref[1])
    if bed_in:
        used = 2 * tall + 1
        parts = bed.shape[1] // LANE
        for i in range(parts):
            messages[0][used + i] = bed[:, i * LANE : (i + 1) * LANE]
        per = cols // LANE
        for i, tile in enumerate(spread(count + 1, bed.shape[1] // cols)):
            for j in range(per):
                messages[0][used + parts + i * per + j] = tile[:, j * LANE : (j + 1) * LANE]


def strip_kernel(layers, vel, flat, halo, beside, top_ref, bottom_ref, shear_ref, z_ref, q_ref, f_ref):
    _, rows, cols = flat.shape
    base = lax.axis_index("wall") * layers
    sub = iota((SUB, cols), 0)
    for side, new in ((0, top_ref), (1, bottom_ref)):
        inside = sub < EDGE if side == 0 else sub >= EDGE
        outer = sub >= SUB - 2 if side == 0 else sub < 2
        first = 0 if side == 0 else rows - SUB
        at = slice(first, first + SUB)
        levels = jnp.where(inside, flat[0, at], beside[0])
        fraction = jnp.where(inside, flat[1, at], beside[1])
        extra = [jnp.where(outer, gain * fraction * beside[2 + c], 0.0) for c in range(2)]

        def read(c, z):
            return jnp.where(inside, vel[c, z, at], halo[c, z])

        def write(c, z, value):
            new[c, z] = value

        sums = brick(read, levels, fraction, base, layers, q_ref, f_ref, write, extra, 4)
        shear_ref[side, 0] = sums[0]
        shear_ref[side, 1] = sums[1]
    start = jnp.where(lax.axis_index("wall") == 0, layers - 2, 0)
    for c in range(3):
        for z in range(2):
            z_ref[c, z] = vel[c, start + z]


def column_strip(vel, levels, fraction, extra, base, layers):
    shape = levels.shape
    width = 2 * EDGE
    here = iota(shape, 1) // width
    layer = (here + base).astype(jnp.float32)
    opened = opened_at(levels, fraction, layer)
    hit = levels == layer
    hit_down = levels == layer - layers
    hit_up = levels == layer + layers
    scale = 1.0 / (0.5 + fraction)
    fresh, shear = [], []
    for c in range(3):
        q = opened * vel[c]
        b = 6.0 * q
        total = sweep(vel[0] * q, b, 1) + sweep(vel[1] * q, b, 0) - 6.0 * b
        flux = vel[2] * q
        plus = ahead(b - 8.0 * flux, width, 1)
        minus = ahead(b + 8.0 * flux, -width, 1)
        plus_far = ahead(flux, 2 * width, 1)
        minus_far = ahead(flux, -2 * width, 1)
        total = total + jnp.where(here <= layers - 2, plus, 0.0) + jnp.where(here <= layers - 3, plus_far, 0.0)
        total = total + jnp.where(here >= 1, minus, 0.0) - jnp.where(here >= 2, minus_far, 0.0)
        value = vel[c] + gain * opened * total
        fresh.append(value)
        if c < 2:
            down = jnp.where(here > layers - 2, plus, 0.0) + jnp.where(here > layers - 3, plus_far, 0.0)
            up = jnp.where(here < 1, minus, 0.0) - jnp.where(here < 2, minus_far, 0.0)
            part = jnp.where(hit, value, 0.0)
            part = part + gain * fraction * (jnp.where(hit_down, down, 0.0) + jnp.where(hit_up, up, 0.0))
            step = LANE // 2
            while step >= width:
                part = part + pltpu.roll(part, step, 1)
                step //= 2
            more = extra if c == 0 else ahead(extra, width, 1)
            more = jnp.concatenate([jnp.zeros((shape[0] - SUB, LANE), jnp.float32), more], axis=0)
            shear.append((part + gain * fraction * more) * scale)
    return fresh, shear


def everywhere(x):
    step = 2 * EDGE
    x = jnp.where(iota(x.shape, 1) < step, x, 0.0)
    while step < LANE:
        x = x + pltpu.roll(x, step, 1)
        step *= 2
    return x


def side_kernel(layers, spans, bed_in, full, far, shear, strips, *rest):
    got = rest[:spans]
    rest = rest[spans:]
    own_message = rest[0]
    fresh_ref, out_ref = rest[2:]
    _, rows, cols = shear.shape
    tiles = rows // SUB
    tall = tiles + 1
    base = lax.axis_index("wall") * layers
    right_first = even("span")
    results = []
    column = lax.rem(iota((tall * SUB, LANE), 1), 2 * EDGE)
    fresh_sides = []
    for side in range(2):
        first = right_first if side == 0 else jnp.logical_not(right_first)

        def other(n):
            return jnp.where(first, got[0][n], got[1][n] if spans > 1 else 0.0)

        given = column >= EDGE if side == 0 else column < EDGE
        back = EDGE if side == 0 else LANE - EDGE
        both = [jnp.concatenate([other(2 * t + i) for t in range(tall)], axis=0) for i in range(2)]
        turned = [jnp.where(given, pltpu.roll(b, back, 1), 0.0) for b in both]
        theirs = [jnp.where(given, both[0], 0.0), turned[0], jnp.where(given, both[1], 0.0)]
        theirs += [everywhere(turned[1]), everywhere(ahead(turned[1], 2 * EDGE, 1))]
        fields = []
        for n in range(5):
            own = full[side, n * tall : (n + 1) * tall].reshape(tall * SUB, LANE)
            fields.append(own + theirs[n])
        extra = far[side] + other(2 * tall)
        fresh, edge_shear = column_strip(fields[:3], fields[3], fields[4], extra, base, layers)
        fresh_sides.append(fresh)
        results.append(edge_shear)
    for c in range(3):
        fresh_ref[c] = jnp.where(column < EDGE, fresh_sides[0][c], fresh_sides[1][c])[:rows]
    lane = iota((SUB, LANE), 1)
    sub = iota((SUB, LANE), 0)
    lanes = cols // LANE
    for c in range(2):
        right, left = results[0][c], results[1][c]
        for t in range(tall):
            at = slice(t * SUB, (t + 1) * SUB)
            for k in range(lanes):
                cut = slice(k * LANE, (k + 1) * LANE)
                if t == tiles:
                    piece = jnp.where(sub < EDGE, strips[1, c, :, cut], strips[0, c, :, cut])
                    piece = jnp.where((sub < 2) | (sub >= SUB - 2), piece, 0.0)
                else:
                    piece = shear[c, at, cut]
                    if t == 0:
                        piece = jnp.where(sub < 2, strips[0, c, :, cut], piece)
                    if t == tiles - 1:
                        piece = jnp.where(sub >= SUB - 2, strips[1, c, :, cut], piece)
                if k == 0:
                    piece = jnp.where(lane < 2, pltpu.roll(left[at], LANE - EDGE, 1), piece)
                if k == lanes - 1:
                    piece = jnp.where(lane >= LANE - 2, pltpu.roll(right[at], LANE - EDGE, 1), piece)
                out_ref[(c * tall + t) * (lanes + 1) + k] = piece
            beyond = jnp.where(lane < 2, pltpu.roll(right[at], LANE - EDGE, 1), 0.0)
            beyond = jnp.where(lane >= LANE - 2, pltpu.roll(left[at], LANE - EDGE, 1), beyond)
            out_ref[(c * tall + t) * (lanes + 1) + lanes] = beyond
    if bed_in:
        used = 2 * tall * (lanes + 1)
        start = 2 * tall + 1
        count = own_message.shape[0] - start
        for i in range(count):
            out_ref[used + i] = own_message[start + i]
            out_ref[used + count + i] = got[0][start + i]


def merge_kernel(layers, new, new_z, strip_top, strip_bottom, fresh, far, flat, final, out_ref, sems):
    _, rows, cols = flat.shape
    lanes = cols // LANE
    wall = lax.axis_index("wall")
    lower = wall == 0
    sub = iota((SUB, LANE), 0)
    lane = iota((SUB, LANE), 1)
    levels = flat[0]
    fraction = flat[1]
    base = wall * layers
    near_from = jnp.where(lower, 0, 1)
    far_from = 1 - near_from
    near_to = jnp.where(lower, layers - 1, 0)
    far_to = jnp.where(lower, layers - 2, 1)
    sign = jnp.where(lower, -1.0, 1.0)
    other = jnp.where(lower, layers, 0)
    near_open = opened_at(levels, fraction, (other + jnp.where(lower, 0, layers - 1)).astype(jnp.float32))
    far_open = opened_at(levels, fraction, (other + jnp.where(lower, 1, layers - 2)).astype(jnp.float32))
    near_gain = gain * opened_at(levels, fraction, (base + near_to).astype(jnp.float32))
    far_gain = gain * opened_at(levels, fraction, (base + far_to).astype(jnp.float32))
    near_w, far_w = far[2, near_from], far[2, far_from]
    copies = []
    for c in range(3):
        for z in range(layers):
            for t in range(rows // SUB):
                at = slice(t * SUB, (t + 1) * SUB)
                side = pltpu.roll(fresh[c, at], (LANE - EDGE - 2 * EDGE * z) % LANE, 1)
                for k in range(lanes):
                    cut = slice(k * LANE, (k + 1) * LANE)
                    piece = new[c, z, at, cut] if c < 2 else new_z[0, z, at, cut]
                    if t == 0:
                        piece = jnp.where(sub < 2, strip_top[c, z, :, cut], piece)
                    if t == rows // SUB - 1:
                        piece = jnp.where(sub >= SUB - 2, strip_bottom[c, z, :, cut], piece)
                    if k == 0:
                        piece = jnp.where(lane < 2, side, piece)
                    if k == lanes - 1:
                        piece = jnp.where(lane >= LANE - 2, side, piece)
                    out_ref[c, z, at, cut] = piece
        near_q = near_open * far[c, near_from]
        near_f = sign * (near_w * near_q)
        far_f = sign * (far_w * (far_open * far[c, far_from]))
        out_ref[c, near_to] = out_ref[c, near_to] + near_gain * (6.0 * near_q + 8.0 * near_f - far_f)
        out_ref[c, far_to] = out_ref[c, far_to] - far_gain * near_f
        part = layers // 4
        for i in range(4):
            at = pl.ds(i * part, part)
            copies.append(pltpu.make_async_copy(out_ref.at[c, at], final.at[c, at], sems.at[4 * c + i]))
            copies[-1].start()
    for copy in copies:
        copy.wait()


def bed_kernel(tall, lanes, bed_in, mine, theirs, *rest):
    out_ref = rest[-1]
    rows = (tall - 1) * SUB
    wide = (lanes + 1) * LANE
    span = lax.axis_index("span")
    wall = lax.axis_index("wall")
    plane = lax.axis_index("plane")

    def sheared(c):
        whole = []
        for t in range(tall):
            first = (c * tall + t) * (lanes + 1)
            whole.append(
                jnp.concatenate([mine[first + k] + theirs[first + k] for k in range(lanes + 1)], axis=1)
            )
        return jnp.concatenate(whole, axis=0)

    shear_x, shear_y = sheared(0), sheared(1)
    if bed_in:
        used = 2 * tall * (lanes + 1)
        parts = 2 * lanes

        def tile_of(s, w, which):
            pieces = []
            for k in range(parts):
                own = used + which * parts + k
                across = own + 2 * parts
                from_mine = jnp.where(span == s, mine[own], mine[across])
                from_theirs = jnp.where(span == s, theirs[own], theirs[across])
                pieces.append(jnp.where(wall == w, from_mine, from_theirs))
            return pieces

        def window(pieces):
            lane = iota((SUB, LANE), 1)
            low = span == 0
            inside = [jnp.where(low, pieces[k], pieces[lanes + k]) for k in range(lanes)]
            beyond = jnp.where(
                low,
                jnp.where(lane < LANE // 2, pieces[lanes], 0.0),
                jnp.where(lane < LANE // 2, 0.0, pieces[lanes - 1]),
            )
            return jnp.concatenate(inside + [beyond], axis=1)

        sub = iota((SUB, LANE), 0)
        whole = [window(tile_of(s, w, 0)) for s in range(2) for w in range(2)]
        after = tile_of(0, 0, 1)
        before = tile_of(1, 1, 1)
        whole.append(window([jnp.where(sub < EDGE, a, b) for a, b in zip(after, before)]))
        bed = jnp.concatenate(whole, axis=0)
    else:
        bed = rest[0][...]
    square = shear_x * shear_x + shear_y * shear_y
    factor = jnp.maximum(square - threshold_sq, 0.0) / (square + threshold_sq)
    load_x = shear_x * factor
    load_y = shear_y * factor
    divergence = 0.5 * (ahead(load_x, 1, 1) - ahead(load_x, -1, 1)) + 0.5 * (
        ahead(load_y, 1, 0) - ahead(load_y, -1, 0)
    )
    row = iota((tall * SUB, wide), 0)
    col = iota((tall * SUB, wide), 1)
    last_plane = plane == lax.axis_size("plane") - 1
    last_span = span == lax.axis_size("span") - 1
    row_low = jnp.where(last_plane, rows, rows + EDGE)
    row_high = jnp.where(plane == 0, rows + SUB, rows + EDGE)
    col_low = jnp.where(last_span, wide - LANE, wide - LANE // 2)
    col_high = jnp.where(span == 0, wide, wide - LANE // 2)
    valid = ((row < row_low) | (row >= row_high)) & ((col < col_low) | (col >= col_high))

    def step(height):
        around = ahead(height, 1, 0) + ahead(height, -1, 0) + ahead(height, 1, 1) + ahead(height, -1, 1)
        return height - bed_step * divergence + bed_step * slope_rate * (around - 4.0 * height)

    first = jnp.where(valid, step(bed), 0.0)
    out_ref[...] = step(first)[:rows, : lanes * LANE]


def pairings(axis):
    size = lax.axis_size(axis)
    lists = []
    for start in (0, 1):
        found = []
        for i in range(start, size - 1, 2):
            found += [(i, i + 1), (i + 1, i)]
        lists.append(found)
    return lists


def bed_around(bed_height, rows, cols):
    spans = lax.axis_size("span")
    whole = lax.all_gather(bed_height, ("span", "wall"), axis=0, tiled=True)
    padded = jnp.pad(whole, ((0, 0), (EDGE, EDGE)))
    piece = lax.dynamic_slice_in_dim(padded, lax.axis_index("span") * cols, cols + 2 * EDGE, axis=1)
    size = lax.axis_size("plane")
    up = [(i, i + 1) for i in range(size - 1)]
    before = lax.ppermute(piece[-EDGE:], "plane", up)
    after = lax.ppermute(piece[:EDGE], "plane", [(j, i) for i, j in up])
    tall = jnp.concatenate([piece, after, before], axis=0)
    gap = jnp.zeros((tall.shape[0], LANE - 2 * EDGE), jnp.float32)
    return jnp.concatenate([tall[:, EDGE:], gap, tall[:, :EDGE]], axis=1)


def body(velocity, levels, fraction, bed_height):
    _, layers, rows, cols = velocity.shape
    tiles = rows // SUB
    tall = tiles + 1
    lanes = cols // LANE
    spans = lax.axis_size("span")
    walls = lax.axis_size("wall")
    assert walls == 2 and layers * 2 * EDGE == LANE
    bed_in = spans == 2 and bed_height.shape == (SUB, 2 * cols)
    count = 3 * layers // 4 + (2 if bed_in else 1)
    dma = pltpu.SemaphoreType.DMA
    sheet = (3, layers, SUB, cols)
    send_a, send_b, vel, flat, bed = call(
        functools.partial(pack_kernel, layers, bed_in),
        [(count, SUB, cols), (count, SUB, cols), velocity.shape, (2, rows, cols), bed_height.shape],
        [pltpu.with_memory_space_constraint(x, pltpu.HBM) for x in (velocity, levels, fraction, bed_height)],
        [pltpu.VMEM(levels.shape, jnp.int32), dma((6,))],
        any_inputs=(0, 1, 2, 3),
        moved=1_000_000,
        limit=10,
    )
    plane_a, plane_b = pairings("plane")
    got_b = lax.ppermute(send_b, "plane", plane_b)
    got_a = lax.ppermute(send_a, "plane", plane_a)

    def inner(comps, more, flops):
        count = len(comps)
        deep = pltpu.VMEM((count, layers + 4, rows, cols), jnp.float32)
        return call(
            functools.partial(inner_kernel, layers, comps),
            [(count, layers, rows, cols)] + more,
            [vel, flat],
            [deep, deep, pltpu.VMEM((count, layers * rows, 4 * cols), jnp.bfloat16)]
            + [pltpu.VMEM((4 * cols, cols), jnp.bfloat16), pltpu.VMEM((count, layers * rows, cols), jnp.float32)],
            flops=flops,
            moved=3_000_000,
        )

    new, shear, edge = inner((0, 1), [(2, rows, cols), (2, 5, tiles, SUB, LANE)], 20_000_000)
    span_lists = [p for p in pairings("span") if p]
    message = (2 * tall + 1 + (4 * lanes if bed_in else 0), SUB, LANE)
    unpacked = call(
        functools.partial(unpack_kernel, layers, bed_in),
        [sheet, (4, SUB, cols), (2, 5 * tall, SUB, LANE), (2, SUB, LANE)] + [message] * len(span_lists),
        [got_a, got_b, edge, bed],
        moved=1_000_000,
        limit=10,
    )
    halo, beside, full, far = unpacked[:4]
    messages = unpacked[4:]
    got = [lax.ppermute(m, "span", pairs) for m, pairs in zip(messages, span_lists)]
    shallow = pltpu.VMEM((3, layers + 4, SUB, cols), jnp.float32)
    new_top, new_bottom, strip_shear, send_z = call(
        functools.partial(strip_kernel, layers),
        [sheet, sheet, (2, 2, SUB, cols), (3, 2, rows, cols)],
        [vel, flat, halo, beside],
        [shallow, shallow],
        flops=10_000_000,
        moved=2_000_000,
    )
    got_z = lax.ppermute(send_z, "wall", pairings("wall")[0])
    shear_count = 2 * tall * (lanes + 1)
    out_count = shear_count + (8 * lanes if bed_in else 0)
    (new_z,) = inner((2,), [], 10_000_000)
    fresh, mine = call(
        functools.partial(side_kernel, layers, len(got), bed_in),
        [(3, rows, LANE), (out_count, SUB, LANE)],
        [full, far, shear, strip_shear] + got + [messages[0], new_z],
        any_inputs=(5 + len(got),),
        moved=1_000_000,
        limit=10,
    )
    theirs = lax.ppermute(mine, "wall", pairings("wall")[0])
    (velocity_next,) = call(
        functools.partial(merge_kernel, layers),
        [velocity.shape],
        [new, new_z, new_top, new_bottom, fresh, got_z, flat],
        [pltpu.VMEM(velocity.shape, jnp.float32), dma((12,))],
        any_outputs=(0,),
        flops=2_000_000,
        moved=4_000_000,
    )
    extra = [] if bed_in else [bed_around(bed_height, rows, cols)]
    (bed_next,) = call(
        functools.partial(bed_kernel, tall, lanes, bed_in),
        [(rows, cols)],
        [mine, theirs] + extra,
        moved=1_000_000,
        limit=10,
    )
    return velocity_next, bed_next


def solution(mesh):
    return jax.shard_map(
        body,
        mesh=mesh,
        in_specs=(
            P("groups", "wall", "plane", "span"),
            P(("groups", "plane"), "span"),
            P(("groups", "plane"), "span"),
            P(("groups", "plane", "span", "wall"), None),
        ),
        out_specs=(P("groups", "wall", "plane", "span"), P(("groups", "plane"), "span")),
        check_vma=False,
    )
```

```python
import functools

import jax
import jax.numpy as jnp
from jax import lax
from jax.experimental import pallas as pl
from jax.experimental.pallas import tpu as pltpu
from jax.sharding import PartitionSpec as P

time_step = 0.1
bed_step = 0.4
slope_rate = 0.25
threshold_sq = 0.25
gain = time_step / 12.0
EDGE = 4
SUB = 8
LANE = 128
VMEM = pltpu.VMEM
MIB = 1024 * 1024


def call(kernel, outs, ins, scratch=(), any_inputs=(), any_outputs=(), flops=0, moved=0, limit=20, aliases=None):
    specs = [pl.BlockSpec(memory_space=pl.ANY if i in any_inputs else VMEM) for i in range(len(ins))]
    shapes = [s if isinstance(s, jax.ShapeDtypeStruct) else jax.ShapeDtypeStruct(s, jnp.float32) for s in outs]
    return pl.pallas_call(
        kernel,
        out_shape=shapes,
        in_specs=specs,
        out_specs=[pl.BlockSpec(memory_space=pl.ANY if i in any_outputs else VMEM) for i in range(len(outs))],
        scratch_shapes=list(scratch),
        input_output_aliases=aliases or {},
        cost_estimate=pl.CostEstimate(flops=flops, bytes_accessed=moved, transcendentals=0),
        compiler_params=pltpu.CompilerParams(vmem_limit_bytes=limit * MIB),
    )(*ins)


def iota(shape, dim):
    return lax.broadcasted_iota(jnp.int32, shape, dim)


def ahead(x, step, axis):
    return pltpu.roll(x, (-step) % x.shape[axis], axis)


def sweep(flux, b, axis):
    a = 8.0 * flux
    return ahead((b - a) + ahead(flux, 1, axis), 1, axis) + ahead((b + a) - ahead(flux, -1, axis), -1, axis)


def opened_at(level, fraction, layer):
    return jnp.where(level == layer, fraction, jnp.where(layer > level, 1.0, 0.0))


def even(axis):
    return lax.rem(lax.axis_index(axis), 2) == 0


def beyond_terms(tile, level, fraction, base, layers, forward):
    near = pltpu.roll(level, SUB - 1, 0) if forward else pltpu.roll(level, 1, 0)
    far = pltpu.roll(level, SUB - 2, 0) if forward else pltpu.roll(level, 2, 0)
    sign = 1.0 if forward else -1.0
    one = [jnp.zeros(level.shape, jnp.float32)] * 2
    two = list(one)
    for z in range(layers):
        layer = (base + z).astype(jnp.float32)
        opened = opened_at(level, fraction, layer)
        near_hit, far_hit = near == layer, far == layer
        for c in range(2):
            q = opened * tile[c, z]
            flux = sign * (tile[1, z] * q)
            one[c] = one[c] + jnp.where(near_hit, 6.0 * q + 8.0 * flux, 0.0)
            two[c] = two[c] - jnp.where(far_hit, flux, 0.0)
    sub = iota(level.shape, 0)
    source = SUB - 3 if forward else 2
    past = source - 1 if forward else source + 1
    shift = 1 if forward else SUB - 1
    shift_two = 2 if forward else SUB - 2
    found = []
    for c in range(2):
        a = pltpu.roll(jnp.where(sub == source, one[c], 0.0), shift, 0)
        b = pltpu.roll(jnp.where((sub == source) | (sub == past), two[c], 0.0), shift_two, 0)
        found.append(a + b)
    return found


def pack_kernel(layers, bed_in, vel_in, lev_in, frac_in, bed_from, a_ref, b_ref, vel, flat, bed, band_ref, lev, sems):
    _, rows, cols = flat.shape
    wall = lax.axis_index("wall")
    base = wall * layers
    small = [
        pltpu.make_async_copy(lev_in, lev, sems.at[0]),
        pltpu.make_async_copy(frac_in, flat.at[1], sems.at[1]),
        pltpu.make_async_copy(bed_from, bed, sems.at[2]),
    ]
    pieces = []
    for i, (start, size) in enumerate(((0, SUB), (rows - SUB, SUB), (SUB, rows - 2 * SUB))):
        at = pl.ds(start, size)
        pieces.append(pltpu.make_async_copy(vel_in.at[:, :, at, :], vel.at[:, :, at, :], sems.at[3 + i]))
    for copy in small + pieces:
        copy.start()
    tall = iota((cols, cols), 0) - iota((cols, cols), 1)
    flux_band = jnp.where(tall == 1, -8.0, jnp.where(tall == -1, 8.0, 0.0))
    flux_band = flux_band + jnp.where(tall == 2, 1.0, jnp.where(tall == -2, -1.0, 0.0))
    field_band = jnp.where(jnp.abs(tall) == 1, 6.0, jnp.where(tall == 0, -36.0, 0.0))
    for i, band in enumerate((flux_band, flux_band, field_band, field_band)):
        band_ref[i * cols : (i + 1) * cols] = band.astype(jnp.bfloat16)
    sub = iota((SUB, cols), 0)
    pair = sub // 2
    is_even = even("plane")

    def put(n, low, high):
        a_ref[n] = jnp.where(is_even, low, high)
        b_ref[n] = jnp.where(is_even, high, low)

    def stack(fields, place):
        tile = jnp.zeros((SUB, cols), jnp.float32)
        for i, field in enumerate(fields):
            tile = jnp.where(pair == i, pltpu.roll(field, (2 * i + place) % SUB, 0), tile)
        return tile

    for copy in small:
        copy.wait()
    flat[0] = lev[...].astype(jnp.float32)
    low_lev, low_frac = flat[0, rows - SUB :], flat[1, rows - SUB :]
    high_lev, high_frac = flat[0, :SUB], flat[1, :SUB]
    count = 3 * layers // 4
    if bed_in:
        halves = [bed[:, i * cols : (i + 1) * cols] for i in range(bed.shape[1] // cols)]
        put(count + 1, stack(halves, 2), stack(halves, 0))
    for copy in pieces[:2]:
        copy.wait()
    top = vel.at[:, :, pl.ds(0, SUB), :]
    bottom = vel.at[:, :, pl.ds(rows - SUB, SUB), :]
    for c in range(3):
        for k in range(layers // 4):
            low = stack([bottom[c, 4 * k + i] for i in range(4)], 2)
            high = stack([top[c, 4 * k + i] for i in range(4)], 0)
            put(c * (layers // 4) + k, low, high)
    low_far = beyond_terms(bottom, low_lev, low_frac, base, layers, True)
    high_far = beyond_terms(top, high_lev, high_frac, base, layers, False)
    put(count, stack([low_lev, low_frac] + low_far, 2), stack([high_lev, high_frac] + high_far, 0))
    pieces[2].wait()


def gather_edges(read, layers, rows, cols, put):
    lane = iota((rows, LANE), 1)
    column = lax.rem(lane, 2 * EDGE)
    for c in range(3):
        right = jnp.zeros((rows, LANE), jnp.float32)
        left = right
        for z in range(layers):
            group = (lane // (2 * EDGE)) == z
            field = read(c, z)
            last = field[:, cols - LANE :]
            first = field[:, :LANE]
            at = 2 * EDGE * z
            right = jnp.where(group, pltpu.roll(last, (at - (LANE - EDGE)) % LANE, 1), right)
            left = jnp.where(group, pltpu.roll(first, (at + EDGE) % LANE, 1), left)
        put(0, c, jnp.where(column < EDGE, right, 0.0))
        put(1, c, jnp.where(column >= EDGE, left, 0.0))


def repeat_edges(field, rows, cols):
    lane = iota((rows, LANE), 1)
    right = jnp.where(lane < EDGE, pltpu.roll(field[:, cols - LANE :], EDGE, 1), 0.0)
    left = pltpu.roll(jnp.where(lane < EDGE, field[:, :LANE], 0.0), EDGE, 1)
    step = 2 * EDGE
    while step < LANE:
        right = right + pltpu.roll(right, step, 1)
        left = left + pltpu.roll(left, step, 1)
        step *= 2
    return right, left


def inner_kernel(layers, comps, vel, flat, band_ref, *refs):
    with_shear = 0 in comps
    new_ref = refs[0]
    q_ref, f_ref, split_ref, x_ref = refs[-4:]
    _, rows, cols = flat.shape
    base = lax.axis_index("wall") * layers
    lanes = cols // LANE
    blank = jnp.zeros((rows, cols), jnp.float32)
    for n in range(len(comps)):
        for z in (0, 1, layers + 2, layers + 3):
            q_ref[n, z] = blank
            f_ref[n, z] = blank

    def halves(x):
        high = x.astype(jnp.bfloat16)
        return high, (x - high.astype(jnp.float32)).astype(jnp.bfloat16)

    def prepare(z, carry):
        layer = (base + z).astype(jnp.float32)
        at = pl.ds(pl.multiple_of(z * rows, rows), rows)
        for k in range(lanes):
            cut = slice(k * LANE, (k + 1) * LANE)
            opened = opened_at(flat[0, :, cut], flat[1, :, cut], layer)
            vel_x, vel_z = vel[0, z, :, cut], vel[2, z, :, cut]
            for n, c in enumerate(comps):
                q = opened * vel[c, z, :, cut]
                q_ref[n, z + 2, :, cut] = q
                f_ref[n, z + 2, :, cut] = vel_z * q
                parts = halves(vel_x * q) + halves(q)
                for i, part in enumerate(parts):
                    split_ref[n, at, i * cols + k * LANE : i * cols + (k + 1) * LANE] = part
        return carry

    lax.fori_loop(0, layers, prepare, 0)
    for n in range(len(comps)):
        x_ref[n] = jnp.dot(split_ref[n], band_ref[...], preferred_element_type=jnp.float32)

    if with_shear:
        shear_ref, edge_ref = refs[1:3]

        def put(side, n, value):
            edge_ref[side, n] = value.reshape(rows // SUB, SUB, LANE)

        gather_edges(lambda c, z: vel[c, z], layers, rows, cols, put)
        for n in range(2):
            right, left = repeat_edges(flat[n], rows, cols)
            put(0, 3 + n, right)
            put(1, 3 + n, left)

    def outside(z, c, cut):
        total = jnp.zeros((rows, LANE), jnp.float32)
        for offset, weight in ((1, -8.0), (-1, 8.0), (2, 1.0), (-2, -1.0)):
            at = z + offset
            if 0 <= at < layers:
                total = total + weight * f_ref[c, at + 2, :, cut]
                if abs(offset) == 1:
                    total = total + 6.0 * q_ref[c, at + 2, :, cut]
        hit = flat[0, :, cut] == (base + z).astype(jnp.float32)
        return jnp.where(hit, gain * flat[1, :, cut] * total, 0.0)

    sums = []
    if with_shear:
        for k in range(lanes):
            cut = slice(k * LANE, (k + 1) * LANE)
            for c in range(2):
                sums.append(sum(outside(z, c, cut) for z in (-2, -1, layers, layers + 1)))

    def update(z, sums):
        sums = list(sums)
        layer = (base + z).astype(jnp.float32)
        at = pl.ds(pl.multiple_of(z * rows, rows), rows)
        for k in range(lanes):
            cut = slice(k * LANE, (k + 1) * LANE)
            level = flat[0, :, cut]
            weight = gain * opened_at(level, flat[1, :, cut], layer)
            hit = level == layer
            vel_y = vel[1, z, :, cut]
            for n, c in enumerate(comps):
                q = q_ref[n, z + 2, :, cut]
                total = x_ref[n, at, cut] + sweep(vel_y * q, 6.0 * q, 0)
                near = f_ref[n, z + 3, :, cut] - f_ref[n, z + 1, :, cut]
                both = q_ref[n, z + 3, :, cut] + q_ref[n, z + 1, :, cut]
                total = total + (6.0 * both - 8.0 * near + (f_ref[n, z + 4, :, cut] - f_ref[n, z, :, cut]))
                fresh = vel[c, z, :, cut] + weight * total
                new_ref[n, z, :, cut] = fresh
                if with_shear:
                    sums[2 * k + c] = sums[2 * k + c] + jnp.where(hit, fresh, 0.0)
        return tuple(sums)

    sums = lax.fori_loop(0, layers, update, tuple(sums))
    if not with_shear:
        return
    for k in range(lanes):
        cut = slice(k * LANE, (k + 1) * LANE)
        scale = 1.0 / (0.5 + flat[1, :, cut])
        for c in range(2):
            shear_ref[c, :, cut] = sums[2 * k + c] * scale


def unpack_kernel(layers, bed_in, got_a, got_b, edge, bed, halo_ref, beside_ref, full_ref, far_ref, *messages):
    cols = halo_ref.shape[3]
    tiles = edge.shape[2]
    tall = tiles + 1
    sub = iota((SUB, cols), 0)
    is_even = even("plane")

    def sides(n):
        one, two = got_a[n], got_b[n]
        return jnp.where(is_even, one, two), jnp.where(is_even, two, one)

    def spread(n, fields):
        low, high = sides(n)
        found = []
        for i in range(fields):
            above = pltpu.roll(high, (SUB - 2 - 2 * i) % SUB, 0)
            below = pltpu.roll(low, (-2 * i) % SUB, 0)
            found.append(jnp.where(sub < 2, below, jnp.where(sub >= SUB - 2, above, 0.0)))
        return found

    for c in range(3):
        for k in range(layers // 4):
            for i, tile in enumerate(spread(c * (layers // 4) + k, 4)):
                halo_ref[c, 4 * k + i] = tile
    count = 3 * layers // 4
    beside = spread(count, 4)
    for i, tile in enumerate(beside):
        beside_ref[i] = tile

    def put(side, n, value):
        full_ref[side, n * tall + tiles] = value

    gather_edges(lambda c, z: halo_ref[c, z], layers, SUB, cols, put)
    for n in range(2):
        right, left = repeat_edges(beside[n], SUB, cols)
        put(0, 3 + n, right)
        put(1, 3 + n, left)
    for side in range(2):
        for n in range(5):
            for t in range(tiles):
                full_ref[side, n * tall + t] = edge[side, n, t]
    lane = iota((SUB, LANE), 1)
    group = lane // (2 * EDGE)
    far_right = [repeat_edges(tile, SUB, cols) for tile in beside[2:]]
    for side in range(2):
        far_ref[side] = jnp.where(group == 0, far_right[0][side], jnp.where(group == 1, far_right[1][side], 0.0))
    right_first = even("span")
    packed = []
    for side, shift in ((0, EDGE), (1, LANE - EDGE)):
        for t in range(tall):
            u, v, w, level, fraction = [full_ref[side, n * tall + t] for n in range(5)]
            last = jnp.where(group == 0, level, jnp.where(group == 1, fraction, 0.0))
            packed.append(u + pltpu.roll(v, shift, 1))
            packed.append(w + pltpu.roll(last, shift, 1))
    for i, message in enumerate(messages):
        is_right = right_first if i == 0 else jnp.logical_not(right_first)
        for n in range(2 * tall):
            message[n] = jnp.where(is_right, packed[n], packed[2 * tall + n])
        message[2 * tall] = jnp.where(is_right, far_ref[0], far_ref[1])
    if bed_in:
        used = 2 * tall + 1
        parts = bed.shape[1] // LANE
        for i in range(parts):
            messages[0][used + i] = bed[:, i * LANE : (i + 1) * LANE]
        per = cols // LANE
        for i, tile in enumerate(spread(count + 1, bed.shape[1] // cols)):
            for j in range(per):
                messages[0][used + parts + i * per + j] = tile[:, j * LANE : (j + 1) * LANE]


def strip_kernel(layers, vel, flat, halo, beside, new_z, fix_ref, shear_ref, z_ref, q_ref, f_ref):
    _, rows, cols = flat.shape
    base = lax.axis_index("wall") * layers
    shape = (SUB, cols)
    sub = iota(shape, 0)
    low, high = sub < 2, sub >= SUB - 2
    blank = jnp.zeros(shape, jnp.float32)

    def faces(first, last):
        return jnp.where(low, first, jnp.where(high, last, 0.0))

    level, fraction = beside[0], beside[1]
    own_level = faces(flat[0, :SUB], flat[0, rows - SUB :])
    own_fraction = faces(flat[1, :SUB], flat[1, rows - SUB :])
    for c in range(2):
        for z in (0, 1, layers + 2, layers + 3):
            q_ref[c, z] = blank
            f_ref[c, z] = blank

    def prepare(z, carry):
        opened = opened_at(level, fraction, (base + z).astype(jnp.float32))
        for c in range(2):
            q = opened * halo[c, z]
            q_ref[c, z + 2] = q
            f_ref[c, z + 2] = halo[2, z] * q
        return carry

    lax.fori_loop(0, layers, prepare, 0, unroll=4)
    sums = []
    for c in range(2):
        found = gain * fraction * beside[2 + c]
        for z in (-2, -1, layers, layers + 1):
            total = blank
            for offset, weight in ((1, -8.0), (-1, 8.0), (2, 1.0), (-2, -1.0)):
                at = z + offset
                if 0 <= at < layers:
                    total = total + weight * f_ref[c, at + 2]
                    if abs(offset) == 1:
                        total = total + 6.0 * q_ref[c, at + 2]
            found = found + jnp.where(level == (base + z).astype(jnp.float32), gain * fraction * total, 0.0)
        sums.append(found)

    def update(z, sums):
        sums = list(sums)
        layer = (base + z).astype(jnp.float32)
        opened = opened_at(level, fraction, layer)
        own_opened = opened_at(own_level, own_fraction, layer)
        weight, own_weight = gain * opened, gain * own_opened
        hit, own_hit = level == layer, own_level == layer
        own_y = faces(vel[1, z, :SUB], vel[1, z, rows - SUB :])
        for c in range(3):
            q = q_ref[c, z + 2] if c < 2 else opened * halo[2, z]
            flux = halo[1, z] * q
            own = own_y if c == 1 else faces(vel[c, z, :SUB], vel[c, z, rows - SUB :])
            own_q = own_opened * own
            own_flux = own_y * own_q
            a, b = 8.0 * flux, 6.0 * q
            own_a, own_b = 8.0 * own_flux, 6.0 * own_q
            less_a, less_b, less = a - own_a, b - own_b, flux - own_flux
            after = jnp.where(sub == 0, less_b - less_a, 0.0) + ahead(jnp.where(low, less, 0.0), 1, 0)
            before = jnp.where(sub == SUB - 1, less_b + less_a, 0.0) - ahead(jnp.where(high, less, 0.0), -1, 0)
            fix = own_weight * faces(ahead(before, -1, 0), ahead(after, 1, 0))
            fix_ref[c, z] = fix
            if c == 2:
                continue
            after = jnp.where(sub == 0, own_b - own_a, b - a) + ahead(jnp.where(low, own_flux, 0.0), 1, 0)
            before = jnp.where(sub == SUB - 1, own_b + own_a, b + a) - ahead(jnp.where(high, own_flux, 0.0), -1, 0)
            total = ahead(after, 1, 0) + ahead(before, -1, 0) + sweep(halo[0, z] * q, b, 1) - 6.0 * b
            near = f_ref[c, z + 3] - f_ref[c, z + 1]
            both = q_ref[c, z + 3] + q_ref[c, z + 1]
            total = total + (6.0 * both - 8.0 * near + (f_ref[c, z + 4] - f_ref[c, z]))
            sums[c] = sums[c] + jnp.where(hit, halo[c, z] + weight * total, 0.0)
            sums[2 + c] = sums[2 + c] + jnp.where(own_hit, fix, 0.0)
        return tuple(sums)

    sums = lax.fori_loop(0, layers, update, (sums[0], sums[1], blank, blank), unroll=4)
    scale = 1.0 / (0.5 + fraction)
    own_scale = 1.0 / (0.5 + own_fraction)
    for c in range(2):
        shear_ref[0, c] = jnp.where(low | high, sums[c] * scale, 0.0)
        shear_ref[1, c] = sums[2 + c] * own_scale
    start = jnp.where(lax.axis_index("wall") == 0, layers - 2, 0)
    for c in range(3):
        for z in range(2):
            z_ref[c, z] = vel[c, start + z]


def column_strip(vel, levels, fraction, extra, base, layers):
    shape = levels.shape
    width = 2 * EDGE
    here = iota(shape, 1) // width
    layer = (here + base).astype(jnp.float32)
    opened = opened_at(levels, fraction, layer)
    hit = levels == layer
    hit_down = levels == layer - layers
    hit_up = levels == layer + layers
    scale = 1.0 / (0.5 + fraction)
    fresh, shear = [], []
    for c in range(3):
        q = opened * vel[c]
        b = 6.0 * q
        total = sweep(vel[0] * q, b, 1) + sweep(vel[1] * q, b, 0) - 6.0 * b
        flux = vel[2] * q
        plus = ahead(b - 8.0 * flux, width, 1)
        minus = ahead(b + 8.0 * flux, -width, 1)
        plus_far = ahead(flux, 2 * width, 1)
        minus_far = ahead(flux, -2 * width, 1)
        total = total + jnp.where(here <= layers - 2, plus, 0.0) + jnp.where(here <= layers - 3, plus_far, 0.0)
        total = total + jnp.where(here >= 1, minus, 0.0) - jnp.where(here >= 2, minus_far, 0.0)
        value = vel[c] + gain * opened * total
        fresh.append(value)
        if c < 2:
            down = jnp.where(here > layers - 2, plus, 0.0) + jnp.where(here > layers - 3, plus_far, 0.0)
            up = jnp.where(here < 1, minus, 0.0) - jnp.where(here < 2, minus_far, 0.0)
            part = jnp.where(hit, value, 0.0)
            part = part + gain * fraction * (jnp.where(hit_down, down, 0.0) + jnp.where(hit_up, up, 0.0))
            step = LANE // 2
            while step >= width:
                part = part + pltpu.roll(part, step, 1)
                step //= 2
            more = extra if c == 0 else ahead(extra, width, 1)
            more = jnp.concatenate([jnp.zeros((shape[0] - SUB, LANE), jnp.float32), more], axis=0)
            shear.append((part + gain * fraction * more) * scale)
    return fresh, shear


def everywhere(x):
    step = 2 * EDGE
    x = jnp.where(iota(x.shape, 1) < step, x, 0.0)
    while step < LANE:
        x = x + pltpu.roll(x, step, 1)
        step *= 2
    return x


def side_kernel(layers, spans, bed_in, full, far, shear, strips, *rest):
    got = rest[:spans]
    rest = rest[spans:]
    own_message = rest[0]
    fresh_ref, out_ref = rest[2:]
    _, rows, cols = shear.shape
    tiles = rows // SUB
    tall = tiles + 1
    base = lax.axis_index("wall") * layers
    right_first = even("span")
    results = []
    column = lax.rem(iota((tall * SUB, LANE), 1), 2 * EDGE)
    fresh_sides = []
    for side in range(2):
        first = right_first if side == 0 else jnp.logical_not(right_first)

        def other(n):
            return jnp.where(first, got[0][n], got[1][n] if spans > 1 else 0.0)

        given = column >= EDGE if side == 0 else column < EDGE
        back = EDGE if side == 0 else LANE - EDGE
        both = [jnp.concatenate([other(2 * t + i) for t in range(tall)], axis=0) for i in range(2)]
        turned = [jnp.where(given, pltpu.roll(b, back, 1), 0.0) for b in both]
        theirs = [jnp.where(given, both[0], 0.0), turned[0], jnp.where(given, both[1], 0.0)]
        theirs += [everywhere(turned[1]), everywhere(ahead(turned[1], 2 * EDGE, 1))]
        fields = []
        for n in range(5):
            own = full[side, n * tall : (n + 1) * tall].reshape(tall * SUB, LANE)
            fields.append(own + theirs[n])
        extra = far[side] + other(2 * tall)
        fresh, edge_shear = column_strip(fields[:3], fields[3], fields[4], extra, base, layers)
        fresh_sides.append(fresh)
        results.append(edge_shear)
    for c in range(3):
        fresh_ref[c] = jnp.where(column < EDGE, fresh_sides[0][c], fresh_sides[1][c])[:rows]
    lane = iota((SUB, LANE), 1)
    sub = iota((SUB, LANE), 0)
    lanes = cols // LANE
    for c in range(2):
        right, left = results[0][c], results[1][c]
        for t in range(tall):
            at = slice(t * SUB, (t + 1) * SUB)
            for k in range(lanes):
                cut = slice(k * LANE, (k + 1) * LANE)
                if t == tiles:
                    piece = strips[0, c, :, cut]
                else:
                    piece = shear[c, at, cut]
                    if t == 0:
                        piece = piece + jnp.where(sub < 2, strips[1, c, :, cut], 0.0)
                    if t == tiles - 1:
                        piece = piece + jnp.where(sub >= SUB - 2, strips[1, c, :, cut], 0.0)
                if k == 0:
                    piece = jnp.where(lane < 2, pltpu.roll(left[at], LANE - EDGE, 1), piece)
                if k == lanes - 1:
                    piece = jnp.where(lane >= LANE - 2, pltpu.roll(right[at], LANE - EDGE, 1), piece)
                out_ref[(c * tall + t) * (lanes + 1) + k] = piece
            beyond = jnp.where(lane < 2, pltpu.roll(right[at], LANE - EDGE, 1), 0.0)
            beyond = jnp.where(lane >= LANE - 2, pltpu.roll(left[at], LANE - EDGE, 1), beyond)
            out_ref[(c * tall + t) * (lanes + 1) + lanes] = beyond
    if bed_in:
        used = 2 * tall * (lanes + 1)
        start = 2 * tall + 1
        count = own_message.shape[0] - start
        for i in range(count):
            out_ref[used + i] = own_message[start + i]
            out_ref[used + count + i] = got[0][start + i]


def merge_kernel(layers, new, new_z, fix, fresh, far, flat, final, out_ref, sems):
    _, rows, cols = flat.shape
    lanes = cols // LANE
    wall = lax.axis_index("wall")
    lower = wall == 0
    sub = iota((SUB, LANE), 0)
    lane = iota((SUB, LANE), 1)
    levels = flat[0]
    fraction = flat[1]
    base = wall * layers
    near_from = jnp.where(lower, 0, 1)
    far_from = 1 - near_from
    near_to = jnp.where(lower, layers - 1, 0)
    far_to = jnp.where(lower, layers - 2, 1)
    sign = jnp.where(lower, -1.0, 1.0)
    other = jnp.where(lower, layers, 0)
    near_open = opened_at(levels, fraction, (other + jnp.where(lower, 0, layers - 1)).astype(jnp.float32))
    far_open = opened_at(levels, fraction, (other + jnp.where(lower, 1, layers - 2)).astype(jnp.float32))
    near_gain = gain * opened_at(levels, fraction, (base + near_to).astype(jnp.float32))
    far_gain = gain * opened_at(levels, fraction, (base + far_to).astype(jnp.float32))
    near_w, far_w = far[2, near_from], far[2, far_from]
    copies = []
    for c in range(3):
        for z in range(layers):
            for t in range(rows // SUB):
                at = slice(t * SUB, (t + 1) * SUB)
                side = pltpu.roll(fresh[c, at], (LANE - EDGE - 2 * EDGE * z) % LANE, 1)
                for k in range(lanes):
                    cut = slice(k * LANE, (k + 1) * LANE)
                    piece = new[c, z, at, cut] if c < 2 else new_z[0, z, at, cut]
                    if t == 0:
                        piece = piece + jnp.where(sub < 2, fix[c, z, :, cut], 0.0)
                    if t == rows // SUB - 1:
                        piece = piece + jnp.where(sub >= SUB - 2, fix[c, z, :, cut], 0.0)
                    if k == 0:
                        piece = jnp.where(lane < 2, side, piece)
                    if k == lanes - 1:
                        piece = jnp.where(lane >= LANE - 2, side, piece)
                    out_ref[c, z, at, cut] = piece
        near_q = near_open * far[c, near_from]
        near_f = sign * (near_w * near_q)
        far_f = sign * (far_w * (far_open * far[c, far_from]))
        out_ref[c, near_to] = out_ref[c, near_to] + near_gain * (6.0 * near_q + 8.0 * near_f - far_f)
        out_ref[c, far_to] = out_ref[c, far_to] - far_gain * near_f
        part = layers // 4
        for i in range(4):
            at = pl.ds(i * part, part)
            copies.append(pltpu.make_async_copy(out_ref.at[c, at], final.at[c, at], sems.at[4 * c + i]))
            copies[-1].start()
    for copy in copies:
        copy.wait()


def bed_kernel(tall, lanes, bed_in, mine, theirs, *rest):
    out_ref = rest[-1]
    rows = (tall - 1) * SUB
    wide = (lanes + 1) * LANE
    span = lax.axis_index("span")
    wall = lax.axis_index("wall")
    plane = lax.axis_index("plane")

    def sheared(c):
        whole = []
        for t in range(tall):
            first = (c * tall + t) * (lanes + 1)
            whole.append(
                jnp.concatenate([mine[first + k] + theirs[first + k] for k in range(lanes + 1)], axis=1)
            )
        return jnp.concatenate(whole, axis=0)

    shear_x, shear_y = sheared(0), sheared(1)
    if bed_in:
        used = 2 * tall * (lanes + 1)
        parts = 2 * lanes

        def tile_of(s, w, which):
            pieces = []
            for k in range(parts):
                own = used + which * parts + k
                across = own + 2 * parts
                from_mine = jnp.where(span == s, mine[own], mine[across])
                from_theirs = jnp.where(span == s, theirs[own], theirs[across])
                pieces.append(jnp.where(wall == w, from_mine, from_theirs))
            return pieces

        def window(pieces):
            lane = iota((SUB, LANE), 1)
            low = span == 0
            inside = [jnp.where(low, pieces[k], pieces[lanes + k]) for k in range(lanes)]
            beyond = jnp.where(
                low,
                jnp.where(lane < LANE // 2, pieces[lanes], 0.0),
                jnp.where(lane < LANE // 2, 0.0, pieces[lanes - 1]),
            )
            return jnp.concatenate(inside + [beyond], axis=1)

        sub = iota((SUB, LANE), 0)
        whole = [window(tile_of(s, w, 0)) for s in range(2) for w in range(2)]
        after = tile_of(0, 0, 1)
        before = tile_of(1, 1, 1)
        whole.append(window([jnp.where(sub < EDGE, a, b) for a, b in zip(after, before)]))
        bed = jnp.concatenate(whole, axis=0)
    else:
        bed = rest[0][...]
    square = shear_x * shear_x + shear_y * shear_y
    factor = jnp.maximum(square - threshold_sq, 0.0) / (square + threshold_sq)
    load_x = shear_x * factor
    load_y = shear_y * factor
    divergence = 0.5 * (ahead(load_x, 1, 1) - ahead(load_x, -1, 1)) + 0.5 * (
        ahead(load_y, 1, 0) - ahead(load_y, -1, 0)
    )
    row = iota((tall * SUB, wide), 0)
    col = iota((tall * SUB, wide), 1)
    last_plane = plane == lax.axis_size("plane") - 1
    last_span = span == lax.axis_size("span") - 1
    row_low = jnp.where(last_plane, rows, rows + EDGE)
    row_high = jnp.where(plane == 0, rows + SUB, rows + EDGE)
    col_low = jnp.where(last_span, wide - LANE, wide - LANE // 2)
    col_high = jnp.where(span == 0, wide, wide - LANE // 2)
    valid = ((row < row_low) | (row >= row_high)) & ((col < col_low) | (col >= col_high))

    def step(height):
        around = ahead(height, 1, 0) + ahead(height, -1, 0) + ahead(height, 1, 1) + ahead(height, -1, 1)
        return height - bed_step * divergence + bed_step * slope_rate * (around - 4.0 * height)

    first = jnp.where(valid, step(bed), 0.0)
    out_ref[...] = step(first)[:rows, : lanes * LANE]


def pairings(axis):
    size = lax.axis_size(axis)
    lists = []
    for start in (0, 1):
        found = []
        for i in range(start, size - 1, 2):
            found += [(i, i + 1), (i + 1, i)]
        lists.append(found)
    return lists


def bed_around(bed_height, rows, cols):
    spans = lax.axis_size("span")
    whole = lax.all_gather(bed_height, ("span", "wall"), axis=0, tiled=True)
    padded = jnp.pad(whole, ((0, 0), (EDGE, EDGE)))
    piece = lax.dynamic_slice_in_dim(padded, lax.axis_index("span") * cols, cols + 2 * EDGE, axis=1)
    size = lax.axis_size("plane")
    up = [(i, i + 1) for i in range(size - 1)]
    before = lax.ppermute(piece[-EDGE:], "plane", up)
    after = lax.ppermute(piece[:EDGE], "plane", [(j, i) for i, j in up])
    tall = jnp.concatenate([piece, after, before], axis=0)
    gap = jnp.zeros((tall.shape[0], LANE - 2 * EDGE), jnp.float32)
    return jnp.concatenate([tall[:, EDGE:], gap, tall[:, :EDGE]], axis=1)


def body(velocity, levels, fraction, bed_height):
    _, layers, rows, cols = velocity.shape
    tiles = rows // SUB
    tall = tiles + 1
    lanes = cols // LANE
    spans = lax.axis_size("span")
    walls = lax.axis_size("wall")
    assert walls == 2 and layers * 2 * EDGE == LANE
    bed_in = spans == 2 and bed_height.shape == (SUB, 2 * cols)
    count = 3 * layers // 4 + (2 if bed_in else 1)
    dma = pltpu.SemaphoreType.DMA
    sheet = (3, layers, SUB, cols)
    send_a, send_b, vel, flat, bed, band = call(
        functools.partial(pack_kernel, layers, bed_in),
        [(count, SUB, cols), (count, SUB, cols), velocity.shape, (2, rows, cols), bed_height.shape]
        + [jax.ShapeDtypeStruct((4 * cols, cols), jnp.bfloat16)],
        [pltpu.with_memory_space_constraint(x, pltpu.HBM) for x in (velocity, levels, fraction, bed_height)],
        [pltpu.VMEM(levels.shape, jnp.int32), dma((6,))],
        any_inputs=(0, 1, 2, 3),
        moved=1_000_000,
        limit=10,
    )
    plane_a, plane_b = pairings("plane")
    got_b = lax.ppermute(send_b, "plane", plane_b)
    got_a = lax.ppermute(send_a, "plane", plane_a)

    def inner(comps, more, flops):
        count = len(comps)
        deep = pltpu.VMEM((count, layers + 4, rows, cols), jnp.float32)
        return call(
            functools.partial(inner_kernel, layers, comps),
            [(count, layers, rows, cols)] + more,
            [vel, flat, band],
            [deep, deep, pltpu.VMEM((count, layers * rows, 4 * cols), jnp.bfloat16)]
            + [pltpu.VMEM((count, layers * rows, cols), jnp.float32)],
            flops=flops,
            moved=3_000_000,
        )

    new, shear, edge = inner((0, 1), [(2, rows, cols), (2, 5, tiles, SUB, LANE)], 20_000_000)
    span_lists = [p for p in pairings("span") if p]
    message = (2 * tall + 1 + (4 * lanes if bed_in else 0), SUB, LANE)
    unpacked = call(
        functools.partial(unpack_kernel, layers, bed_in),
        [sheet, (4, SUB, cols), (2, 5 * tall, SUB, LANE), (2, SUB, LANE)] + [message] * len(span_lists),
        [got_a, got_b, edge, bed],
        moved=1_000_000,
        limit=10,
    )
    halo, beside, full, far = unpacked[:4]
    messages = unpacked[4:]
    got = [lax.ppermute(m, "span", pairs) for m, pairs in zip(messages, span_lists)]
    shallow = pltpu.VMEM((2, layers + 4, SUB, cols), jnp.float32)
    (new_z,) = inner((2,), [], 10_000_000)
    fix, strip_shear, send_z = call(
        functools.partial(strip_kernel, layers),
        [sheet, (2, 2, SUB, cols), (3, 2, rows, cols)],
        [vel, flat, halo, beside, new_z],
        [shallow, shallow],
        any_inputs=(4,),
        flops=10_000_000,
        moved=2_000_000,
    )
    got_z = lax.ppermute(send_z, "wall", pairings("wall")[0])
    shear_count = 2 * tall * (lanes + 1)
    out_count = shear_count + (8 * lanes if bed_in else 0)
    fresh, mine = call(
        functools.partial(side_kernel, layers, len(got), bed_in),
        [(3, rows, LANE), (out_count, SUB, LANE)],
        [full, far, shear, strip_shear] + got + [messages[0], new_z],
        any_inputs=(5 + len(got),),
        moved=1_000_000,
        limit=10,
    )
    theirs = lax.ppermute(mine, "wall", pairings("wall")[0])
    (velocity_next,) = call(
        functools.partial(merge_kernel, layers),
        [velocity.shape],
        [new, new_z, fix, fresh, got_z, flat],
        [pltpu.VMEM(velocity.shape, jnp.float32), dma((12,))],
        any_outputs=(0,),
        flops=2_000_000,
        moved=4_000_000,
    )
    extra = [] if bed_in else [bed_around(bed_height, rows, cols)]
    (bed_next,) = call(
        functools.partial(bed_kernel, tall, lanes, bed_in),
        [(rows, cols)],
        [mine, theirs] + extra,
        moved=1_000_000,
        limit=10,
    )
    return velocity_next, bed_next


def solution(mesh):
    return jax.shard_map(
        body,
        mesh=mesh,
        in_specs=(
            P("groups", "wall", "plane", "span"),
            P(("groups", "plane"), "span"),
            P(("groups", "plane"), "span"),
            P(("groups", "plane", "span", "wall"), None),
        ),
        out_specs=(P("groups", "wall", "plane", "span"), P(("groups", "plane"), "span")),
        check_vma=False,
    )
```

```python
import functools

import jax
import jax.numpy as jnp
from jax import lax
from jax.experimental import pallas as pl
from jax.experimental.pallas import tpu as pltpu
from jax.sharding import PartitionSpec as P

time_step = 0.1
bed_step = 0.4
slope_rate = 0.25
threshold_sq = 0.25
gain = time_step / 12.0
EDGE = 4
SUB = 8
LANE = 128
VMEM = pltpu.VMEM
MIB = 1024 * 1024


def call(kernel, outs, ins, scratch=(), any_inputs=(), any_outputs=(), flops=0, moved=0, limit=20, aliases=None):
    specs = [pl.BlockSpec(memory_space=pl.ANY if i in any_inputs else VMEM) for i in range(len(ins))]
    shapes = [s if isinstance(s, jax.ShapeDtypeStruct) else jax.ShapeDtypeStruct(s, jnp.float32) for s in outs]
    return pl.pallas_call(
        kernel,
        out_shape=shapes,
        in_specs=specs,
        out_specs=[pl.BlockSpec(memory_space=pl.ANY if i in any_outputs else VMEM) for i in range(len(outs))],
        scratch_shapes=list(scratch),
        input_output_aliases=aliases or {},
        cost_estimate=pl.CostEstimate(flops=flops, bytes_accessed=moved, transcendentals=0),
        compiler_params=pltpu.CompilerParams(vmem_limit_bytes=limit * MIB),
    )(*ins)


def iota(shape, dim):
    return lax.broadcasted_iota(jnp.int32, shape, dim)


def ahead(x, step, axis):
    return pltpu.roll(x, (-step) % x.shape[axis], axis)


def sweep(flux, b, axis):
    a = 8.0 * flux
    return ahead((b - a) + ahead(flux, 1, axis), 1, axis) + ahead((b + a) - ahead(flux, -1, axis), -1, axis)


def opened_at(level, fraction, layer):
    return jnp.where(level == layer, fraction, jnp.where(layer > level, 1.0, 0.0))


def even(axis):
    return lax.rem(lax.axis_index(axis), 2) == 0


def beyond_terms(tile, level, fraction, base, layers, forward):
    near = pltpu.roll(level, SUB - 1, 0) if forward else pltpu.roll(level, 1, 0)
    far = pltpu.roll(level, SUB - 2, 0) if forward else pltpu.roll(level, 2, 0)
    sign = 1.0 if forward else -1.0
    one = [jnp.zeros(level.shape, jnp.float32)] * 2
    two = list(one)
    for z in range(layers):
        layer = (base + z).astype(jnp.float32)
        opened = opened_at(level, fraction, layer)
        near_hit, far_hit = near == layer, far == layer
        for c in range(2):
            q = opened * tile[c, z]
            flux = sign * (tile[1, z] * q)
            one[c] = one[c] + jnp.where(near_hit, 6.0 * q + 8.0 * flux, 0.0)
            two[c] = two[c] - jnp.where(far_hit, flux, 0.0)
    sub = iota(level.shape, 0)
    source = SUB - 3 if forward else 2
    past = source - 1 if forward else source + 1
    shift = 1 if forward else SUB - 1
    shift_two = 2 if forward else SUB - 2
    found = []
    for c in range(2):
        a = pltpu.roll(jnp.where(sub == source, one[c], 0.0), shift, 0)
        b = pltpu.roll(jnp.where((sub == source) | (sub == past), two[c], 0.0), shift_two, 0)
        found.append(a + b)
    return found


def pack_kernel(layers, bed_in, vel_in, lev_in, frac_in, bed_from, a_ref, b_ref, vel, flat, bed, band_ref, lev, sems):
    _, rows, cols = flat.shape
    wall = lax.axis_index("wall")
    base = wall * layers
    small = [
        pltpu.make_async_copy(lev_in, lev, sems.at[0]),
        pltpu.make_async_copy(frac_in, flat.at[1], sems.at[1]),
        pltpu.make_async_copy(bed_from, bed, sems.at[2]),
    ]
    pieces = []
    for i, (start, size) in enumerate(((0, SUB), (rows - SUB, SUB), (SUB, rows - 2 * SUB))):
        at = pl.ds(start, size)
        pieces.append(pltpu.make_async_copy(vel_in.at[:, :, at, :], vel.at[:, :, at, :], sems.at[3 + i]))
    for copy in small + pieces:
        copy.start()
    tall = iota((cols, cols), 0) - iota((cols, cols), 1)
    flux_band = jnp.where(tall == 1, -8.0, jnp.where(tall == -1, 8.0, 0.0))
    flux_band = flux_band + jnp.where(tall == 2, 1.0, jnp.where(tall == -2, -1.0, 0.0))
    field_band = jnp.where(jnp.abs(tall) == 1, 6.0, jnp.where(tall == 0, -36.0, 0.0))
    for i, band in enumerate((flux_band, flux_band, field_band, field_band)):
        band_ref[i * cols : (i + 1) * cols] = band.astype(jnp.bfloat16)
    sub = iota((SUB, cols), 0)
    pair = sub // 2
    is_even = even("plane")

    def put(n, low, high):
        a_ref[n] = jnp.where(is_even, low, high)
        b_ref[n] = jnp.where(is_even, high, low)

    def stack(fields, place):
        tile = jnp.zeros((SUB, cols), jnp.float32)
        for i, field in enumerate(fields):
            tile = jnp.where(pair == i, pltpu.roll(field, (2 * i + place) % SUB, 0), tile)
        return tile

    for copy in small:
        copy.wait()
    flat[0] = lev[...].astype(jnp.float32)
    low_lev, low_frac = flat[0, rows - SUB :], flat[1, rows - SUB :]
    high_lev, high_frac = flat[0, :SUB], flat[1, :SUB]
    count = 3 * layers // 4
    if bed_in:
        halves = [bed[:, i * cols : (i + 1) * cols] for i in range(bed.shape[1] // cols)]
        put(count + 1, stack(halves, 2), stack(halves, 0))
    for copy in pieces[:2]:
        copy.wait()
    top = vel.at[:, :, pl.ds(0, SUB), :]
    bottom = vel.at[:, :, pl.ds(rows - SUB, SUB), :]
    for c in range(3):
        for k in range(layers // 4):
            low = stack([bottom[c, 4 * k + i] for i in range(4)], 2)
            high = stack([top[c, 4 * k + i] for i in range(4)], 0)
            put(c * (layers // 4) + k, low, high)
    low_far = beyond_terms(bottom, low_lev, low_frac, base, layers, True)
    high_far = beyond_terms(top, high_lev, high_frac, base, layers, False)
    put(count, stack([low_lev, low_frac] + low_far, 2), stack([high_lev, high_frac] + high_far, 0))
    pieces[2].wait()


def gather_edges(read, layers, rows, cols, put):
    lane = iota((rows, LANE), 1)
    column = lax.rem(lane, 2 * EDGE)
    for c in range(3):
        right = jnp.zeros((rows, LANE), jnp.float32)
        left = right
        for z in range(layers):
            group = (lane // (2 * EDGE)) == z
            field = read(c, z)
            last = field[:, cols - LANE :]
            first = field[:, :LANE]
            at = 2 * EDGE * z
            right = jnp.where(group, pltpu.roll(last, (at - (LANE - EDGE)) % LANE, 1), right)
            left = jnp.where(group, pltpu.roll(first, (at + EDGE) % LANE, 1), left)
        put(0, c, jnp.where(column < EDGE, right, 0.0))
        put(1, c, jnp.where(column >= EDGE, left, 0.0))


def repeat_edges(field, rows, cols):
    lane = iota((rows, LANE), 1)
    right = jnp.where(lane < EDGE, pltpu.roll(field[:, cols - LANE :], EDGE, 1), 0.0)
    left = pltpu.roll(jnp.where(lane < EDGE, field[:, :LANE], 0.0), EDGE, 1)
    step = 2 * EDGE
    while step < LANE:
        right = right + pltpu.roll(right, step, 1)
        left = left + pltpu.roll(left, step, 1)
        step *= 2
    return right, left


def inner_kernel(layers, comps, vel, flat, band_ref, *refs):
    with_shear = 0 in comps
    new_ref = refs[0]
    q_ref, f_ref, split_ref, x_ref = refs[-4:]
    _, rows, cols = flat.shape
    base = lax.axis_index("wall") * layers
    lanes = cols // LANE
    blank = jnp.zeros((rows, cols), jnp.float32)
    for n in range(len(comps)):
        for z in (0, 1, layers + 2, layers + 3):
            q_ref[n, z] = blank
            f_ref[n, z] = blank

    def halves(x):
        high = x.astype(jnp.bfloat16)
        return high, (x - high.astype(jnp.float32)).astype(jnp.bfloat16)

    def prepare(z, carry):
        layer = (base + z).astype(jnp.float32)
        at = pl.ds(pl.multiple_of(z * rows, rows), rows)
        for k in range(lanes):
            cut = slice(k * LANE, (k + 1) * LANE)
            opened = opened_at(flat[0, :, cut], flat[1, :, cut], layer)
            vel_x, vel_z = vel[0, z, :, cut], vel[2, z, :, cut]
            for n, c in enumerate(comps):
                q = opened * vel[c, z, :, cut]
                q_ref[n, z + 2, :, cut] = q
                f_ref[n, z + 2, :, cut] = vel_z * q
                parts = halves(vel_x * q) + halves(q)
                for i, part in enumerate(parts):
                    split_ref[n, at, i * cols + k * LANE : i * cols + (k + 1) * LANE] = part
        return carry

    lax.fori_loop(0, layers, prepare, 0)
    for n in range(len(comps)):
        x_ref[n] = jnp.dot(split_ref[n], band_ref[...], preferred_element_type=jnp.float32)

    if with_shear:
        shear_ref, edge_ref = refs[1:3]

        def put(side, n, value):
            edge_ref[side, n] = value.reshape(rows // SUB, SUB, LANE)

        gather_edges(lambda c, z: vel[c, z], layers, rows, cols, put)
        for n in range(2):
            right, left = repeat_edges(flat[n], rows, cols)
            put(0, 3 + n, right)
            put(1, 3 + n, left)

    def outside(z, c, cut):
        total = jnp.zeros((rows, LANE), jnp.float32)
        for offset, weight in ((1, -8.0), (-1, 8.0), (2, 1.0), (-2, -1.0)):
            at = z + offset
            if 0 <= at < layers:
                total = total + weight * f_ref[c, at + 2, :, cut]
                if abs(offset) == 1:
                    total = total + 6.0 * q_ref[c, at + 2, :, cut]
        hit = flat[0, :, cut] == (base + z).astype(jnp.float32)
        return jnp.where(hit, gain * flat[1, :, cut] * total, 0.0)

    sums = []
    if with_shear:
        for k in range(lanes):
            cut = slice(k * LANE, (k + 1) * LANE)
            for c in range(2):
                sums.append(sum(outside(z, c, cut) for z in (-2, -1, layers, layers + 1)))

    def update(z, sums):
        sums = list(sums)
        layer = (base + z).astype(jnp.float32)
        at = pl.ds(pl.multiple_of(z * rows, rows), rows)
        for k in range(lanes):
            cut = slice(k * LANE, (k + 1) * LANE)
            level = flat[0, :, cut]
            weight = gain * opened_at(level, flat[1, :, cut], layer)
            hit = level == layer
            vel_y = vel[1, z, :, cut]
            for n, c in enumerate(comps):
                q = q_ref[n, z + 2, :, cut]
                total = x_ref[n, at, cut] + sweep(vel_y * q, 6.0 * q, 0)
                near = f_ref[n, z + 3, :, cut] - f_ref[n, z + 1, :, cut]
                both = q_ref[n, z + 3, :, cut] + q_ref[n, z + 1, :, cut]
                total = total + (6.0 * both - 8.0 * near + (f_ref[n, z + 4, :, cut] - f_ref[n, z, :, cut]))
                fresh = vel[c, z, :, cut] + weight * total
                new_ref[n, z, :, cut] = fresh
                if with_shear:
                    sums[2 * k + c] = sums[2 * k + c] + jnp.where(hit, fresh, 0.0)
        return tuple(sums)

    sums = lax.fori_loop(0, layers, update, tuple(sums))
    if not with_shear:
        return
    for k in range(lanes):
        cut = slice(k * LANE, (k + 1) * LANE)
        scale = 1.0 / (0.5 + flat[1, :, cut])
        for c in range(2):
            shear_ref[c, :, cut] = sums[2 * k + c] * scale


def unpack_kernel(layers, bed_in, got_a, got_b, edge, bed, halo_ref, beside_ref, full_ref, far_ref, *messages):
    cols = halo_ref.shape[3]
    tiles = edge.shape[2]
    tall = tiles + 1
    sub = iota((SUB, cols), 0)
    is_even = even("plane")

    plane = lax.axis_index("plane")
    has_after, has_before = plane < lax.axis_size("plane") - 1, plane > 0

    def sides(n):
        one, two = got_a[n], got_b[n]
        after, before = jnp.where(is_even, one, two), jnp.where(is_even, two, one)
        return jnp.where(has_after, after, 0.0), jnp.where(has_before, before, 0.0)

    def spread(n, fields):
        low, high = sides(n)
        found = []
        for i in range(fields):
            above = pltpu.roll(high, (SUB - 2 - 2 * i) % SUB, 0)
            below = pltpu.roll(low, (-2 * i) % SUB, 0)
            found.append(jnp.where(sub < 2, below, jnp.where(sub >= SUB - 2, above, 0.0)))
        return found

    for c in range(3):
        for k in range(layers // 4):
            for i, tile in enumerate(spread(c * (layers // 4) + k, 4)):
                halo_ref[c, 4 * k + i] = tile
    count = 3 * layers // 4
    beside = spread(count, 4)
    for i, tile in enumerate(beside):
        beside_ref[i] = tile

    def put(side, n, value):
        full_ref[side, n * tall + tiles] = value

    gather_edges(lambda c, z: halo_ref[c, z], layers, SUB, cols, put)
    for n in range(2):
        right, left = repeat_edges(beside[n], SUB, cols)
        put(0, 3 + n, right)
        put(1, 3 + n, left)
    for side in range(2):
        for n in range(5):
            for t in range(tiles):
                full_ref[side, n * tall + t] = edge[side, n, t]
    lane = iota((SUB, LANE), 1)
    group = lane // (2 * EDGE)
    far_right = [repeat_edges(tile, SUB, cols) for tile in beside[2:]]
    for side in range(2):
        far_ref[side] = jnp.where(group == 0, far_right[0][side], jnp.where(group == 1, far_right[1][side], 0.0))
    right_first = even("span")
    packed = []
    for side, shift in ((0, EDGE), (1, LANE - EDGE)):
        for t in range(tall):
            u, v, w, level, fraction = [full_ref[side, n * tall + t] for n in range(5)]
            last = jnp.where(group == 0, level, jnp.where(group == 1, fraction, 0.0))
            packed.append(u + pltpu.roll(v, shift, 1))
            packed.append(w + pltpu.roll(last, shift, 1))
    for i, message in enumerate(messages):
        is_right = right_first if i == 0 else jnp.logical_not(right_first)
        for n in range(2 * tall):
            message[n] = jnp.where(is_right, packed[n], packed[2 * tall + n])
        message[2 * tall] = jnp.where(is_right, far_ref[0], far_ref[1])
    if bed_in:
        used = 2 * tall + 1
        parts = bed.shape[1] // LANE
        for i in range(parts):
            messages[0][used + i] = bed[:, i * LANE : (i + 1) * LANE]
        per = cols // LANE
        for i, tile in enumerate(spread(count + 1, bed.shape[1] // cols)):
            for j in range(per):
                messages[0][used + parts + i * per + j] = tile[:, j * LANE : (j + 1) * LANE]


def strip_kernel(layers, vel, flat, halo, beside, new_z, fix_ref, shear_ref, z_ref, q_ref, f_ref):
    _, rows, cols = flat.shape
    base = lax.axis_index("wall") * layers
    shape = (SUB, cols)
    sub = iota(shape, 0)
    low, high = sub < 2, sub >= SUB - 2
    blank = jnp.zeros(shape, jnp.float32)

    def faces(first, last):
        return jnp.where(low, first, jnp.where(high, last, 0.0))

    level, fraction = beside[0], beside[1]
    own_level = faces(flat[0, :SUB], flat[0, rows - SUB :])
    own_fraction = faces(flat[1, :SUB], flat[1, rows - SUB :])
    for c in range(2):
        for z in (0, 1, layers + 2, layers + 3):
            q_ref[c, z] = blank
            f_ref[c, z] = blank

    def prepare(z, carry):
        opened = opened_at(level, fraction, (base + z).astype(jnp.float32))
        for c in range(2):
            q = opened * halo[c, z]
            q_ref[c, z + 2] = q
            f_ref[c, z + 2] = halo[2, z] * q
        return carry

    lax.fori_loop(0, layers, prepare, 0, unroll=4)
    sums = []
    for c in range(2):
        found = gain * fraction * beside[2 + c]
        for z in (-2, -1, layers, layers + 1):
            total = blank
            for offset, weight in ((1, -8.0), (-1, 8.0), (2, 1.0), (-2, -1.0)):
                at = z + offset
                if 0 <= at < layers:
                    total = total + weight * f_ref[c, at + 2]
                    if abs(offset) == 1:
                        total = total + 6.0 * q_ref[c, at + 2]
            found = found + jnp.where(level == (base + z).astype(jnp.float32), gain * fraction * total, 0.0)
        sums.append(found)

    def update(z, sums):
        sums = list(sums)
        layer = (base + z).astype(jnp.float32)
        opened = opened_at(level, fraction, layer)
        own_opened = opened_at(own_level, own_fraction, layer)
        weight, own_weight = gain * opened, gain * own_opened
        hit, own_hit = level == layer, own_level == layer
        own_y = faces(vel[1, z, :SUB], vel[1, z, rows - SUB :])
        for c in range(3):
            q = q_ref[c, z + 2] if c < 2 else opened * halo[2, z]
            flux = halo[1, z] * q
            own = own_y if c == 1 else faces(vel[c, z, :SUB], vel[c, z, rows - SUB :])
            own_q = own_opened * own
            own_flux = own_y * own_q
            a, b = 8.0 * flux, 6.0 * q
            own_a, own_b = 8.0 * own_flux, 6.0 * own_q
            less_a, less_b, less = a - own_a, b - own_b, flux - own_flux
            after = jnp.where(sub == 0, less_b - less_a, 0.0) + ahead(jnp.where(low, less, 0.0), 1, 0)
            before = jnp.where(sub == SUB - 1, less_b + less_a, 0.0) - ahead(jnp.where(high, less, 0.0), -1, 0)
            fix = own_weight * faces(ahead(before, -1, 0), ahead(after, 1, 0))
            fix_ref[c, z] = fix
            if c == 2:
                continue
            after = jnp.where(sub == 0, own_b - own_a, b - a) + ahead(jnp.where(low, own_flux, 0.0), 1, 0)
            before = jnp.where(sub == SUB - 1, own_b + own_a, b + a) - ahead(jnp.where(high, own_flux, 0.0), -1, 0)
            total = ahead(after, 1, 0) + ahead(before, -1, 0) + sweep(halo[0, z] * q, b, 1) - 6.0 * b
            near = f_ref[c, z + 3] - f_ref[c, z + 1]
            both = q_ref[c, z + 3] + q_ref[c, z + 1]
            total = total + (6.0 * both - 8.0 * near + (f_ref[c, z + 4] - f_ref[c, z]))
            sums[c] = sums[c] + jnp.where(hit, halo[c, z] + weight * total, 0.0)
            sums[2 + c] = sums[2 + c] + jnp.where(own_hit, fix, 0.0)
        return tuple(sums)

    sums = lax.fori_loop(0, layers, update, (sums[0], sums[1], blank, blank), unroll=4)
    scale = 1.0 / (0.5 + fraction)
    own_scale = 1.0 / (0.5 + own_fraction)
    for c in range(2):
        shear_ref[0, c] = jnp.where(low | high, sums[c] * scale, 0.0)
        shear_ref[1, c] = sums[2 + c] * own_scale
    start = jnp.where(lax.axis_index("wall") == 0, layers - 2, 0)
    for c in range(3):
        for z in range(2):
            z_ref[c, z] = vel[c, start + z]


def column_strip(vel, levels, fraction, extra, base, layers):
    shape = levels.shape
    width = 2 * EDGE
    here = iota(shape, 1) // width
    layer = (here + base).astype(jnp.float32)
    opened = opened_at(levels, fraction, layer)
    hit = levels == layer
    hit_down = levels == layer - layers
    hit_up = levels == layer + layers
    scale = 1.0 / (0.5 + fraction)
    fresh, shear = [], []
    for c in range(3):
        q = opened * vel[c]
        b = 6.0 * q
        total = sweep(vel[0] * q, b, 1) + sweep(vel[1] * q, b, 0) - 6.0 * b
        flux = vel[2] * q
        plus = ahead(b - 8.0 * flux, width, 1)
        minus = ahead(b + 8.0 * flux, -width, 1)
        plus_far = ahead(flux, 2 * width, 1)
        minus_far = ahead(flux, -2 * width, 1)
        total = total + jnp.where(here <= layers - 2, plus, 0.0) + jnp.where(here <= layers - 3, plus_far, 0.0)
        total = total + jnp.where(here >= 1, minus, 0.0) - jnp.where(here >= 2, minus_far, 0.0)
        value = vel[c] + gain * opened * total
        fresh.append(value)
        if c < 2:
            down = jnp.where(here > layers - 2, plus, 0.0) + jnp.where(here > layers - 3, plus_far, 0.0)
            up = jnp.where(here < 1, minus, 0.0) - jnp.where(here < 2, minus_far, 0.0)
            part = jnp.where(hit, value, 0.0)
            part = part + gain * fraction * (jnp.where(hit_down, down, 0.0) + jnp.where(hit_up, up, 0.0))
            step = LANE // 2
            while step >= width:
                part = part + pltpu.roll(part, step, 1)
                step //= 2
            more = extra if c == 0 else ahead(extra, width, 1)
            more = jnp.concatenate([jnp.zeros((shape[0] - SUB, LANE), jnp.float32), more], axis=0)
            shear.append((part + gain * fraction * more) * scale)
    return fresh, shear


def everywhere(x):
    step = 2 * EDGE
    x = jnp.where(iota(x.shape, 1) < step, x, 0.0)
    while step < LANE:
        x = x + pltpu.roll(x, step, 1)
        step *= 2
    return x


def side_kernel(layers, spans, bed_in, full, far, shear, strips, *rest):
    got = rest[:spans]
    rest = rest[spans:]
    own_message = rest[0]
    fresh_ref, out_ref = rest[2:]
    _, rows, cols = shear.shape
    tiles = rows // SUB
    tall = tiles + 1
    base = lax.axis_index("wall") * layers
    right_first = even("span")
    results = []
    column = lax.rem(iota((tall * SUB, LANE), 1), 2 * EDGE)
    fresh_sides = []
    for side in range(2):
        first = right_first if side == 0 else jnp.logical_not(right_first)

        def other(n):
            return jnp.where(first, got[0][n], got[1][n] if spans > 1 else 0.0)

        given = column >= EDGE if side == 0 else column < EDGE
        back = EDGE if side == 0 else LANE - EDGE
        both = [jnp.concatenate([other(2 * t + i) for t in range(tall)], axis=0) for i in range(2)]
        turned = [jnp.where(given, pltpu.roll(b, back, 1), 0.0) for b in both]
        theirs = [jnp.where(given, both[0], 0.0), turned[0], jnp.where(given, both[1], 0.0)]
        theirs += [everywhere(turned[1]), everywhere(ahead(turned[1], 2 * EDGE, 1))]
        fields = []
        for n in range(5):
            own = full[side, n * tall : (n + 1) * tall].reshape(tall * SUB, LANE)
            fields.append(own + theirs[n])
        extra = far[side] + other(2 * tall)
        fresh, edge_shear = column_strip(fields[:3], fields[3], fields[4], extra, base, layers)
        fresh_sides.append(fresh)
        results.append(edge_shear)
    for c in range(3):
        fresh_ref[c] = jnp.where(column < EDGE, fresh_sides[0][c], fresh_sides[1][c])[:rows]
    lane = iota((SUB, LANE), 1)
    sub = iota((SUB, LANE), 0)
    lanes = cols // LANE
    for c in range(2):
        right, left = results[0][c], results[1][c]
        for t in range(tall):
            at = slice(t * SUB, (t + 1) * SUB)
            for k in range(lanes):
                cut = slice(k * LANE, (k + 1) * LANE)
                if t == tiles:
                    piece = strips[0, c, :, cut]
                else:
                    piece = shear[c, at, cut]
                    if t == 0:
                        piece = piece + jnp.where(sub < 2, strips[1, c, :, cut], 0.0)
                    if t == tiles - 1:
                        piece = piece + jnp.where(sub >= SUB - 2, strips[1, c, :, cut], 0.0)
                if k == 0:
                    piece = jnp.where(lane < 2, pltpu.roll(left[at], LANE - EDGE, 1), piece)
                if k == lanes - 1:
                    piece = jnp.where(lane >= LANE - 2, pltpu.roll(right[at], LANE - EDGE, 1), piece)
                out_ref[(c * tall + t) * (lanes + 1) + k] = piece
            beyond = jnp.where(lane < 2, pltpu.roll(right[at], LANE - EDGE, 1), 0.0)
            beyond = jnp.where(lane >= LANE - 2, pltpu.roll(left[at], LANE - EDGE, 1), beyond)
            out_ref[(c * tall + t) * (lanes + 1) + lanes] = beyond
    if bed_in:
        used = 2 * tall * (lanes + 1)
        start = 2 * tall + 1
        count = own_message.shape[0] - start
        for i in range(count):
            out_ref[used + i] = own_message[start + i]
            out_ref[used + count + i] = got[0][start + i]


def merge_kernel(layers, new, new_z, fix, fresh, far, flat, final, out_ref, sems):
    _, rows, cols = flat.shape
    lanes = cols // LANE
    wall = lax.axis_index("wall")
    lower = wall == 0
    sub = iota((SUB, LANE), 0)
    lane = iota((SUB, LANE), 1)
    levels = flat[0]
    fraction = flat[1]
    base = wall * layers
    near_from = jnp.where(lower, 0, 1)
    far_from = 1 - near_from
    near_to = jnp.where(lower, layers - 1, 0)
    far_to = jnp.where(lower, layers - 2, 1)
    sign = jnp.where(lower, -1.0, 1.0)
    other = jnp.where(lower, layers, 0)
    near_open = opened_at(levels, fraction, (other + jnp.where(lower, 0, layers - 1)).astype(jnp.float32))
    far_open = opened_at(levels, fraction, (other + jnp.where(lower, 1, layers - 2)).astype(jnp.float32))
    near_gain = gain * opened_at(levels, fraction, (base + near_to).astype(jnp.float32))
    far_gain = gain * opened_at(levels, fraction, (base + far_to).astype(jnp.float32))
    near_w, far_w = far[2, near_from], far[2, far_from]
    copies = []
    for c in range(3):
        for z in range(layers):
            for t in range(rows // SUB):
                at = slice(t * SUB, (t + 1) * SUB)
                side = pltpu.roll(fresh[c, at], (LANE - EDGE - 2 * EDGE * z) % LANE, 1)
                for k in range(lanes):
                    cut = slice(k * LANE, (k + 1) * LANE)
                    piece = new[c, z, at, cut] if c < 2 else new_z[0, z, at, cut]
                    if t == 0:
                        piece = piece + jnp.where(sub < 2, fix[c, z, :, cut], 0.0)
                    if t == rows // SUB - 1:
                        piece = piece + jnp.where(sub >= SUB - 2, fix[c, z, :, cut], 0.0)
                    if k == 0:
                        piece = jnp.where(lane < 2, side, piece)
                    if k == lanes - 1:
                        piece = jnp.where(lane >= LANE - 2, side, piece)
                    out_ref[c, z, at, cut] = piece
        near_q = near_open * far[c, near_from]
        near_f = sign * (near_w * near_q)
        far_f = sign * (far_w * (far_open * far[c, far_from]))
        out_ref[c, near_to] = out_ref[c, near_to] + near_gain * (6.0 * near_q + 8.0 * near_f - far_f)
        out_ref[c, far_to] = out_ref[c, far_to] - far_gain * near_f
        part = layers // 4
        for i in range(4):
            at = pl.ds(i * part, part)
            copies.append(pltpu.make_async_copy(out_ref.at[c, at], final.at[c, at], sems.at[4 * c + i]))
            copies[-1].start()
    for copy in copies:
        copy.wait()


def bed_kernel(tall, lanes, bed_in, mine, theirs, *rest):
    out_ref = rest[-1]
    rows = (tall - 1) * SUB
    wide = (lanes + 1) * LANE
    span = lax.axis_index("span")
    wall = lax.axis_index("wall")
    plane = lax.axis_index("plane")

    def sheared(c):
        whole = []
        for t in range(tall):
            first = (c * tall + t) * (lanes + 1)
            whole.append(
                jnp.concatenate([mine[first + k] + theirs[first + k] for k in range(lanes + 1)], axis=1)
            )
        return jnp.concatenate(whole, axis=0)

    shear_x, shear_y = sheared(0), sheared(1)
    if bed_in:
        used = 2 * tall * (lanes + 1)
        parts = 2 * lanes

        def tile_of(s, w, which):
            pieces = []
            for k in range(parts):
                own = used + which * parts + k
                across = own + 2 * parts
                from_mine = jnp.where(span == s, mine[own], mine[across])
                from_theirs = jnp.where(span == s, theirs[own], theirs[across])
                pieces.append(jnp.where(wall == w, from_mine, from_theirs))
            return pieces

        def window(pieces):
            lane = iota((SUB, LANE), 1)
            low = span == 0
            inside = [jnp.where(low, pieces[k], pieces[lanes + k]) for k in range(lanes)]
            beyond = jnp.where(
                low,
                jnp.where(lane < LANE // 2, pieces[lanes], 0.0),
                jnp.where(lane < LANE // 2, 0.0, pieces[lanes - 1]),
            )
            return jnp.concatenate(inside + [beyond], axis=1)

        sub = iota((SUB, LANE), 0)
        whole = [window(tile_of(s, w, 0)) for s in range(2) for w in range(2)]
        after = tile_of(0, 0, 1)
        before = tile_of(1, 1, 1)
        whole.append(window([jnp.where(sub < EDGE, a, b) for a, b in zip(after, before)]))
        bed = jnp.concatenate(whole, axis=0)
    else:
        bed = rest[0][...]
    square = shear_x * shear_x + shear_y * shear_y
    factor = jnp.maximum(square - threshold_sq, 0.0) / (square + threshold_sq)
    load_x = shear_x * factor
    load_y = shear_y * factor
    divergence = 0.5 * (ahead(load_x, 1, 1) - ahead(load_x, -1, 1)) + 0.5 * (
        ahead(load_y, 1, 0) - ahead(load_y, -1, 0)
    )
    row = iota((tall * SUB, wide), 0)
    col = iota((tall * SUB, wide), 1)
    last_plane = plane == lax.axis_size("plane") - 1
    last_span = span == lax.axis_size("span") - 1
    row_low = jnp.where(last_plane, rows, rows + EDGE)
    row_high = jnp.where(plane == 0, rows + SUB, rows + EDGE)
    col_low = jnp.where(last_span, wide - LANE, wide - LANE // 2)
    col_high = jnp.where(span == 0, wide, wide - LANE // 2)
    valid = ((row < row_low) | (row >= row_high)) & ((col < col_low) | (col >= col_high))

    def step(height):
        around = ahead(height, 1, 0) + ahead(height, -1, 0) + ahead(height, 1, 1) + ahead(height, -1, 1)
        return height - bed_step * divergence + bed_step * slope_rate * (around - 4.0 * height)

    first = jnp.where(valid, step(bed), 0.0)
    out_ref[...] = step(first)[:rows, : lanes * LANE]


def pairings(axis):
    size = lax.axis_size(axis)
    lists = []
    for start in (0, 1):
        found = []
        for i in range(start, size - 1, 2):
            found += [(i, i + 1), (i + 1, i)]
        lists.append(found)
    return lists


def everyone(axis, lists):
    walls = lax.axis_size("wall")
    full = []
    for pairs in lists:
        target = dict(pairs)
        found = []
        for i in range(lax.axis_size(axis)):
            for w in range(walls):
                to = target[i] * walls + w if i in target else i * walls + walls - 1 - w
                found.append((i * walls + w, to))
        full.append(found)
    return full


def bed_around(bed_height, rows, cols):
    spans = lax.axis_size("span")
    whole = lax.all_gather(bed_height, ("span", "wall"), axis=0, tiled=True)
    padded = jnp.pad(whole, ((0, 0), (EDGE, EDGE)))
    piece = lax.dynamic_slice_in_dim(padded, lax.axis_index("span") * cols, cols + 2 * EDGE, axis=1)
    size = lax.axis_size("plane")
    up = [(i, i + 1) for i in range(size - 1)]
    before = lax.ppermute(piece[-EDGE:], "plane", up)
    after = lax.ppermute(piece[:EDGE], "plane", [(j, i) for i, j in up])
    tall = jnp.concatenate([piece, after, before], axis=0)
    gap = jnp.zeros((tall.shape[0], LANE - 2 * EDGE), jnp.float32)
    return jnp.concatenate([tall[:, EDGE:], gap, tall[:, :EDGE]], axis=1)


def body(velocity, levels, fraction, bed_height):
    _, layers, rows, cols = velocity.shape
    tiles = rows // SUB
    tall = tiles + 1
    lanes = cols // LANE
    spans = lax.axis_size("span")
    walls = lax.axis_size("wall")
    assert walls == 2 and layers * 2 * EDGE == LANE
    bed_in = spans == 2 and bed_height.shape == (SUB, 2 * cols)
    count = 3 * layers // 4 + (2 if bed_in else 1)
    dma = pltpu.SemaphoreType.DMA
    sheet = (3, layers, SUB, cols)
    send_a, send_b, vel, flat, bed, band = call(
        functools.partial(pack_kernel, layers, bed_in),
        [(count, SUB, cols), (count, SUB, cols), velocity.shape, (2, rows, cols), bed_height.shape]
        + [jax.ShapeDtypeStruct((4 * cols, cols), jnp.bfloat16)],
        [pltpu.with_memory_space_constraint(x, pltpu.HBM) for x in (velocity, levels, fraction, bed_height)],
        [pltpu.VMEM(levels.shape, jnp.int32), dma((6,))],
        any_inputs=(0, 1, 2, 3),
        moved=1_000_000,
        limit=10,
    )
    plane_a, plane_b = everyone("plane", pairings("plane"))
    got_b = lax.ppermute(send_b, ("plane", "wall"), plane_b)
    got_a = lax.ppermute(send_a, ("plane", "wall"), plane_a)

    def inner(comps, more, flops):
        count = len(comps)
        deep = pltpu.VMEM((count, layers + 4, rows, cols), jnp.float32)
        return call(
            functools.partial(inner_kernel, layers, comps),
            [(count, layers, rows, cols)] + more,
            [vel, flat, band],
            [deep, deep, pltpu.VMEM((count, layers * rows, 4 * cols), jnp.bfloat16)]
            + [pltpu.VMEM((count, layers * rows, cols), jnp.float32)],
            flops=flops,
            moved=3_000_000,
        )

    new, shear, edge = inner((0, 1), [(2, rows, cols), (2, 5, tiles, SUB, LANE)], 20_000_000)
    span_lists = [p for p in pairings("span") if p]
    message = (2 * tall + 1 + (4 * lanes if bed_in else 0), SUB, LANE)
    unpacked = call(
        functools.partial(unpack_kernel, layers, bed_in),
        [sheet, (4, SUB, cols), (2, 5 * tall, SUB, LANE), (2, SUB, LANE)] + [message] * len(span_lists),
        [got_a, got_b, edge, bed],
        moved=1_000_000,
        limit=10,
    )
    halo, beside, full, far = unpacked[:4]
    messages = unpacked[4:]
    got = [lax.ppermute(m, "span", pairs) for m, pairs in zip(messages, span_lists)]
    shallow = pltpu.VMEM((2, layers + 4, SUB, cols), jnp.float32)
    (new_z,) = inner((2,), [], 10_000_000)
    fix, strip_shear, send_z = call(
        functools.partial(strip_kernel, layers),
        [sheet, (2, 2, SUB, cols), (3, 2, rows, cols)],
        [vel, flat, halo, beside, new_z],
        [shallow, shallow],
        any_inputs=(4,),
        flops=10_000_000,
        moved=2_000_000,
    )
    got_z = lax.ppermute(send_z, "wall", pairings("wall")[0])
    shear_count = 2 * tall * (lanes + 1)
    out_count = shear_count + (8 * lanes if bed_in else 0)
    fresh, mine = call(
        functools.partial(side_kernel, layers, len(got), bed_in),
        [(3, rows, LANE), (out_count, SUB, LANE)],
        [full, far, shear, strip_shear] + got + [messages[0], new_z],
        any_inputs=(5 + len(got),),
        moved=1_000_000,
        limit=10,
    )
    theirs = lax.ppermute(mine, "wall", pairings("wall")[0])
    (velocity_next,) = call(
        functools.partial(merge_kernel, layers),
        [velocity.shape],
        [new, new_z, fix, fresh, got_z, flat],
        [pltpu.VMEM(velocity.shape, jnp.float32), dma((12,))],
        any_outputs=(0,),
        flops=2_000_000,
        moved=4_000_000,
    )
    extra = [] if bed_in else [bed_around(bed_height, rows, cols)]
    (bed_next,) = call(
        functools.partial(bed_kernel, tall, lanes, bed_in),
        [(rows, cols)],
        [mine, theirs] + extra,
        moved=1_000_000,
        limit=10,
    )
    return velocity_next, bed_next


def solution(mesh):
    return jax.shard_map(
        body,
        mesh=mesh,
        in_specs=(
            P("groups", "wall", "plane", "span"),
            P(("groups", "plane"), "span"),
            P(("groups", "plane"), "span"),
            P(("groups", "plane", "span", "wall"), None),
        ),
        out_specs=(P("groups", "wall", "plane", "span"), P(("groups", "plane"), "span")),
        check_vma=False,
    )
```

```python
import functools

import jax
import jax.numpy as jnp
from jax import lax
from jax.experimental import pallas as pl
from jax.experimental.pallas import tpu as pltpu
from jax.sharding import PartitionSpec as P

time_step = 0.1
bed_step = 0.4
slope_rate = 0.25
threshold_sq = 0.25
gain = time_step / 12.0
EDGE = 4
SUB = 8
LANE = 128
VMEM = pltpu.VMEM
MIB = 1024 * 1024


def call(kernel, outs, ins, scratch=(), any_inputs=(), any_outputs=(), flops=0, moved=0, limit=20, aliases=None):
    specs = [pl.BlockSpec(memory_space=pl.ANY if i in any_inputs else VMEM) for i in range(len(ins))]
    shapes = [s if isinstance(s, jax.ShapeDtypeStruct) else jax.ShapeDtypeStruct(s, jnp.float32) for s in outs]
    return pl.pallas_call(
        kernel,
        out_shape=shapes,
        in_specs=specs,
        out_specs=[pl.BlockSpec(memory_space=pl.ANY if i in any_outputs else VMEM) for i in range(len(outs))],
        scratch_shapes=list(scratch),
        input_output_aliases=aliases or {},
        cost_estimate=pl.CostEstimate(flops=flops, bytes_accessed=moved, transcendentals=0),
        compiler_params=pltpu.CompilerParams(vmem_limit_bytes=limit * MIB),
    )(*ins)


def iota(shape, dim):
    return lax.broadcasted_iota(jnp.int32, shape, dim)


def ahead(x, step, axis):
    return pltpu.roll(x, (-step) % x.shape[axis], axis)


def sweep(flux, b, axis):
    a = 8.0 * flux
    return ahead((b - a) + ahead(flux, 1, axis), 1, axis) + ahead((b + a) - ahead(flux, -1, axis), -1, axis)


def opened_at(level, fraction, layer):
    return jnp.where(level == layer, fraction, jnp.where(layer > level, 1.0, 0.0))


def even(axis):
    return lax.rem(lax.axis_index(axis), 2) == 0


def beyond_terms(tile, level, fraction, base, layers, forward):
    near = pltpu.roll(level, SUB - 1, 0) if forward else pltpu.roll(level, 1, 0)
    far = pltpu.roll(level, SUB - 2, 0) if forward else pltpu.roll(level, 2, 0)
    sign = 1.0 if forward else -1.0
    one = [jnp.zeros(level.shape, jnp.float32)] * 2
    two = list(one)
    for z in range(layers):
        layer = (base + z).astype(jnp.float32)
        opened = opened_at(level, fraction, layer)
        near_hit, far_hit = near == layer, far == layer
        for c in range(2):
            q = opened * tile[c, z]
            flux = sign * (tile[1, z] * q)
            one[c] = one[c] + jnp.where(near_hit, 6.0 * q + 8.0 * flux, 0.0)
            two[c] = two[c] - jnp.where(far_hit, flux, 0.0)
    sub = iota(level.shape, 0)
    source = SUB - 3 if forward else 2
    past = source - 1 if forward else source + 1
    shift = 1 if forward else SUB - 1
    shift_two = 2 if forward else SUB - 2
    found = []
    for c in range(2):
        a = pltpu.roll(jnp.where(sub == source, one[c], 0.0), shift, 0)
        b = pltpu.roll(jnp.where((sub == source) | (sub == past), two[c], 0.0), shift_two, 0)
        found.append(a + b)
    return found


def pack_kernel(layers, bed_in, vel_in, lev_in, frac_in, bed_from, a_ref, b_ref, vel, flat, bed, band_ref, lev, sems):
    _, rows, cols = flat.shape
    wall = lax.axis_index("wall")
    base = wall * layers
    small = [
        pltpu.make_async_copy(lev_in, lev, sems.at[0]),
        pltpu.make_async_copy(frac_in, flat.at[1], sems.at[1]),
        pltpu.make_async_copy(bed_from, bed, sems.at[2]),
    ]
    pieces = []
    for i, (start, size) in enumerate(((0, SUB), (rows - SUB, SUB), (SUB, rows - 2 * SUB))):
        at = pl.ds(start, size)
        pieces.append(pltpu.make_async_copy(vel_in.at[:, :, at, :], vel.at[:, :, at, :], sems.at[3 + i]))
    for copy in small + pieces:
        copy.start()
    tall = iota((cols, cols), 0) - iota((cols, cols), 1)
    flux_band = jnp.where(tall == 1, -8.0, jnp.where(tall == -1, 8.0, 0.0))
    flux_band = flux_band + jnp.where(tall == 2, 1.0, jnp.where(tall == -2, -1.0, 0.0))
    field_band = jnp.where(jnp.abs(tall) == 1, 6.0, jnp.where(tall == 0, -36.0, 0.0))
    for i, band in enumerate((flux_band, flux_band, field_band, field_band)):
        band_ref[i * cols : (i + 1) * cols] = band.astype(jnp.bfloat16)
    sub = iota((SUB, cols), 0)
    pair = sub // 2
    is_even = even("plane")

    def put(n, low, high):
        a_ref[n] = jnp.where(is_even, low, high)
        b_ref[n] = jnp.where(is_even, high, low)

    def stack(fields, place):
        tile = jnp.zeros((SUB, cols), jnp.float32)
        for i, field in enumerate(fields):
            tile = jnp.where(pair == i, pltpu.roll(field, (2 * i + place) % SUB, 0), tile)
        return tile

    for copy in small:
        copy.wait()
    flat[0] = lev[...].astype(jnp.float32)
    low_lev, low_frac = flat[0, rows - SUB :], flat[1, rows - SUB :]
    high_lev, high_frac = flat[0, :SUB], flat[1, :SUB]
    count = 3 * layers // 4
    if bed_in:
        halves = [bed[:, i * cols : (i + 1) * cols] for i in range(bed.shape[1] // cols)]
        put(count + 1, stack(halves, 2), stack(halves, 0))
    top = vel.at[:, :, pl.ds(0, SUB), :]
    bottom = vel.at[:, :, pl.ds(rows - SUB, SUB), :]
    quads = [(c, k) for c in range(3) for k in range(layers // 4)]
    pieces[0].wait()
    high = [stack([top[c, 4 * k + i] for i in range(4)], 0) for c, k in quads]
    high_far = beyond_terms(top, high_lev, high_frac, base, layers, False)
    pieces[1].wait()
    for n, (c, k) in enumerate(quads):
        put(n, stack([bottom[c, 4 * k + i] for i in range(4)], 2), high[n])
    low_far = beyond_terms(bottom, low_lev, low_frac, base, layers, True)
    put(count, stack([low_lev, low_frac] + low_far, 2), stack([high_lev, high_frac] + high_far, 0))
    pieces[2].wait()


def gather_edges(read, layers, rows, cols, put):
    lane = iota((rows, LANE), 1)
    column = lax.rem(lane, 2 * EDGE)
    for c in range(3):
        right = jnp.zeros((rows, LANE), jnp.float32)
        left = right
        for z in range(layers):
            group = (lane // (2 * EDGE)) == z
            field = read(c, z)
            last = field[:, cols - LANE :]
            first = field[:, :LANE]
            at = 2 * EDGE * z
            right = jnp.where(group, pltpu.roll(last, (at - (LANE - EDGE)) % LANE, 1), right)
            left = jnp.where(group, pltpu.roll(first, (at + EDGE) % LANE, 1), left)
        put(0, c, jnp.where(column < EDGE, right, 0.0))
        put(1, c, jnp.where(column >= EDGE, left, 0.0))


def over_groups(x):
    step = 2 * EDGE
    while step < LANE:
        x = x + pltpu.roll(x, step, 1) + (pltpu.roll(x, 2 * step, 1) + pltpu.roll(x, 3 * step, 1))
        step *= 4
    return x


def repeat_edges(field, rows, cols):
    lane = iota((rows, LANE), 1)
    right = jnp.where(lane < EDGE, pltpu.roll(field[:, cols - LANE :], EDGE, 1), 0.0)
    left = pltpu.roll(jnp.where(lane < EDGE, field[:, :LANE], 0.0), EDGE, 1)
    return over_groups(right), over_groups(left)


def inner_kernel(layers, comps, vel, flat, band_ref, *refs):
    with_shear = 0 in comps
    new_ref = refs[0]
    q_ref, f_ref, split_ref, x_ref = refs[-4:]
    _, rows, cols = flat.shape
    base = lax.axis_index("wall") * layers
    lanes = cols // LANE
    blank = jnp.zeros((rows, cols), jnp.float32)
    for n in range(len(comps)):
        for z in (0, 1, layers + 2, layers + 3):
            q_ref[n, z] = blank
            f_ref[n, z] = blank

    def halves(x):
        high = x.astype(jnp.bfloat16)
        return high, (x - high.astype(jnp.float32)).astype(jnp.bfloat16)

    def prepare(z, carry):
        layer = (base + z).astype(jnp.float32)
        at = pl.ds(pl.multiple_of(z * rows, rows), rows)
        for k in range(lanes):
            cut = slice(k * LANE, (k + 1) * LANE)
            opened = opened_at(flat[0, :, cut], flat[1, :, cut], layer)
            vel_x, vel_z = vel[0, z, :, cut], vel[2, z, :, cut]
            for n, c in enumerate(comps):
                q = opened * vel[c, z, :, cut]
                q_ref[n, z + 2, :, cut] = q
                f_ref[n, z + 2, :, cut] = vel_z * q
                parts = halves(vel_x * q) + halves(q)
                for i, part in enumerate(parts):
                    split_ref[n, at, i * cols + k * LANE : i * cols + (k + 1) * LANE] = part
        return carry

    lax.fori_loop(0, layers, prepare, 0)
    for n in range(len(comps)):
        x_ref[n] = jnp.dot(split_ref[n], band_ref[...], preferred_element_type=jnp.float32)

    if with_shear:
        shear_ref, edge_ref = refs[1:3]

        def put(side, n, value):
            edge_ref[side, n] = value.reshape(rows // SUB, SUB, LANE)

        gather_edges(lambda c, z: vel[c, z], layers, rows, cols, put)
        for n in range(2):
            right, left = repeat_edges(flat[n], rows, cols)
            put(0, 3 + n, right)
            put(1, 3 + n, left)

    def outside(z, c, cut):
        total = jnp.zeros((rows, LANE), jnp.float32)
        for offset, weight in ((1, -8.0), (-1, 8.0), (2, 1.0), (-2, -1.0)):
            at = z + offset
            if 0 <= at < layers:
                total = total + weight * f_ref[c, at + 2, :, cut]
                if abs(offset) == 1:
                    total = total + 6.0 * q_ref[c, at + 2, :, cut]
        hit = flat[0, :, cut] == (base + z).astype(jnp.float32)
        return jnp.where(hit, gain * flat[1, :, cut] * total, 0.0)

    sums = []
    if with_shear:
        for k in range(lanes):
            cut = slice(k * LANE, (k + 1) * LANE)
            for c in range(2):
                sums.append(sum(outside(z, c, cut) for z in (-2, -1, layers, layers + 1)))

    def update(z, sums):
        sums = list(sums)
        layer = (base + z).astype(jnp.float32)
        at = pl.ds(pl.multiple_of(z * rows, rows), rows)
        for k in range(lanes):
            cut = slice(k * LANE, (k + 1) * LANE)
            level = flat[0, :, cut]
            weight = gain * opened_at(level, flat[1, :, cut], layer)
            hit = level == layer
            vel_y = vel[1, z, :, cut]
            for n, c in enumerate(comps):
                q = q_ref[n, z + 2, :, cut]
                total = x_ref[n, at, cut] + sweep(vel_y * q, 6.0 * q, 0)
                near = f_ref[n, z + 3, :, cut] - f_ref[n, z + 1, :, cut]
                both = q_ref[n, z + 3, :, cut] + q_ref[n, z + 1, :, cut]
                total = total + (6.0 * both - 8.0 * near + (f_ref[n, z + 4, :, cut] - f_ref[n, z, :, cut]))
                fresh = vel[c, z, :, cut] + weight * total
                new_ref[n, z, :, cut] = fresh
                if with_shear:
                    sums[2 * k + c] = sums[2 * k + c] + jnp.where(hit, fresh, 0.0)
        return tuple(sums)

    sums = lax.fori_loop(0, layers, update, tuple(sums))
    if not with_shear:
        return
    for k in range(lanes):
        cut = slice(k * LANE, (k + 1) * LANE)
        scale = 1.0 / (0.5 + flat[1, :, cut])
        for c in range(2):
            shear_ref[c, :, cut] = sums[2 * k + c] * scale


def unpack_kernel(layers, bed_in, got_a, got_b, edge, bed, halo_ref, beside_ref, full_ref, far_ref, *messages):
    cols = halo_ref.shape[3]
    tiles = edge.shape[2]
    tall = tiles + 1
    sub = iota((SUB, cols), 0)
    is_even = even("plane")

    plane = lax.axis_index("plane")
    has_after, has_before = plane < lax.axis_size("plane") - 1, plane > 0

    def sides(n):
        one, two = got_a[n], got_b[n]
        after, before = jnp.where(is_even, one, two), jnp.where(is_even, two, one)
        return jnp.where(has_after, after, 0.0), jnp.where(has_before, before, 0.0)

    def spread(n, fields):
        low, high = sides(n)
        found = []
        for i in range(fields):
            above = pltpu.roll(high, (SUB - 2 - 2 * i) % SUB, 0)
            below = pltpu.roll(low, (-2 * i) % SUB, 0)
            found.append(jnp.where(sub < 2, below, jnp.where(sub >= SUB - 2, above, 0.0)))
        return found

    for c in range(3):
        for k in range(layers // 4):
            for i, tile in enumerate(spread(c * (layers // 4) + k, 4)):
                halo_ref[c, 4 * k + i] = tile
    count = 3 * layers // 4
    beside = spread(count, 4)
    for i, tile in enumerate(beside):
        beside_ref[i] = tile

    def put(side, n, value):
        full_ref[side, n * tall + tiles] = value

    gather_edges(lambda c, z: halo_ref[c, z], layers, SUB, cols, put)
    for n in range(2):
        right, left = repeat_edges(beside[n], SUB, cols)
        put(0, 3 + n, right)
        put(1, 3 + n, left)
    for side in range(2):
        for n in range(5):
            for t in range(tiles):
                full_ref[side, n * tall + t] = edge[side, n, t]
    lane = iota((SUB, LANE), 1)
    group = lane // (2 * EDGE)
    far_right = [repeat_edges(tile, SUB, cols) for tile in beside[2:]]
    for side in range(2):
        far_ref[side] = jnp.where(group == 0, far_right[0][side], jnp.where(group == 1, far_right[1][side], 0.0))
    right_first = even("span")
    packed = []
    for side, shift in ((0, EDGE), (1, LANE - EDGE)):
        for t in range(tall):
            u, v, w, level, fraction = [full_ref[side, n * tall + t] for n in range(5)]
            last = jnp.where(lax.rem(group, 2) == 0, level, fraction)
            packed.append(u + pltpu.roll(v, shift, 1))
            packed.append(w + pltpu.roll(last, shift, 1))
    for i, message in enumerate(messages):
        is_right = right_first if i == 0 else jnp.logical_not(right_first)
        for n in range(2 * tall):
            message[n] = jnp.where(is_right, packed[n], packed[2 * tall + n])
        message[2 * tall] = jnp.where(is_right, far_ref[0], far_ref[1])
    if bed_in:
        used = 2 * tall + 1
        parts = bed.shape[1] // LANE
        for i in range(parts):
            messages[0][used + i] = bed[:, i * LANE : (i + 1) * LANE]
        per = cols // LANE
        for i, tile in enumerate(spread(count + 1, bed.shape[1] // cols)):
            for j in range(per):
                messages[0][used + parts + i * per + j] = tile[:, j * LANE : (j + 1) * LANE]


def strip_kernel(layers, vel, flat, halo, beside, new_z, fix_ref, shear_ref, z_ref, q_ref, f_ref):
    _, rows, cols = flat.shape
    base = lax.axis_index("wall") * layers
    shape = (SUB, cols)
    sub = iota(shape, 0)
    low, high = sub < 2, sub >= SUB - 2
    blank = jnp.zeros(shape, jnp.float32)

    def faces(first, last):
        return jnp.where(low, first, jnp.where(high, last, 0.0))

    level, fraction = beside[0], beside[1]
    own_level = faces(flat[0, :SUB], flat[0, rows - SUB :])
    own_fraction = faces(flat[1, :SUB], flat[1, rows - SUB :])
    for c in range(2):
        for z in (0, 1, layers + 2, layers + 3):
            q_ref[c, z] = blank
            f_ref[c, z] = blank

    def prepare(z, carry):
        opened = opened_at(level, fraction, (base + z).astype(jnp.float32))
        for c in range(2):
            q = opened * halo[c, z]
            q_ref[c, z + 2] = q
            f_ref[c, z + 2] = halo[2, z] * q
        return carry

    lax.fori_loop(0, layers, prepare, 0, unroll=4)
    sums = []
    for c in range(2):
        found = gain * fraction * beside[2 + c]
        for z in (-2, -1, layers, layers + 1):
            total = blank
            for offset, weight in ((1, -8.0), (-1, 8.0), (2, 1.0), (-2, -1.0)):
                at = z + offset
                if 0 <= at < layers:
                    total = total + weight * f_ref[c, at + 2]
                    if abs(offset) == 1:
                        total = total + 6.0 * q_ref[c, at + 2]
            found = found + jnp.where(level == (base + z).astype(jnp.float32), gain * fraction * total, 0.0)
        sums.append(found)

    def update(z, sums):
        sums = list(sums)
        layer = (base + z).astype(jnp.float32)
        opened = opened_at(level, fraction, layer)
        own_opened = opened_at(own_level, own_fraction, layer)
        weight, own_weight = gain * opened, gain * own_opened
        hit, own_hit = level == layer, own_level == layer
        own_y = faces(vel[1, z, :SUB], vel[1, z, rows - SUB :])
        for c in range(3):
            q = q_ref[c, z + 2] if c < 2 else opened * halo[2, z]
            flux = halo[1, z] * q
            own = own_y if c == 1 else faces(vel[c, z, :SUB], vel[c, z, rows - SUB :])
            own_q = own_opened * own
            own_flux = own_y * own_q
            a, b = 8.0 * flux, 6.0 * q
            own_a, own_b = 8.0 * own_flux, 6.0 * own_q
            less_a, less_b, less = a - own_a, b - own_b, flux - own_flux
            after = jnp.where(sub == 0, less_b - less_a, 0.0) + ahead(jnp.where(low, less, 0.0), 1, 0)
            before = jnp.where(sub == SUB - 1, less_b + less_a, 0.0) - ahead(jnp.where(high, less, 0.0), -1, 0)
            fix = own_weight * faces(ahead(before, -1, 0), ahead(after, 1, 0))
            fix_ref[c, z] = fix
            if c == 2:
                continue
            after = jnp.where(sub == 0, own_b - own_a, b - a) + ahead(jnp.where(low, own_flux, 0.0), 1, 0)
            before = jnp.where(sub == SUB - 1, own_b + own_a, b + a) - ahead(jnp.where(high, own_flux, 0.0), -1, 0)
            total = ahead(after, 1, 0) + ahead(before, -1, 0) + sweep(halo[0, z] * q, b, 1) - 6.0 * b
            near = f_ref[c, z + 3] - f_ref[c, z + 1]
            both = q_ref[c, z + 3] + q_ref[c, z + 1]
            total = total + (6.0 * both - 8.0 * near + (f_ref[c, z + 4] - f_ref[c, z]))
            sums[c] = sums[c] + jnp.where(hit, halo[c, z] + weight * total, 0.0)
            sums[2 + c] = sums[2 + c] + jnp.where(own_hit, fix, 0.0)
        return tuple(sums)

    sums = lax.fori_loop(0, layers, update, (sums[0], sums[1], blank, blank), unroll=4)
    scale = 1.0 / (0.5 + fraction)
    own_scale = 1.0 / (0.5 + own_fraction)
    for c in range(2):
        shear_ref[0, c] = jnp.where(low | high, sums[c] * scale, 0.0)
        shear_ref[1, c] = sums[2 + c] * own_scale
    start = jnp.where(lax.axis_index("wall") == 0, layers - 2, 0)
    for c in range(3):
        for z in range(2):
            z_ref[c, z] = vel[c, start + z]


def column_strip(vel, levels, fraction, extra, base, layers):
    shape = levels.shape
    width = 2 * EDGE
    here = iota(shape, 1) // width
    layer = (here + base).astype(jnp.float32)
    opened = opened_at(levels, fraction, layer)
    hit = levels == layer
    hit_down = levels == layer - layers
    hit_up = levels == layer + layers
    scale = 1.0 / (0.5 + fraction)
    fresh, shear = [], []
    for c in range(3):
        q = opened * vel[c]
        b = 6.0 * q
        total = sweep(vel[0] * q, b, 1) + sweep(vel[1] * q, b, 0) - 6.0 * b
        flux = vel[2] * q
        plus = ahead(b - 8.0 * flux, width, 1)
        minus = ahead(b + 8.0 * flux, -width, 1)
        plus_far = ahead(flux, 2 * width, 1)
        minus_far = ahead(flux, -2 * width, 1)
        total = total + jnp.where(here <= layers - 2, plus, 0.0) + jnp.where(here <= layers - 3, plus_far, 0.0)
        total = total + jnp.where(here >= 1, minus, 0.0) - jnp.where(here >= 2, minus_far, 0.0)
        value = vel[c] + gain * opened * total
        fresh.append(value)
        if c < 2:
            down = jnp.where(here > layers - 2, plus, 0.0) + jnp.where(here > layers - 3, plus_far, 0.0)
            up = jnp.where(here < 1, minus, 0.0) - jnp.where(here < 2, minus_far, 0.0)
            part = jnp.where(hit, value, 0.0)
            part = part + gain * fraction * (jnp.where(hit_down, down, 0.0) + jnp.where(hit_up, up, 0.0))
            part = over_groups(part)
            more = extra if c == 0 else ahead(extra, width, 1)
            more = jnp.concatenate([jnp.zeros((shape[0] - SUB, LANE), jnp.float32), more], axis=0)
            shear.append((part + gain * fraction * more) * scale)
    return fresh, shear


def side_kernel(layers, spans, bed_in, full, far, shear, strips, *rest):
    got = rest[:spans]
    rest = rest[spans:]
    own_message = rest[0]
    fresh_ref, out_ref = rest[2:]
    _, rows, cols = shear.shape
    tiles = rows // SUB
    tall = tiles + 1
    base = lax.axis_index("wall") * layers
    right_first = even("span")
    results = []
    column = lax.rem(iota((tall * SUB, LANE), 1), 2 * EDGE)
    alternate = lax.rem(iota((tall * SUB, LANE), 1) // (2 * EDGE), 2)
    fresh_sides = []
    for side in range(2):
        first = right_first if side == 0 else jnp.logical_not(right_first)

        def other(n):
            return jnp.where(first, got[0][n], got[1][n] if spans > 1 else 0.0)

        given = column >= EDGE if side == 0 else column < EDGE
        back = EDGE if side == 0 else LANE - EDGE
        both = [jnp.concatenate([other(2 * t + i) for t in range(tall)], axis=0) for i in range(2)]
        turned = [jnp.where(given, pltpu.roll(b, back, 1), 0.0) for b in both]
        theirs = [jnp.where(given, both[0], 0.0), turned[0], jnp.where(given, both[1], 0.0)]
        theirs.append(jnp.where(alternate == 0, turned[1], pltpu.roll(turned[1], 2 * EDGE, 1)))
        theirs.append(jnp.where(alternate == 1, turned[1], ahead(turned[1], 2 * EDGE, 1)))
        fields = []
        for n in range(5):
            own = full[side, n * tall : (n + 1) * tall].reshape(tall * SUB, LANE)
            fields.append(own + theirs[n])
        extra = far[side] + other(2 * tall)
        fresh, edge_shear = column_strip(fields[:3], fields[3], fields[4], extra, base, layers)
        fresh_sides.append(fresh)
        results.append(edge_shear)
    for c in range(3):
        fresh_ref[c] = jnp.where(column < EDGE, fresh_sides[0][c], fresh_sides[1][c])[:rows]
    lane = iota((SUB, LANE), 1)
    sub = iota((SUB, LANE), 0)
    lanes = cols // LANE
    for c in range(2):
        right, left = results[0][c], results[1][c]
        for t in range(tall):
            at = slice(t * SUB, (t + 1) * SUB)
            for k in range(lanes):
                cut = slice(k * LANE, (k + 1) * LANE)
                if t == tiles:
                    piece = strips[0, c, :, cut]
                else:
                    piece = shear[c, at, cut]
                    if t == 0:
                        piece = piece + jnp.where(sub < 2, strips[1, c, :, cut], 0.0)
                    if t == tiles - 1:
                        piece = piece + jnp.where(sub >= SUB - 2, strips[1, c, :, cut], 0.0)
                if k == 0:
                    piece = jnp.where(lane < 2, pltpu.roll(left[at], LANE - EDGE, 1), piece)
                if k == lanes - 1:
                    piece = jnp.where(lane >= LANE - 2, pltpu.roll(right[at], LANE - EDGE, 1), piece)
                out_ref[(c * tall + t) * (lanes + 1) + k] = piece
            beyond = jnp.where(lane < 2, pltpu.roll(right[at], LANE - EDGE, 1), 0.0)
            beyond = jnp.where(lane >= LANE - 2, pltpu.roll(left[at], LANE - EDGE, 1), beyond)
            out_ref[(c * tall + t) * (lanes + 1) + lanes] = beyond
    if bed_in:
        used = 2 * tall * (lanes + 1)
        start = 2 * tall + 1
        count = own_message.shape[0] - start
        for i in range(count):
            out_ref[used + i] = own_message[start + i]
            out_ref[used + count + i] = got[0][start + i]


def merge_kernel(layers, new, new_z, fix, fresh, far, flat, final, out_ref, sems):
    _, rows, cols = flat.shape
    lanes = cols // LANE
    wall = lax.axis_index("wall")
    lower = wall == 0
    sub = iota((SUB, LANE), 0)
    lane = iota((SUB, LANE), 1)
    levels = flat[0]
    fraction = flat[1]
    base = wall * layers
    near_from = jnp.where(lower, 0, 1)
    far_from = 1 - near_from
    near_to = jnp.where(lower, layers - 1, 0)
    far_to = jnp.where(lower, layers - 2, 1)
    sign = jnp.where(lower, -1.0, 1.0)
    other = jnp.where(lower, layers, 0)
    near_open = opened_at(levels, fraction, (other + jnp.where(lower, 0, layers - 1)).astype(jnp.float32))
    far_open = opened_at(levels, fraction, (other + jnp.where(lower, 1, layers - 2)).astype(jnp.float32))
    near_gain = gain * opened_at(levels, fraction, (base + near_to).astype(jnp.float32))
    far_gain = gain * opened_at(levels, fraction, (base + far_to).astype(jnp.float32))
    near_w, far_w = far[2, near_from], far[2, far_from]
    copies = []
    part = layers // 4

    def merge(c, z):
        for t in range(rows // SUB):
            at = slice(t * SUB, (t + 1) * SUB)
            side = pltpu.roll(fresh[c, at], (LANE - EDGE - 2 * EDGE * z) % LANE, 1)
            for k in range(lanes):
                cut = slice(k * LANE, (k + 1) * LANE)
                piece = new[c, z, at, cut] if c < 2 else new_z[0, z, at, cut]
                if t == 0:
                    piece = piece + jnp.where(sub < 2, fix[c, z, :, cut], 0.0)
                if t == rows // SUB - 1:
                    piece = piece + jnp.where(sub >= SUB - 2, fix[c, z, :, cut], 0.0)
                if k == 0:
                    piece = jnp.where(lane < 2, side, piece)
                if k == lanes - 1:
                    piece = jnp.where(lane >= LANE - 2, side, piece)
                out_ref[c, z, at, cut] = piece

    def send(c, i):
        at = pl.ds(i * part, part)
        copies.append(pltpu.make_async_copy(out_ref.at[c, at], final.at[c, at], sems.at[4 * c + i]))
        copies[-1].start()

    for c in range(3):
        for i in (0, 3, 1, 2):
            for z in range(i * part, (i + 1) * part):
                merge(c, z)
            if i == 3:
                near_q = near_open * far[c, near_from]
                near_f = sign * (near_w * near_q)
                far_f = sign * (far_w * (far_open * far[c, far_from]))
                out_ref[c, near_to] = out_ref[c, near_to] + near_gain * (6.0 * near_q + 8.0 * near_f - far_f)
                out_ref[c, far_to] = out_ref[c, far_to] - far_gain * near_f
                send(c, 0)
            if i > 0:
                send(c, i)
    for copy in copies:
        copy.wait()


def bed_kernel(tall, lanes, bed_in, mine, theirs, *rest):
    out_ref = rest[-1]
    rows = (tall - 1) * SUB
    wide = (lanes + 1) * LANE
    span = lax.axis_index("span")
    wall = lax.axis_index("wall")
    plane = lax.axis_index("plane")

    def sheared(c):
        whole = []
        for t in range(tall):
            first = (c * tall + t) * (lanes + 1)
            whole.append(
                jnp.concatenate([mine[first + k] + theirs[first + k] for k in range(lanes + 1)], axis=1)
            )
        return jnp.concatenate(whole, axis=0)

    shear_x, shear_y = sheared(0), sheared(1)
    if bed_in:
        used = 2 * tall * (lanes + 1)
        parts = 2 * lanes

        def tile_of(s, w, which):
            pieces = []
            for k in range(parts):
                own = used + which * parts + k
                across = own + 2 * parts
                from_mine = jnp.where(span == s, mine[own], mine[across])
                from_theirs = jnp.where(span == s, theirs[own], theirs[across])
                pieces.append(jnp.where(wall == w, from_mine, from_theirs))
            return pieces

        def window(pieces):
            lane = iota((SUB, LANE), 1)
            low = span == 0
            inside = [jnp.where(low, pieces[k], pieces[lanes + k]) for k in range(lanes)]
            beyond = jnp.where(
                low,
                jnp.where(lane < LANE // 2, pieces[lanes], 0.0),
                jnp.where(lane < LANE // 2, 0.0, pieces[lanes - 1]),
            )
            return jnp.concatenate(inside + [beyond], axis=1)

        sub = iota((SUB, LANE), 0)
        whole = [window(tile_of(s, w, 0)) for s in range(2) for w in range(2)]
        after = tile_of(0, 0, 1)
        before = tile_of(1, 1, 1)
        whole.append(window([jnp.where(sub < EDGE, a, b) for a, b in zip(after, before)]))
        bed = jnp.concatenate(whole, axis=0)
    else:
        bed = rest[0][...]
    square = shear_x * shear_x + shear_y * shear_y
    factor = jnp.maximum(square - threshold_sq, 0.0) / (square + threshold_sq)
    load_x = shear_x * factor
    load_y = shear_y * factor
    divergence = 0.5 * (ahead(load_x, 1, 1) - ahead(load_x, -1, 1)) + 0.5 * (
        ahead(load_y, 1, 0) - ahead(load_y, -1, 0)
    )
    row = iota((tall * SUB, wide), 0)
    col = iota((tall * SUB, wide), 1)
    last_plane = plane == lax.axis_size("plane") - 1
    last_span = span == lax.axis_size("span") - 1
    row_low = jnp.where(last_plane, rows, rows + EDGE)
    row_high = jnp.where(plane == 0, rows + SUB, rows + EDGE)
    col_low = jnp.where(last_span, wide - LANE, wide - LANE // 2)
    col_high = jnp.where(span == 0, wide, wide - LANE // 2)
    valid = ((row < row_low) | (row >= row_high)) & ((col < col_low) | (col >= col_high))

    def step(height):
        around = ahead(height, 1, 0) + ahead(height, -1, 0) + ahead(height, 1, 1) + ahead(height, -1, 1)
        return height - bed_step * divergence + bed_step * slope_rate * (around - 4.0 * height)

    first = jnp.where(valid, step(bed), 0.0)
    out_ref[...] = step(first)[:rows, : lanes * LANE]


def pairings(axis):
    size = lax.axis_size(axis)
    lists = []
    for start in (0, 1):
        found = []
        for i in range(start, size - 1, 2):
            found += [(i, i + 1), (i + 1, i)]
        lists.append(found)
    return lists


def everyone(axis, lists):
    walls = lax.axis_size("wall")
    full = []
    for pairs in lists:
        target = dict(pairs)
        found = []
        for i in range(lax.axis_size(axis)):
            for w in range(walls):
                to = target[i] * walls + w if i in target else i * walls + walls - 1 - w
                found.append((i * walls + w, to))
        full.append(found)
    return full


def bed_around(bed_height, rows, cols):
    spans = lax.axis_size("span")
    whole = lax.all_gather(bed_height, ("span", "wall"), axis=0, tiled=True)
    padded = jnp.pad(whole, ((0, 0), (EDGE, EDGE)))
    piece = lax.dynamic_slice_in_dim(padded, lax.axis_index("span") * cols, cols + 2 * EDGE, axis=1)
    size = lax.axis_size("plane")
    up = [(i, i + 1) for i in range(size - 1)]
    before = lax.ppermute(piece[-EDGE:], "plane", up)
    after = lax.ppermute(piece[:EDGE], "plane", [(j, i) for i, j in up])
    tall = jnp.concatenate([piece, after, before], axis=0)
    gap = jnp.zeros((tall.shape[0], LANE - 2 * EDGE), jnp.float32)
    return jnp.concatenate([tall[:, EDGE:], gap, tall[:, :EDGE]], axis=1)


def body(velocity, levels, fraction, bed_height):
    _, layers, rows, cols = velocity.shape
    tiles = rows // SUB
    tall = tiles + 1
    lanes = cols // LANE
    spans = lax.axis_size("span")
    walls = lax.axis_size("wall")
    assert walls == 2 and layers * 2 * EDGE == LANE
    bed_in = spans == 2 and bed_height.shape == (SUB, 2 * cols)
    count = 3 * layers // 4 + (2 if bed_in else 1)
    dma = pltpu.SemaphoreType.DMA
    sheet = (3, layers, SUB, cols)
    send_a, send_b, vel, flat, bed, band = call(
        functools.partial(pack_kernel, layers, bed_in),
        [(count, SUB, cols), (count, SUB, cols), velocity.shape, (2, rows, cols), bed_height.shape]
        + [jax.ShapeDtypeStruct((4 * cols, cols), jnp.bfloat16)],
        [pltpu.with_memory_space_constraint(x, pltpu.HBM) for x in (velocity, levels, fraction, bed_height)],
        [pltpu.VMEM(levels.shape, jnp.int32), dma((6,))],
        any_inputs=(0, 1, 2, 3),
        moved=1_000_000,
        limit=10,
    )
    plane_a, plane_b = everyone("plane", pairings("plane"))
    got_b = lax.ppermute(send_b, ("plane", "wall"), plane_b)
    got_a = lax.ppermute(send_a, ("plane", "wall"), plane_a)

    def inner(comps, more, flops):
        count = len(comps)
        deep = pltpu.VMEM((count, layers + 4, rows, cols), jnp.float32)
        return call(
            functools.partial(inner_kernel, layers, comps),
            [(count, layers, rows, cols)] + more,
            [vel, flat, band],
            [deep, deep, pltpu.VMEM((count, layers * rows, 4 * cols), jnp.bfloat16)]
            + [pltpu.VMEM((count, layers * rows, cols), jnp.float32)],
            flops=flops,
            moved=3_000_000,
        )

    new, shear, edge = inner((0, 1), [(2, rows, cols), (2, 5, tiles, SUB, LANE)], 20_000_000)
    span_lists = [p for p in pairings("span") if p]
    message = (2 * tall + 1 + (4 * lanes if bed_in else 0), SUB, LANE)
    unpacked = call(
        functools.partial(unpack_kernel, layers, bed_in),
        [sheet, (4, SUB, cols), (2, 5 * tall, SUB, LANE), (2, SUB, LANE)] + [message] * len(span_lists),
        [got_a, got_b, edge, bed],
        moved=1_000_000,
        limit=10,
    )
    halo, beside, full, far = unpacked[:4]
    messages = unpacked[4:]
    got = [lax.ppermute(m, "span", pairs) for m, pairs in zip(messages, span_lists)]
    shallow = pltpu.VMEM((2, layers + 4, SUB, cols), jnp.float32)
    (new_z,) = inner((2,), [], 10_000_000)
    fix, strip_shear, send_z = call(
        functools.partial(strip_kernel, layers),
        [sheet, (2, 2, SUB, cols), (3, 2, rows, cols)],
        [vel, flat, halo, beside, new_z],
        [shallow, shallow],
        any_inputs=(4,),
        flops=10_000_000,
        moved=2_000_000,
    )
    got_z = lax.ppermute(send_z, "wall", pairings("wall")[0])
    shear_count = 2 * tall * (lanes + 1)
    out_count = shear_count + (8 * lanes if bed_in else 0)
    fresh, mine = call(
        functools.partial(side_kernel, layers, len(got), bed_in),
        [(3, rows, LANE), (out_count, SUB, LANE)],
        [full, far, shear, strip_shear] + got + [messages[0], new_z],
        any_inputs=(5 + len(got),),
        moved=1_000_000,
        limit=10,
    )
    theirs = lax.ppermute(mine, "wall", pairings("wall")[0])
    (velocity_next,) = call(
        functools.partial(merge_kernel, layers),
        [velocity.shape],
        [new, new_z, fix, fresh, got_z, flat],
        [pltpu.VMEM(velocity.shape, jnp.float32), dma((12,))],
        any_outputs=(0,),
        flops=2_000_000,
        moved=4_000_000,
    )
    extra = [] if bed_in else [bed_around(bed_height, rows, cols)]
    (bed_next,) = call(
        functools.partial(bed_kernel, tall, lanes, bed_in),
        [(rows, cols)],
        [mine, theirs] + extra,
        moved=1_000_000,
        limit=10,
    )
    return velocity_next, bed_next


def solution(mesh):
    return jax.shard_map(
        body,
        mesh=mesh,
        in_specs=(
            P("groups", "wall", "plane", "span"),
            P(("groups", "plane"), "span"),
            P(("groups", "plane"), "span"),
            P(("groups", "plane", "span", "wall"), None),
        ),
        out_specs=(P("groups", "wall", "plane", "span"), P(("groups", "plane"), "span")),
        check_vma=False,
    )
```

```python
import functools

import jax
import jax.numpy as jnp
from jax import lax
from jax.experimental import pallas as pl
from jax.experimental.pallas import tpu as pltpu
from jax.sharding import PartitionSpec as P

time_step = 0.1
bed_step = 0.4
slope_rate = 0.25
threshold_sq = 0.25
gain = time_step / 12.0
EDGE = 4
SUB = 8
LANE = 128
VMEM = pltpu.VMEM
MIB = 1024 * 1024


def call(kernel, outs, ins, scratch=(), any_inputs=(), any_outputs=(), flops=0, moved=0, limit=20, aliases=None):
    specs = [pl.BlockSpec(memory_space=pl.ANY if i in any_inputs else VMEM) for i in range(len(ins))]
    shapes = [s if isinstance(s, jax.ShapeDtypeStruct) else jax.ShapeDtypeStruct(s, jnp.float32) for s in outs]
    return pl.pallas_call(
        kernel,
        out_shape=shapes,
        in_specs=specs,
        out_specs=[pl.BlockSpec(memory_space=pl.ANY if i in any_outputs else VMEM) for i in range(len(outs))],
        scratch_shapes=list(scratch),
        input_output_aliases=aliases or {},
        cost_estimate=pl.CostEstimate(flops=flops, bytes_accessed=moved, transcendentals=0),
        compiler_params=pltpu.CompilerParams(vmem_limit_bytes=limit * MIB),
    )(*ins)


def iota(shape, dim):
    return lax.broadcasted_iota(jnp.int32, shape, dim)


def ahead(x, step, axis):
    return pltpu.roll(x, (-step) % x.shape[axis], axis)


def sweep(flux, b, axis):
    a = 8.0 * flux
    return ahead((b - a) + ahead(flux, 1, axis), 1, axis) + ahead((b + a) - ahead(flux, -1, axis), -1, axis)


def opened_at(level, fraction, layer):
    return jnp.where(level == layer, fraction, jnp.where(layer > level, 1.0, 0.0))


def even(axis):
    return lax.rem(lax.axis_index(axis), 2) == 0


def beyond_terms(tile, level, fraction, base, layers, forward):
    near = pltpu.roll(level, SUB - 1, 0) if forward else pltpu.roll(level, 1, 0)
    far = pltpu.roll(level, SUB - 2, 0) if forward else pltpu.roll(level, 2, 0)
    sign = 1.0 if forward else -1.0
    one = [jnp.zeros(level.shape, jnp.float32)] * 2
    two = list(one)
    for z in range(layers):
        layer = (base + z).astype(jnp.float32)
        opened = opened_at(level, fraction, layer)
        near_hit, far_hit = near == layer, far == layer
        for c in range(2):
            q = opened * tile[c, z]
            flux = sign * (tile[1, z] * q)
            one[c] = one[c] + jnp.where(near_hit, 6.0 * q + 8.0 * flux, 0.0)
            two[c] = two[c] - jnp.where(far_hit, flux, 0.0)
    sub = iota(level.shape, 0)
    source = SUB - 3 if forward else 2
    past = source - 1 if forward else source + 1
    shift = 1 if forward else SUB - 1
    shift_two = 2 if forward else SUB - 2
    found = []
    for c in range(2):
        a = pltpu.roll(jnp.where(sub == source, one[c], 0.0), shift, 0)
        b = pltpu.roll(jnp.where((sub == source) | (sub == past), two[c], 0.0), shift_two, 0)
        found.append(a + b)
    return found


def pack_kernel(layers, bed_in, vel_in, lev_in, frac_in, bed_from, a_ref, b_ref, vel, flat, bed, band_ref, lev, sems):
    _, rows, cols = flat.shape
    wall = lax.axis_index("wall")
    base = wall * layers
    small = [
        pltpu.make_async_copy(lev_in, lev, sems.at[0]),
        pltpu.make_async_copy(frac_in, flat.at[1], sems.at[1]),
        pltpu.make_async_copy(bed_from, bed, sems.at[2]),
    ]
    pieces = []
    for i, (start, size) in enumerate(((0, SUB), (rows - SUB, SUB), (SUB, rows - 2 * SUB))):
        at = pl.ds(start, size)
        pieces.append(pltpu.make_async_copy(vel_in.at[:, :, at, :], vel.at[:, :, at, :], sems.at[3 + i]))
    for copy in small + pieces:
        copy.start()
    tall = iota((cols, cols), 0) - iota((cols, cols), 1)
    flux_band = jnp.where(tall == 1, -8.0, jnp.where(tall == -1, 8.0, 0.0))
    flux_band = flux_band + jnp.where(tall == 2, 1.0, jnp.where(tall == -2, -1.0, 0.0))
    field_band = jnp.where(jnp.abs(tall) == 1, 6.0, jnp.where(tall == 0, -36.0, 0.0))
    for i, band in enumerate((flux_band, flux_band, field_band, field_band)):
        band_ref[i * cols : (i + 1) * cols] = band.astype(jnp.bfloat16)
    sub = iota((SUB, cols), 0)
    pair = sub // 2
    is_even = even("plane")

    def put(n, low, high):
        a_ref[n] = jnp.where(is_even, low, high)
        b_ref[n] = jnp.where(is_even, high, low)

    def stack(fields, place):
        tile = jnp.zeros((SUB, cols), jnp.float32)
        for i, field in enumerate(fields):
            tile = jnp.where(pair == i, pltpu.roll(field, (2 * i + place) % SUB, 0), tile)
        return tile

    for copy in small:
        copy.wait()
    flat[0] = lev[...].astype(jnp.float32)
    low_lev, low_frac = flat[0, rows - SUB :], flat[1, rows - SUB :]
    high_lev, high_frac = flat[0, :SUB], flat[1, :SUB]
    count = 3 * layers // 4
    if bed_in:
        halves = [bed[:, i * cols : (i + 1) * cols] for i in range(bed.shape[1] // cols)]
        put(count + 1, stack(halves, 2), stack(halves, 0))
    top = vel.at[:, :, pl.ds(0, SUB), :]
    bottom = vel.at[:, :, pl.ds(rows - SUB, SUB), :]
    quads = [(c, k) for c in range(3) for k in range(layers // 4)]
    pieces[0].wait()
    high = [stack([top[c, 4 * k + i] for i in range(4)], 0) for c, k in quads]
    high_far = beyond_terms(top, high_lev, high_frac, base, layers, False)
    pieces[1].wait()
    for n, (c, k) in enumerate(quads):
        put(n, stack([bottom[c, 4 * k + i] for i in range(4)], 2), high[n])
    low_far = beyond_terms(bottom, low_lev, low_frac, base, layers, True)
    put(count, stack([low_lev, low_frac] + low_far, 2), stack([high_lev, high_frac] + high_far, 0))
    pieces[2].wait()


def gather_edges(read, layers, rows, cols, put):
    lane = iota((rows, LANE), 1)
    column = lax.rem(lane, 2 * EDGE)
    for c in range(3):
        right = jnp.zeros((rows, LANE), jnp.float32)
        left = right
        for z in range(layers):
            group = (lane // (2 * EDGE)) == z
            field = read(c, z)
            last = field[:, cols - LANE :]
            first = field[:, :LANE]
            at = 2 * EDGE * z
            right = jnp.where(group, pltpu.roll(last, (at - (LANE - EDGE)) % LANE, 1), right)
            left = jnp.where(group, pltpu.roll(first, (at + EDGE) % LANE, 1), left)
        put(0, c, jnp.where(column < EDGE, right, 0.0))
        put(1, c, jnp.where(column >= EDGE, left, 0.0))


def over_groups(x):
    step = 2 * EDGE
    while step < LANE:
        x = x + pltpu.roll(x, step, 1) + (pltpu.roll(x, 2 * step, 1) + pltpu.roll(x, 3 * step, 1))
        step *= 4
    return x


def repeat_edges(field, rows, cols):
    lane = iota((rows, LANE), 1)
    right = jnp.where(lane < EDGE, pltpu.roll(field[:, cols - LANE :], EDGE, 1), 0.0)
    left = pltpu.roll(jnp.where(lane < EDGE, field[:, :LANE], 0.0), EDGE, 1)
    return over_groups(right), over_groups(left)


def inner_kernel(layers, comps, vel, flat, band_ref, *refs):
    with_shear = 0 in comps
    new_ref = refs[0]
    q_ref, f_ref, split_ref, x_ref = refs[-4:]
    _, rows, cols = flat.shape
    base = lax.axis_index("wall") * layers
    lanes = cols // LANE
    blank = jnp.zeros((rows, cols), jnp.float32)
    for n in range(len(comps)):
        for z in (0, 1, layers + 2, layers + 3):
            q_ref[n, z] = blank
            f_ref[n, z] = blank

    def halves(x):
        high = x.astype(jnp.bfloat16)
        return high, (x - high.astype(jnp.float32)).astype(jnp.bfloat16)

    def prepare(z, carry):
        layer = (base + z).astype(jnp.float32)
        at = pl.ds(pl.multiple_of(z * rows, rows), rows)
        for k in range(lanes):
            cut = slice(k * LANE, (k + 1) * LANE)
            opened = opened_at(flat[0, :, cut], flat[1, :, cut], layer)
            vel_x, vel_z = vel[0, z, :, cut], vel[2, z, :, cut]
            for n, c in enumerate(comps):
                q = opened * vel[c, z, :, cut]
                q_ref[n, z + 2, :, cut] = q
                f_ref[n, z + 2, :, cut] = vel_z * q
                parts = halves(vel_x * q) + halves(q)
                for i, part in enumerate(parts):
                    split_ref[n, at, i * cols + k * LANE : i * cols + (k + 1) * LANE] = part
        return carry

    lax.fori_loop(0, layers, prepare, 0, unroll=2)
    for n in range(len(comps)):
        x_ref[n] = jnp.dot(split_ref[n], band_ref[...], preferred_element_type=jnp.float32)

    if with_shear:
        shear_ref, edge_ref = refs[1:3]

        def put(side, n, value):
            edge_ref[side, n] = value.reshape(rows // SUB, SUB, LANE)

        gather_edges(lambda c, z: vel[c, z], layers, rows, cols, put)
        for n in range(2):
            right, left = repeat_edges(flat[n], rows, cols)
            put(0, 3 + n, right)
            put(1, 3 + n, left)

    def outside(z, c, cut):
        total = jnp.zeros((rows, LANE), jnp.float32)
        for offset, weight in ((1, -8.0), (-1, 8.0), (2, 1.0), (-2, -1.0)):
            at = z + offset
            if 0 <= at < layers:
                total = total + weight * f_ref[c, at + 2, :, cut]
                if abs(offset) == 1:
                    total = total + 6.0 * q_ref[c, at + 2, :, cut]
        hit = flat[0, :, cut] == (base + z).astype(jnp.float32)
        return jnp.where(hit, gain * flat[1, :, cut] * total, 0.0)

    sums = []
    if with_shear:
        for k in range(lanes):
            cut = slice(k * LANE, (k + 1) * LANE)
            for c in range(2):
                sums.append(sum(outside(z, c, cut) for z in (-2, -1, layers, layers + 1)))

    def update(z, sums):
        sums = list(sums)
        layer = (base + z).astype(jnp.float32)
        at = pl.ds(pl.multiple_of(z * rows, rows), rows)
        for k in range(lanes):
            cut = slice(k * LANE, (k + 1) * LANE)
            level = flat[0, :, cut]
            weight = gain * opened_at(level, flat[1, :, cut], layer)
            hit = level == layer
            vel_y = vel[1, z, :, cut]
            for n, c in enumerate(comps):
                q = q_ref[n, z + 2, :, cut]
                total = x_ref[n, at, cut] + sweep(vel_y * q, 6.0 * q, 0)
                near = f_ref[n, z + 3, :, cut] - f_ref[n, z + 1, :, cut]
                both = q_ref[n, z + 3, :, cut] + q_ref[n, z + 1, :, cut]
                total = total + (6.0 * both - 8.0 * near + (f_ref[n, z + 4, :, cut] - f_ref[n, z, :, cut]))
                fresh = vel[c, z, :, cut] + weight * total
                new_ref[n, z, :, cut] = fresh
                if with_shear:
                    sums[2 * k + c] = sums[2 * k + c] + jnp.where(hit, fresh, 0.0)
        return tuple(sums)

    sums = lax.fori_loop(0, layers, update, tuple(sums), unroll=1 if with_shear else 2)
    if not with_shear:
        return
    for k in range(lanes):
        cut = slice(k * LANE, (k + 1) * LANE)
        scale = 1.0 / (0.5 + flat[1, :, cut])
        for c in range(2):
            shear_ref[c, :, cut] = sums[2 * k + c] * scale


def bed_window(tiles, first):
    lane = iota((SUB, LANE), 1)
    inside = [jnp.where(first, tiles[k], tiles[2 + k]) for k in range(2)]
    after = jnp.where(lane < 2, tiles[2], 0.0)
    before = jnp.where(lane >= LANE - 2, tiles[1], 0.0)
    return inside + [jnp.where(first, after, before)]


def unpack_kernel(layers, bed_in, got_a, got_b, edge, bed, halo_ref, beside_ref, full_ref, far_ref, bed_ref, *messages):
    cols = halo_ref.shape[3]
    tiles = edge.shape[2]
    tall = tiles + 1
    sub = iota((SUB, cols), 0)
    is_even = even("plane")

    plane = lax.axis_index("plane")
    has_after, has_before = plane < lax.axis_size("plane") - 1, plane > 0

    def sides(n):
        one, two = got_a[n], got_b[n]
        after, before = jnp.where(is_even, one, two), jnp.where(is_even, two, one)
        return jnp.where(has_after, after, 0.0), jnp.where(has_before, before, 0.0)

    def spread(n, fields):
        low, high = sides(n)
        found = []
        for i in range(fields):
            above = pltpu.roll(high, (SUB - 2 - 2 * i) % SUB, 0)
            below = pltpu.roll(low, (-2 * i) % SUB, 0)
            found.append(jnp.where(sub < 2, below, jnp.where(sub >= SUB - 2, above, 0.0)))
        return found

    for c in range(3):
        for k in range(layers // 4):
            for i, tile in enumerate(spread(c * (layers // 4) + k, 4)):
                halo_ref[c, 4 * k + i] = tile
    count = 3 * layers // 4
    beside = spread(count, 4)
    for i, tile in enumerate(beside):
        beside_ref[i] = tile

    def put(side, n, value):
        full_ref[side, n * tall + tiles] = value

    gather_edges(lambda c, z: halo_ref[c, z], layers, SUB, cols, put)
    for n in range(2):
        right, left = repeat_edges(beside[n], SUB, cols)
        put(0, 3 + n, right)
        put(1, 3 + n, left)
    for side in range(2):
        for n in range(5):
            for t in range(tiles):
                full_ref[side, n * tall + t] = edge[side, n, t]
    lane = iota((SUB, LANE), 1)
    group = lane // (2 * EDGE)
    far_right = [repeat_edges(tile, SUB, cols) for tile in beside[2:]]
    for side in range(2):
        far_ref[side] = jnp.where(group == 0, far_right[0][side], jnp.where(group == 1, far_right[1][side], 0.0))
    right_first = even("span")
    packed = []
    for side, shift in ((0, EDGE), (1, LANE - EDGE)):
        for t in range(tall):
            u, v, w, level, fraction = [full_ref[side, n * tall + t] for n in range(5)]
            last = jnp.where(lax.rem(group, 2) == 0, level, fraction)
            packed.append(u + pltpu.roll(v, shift, 1))
            packed.append(w + pltpu.roll(last, shift, 1))
    for i, message in enumerate(messages):
        is_right = right_first if i == 0 else jnp.logical_not(right_first)
        for n in range(2 * tall):
            message[n] = jnp.where(is_right, packed[n], packed[2 * tall + n])
        message[2 * tall] = jnp.where(is_right, far_ref[0], far_ref[1])
    if bed_in:
        used = 2 * tall + 1
        first = lax.axis_index("span") == 0
        own = [bed[:, i * LANE : (i + 1) * LANE] for i in range(4)]
        past = [tile[:, k * LANE : (k + 1) * LANE] for tile in spread(count + 1, 2) for k in range(2)]
        for i, tile in enumerate(bed_window(own, first) + bed_window(past, first)):
            bed_ref[i] = tile
        there = jnp.logical_not(first)
        one, two, three = bed_window(own, there)
        four, five, six = bed_window(past, there)
        row = iota((SUB, LANE), 0)
        messages[0][used] = one
        messages[0][used + 1] = two
        moved = jnp.where(row < EDGE, pltpu.roll(five, 2, 0), pltpu.roll(five, SUB - 2, 0))
        messages[0][used + 2] = jnp.where((row < 2) | (row >= SUB - 2), four, moved)
        rest = pltpu.roll(three, LANE // 4, 1) + pltpu.roll(six, LANE // 2, 1)
        messages[0][used - 1] = jnp.where(first, far_ref[0], far_ref[1]) + rest
    else:
        bed_ref[0] = jnp.zeros((SUB, LANE), jnp.float32)


def strip_kernel(layers, vel, flat, halo, beside, new_z, fix_ref, shear_ref, z_ref, q_ref, f_ref):
    _, rows, cols = flat.shape
    base = lax.axis_index("wall") * layers
    shape = (SUB, cols)
    sub = iota(shape, 0)
    low, high = sub < 2, sub >= SUB - 2
    blank = jnp.zeros(shape, jnp.float32)

    def faces(first, last):
        return jnp.where(low, first, jnp.where(high, last, 0.0))

    level, fraction = beside[0], beside[1]
    own_level = faces(flat[0, :SUB], flat[0, rows - SUB :])
    own_fraction = faces(flat[1, :SUB], flat[1, rows - SUB :])
    for c in range(2):
        for z in (0, 1, layers + 2, layers + 3):
            q_ref[c, z] = blank
            f_ref[c, z] = blank

    def prepare(z, carry):
        opened = opened_at(level, fraction, (base + z).astype(jnp.float32))
        for c in range(2):
            q = opened * halo[c, z]
            q_ref[c, z + 2] = q
            f_ref[c, z + 2] = halo[2, z] * q
        return carry

    lax.fori_loop(0, layers, prepare, 0, unroll=4)
    sums = []
    for c in range(2):
        found = gain * fraction * beside[2 + c]
        for z in (-2, -1, layers, layers + 1):
            total = blank
            for offset, weight in ((1, -8.0), (-1, 8.0), (2, 1.0), (-2, -1.0)):
                at = z + offset
                if 0 <= at < layers:
                    total = total + weight * f_ref[c, at + 2]
                    if abs(offset) == 1:
                        total = total + 6.0 * q_ref[c, at + 2]
            found = found + jnp.where(level == (base + z).astype(jnp.float32), gain * fraction * total, 0.0)
        sums.append(found)

    def update(z, sums):
        sums = list(sums)
        layer = (base + z).astype(jnp.float32)
        opened = opened_at(level, fraction, layer)
        own_opened = opened_at(own_level, own_fraction, layer)
        weight, own_weight = gain * opened, gain * own_opened
        hit, own_hit = level == layer, own_level == layer
        own_y = faces(vel[1, z, :SUB], vel[1, z, rows - SUB :])
        for c in range(3):
            q = q_ref[c, z + 2] if c < 2 else opened * halo[2, z]
            flux = halo[1, z] * q
            own = own_y if c == 1 else faces(vel[c, z, :SUB], vel[c, z, rows - SUB :])
            own_q = own_opened * own
            own_flux = own_y * own_q
            a, b = 8.0 * flux, 6.0 * q
            own_a, own_b = 8.0 * own_flux, 6.0 * own_q
            less_a, less_b, less = a - own_a, b - own_b, flux - own_flux
            after = jnp.where(sub == 0, less_b - less_a, 0.0) + ahead(jnp.where(low, less, 0.0), 1, 0)
            before = jnp.where(sub == SUB - 1, less_b + less_a, 0.0) - ahead(jnp.where(high, less, 0.0), -1, 0)
            fix = own_weight * faces(ahead(before, -1, 0), ahead(after, 1, 0))
            fix_ref[c, z] = fix
            if c == 2:
                continue
            after = jnp.where(sub == 0, own_b - own_a, b - a) + ahead(jnp.where(low, own_flux, 0.0), 1, 0)
            before = jnp.where(sub == SUB - 1, own_b + own_a, b + a) - ahead(jnp.where(high, own_flux, 0.0), -1, 0)
            total = ahead(after, 1, 0) + ahead(before, -1, 0) + sweep(halo[0, z] * q, b, 1) - 6.0 * b
            near = f_ref[c, z + 3] - f_ref[c, z + 1]
            both = q_ref[c, z + 3] + q_ref[c, z + 1]
            total = total + (6.0 * both - 8.0 * near + (f_ref[c, z + 4] - f_ref[c, z]))
            sums[c] = sums[c] + jnp.where(hit, halo[c, z] + weight * total, 0.0)
            sums[2 + c] = sums[2 + c] + jnp.where(own_hit, fix, 0.0)
        return tuple(sums)

    sums = lax.fori_loop(0, layers, update, (sums[0], sums[1], blank, blank), unroll=8)
    scale = 1.0 / (0.5 + fraction)
    own_scale = 1.0 / (0.5 + own_fraction)
    for c in range(2):
        shear_ref[0, c] = jnp.where(low | high, sums[c] * scale, 0.0)
        shear_ref[1, c] = sums[2 + c] * own_scale
    start = jnp.where(lax.axis_index("wall") == 0, layers - 2, 0)
    for c in range(3):
        for z in range(2):
            z_ref[c, z] = vel[c, start + z]


def column_strip(vel, levels, fraction, extra, base, layers):
    shape = levels.shape
    width = 2 * EDGE
    here = iota(shape, 1) // width
    layer = (here + base).astype(jnp.float32)
    opened = opened_at(levels, fraction, layer)
    hit = levels == layer
    hit_down = levels == layer - layers
    hit_up = levels == layer + layers
    scale = 1.0 / (0.5 + fraction)
    fresh, shear = [], []
    for c in range(3):
        q = opened * vel[c]
        b = 6.0 * q
        total = sweep(vel[0] * q, b, 1) + sweep(vel[1] * q, b, 0) - 6.0 * b
        flux = vel[2] * q
        plus = ahead(b - 8.0 * flux, width, 1)
        minus = ahead(b + 8.0 * flux, -width, 1)
        plus_far = ahead(flux, 2 * width, 1)
        minus_far = ahead(flux, -2 * width, 1)
        total = total + jnp.where(here <= layers - 2, plus, 0.0) + jnp.where(here <= layers - 3, plus_far, 0.0)
        total = total + jnp.where(here >= 1, minus, 0.0) - jnp.where(here >= 2, minus_far, 0.0)
        value = vel[c] + gain * opened * total
        fresh.append(value)
        if c < 2:
            down = jnp.where(here > layers - 2, plus, 0.0) + jnp.where(here > layers - 3, plus_far, 0.0)
            up = jnp.where(here < 1, minus, 0.0) - jnp.where(here < 2, minus_far, 0.0)
            part = jnp.where(hit, value, 0.0)
            part = part + gain * fraction * (jnp.where(hit_down, down, 0.0) + jnp.where(hit_up, up, 0.0))
            part = over_groups(part)
            more = extra if c == 0 else ahead(extra, width, 1)
            more = jnp.concatenate([jnp.zeros((shape[0] - SUB, LANE), jnp.float32), more], axis=0)
            shear.append((part + gain * fraction * more) * scale)
    return fresh, shear


def side_kernel(layers, spans, bed_in, full, far, shear, strips, *rest):
    got = rest[:spans]
    rest = rest[spans:]
    own_bed = rest[0]
    fresh_ref, out_ref = rest[2:]
    _, rows, cols = shear.shape
    tiles = rows // SUB
    tall = tiles + 1
    base = lax.axis_index("wall") * layers
    right_first = even("span")
    results = []
    column = lax.rem(iota((tall * SUB, LANE), 1), 2 * EDGE)
    alternate = lax.rem(iota((tall * SUB, LANE), 1) // (2 * EDGE), 2)
    fresh_sides = []
    for side in range(2):
        first = right_first if side == 0 else jnp.logical_not(right_first)

        def other(n):
            return jnp.where(first, got[0][n], got[1][n] if spans > 1 else 0.0)

        given = column >= EDGE if side == 0 else column < EDGE
        back = EDGE if side == 0 else LANE - EDGE
        both = [jnp.concatenate([other(2 * t + i) for t in range(tall)], axis=0) for i in range(2)]
        turned = [jnp.where(given, pltpu.roll(b, back, 1), 0.0) for b in both]
        theirs = [jnp.where(given, both[0], 0.0), turned[0], jnp.where(given, both[1], 0.0)]
        theirs.append(jnp.where(alternate == 0, turned[1], pltpu.roll(turned[1], 2 * EDGE, 1)))
        theirs.append(jnp.where(alternate == 1, turned[1], ahead(turned[1], 2 * EDGE, 1)))
        fields = []
        for n in range(5):
            own = full[side, n * tall : (n + 1) * tall].reshape(tall * SUB, LANE)
            fields.append(own + theirs[n])
        extra = far[side] + other(2 * tall)
        fresh, edge_shear = column_strip(fields[:3], fields[3], fields[4], extra, base, layers)
        fresh_sides.append(fresh)
        results.append(edge_shear)
    for c in range(3):
        fresh_ref[c] = jnp.where(column < EDGE, fresh_sides[0][c], fresh_sides[1][c])[:rows]
    lane = iota((SUB, LANE), 1)
    sub = iota((SUB, LANE), 0)
    lanes = cols // LANE
    for c in range(2):
        right, left = results[0][c], results[1][c]
        for t in range(tall):
            at = slice(t * SUB, (t + 1) * SUB)
            for k in range(lanes):
                cut = slice(k * LANE, (k + 1) * LANE)
                if t == tiles:
                    piece = strips[0, c, :, cut]
                else:
                    piece = shear[c, at, cut]
                    if t == 0:
                        piece = piece + jnp.where(sub < 2, strips[1, c, :, cut], 0.0)
                    if t == tiles - 1:
                        piece = piece + jnp.where(sub >= SUB - 2, strips[1, c, :, cut], 0.0)
                if k == 0:
                    piece = jnp.where(lane < 2, pltpu.roll(left[at], LANE - EDGE, 1), piece)
                if k == lanes - 1:
                    piece = jnp.where(lane >= LANE - 2, pltpu.roll(right[at], LANE - EDGE, 1), piece)
                out_ref[(c * tall + t) * (lanes + 1) + k] = piece
            beyond = jnp.where(lane < 2, pltpu.roll(right[at], LANE - EDGE, 1), 0.0)
            beyond = jnp.where(lane >= LANE - 2, pltpu.roll(left[at], LANE - EDGE, 1), beyond)
            out_ref[(c * tall + t) * (lanes + 1) + lanes] = beyond
    if bed_in:
        used = 2 * tall * (lanes + 1)
        start = 2 * tall + 1
        beyond = (lane < 2) | (lane >= LANE - 2)
        outer = (sub < 2) | (sub >= SUB - 2)
        rest, pack = got[0][start - 1], got[0][start + 2]
        moved = jnp.where(sub < EDGE, pltpu.roll(pack, SUB - 2, 0), pltpu.roll(pack, 2, 0))
        theirs = [got[0][start], got[0][start + 1], jnp.where(beyond, pltpu.roll(rest, LANE - LANE // 4, 1), 0.0)]
        theirs += [jnp.where(outer, pack, 0.0), jnp.where(outer, moved, 0.0)]
        theirs.append(jnp.where(beyond, pltpu.roll(rest, LANE // 2, 1), 0.0))
        for i in range(6):
            out_ref[used + i] = own_bed[i]
            out_ref[used + 6 + i] = theirs[i]


def merge_kernel(layers, new, new_z, fix, fresh, far, flat, final, out_ref, sems):
    _, rows, cols = flat.shape
    lanes = cols // LANE
    wall = lax.axis_index("wall")
    lower = wall == 0
    sub = iota((SUB, LANE), 0)
    lane = iota((SUB, LANE), 1)
    levels = flat[0]
    fraction = flat[1]
    base = wall * layers
    near_from = jnp.where(lower, 0, 1)
    far_from = 1 - near_from
    near_to = jnp.where(lower, layers - 1, 0)
    far_to = jnp.where(lower, layers - 2, 1)
    sign = jnp.where(lower, -1.0, 1.0)
    other = jnp.where(lower, layers, 0)
    near_open = opened_at(levels, fraction, (other + jnp.where(lower, 0, layers - 1)).astype(jnp.float32))
    far_open = opened_at(levels, fraction, (other + jnp.where(lower, 1, layers - 2)).astype(jnp.float32))
    near_gain = gain * opened_at(levels, fraction, (base + near_to).astype(jnp.float32))
    far_gain = gain * opened_at(levels, fraction, (base + far_to).astype(jnp.float32))
    near_w, far_w = far[2, near_from], far[2, far_from]
    copies = []
    part = layers // 4

    def merge(c, z):
        for t in range(rows // SUB):
            at = slice(t * SUB, (t + 1) * SUB)
            side = pltpu.roll(fresh[c, at], (LANE - EDGE - 2 * EDGE * z) % LANE, 1)
            for k in range(lanes):
                cut = slice(k * LANE, (k + 1) * LANE)
                piece = new[c, z, at, cut] if c < 2 else new_z[0, z, at, cut]
                if t == 0:
                    piece = piece + jnp.where(sub < 2, fix[c, z, :, cut], 0.0)
                if t == rows // SUB - 1:
                    piece = piece + jnp.where(sub >= SUB - 2, fix[c, z, :, cut], 0.0)
                if k == 0:
                    piece = jnp.where(lane < 2, side, piece)
                if k == lanes - 1:
                    piece = jnp.where(lane >= LANE - 2, side, piece)
                out_ref[c, z, at, cut] = piece

    def send(c, i):
        at = pl.ds(i * part, part)
        copies.append(pltpu.make_async_copy(out_ref.at[c, at], final.at[c, at], sems.at[4 * c + i]))
        copies[-1].start()

    for c in range(3):
        for i in (0, 3, 1, 2):
            for z in range(i * part, (i + 1) * part):
                merge(c, z)
            if i == 3:
                near_q = near_open * far[c, near_from]
                near_f = sign * (near_w * near_q)
                far_f = sign * (far_w * (far_open * far[c, far_from]))
                out_ref[c, near_to] = out_ref[c, near_to] + near_gain * (6.0 * near_q + 8.0 * near_f - far_f)
                out_ref[c, far_to] = out_ref[c, far_to] - far_gain * near_f
                send(c, 0)
            if i > 0:
                send(c, i)
    for copy in copies:
        copy.wait()


def bed_kernel(tall, lanes, bed_in, mine, theirs, *rest):
    out_ref = rest[-1]
    rows = (tall - 1) * SUB
    wide = (lanes + 1) * LANE
    span = lax.axis_index("span")
    wall = lax.axis_index("wall")
    plane = lax.axis_index("plane")

    def sheared(c):
        whole = []
        for t in range(tall):
            first = (c * tall + t) * (lanes + 1)
            whole.append(
                jnp.concatenate([mine[first + k] + theirs[first + k] for k in range(lanes + 1)], axis=1)
            )
        return jnp.concatenate(whole, axis=0)

    shear_x, shear_y = sheared(0), sheared(1)
    if bed_in:
        used = 2 * tall * (lanes + 1)

        def tile_of(s, w, which):
            pieces = []
            for k in range(lanes + 1):
                own = used + 3 * which + k
                from_mine = jnp.where(span == s, mine[own], mine[own + 6])
                from_theirs = jnp.where(span == s, theirs[own], theirs[own + 6])
                pieces.append(jnp.where(wall == w, from_mine, from_theirs))
            return pieces

        def window(pieces):
            return jnp.concatenate(pieces, axis=1)

        sub = iota((SUB, LANE), 0)
        whole = [window(tile_of(s, w, 0)) for s in range(2) for w in range(2)]
        after = tile_of(0, 0, 1)
        before = tile_of(1, 1, 1)
        whole.append(window([jnp.where(sub < EDGE, a, b) for a, b in zip(after, before)]))
        bed = jnp.concatenate(whole, axis=0)
    else:
        bed = rest[0][...]
    square = shear_x * shear_x + shear_y * shear_y
    factor = jnp.maximum(square - threshold_sq, 0.0) / (square + threshold_sq)
    load_x = shear_x * factor
    load_y = shear_y * factor
    divergence = 0.5 * (ahead(load_x, 1, 1) - ahead(load_x, -1, 1)) + 0.5 * (
        ahead(load_y, 1, 0) - ahead(load_y, -1, 0)
    )
    row = iota((tall * SUB, wide), 0)
    col = iota((tall * SUB, wide), 1)
    last_plane = plane == lax.axis_size("plane") - 1
    last_span = span == lax.axis_size("span") - 1
    row_low = jnp.where(last_plane, rows, rows + EDGE)
    row_high = jnp.where(plane == 0, rows + SUB, rows + EDGE)
    col_low = jnp.where(last_span, wide - LANE, wide - LANE // 2)
    col_high = jnp.where(span == 0, wide, wide - LANE // 2)
    valid = ((row < row_low) | (row >= row_high)) & ((col < col_low) | (col >= col_high))

    def step(height):
        around = ahead(height, 1, 0) + ahead(height, -1, 0) + ahead(height, 1, 1) + ahead(height, -1, 1)
        return height - bed_step * divergence + bed_step * slope_rate * (around - 4.0 * height)

    first = jnp.where(valid, step(bed), 0.0)
    out_ref[...] = step(first)[:rows, : lanes * LANE]


def pairings(axis):
    size = lax.axis_size(axis)
    lists = []
    for start in (0, 1):
        found = []
        for i in range(start, size - 1, 2):
            found += [(i, i + 1), (i + 1, i)]
        lists.append(found)
    return lists


def everyone(axis, lists):
    walls = lax.axis_size("wall")
    full = []
    for pairs in lists:
        target = dict(pairs)
        found = []
        for i in range(lax.axis_size(axis)):
            for w in range(walls):
                to = target[i] * walls + w if i in target else i * walls + walls - 1 - w
                found.append((i * walls + w, to))
        full.append(found)
    return full


def bed_around(bed_height, rows, cols):
    spans = lax.axis_size("span")
    whole = lax.all_gather(bed_height, ("span", "wall"), axis=0, tiled=True)
    padded = jnp.pad(whole, ((0, 0), (EDGE, EDGE)))
    piece = lax.dynamic_slice_in_dim(padded, lax.axis_index("span") * cols, cols + 2 * EDGE, axis=1)
    size = lax.axis_size("plane")
    up = [(i, i + 1) for i in range(size - 1)]
    before = lax.ppermute(piece[-EDGE:], "plane", up)
    after = lax.ppermute(piece[:EDGE], "plane", [(j, i) for i, j in up])
    tall = jnp.concatenate([piece, after, before], axis=0)
    gap = jnp.zeros((tall.shape[0], LANE - 2 * EDGE), jnp.float32)
    return jnp.concatenate([tall[:, EDGE:], gap, tall[:, :EDGE]], axis=1)


def body(velocity, levels, fraction, bed_height):
    _, layers, rows, cols = velocity.shape
    tiles = rows // SUB
    tall = tiles + 1
    lanes = cols // LANE
    spans = lax.axis_size("span")
    walls = lax.axis_size("wall")
    assert walls == 2 and layers * 2 * EDGE == LANE
    bed_in = spans == 2 and lanes == 2 and bed_height.shape == (SUB, 2 * cols)
    count = 3 * layers // 4 + (2 if bed_in else 1)
    dma = pltpu.SemaphoreType.DMA
    sheet = (3, layers, SUB, cols)
    send_a, send_b, vel, flat, bed, band = call(
        functools.partial(pack_kernel, layers, bed_in),
        [(count, SUB, cols), (count, SUB, cols), velocity.shape, (2, rows, cols), bed_height.shape]
        + [jax.ShapeDtypeStruct((4 * cols, cols), jnp.bfloat16)],
        [pltpu.with_memory_space_constraint(x, pltpu.HBM) for x in (velocity, levels, fraction, bed_height)],
        [pltpu.VMEM(levels.shape, jnp.int32), dma((6,))],
        any_inputs=(0, 1, 2, 3),
        moved=1_000_000,
        limit=10,
    )
    plane_a, plane_b = everyone("plane", pairings("plane"))
    got_b = lax.ppermute(send_b, ("plane", "wall"), plane_b)
    got_a = lax.ppermute(send_a, ("plane", "wall"), plane_a)

    def inner(comps, more, flops):
        count = len(comps)
        deep = pltpu.VMEM((count, layers + 4, rows, cols), jnp.float32)
        return call(
            functools.partial(inner_kernel, layers, comps),
            [(count, layers, rows, cols)] + more,
            [vel, flat, band],
            [deep, deep, pltpu.VMEM((count, layers * rows, 4 * cols), jnp.bfloat16)]
            + [pltpu.VMEM((count, layers * rows, cols), jnp.float32)],
            flops=flops,
            moved=3_000_000,
        )

    new, shear, edge = inner((0, 1), [(2, rows, cols), (2, 5, tiles, SUB, LANE)], 20_000_000)
    span_lists = [p for p in pairings("span") if p]
    message = (2 * tall + 1 + (3 if bed_in else 0), SUB, LANE)
    unpacked = call(
        functools.partial(unpack_kernel, layers, bed_in),
        [sheet, (4, SUB, cols), (2, 5 * tall, SUB, LANE), (2, SUB, LANE), (6, SUB, LANE)]
        + [message] * len(span_lists),
        [got_a, got_b, edge, bed],
        moved=1_000_000,
        limit=10,
    )
    halo, beside, full, far, own_bed = unpacked[:5]
    messages = unpacked[5:]
    got = [lax.ppermute(m, "span", pairs) for m, pairs in zip(messages, span_lists)]
    shallow = pltpu.VMEM((2, layers + 4, SUB, cols), jnp.float32)
    (new_z,) = inner((2,), [], 10_000_000)
    fix, strip_shear, send_z = call(
        functools.partial(strip_kernel, layers),
        [sheet, (2, 2, SUB, cols), (3, 2, rows, cols)],
        [vel, flat, halo, beside, new_z],
        [shallow, shallow],
        any_inputs=(4,),
        flops=10_000_000,
        moved=2_000_000,
    )
    got_z = lax.ppermute(send_z, "wall", pairings("wall")[0])
    shear_count = 2 * tall * (lanes + 1)
    out_count = shear_count + (12 if bed_in else 0)
    fresh, mine = call(
        functools.partial(side_kernel, layers, len(got), bed_in),
        [(3, rows, LANE), (out_count, SUB, LANE)],
        [full, far, shear, strip_shear] + got + [own_bed, new_z],
        any_inputs=(5 + len(got),),
        moved=1_000_000,
        limit=10,
    )
    theirs = lax.ppermute(mine, "wall", pairings("wall")[0])
    (velocity_next,) = call(
        functools.partial(merge_kernel, layers),
        [velocity.shape],
        [new, new_z, fix, fresh, got_z, flat],
        [pltpu.VMEM(velocity.shape, jnp.float32), dma((12,))],
        any_outputs=(0,),
        flops=2_000_000,
        moved=4_000_000,
    )
    extra = [] if bed_in else [bed_around(bed_height, rows, cols)]
    (bed_next,) = call(
        functools.partial(bed_kernel, tall, lanes, bed_in),
        [(rows, cols)],
        [mine, theirs] + extra,
        moved=1_000_000,
        limit=10,
    )
    return velocity_next, bed_next


def solution(mesh):
    return jax.shard_map(
        body,
        mesh=mesh,
        in_specs=(
            P("groups", "wall", "plane", "span"),
            P(("groups", "plane"), "span"),
            P(("groups", "plane"), "span"),
            P(("groups", "plane", "span", "wall"), None),
        ),
        out_specs=(P("groups", "wall", "plane", "span"), P(("groups", "plane"), "span")),
        check_vma=False,
    )
```

```python
import functools

import jax
import jax.numpy as jnp
from jax import lax
from jax.experimental import pallas as pl
from jax.experimental.pallas import tpu as pltpu
from jax.sharding import PartitionSpec as P

time_step = 0.1
bed_step = 0.4
slope_rate = 0.25
threshold_sq = 0.25
gain = time_step / 12.0
EDGE = 4
SUB = 8
LANE = 128
VMEM = pltpu.VMEM
MIB = 1024 * 1024


def call(kernel, outs, ins, scratch=(), any_inputs=(), any_outputs=(), flops=0, moved=0, limit=20, aliases=None):
    specs = [pl.BlockSpec(memory_space=pl.ANY if i in any_inputs else VMEM) for i in range(len(ins))]
    shapes = [s if isinstance(s, jax.ShapeDtypeStruct) else jax.ShapeDtypeStruct(s, jnp.float32) for s in outs]
    return pl.pallas_call(
        kernel,
        out_shape=shapes,
        in_specs=specs,
        out_specs=[pl.BlockSpec(memory_space=pl.ANY if i in any_outputs else VMEM) for i in range(len(outs))],
        scratch_shapes=list(scratch),
        input_output_aliases=aliases or {},
        cost_estimate=pl.CostEstimate(flops=flops, bytes_accessed=moved, transcendentals=0),
        compiler_params=pltpu.CompilerParams(vmem_limit_bytes=limit * MIB),
    )(*ins)


def iota(shape, dim):
    return lax.broadcasted_iota(jnp.int32, shape, dim)


def ahead(x, step, axis):
    return pltpu.roll(x, (-step) % x.shape[axis], axis)


def sweep(flux, b, axis):
    a = 8.0 * flux
    return ahead((b - a) + ahead(flux, 1, axis), 1, axis) + ahead((b + a) - ahead(flux, -1, axis), -1, axis)


def opened_at(level, fraction, layer):
    return jnp.where(level == layer, fraction, jnp.where(layer > level, 1.0, 0.0))


def even(axis):
    return lax.rem(lax.axis_index(axis), 2) == 0


def beyond_terms(tile, level, fraction, base, layers, forward):
    near = pltpu.roll(level, SUB - 1, 0) if forward else pltpu.roll(level, 1, 0)
    far = pltpu.roll(level, SUB - 2, 0) if forward else pltpu.roll(level, 2, 0)
    sign = 1.0 if forward else -1.0
    one = [jnp.zeros(level.shape, jnp.float32)] * 2
    two = list(one)
    for z in range(layers):
        layer = (base + z).astype(jnp.float32)
        opened = opened_at(level, fraction, layer)
        near_hit, far_hit = near == layer, far == layer
        for c in range(2):
            q = opened * tile[c, z]
            flux = sign * (tile[1, z] * q)
            one[c] = one[c] + jnp.where(near_hit, 6.0 * q + 8.0 * flux, 0.0)
            two[c] = two[c] - jnp.where(far_hit, flux, 0.0)
    sub = iota(level.shape, 0)
    source = SUB - 3 if forward else 2
    past = source - 1 if forward else source + 1
    shift = 1 if forward else SUB - 1
    shift_two = 2 if forward else SUB - 2
    found = []
    for c in range(2):
        a = pltpu.roll(jnp.where(sub == source, one[c], 0.0), shift, 0)
        b = pltpu.roll(jnp.where((sub == source) | (sub == past), two[c], 0.0), shift_two, 0)
        found.append(a + b)
    return found


def pack_kernel(layers, bed_in, vel_in, lev_in, frac_in, bed_from, a_ref, b_ref, vel, flat, bed, band_ref, lev, sems):
    _, rows, cols = flat.shape
    wall = lax.axis_index("wall")
    base = wall * layers
    small = [
        pltpu.make_async_copy(lev_in, lev, sems.at[0]),
        pltpu.make_async_copy(frac_in, flat.at[1], sems.at[1]),
        pltpu.make_async_copy(bed_from, bed, sems.at[2]),
    ]
    pieces = []
    for i, (start, size) in enumerate(((0, SUB), (rows - SUB, SUB), (SUB, rows - 2 * SUB))):
        at = pl.ds(start, size)
        pieces.append(pltpu.make_async_copy(vel_in.at[:, :, at, :], vel.at[:, :, at, :], sems.at[3 + i]))
    for copy in small + pieces:
        copy.start()
    tall = iota((cols, cols), 0) - iota((cols, cols), 1)
    flux_band = jnp.where(tall == 1, -8.0, jnp.where(tall == -1, 8.0, 0.0))
    flux_band = flux_band + jnp.where(tall == 2, 1.0, jnp.where(tall == -2, -1.0, 0.0))
    field_band = jnp.where(jnp.abs(tall) == 1, 6.0, jnp.where(tall == 0, -36.0, 0.0))
    for i, band in enumerate((flux_band, flux_band, field_band, field_band)):
        band_ref[i * cols : (i + 1) * cols] = band.astype(jnp.bfloat16)
    sub = iota((SUB, cols), 0)
    pair = sub // 2
    is_even = even("plane")

    def put(n, low, high):
        a_ref[n] = jnp.where(is_even, low, high)
        b_ref[n] = jnp.where(is_even, high, low)

    def stack(fields, place):
        tile = jnp.zeros((SUB, cols), jnp.float32)
        for i, field in enumerate(fields):
            tile = jnp.where(pair == i, pltpu.roll(field, (2 * i + place) % SUB, 0), tile)
        return tile

    for copy in small:
        copy.wait()
    flat[0] = lev[...].astype(jnp.float32)
    low_lev, low_frac = flat[0, rows - SUB :], flat[1, rows - SUB :]
    high_lev, high_frac = flat[0, :SUB], flat[1, :SUB]
    count = 3 * layers // 4
    if bed_in:
        halves = [bed[:, i * cols : (i + 1) * cols] for i in range(bed.shape[1] // cols)]
        put(count + 1, stack(halves, 2), stack(halves, 0))
    top = vel.at[:, :, pl.ds(0, SUB), :]
    bottom = vel.at[:, :, pl.ds(rows - SUB, SUB), :]
    quads = [(c, k) for c in range(3) for k in range(layers // 4)]
    pieces[0].wait()
    high = [stack([top[c, 4 * k + i] for i in range(4)], 0) for c, k in quads]
    high_far = beyond_terms(top, high_lev, high_frac, base, layers, False)
    pieces[1].wait()
    for n, (c, k) in enumerate(quads):
        put(n, stack([bottom[c, 4 * k + i] for i in range(4)], 2), high[n])
    low_far = beyond_terms(bottom, low_lev, low_frac, base, layers, True)
    put(count, stack([low_lev, low_frac] + low_far, 2), stack([high_lev, high_frac] + high_far, 0))
    pieces[2].wait()


def gather_edges(read, layers, rows, cols, put):
    lane = iota((rows, LANE), 1)
    column = lax.rem(lane, 2 * EDGE)
    for c in range(3):
        right = jnp.zeros((rows, LANE), jnp.float32)
        left = right
        for z in range(layers):
            group = (lane // (2 * EDGE)) == z
            field = read(c, z)
            last = field[:, cols - LANE :]
            first = field[:, :LANE]
            at = 2 * EDGE * z
            right = jnp.where(group, pltpu.roll(last, (at - (LANE - EDGE)) % LANE, 1), right)
            left = jnp.where(group, pltpu.roll(first, (at + EDGE) % LANE, 1), left)
        put(0, c, jnp.where(column < EDGE, right, 0.0))
        put(1, c, jnp.where(column >= EDGE, left, 0.0))


def over_groups(x):
    step = 2 * EDGE
    while step < LANE:
        x = x + pltpu.roll(x, step, 1) + (pltpu.roll(x, 2 * step, 1) + pltpu.roll(x, 3 * step, 1))
        step *= 4
    return x


def repeat_edges(field, rows, cols):
    lane = iota((rows, LANE), 1)
    right = jnp.where(lane < EDGE, pltpu.roll(field[:, cols - LANE :], EDGE, 1), 0.0)
    left = pltpu.roll(jnp.where(lane < EDGE, field[:, :LANE], 0.0), EDGE, 1)
    return over_groups(right), over_groups(left)


def inner_change(z, cut, vel_y, q_ref, f_ref, x_ref):
    q = q_ref[z + 2, :, cut]
    rows = q.shape[0]
    total = x_ref[pl.ds(pl.multiple_of(z * rows, rows), rows), cut] + sweep(vel_y * q, 6.0 * q, 0)
    near = f_ref[z + 3, :, cut] - f_ref[z + 1, :, cut]
    both = q_ref[z + 3, :, cut] + q_ref[z + 1, :, cut]
    return total + (6.0 * both - 8.0 * near + (f_ref[z + 4, :, cut] - f_ref[z, :, cut]))


def third_kernel(layers, vel, flat, q_ref, f_ref, x_ref, new_ref):
    _, rows, cols = flat.shape
    base = lax.axis_index("wall") * layers

    def update(z, carry):
        layer = (base + z).astype(jnp.float32)
        for k in range(cols // LANE):
            cut = slice(k * LANE, (k + 1) * LANE)
            weight = gain * opened_at(flat[0, :, cut], flat[1, :, cut], layer)
            change = inner_change(z, cut, vel[1, z, :, cut], q_ref, f_ref, x_ref)
            new_ref[0, z, :, cut] = vel[2, z, :, cut] + weight * change
        return carry

    lax.fori_loop(0, layers, update, 0, unroll=2)


def inner_kernel(layers, vel, flat, band_ref, new_ref, shear_ref, edge_ref, third_q, third_f, third_x, *scratch):
    q_pair, f_pair, split_ref, x_pair = scratch
    q_ref = [q_pair.at[0], q_pair.at[1], third_q]
    f_ref = [f_pair.at[0], f_pair.at[1], third_f]
    x_ref = [x_pair.at[0], x_pair.at[1], third_x]
    _, rows, cols = flat.shape
    base = lax.axis_index("wall") * layers
    lanes = cols // LANE
    blank = jnp.zeros((rows, cols), jnp.float32)
    for c in range(3):
        for z in (0, 1, layers + 2, layers + 3):
            q_ref[c][z] = blank
            f_ref[c][z] = blank

    def halves(x):
        high = x.astype(jnp.bfloat16)
        return high, (x - high.astype(jnp.float32)).astype(jnp.bfloat16)

    def prepare(z, carry):
        layer = (base + z).astype(jnp.float32)
        at = pl.ds(pl.multiple_of(z * rows, rows), rows)
        for k in range(lanes):
            cut = slice(k * LANE, (k + 1) * LANE)
            opened = opened_at(flat[0, :, cut], flat[1, :, cut], layer)
            vel_x, vel_z = vel[0, z, :, cut], vel[2, z, :, cut]
            for c in range(3):
                q = opened * vel[c, z, :, cut]
                q_ref[c][z + 2, :, cut] = q
                f_ref[c][z + 2, :, cut] = vel_z * q
                parts = halves(vel_x * q) + halves(q)
                for i, part in enumerate(parts):
                    split_ref[c, at, i * cols + k * LANE : i * cols + (k + 1) * LANE] = part
        return carry

    lax.fori_loop(0, layers, prepare, 0, unroll=2)
    for c in range(3):
        x_ref[c][...] = jnp.dot(split_ref[c], band_ref[...], preferred_element_type=jnp.float32)

    def put(side, n, value):
        edge_ref[side, n] = value.reshape(rows // SUB, SUB, LANE)

    gather_edges(lambda c, z: vel[c, z], layers, rows, cols, put)
    for n in range(2):
        right, left = repeat_edges(flat[n], rows, cols)
        put(0, 3 + n, right)
        put(1, 3 + n, left)

    def outside(z, c, cut):
        total = jnp.zeros((rows, LANE), jnp.float32)
        for offset, weight in ((1, -8.0), (-1, 8.0), (2, 1.0), (-2, -1.0)):
            at = z + offset
            if 0 <= at < layers:
                total = total + weight * f_ref[c][at + 2, :, cut]
                if abs(offset) == 1:
                    total = total + 6.0 * q_ref[c][at + 2, :, cut]
        hit = flat[0, :, cut] == (base + z).astype(jnp.float32)
        return jnp.where(hit, gain * flat[1, :, cut] * total, 0.0)

    sums = []
    for k in range(lanes):
        cut = slice(k * LANE, (k + 1) * LANE)
        for c in range(2):
            sums.append(sum(outside(z, c, cut) for z in (-2, -1, layers, layers + 1)))

    def update(z, sums):
        sums = list(sums)
        layer = (base + z).astype(jnp.float32)
        for k in range(lanes):
            cut = slice(k * LANE, (k + 1) * LANE)
            level = flat[0, :, cut]
            weight = gain * opened_at(level, flat[1, :, cut], layer)
            hit = level == layer
            vel_y = vel[1, z, :, cut]
            for c in range(2):
                change = inner_change(z, cut, vel_y, q_ref[c], f_ref[c], x_ref[c])
                fresh = vel[c, z, :, cut] + weight * change
                new_ref[c, z, :, cut] = fresh
                sums[2 * k + c] = sums[2 * k + c] + jnp.where(hit, fresh, 0.0)
        return tuple(sums)

    sums = lax.fori_loop(0, layers, update, tuple(sums))
    for k in range(lanes):
        cut = slice(k * LANE, (k + 1) * LANE)
        scale = 1.0 / (0.5 + flat[1, :, cut])
        for c in range(2):
            shear_ref[c, :, cut] = sums[2 * k + c] * scale


def bed_window(tiles, first):
    lane = iota((SUB, LANE), 1)
    inside = [jnp.where(first, tiles[k], tiles[2 + k]) for k in range(2)]
    after = jnp.where(lane < 2, tiles[2], 0.0)
    before = jnp.where(lane >= LANE - 2, tiles[1], 0.0)
    return inside + [jnp.where(first, after, before)]


def unpack_kernel(layers, bed_in, got_a, got_b, edge, bed, halo_ref, beside_ref, full_ref, far_ref, bed_ref, *messages):
    cols = halo_ref.shape[3]
    tiles = edge.shape[2]
    tall = tiles + 1
    sub = iota((SUB, cols), 0)
    is_even = even("plane")

    plane = lax.axis_index("plane")
    has_after, has_before = plane < lax.axis_size("plane") - 1, plane > 0

    def sides(n):
        one, two = got_a[n], got_b[n]
        after, before = jnp.where(is_even, one, two), jnp.where(is_even, two, one)
        return jnp.where(has_after, after, 0.0), jnp.where(has_before, before, 0.0)

    def spread(n, fields):
        low, high = sides(n)
        found = []
        for i in range(fields):
            above = pltpu.roll(high, (SUB - 2 - 2 * i) % SUB, 0)
            below = pltpu.roll(low, (-2 * i) % SUB, 0)
            found.append(jnp.where(sub < 2, below, jnp.where(sub >= SUB - 2, above, 0.0)))
        return found

    for c in range(3):
        for k in range(layers // 4):
            for i, tile in enumerate(spread(c * (layers // 4) + k, 4)):
                halo_ref[c, 4 * k + i] = tile
    count = 3 * layers // 4
    beside = spread(count, 4)
    for i, tile in enumerate(beside):
        beside_ref[i] = tile

    def put(side, n, value):
        full_ref[side, n * tall + tiles] = value

    gather_edges(lambda c, z: halo_ref[c, z], layers, SUB, cols, put)
    for n in range(2):
        right, left = repeat_edges(beside[n], SUB, cols)
        put(0, 3 + n, right)
        put(1, 3 + n, left)
    for side in range(2):
        for n in range(5):
            for t in range(tiles):
                full_ref[side, n * tall + t] = edge[side, n, t]
    lane = iota((SUB, LANE), 1)
    group = lane // (2 * EDGE)
    far_right = [repeat_edges(tile, SUB, cols) for tile in beside[2:]]
    for side in range(2):
        far_ref[side] = jnp.where(group == 0, far_right[0][side], jnp.where(group == 1, far_right[1][side], 0.0))
    right_first = even("span")
    packed = []
    for side, shift in ((0, EDGE), (1, LANE - EDGE)):
        for t in range(tall):
            u, v, w, level, fraction = [full_ref[side, n * tall + t] for n in range(5)]
            last = jnp.where(lax.rem(group, 2) == 0, level, fraction)
            packed.append(u + pltpu.roll(v, shift, 1))
            packed.append(w + pltpu.roll(last, shift, 1))
    for i, message in enumerate(messages):
        is_right = right_first if i == 0 else jnp.logical_not(right_first)
        for n in range(2 * tall):
            message[n] = jnp.where(is_right, packed[n], packed[2 * tall + n])
        message[2 * tall] = jnp.where(is_right, far_ref[0], far_ref[1])
    if bed_in:
        used = 2 * tall + 1
        first = lax.axis_index("span") == 0
        own = [bed[:, i * LANE : (i + 1) * LANE] for i in range(4)]
        past = [tile[:, k * LANE : (k + 1) * LANE] for tile in spread(count + 1, 2) for k in range(2)]
        for i, tile in enumerate(bed_window(own, first) + bed_window(past, first)):
            bed_ref[i] = tile
        there = jnp.logical_not(first)
        one, two, three = bed_window(own, there)
        four, five, six = bed_window(past, there)
        row = iota((SUB, LANE), 0)
        messages[0][used] = one
        messages[0][used + 1] = two
        moved = jnp.where(row < EDGE, pltpu.roll(five, 2, 0), pltpu.roll(five, SUB - 2, 0))
        messages[0][used + 2] = jnp.where((row < 2) | (row >= SUB - 2), four, moved)
        rest = pltpu.roll(three, LANE // 4, 1) + pltpu.roll(six, LANE // 2, 1)
        messages[0][used - 1] = jnp.where(first, far_ref[0], far_ref[1]) + rest
    else:
        bed_ref[0] = jnp.zeros((SUB, LANE), jnp.float32)


def strip_kernel(layers, vel, flat, halo, beside, new_z, fix_ref, shear_ref, z_ref, q_ref, f_ref):
    _, rows, cols = flat.shape
    base = lax.axis_index("wall") * layers
    shape = (SUB, cols)
    sub = iota(shape, 0)
    low, high = sub < 2, sub >= SUB - 2
    blank = jnp.zeros(shape, jnp.float32)

    def faces(first, last):
        return jnp.where(low, first, jnp.where(high, last, 0.0))

    level, fraction = beside[0], beside[1]
    own_level = faces(flat[0, :SUB], flat[0, rows - SUB :])
    own_fraction = faces(flat[1, :SUB], flat[1, rows - SUB :])
    for c in range(2):
        for z in (0, 1, layers + 2, layers + 3):
            q_ref[c, z] = blank
            f_ref[c, z] = blank

    def prepare(z, carry):
        opened = opened_at(level, fraction, (base + z).astype(jnp.float32))
        for c in range(2):
            q = opened * halo[c, z]
            q_ref[c, z + 2] = q
            f_ref[c, z + 2] = halo[2, z] * q
        return carry

    lax.fori_loop(0, layers, prepare, 0, unroll=4)
    sums = []
    for c in range(2):
        found = gain * fraction * beside[2 + c]
        for z in (-2, -1, layers, layers + 1):
            total = blank
            for offset, weight in ((1, -8.0), (-1, 8.0), (2, 1.0), (-2, -1.0)):
                at = z + offset
                if 0 <= at < layers:
                    total = total + weight * f_ref[c, at + 2]
                    if abs(offset) == 1:
                        total = total + 6.0 * q_ref[c, at + 2]
            found = found + jnp.where(level == (base + z).astype(jnp.float32), gain * fraction * total, 0.0)
        sums.append(found)

    def update(z, sums):
        sums = list(sums)
        layer = (base + z).astype(jnp.float32)
        opened = opened_at(level, fraction, layer)
        own_opened = opened_at(own_level, own_fraction, layer)
        weight, own_weight = gain * opened, gain * own_opened
        hit, own_hit = level == layer, own_level == layer
        own_y = faces(vel[1, z, :SUB], vel[1, z, rows - SUB :])
        for c in range(3):
            q = q_ref[c, z + 2] if c < 2 else opened * halo[2, z]
            flux = halo[1, z] * q
            own = own_y if c == 1 else faces(vel[c, z, :SUB], vel[c, z, rows - SUB :])
            own_q = own_opened * own
            own_flux = own_y * own_q
            a, b = 8.0 * flux, 6.0 * q
            own_a, own_b = 8.0 * own_flux, 6.0 * own_q
            less_a, less_b, less = a - own_a, b - own_b, flux - own_flux
            after = jnp.where(sub == 0, less_b - less_a, 0.0) + ahead(jnp.where(low, less, 0.0), 1, 0)
            before = jnp.where(sub == SUB - 1, less_b + less_a, 0.0) - ahead(jnp.where(high, less, 0.0), -1, 0)
            fix = own_weight * faces(ahead(before, -1, 0), ahead(after, 1, 0))
            fix_ref[c, z] = fix
            if c == 2:
                continue
            after = jnp.where(sub == 0, own_b - own_a, b - a) + ahead(jnp.where(low, own_flux, 0.0), 1, 0)
            before = jnp.where(sub == SUB - 1, own_b + own_a, b + a) - ahead(jnp.where(high, own_flux, 0.0), -1, 0)
            total = ahead(after, 1, 0) + ahead(before, -1, 0) + sweep(halo[0, z] * q, b, 1) - 6.0 * b
            near = f_ref[c, z + 3] - f_ref[c, z + 1]
            both = q_ref[c, z + 3] + q_ref[c, z + 1]
            total = total + (6.0 * both - 8.0 * near + (f_ref[c, z + 4] - f_ref[c, z]))
            sums[c] = sums[c] + jnp.where(hit, halo[c, z] + weight * total, 0.0)
            sums[2 + c] = sums[2 + c] + jnp.where(own_hit, fix, 0.0)
        return tuple(sums)

    sums = lax.fori_loop(0, layers, update, (sums[0], sums[1], blank, blank), unroll=8)
    scale = 1.0 / (0.5 + fraction)
    own_scale = 1.0 / (0.5 + own_fraction)
    for c in range(2):
        shear_ref[0, c] = jnp.where(low | high, sums[c] * scale, 0.0)
        shear_ref[1, c] = sums[2 + c] * own_scale
    start = jnp.where(lax.axis_index("wall") == 0, layers - 2, 0)
    for c in range(3):
        for z in range(2):
            z_ref[c, z] = vel[c, start + z]


def column_strip(vel, levels, fraction, extra, base, layers):
    shape = levels.shape
    width = 2 * EDGE
    here = iota(shape, 1) // width
    layer = (here + base).astype(jnp.float32)
    opened = opened_at(levels, fraction, layer)
    hit = levels == layer
    hit_down = levels == layer - layers
    hit_up = levels == layer + layers
    scale = 1.0 / (0.5 + fraction)
    fresh, shear = [], []
    for c in range(3):
        q = opened * vel[c]
        b = 6.0 * q
        total = sweep(vel[0] * q, b, 1) + sweep(vel[1] * q, b, 0) - 6.0 * b
        flux = vel[2] * q
        plus = ahead(b - 8.0 * flux, width, 1)
        minus = ahead(b + 8.0 * flux, -width, 1)
        plus_far = ahead(flux, 2 * width, 1)
        minus_far = ahead(flux, -2 * width, 1)
        total = total + jnp.where(here <= layers - 2, plus, 0.0) + jnp.where(here <= layers - 3, plus_far, 0.0)
        total = total + jnp.where(here >= 1, minus, 0.0) - jnp.where(here >= 2, minus_far, 0.0)
        value = vel[c] + gain * opened * total
        fresh.append(value)
        if c < 2:
            down = jnp.where(here > layers - 2, plus, 0.0) + jnp.where(here > layers - 3, plus_far, 0.0)
            up = jnp.where(here < 1, minus, 0.0) - jnp.where(here < 2, minus_far, 0.0)
            part = jnp.where(hit, value, 0.0)
            part = part + gain * fraction * (jnp.where(hit_down, down, 0.0) + jnp.where(hit_up, up, 0.0))
            part = over_groups(part)
            more = extra if c == 0 else ahead(extra, width, 1)
            more = jnp.concatenate([jnp.zeros((shape[0] - SUB, LANE), jnp.float32), more], axis=0)
            shear.append((part + gain * fraction * more) * scale)
    return fresh, shear


def side_kernel(layers, spans, bed_in, full, far, shear, strips, *rest):
    got = rest[:spans]
    rest = rest[spans:]
    own_bed = rest[0]
    fresh_ref, out_ref = rest[2:]
    _, rows, cols = shear.shape
    tiles = rows // SUB
    tall = tiles + 1
    base = lax.axis_index("wall") * layers
    right_first = even("span")
    results = []
    column = lax.rem(iota((tall * SUB, LANE), 1), 2 * EDGE)
    alternate = lax.rem(iota((tall * SUB, LANE), 1) // (2 * EDGE), 2)
    fresh_sides = []
    for side in range(2):
        first = right_first if side == 0 else jnp.logical_not(right_first)

        def other(n):
            return jnp.where(first, got[0][n], got[1][n] if spans > 1 else 0.0)

        given = column >= EDGE if side == 0 else column < EDGE
        back = EDGE if side == 0 else LANE - EDGE
        both = [jnp.concatenate([other(2 * t + i) for t in range(tall)], axis=0) for i in range(2)]
        turned = [jnp.where(given, pltpu.roll(b, back, 1), 0.0) for b in both]
        theirs = [jnp.where(given, both[0], 0.0), turned[0], jnp.where(given, both[1], 0.0)]
        theirs.append(jnp.where(alternate == 0, turned[1], pltpu.roll(turned[1], 2 * EDGE, 1)))
        theirs.append(jnp.where(alternate == 1, turned[1], ahead(turned[1], 2 * EDGE, 1)))
        fields = []
        for n in range(5):
            own = full[side, n * tall : (n + 1) * tall].reshape(tall * SUB, LANE)
            fields.append(own + theirs[n])
        extra = far[side] + other(2 * tall)
        fresh, edge_shear = column_strip(fields[:3], fields[3], fields[4], extra, base, layers)
        fresh_sides.append(fresh)
        results.append(edge_shear)
    for c in range(3):
        fresh_ref[c] = jnp.where(column < EDGE, fresh_sides[0][c], fresh_sides[1][c])[:rows]
    lane = iota((SUB, LANE), 1)
    sub = iota((SUB, LANE), 0)
    lanes = cols // LANE
    for c in range(2):
        right, left = results[0][c], results[1][c]
        for t in range(tall):
            at = slice(t * SUB, (t + 1) * SUB)
            for k in range(lanes):
                cut = slice(k * LANE, (k + 1) * LANE)
                if t == tiles:
                    piece = strips[0, c, :, cut]
                else:
                    piece = shear[c, at, cut]
                    if t == 0:
                        piece = piece + jnp.where(sub < 2, strips[1, c, :, cut], 0.0)
                    if t == tiles - 1:
                        piece = piece + jnp.where(sub >= SUB - 2, strips[1, c, :, cut], 0.0)
                if k == 0:
                    piece = jnp.where(lane < 2, pltpu.roll(left[at], LANE - EDGE, 1), piece)
                if k == lanes - 1:
                    piece = jnp.where(lane >= LANE - 2, pltpu.roll(right[at], LANE - EDGE, 1), piece)
                out_ref[(c * tall + t) * (lanes + 1) + k] = piece
            beyond = jnp.where(lane < 2, pltpu.roll(right[at], LANE - EDGE, 1), 0.0)
            beyond = jnp.where(lane >= LANE - 2, pltpu.roll(left[at], LANE - EDGE, 1), beyond)
            out_ref[(c * tall + t) * (lanes + 1) + lanes] = beyond
    if bed_in:
        used = 2 * tall * (lanes + 1)
        start = 2 * tall + 1
        beyond = (lane < 2) | (lane >= LANE - 2)
        outer = (sub < 2) | (sub >= SUB - 2)
        rest, pack = got[0][start - 1], got[0][start + 2]
        moved = jnp.where(sub < EDGE, pltpu.roll(pack, SUB - 2, 0), pltpu.roll(pack, 2, 0))
        theirs = [got[0][start], got[0][start + 1], jnp.where(beyond, pltpu.roll(rest, LANE - LANE // 4, 1), 0.0)]
        theirs += [jnp.where(outer, pack, 0.0), jnp.where(outer, moved, 0.0)]
        theirs.append(jnp.where(beyond, pltpu.roll(rest, LANE // 2, 1), 0.0))
        for i in range(6):
            out_ref[used + i] = own_bed[i]
            out_ref[used + 6 + i] = theirs[i]


def merge_kernel(layers, new, new_z, fix, fresh, far, flat, final, out_ref, sems):
    _, rows, cols = flat.shape
    lanes = cols // LANE
    wall = lax.axis_index("wall")
    lower = wall == 0
    sub = iota((SUB, LANE), 0)
    lane = iota((SUB, LANE), 1)
    levels = flat[0]
    fraction = flat[1]
    base = wall * layers
    near_from = jnp.where(lower, 0, 1)
    far_from = 1 - near_from
    near_to = jnp.where(lower, layers - 1, 0)
    far_to = jnp.where(lower, layers - 2, 1)
    sign = jnp.where(lower, -1.0, 1.0)
    other = jnp.where(lower, layers, 0)
    near_open = opened_at(levels, fraction, (other + jnp.where(lower, 0, layers - 1)).astype(jnp.float32))
    far_open = opened_at(levels, fraction, (other + jnp.where(lower, 1, layers - 2)).astype(jnp.float32))
    near_gain = gain * opened_at(levels, fraction, (base + near_to).astype(jnp.float32))
    far_gain = gain * opened_at(levels, fraction, (base + far_to).astype(jnp.float32))
    near_w, far_w = far[2, near_from], far[2, far_from]
    copies = []
    part = layers // 4

    def merge(c, z):
        for t in range(rows // SUB):
            at = slice(t * SUB, (t + 1) * SUB)
            side = pltpu.roll(fresh[c, at], (LANE - EDGE - 2 * EDGE * z) % LANE, 1)
            for k in range(lanes):
                cut = slice(k * LANE, (k + 1) * LANE)
                piece = new[c, z, at, cut] if c < 2 else new_z[0, z, at, cut]
                if t == 0:
                    piece = piece + jnp.where(sub < 2, fix[c, z, :, cut], 0.0)
                if t == rows // SUB - 1:
                    piece = piece + jnp.where(sub >= SUB - 2, fix[c, z, :, cut], 0.0)
                if k == 0:
                    piece = jnp.where(lane < 2, side, piece)
                if k == lanes - 1:
                    piece = jnp.where(lane >= LANE - 2, side, piece)
                out_ref[c, z, at, cut] = piece

    def send(c, i):
        at = pl.ds(i * part, part)
        copies.append(pltpu.make_async_copy(out_ref.at[c, at], final.at[c, at], sems.at[4 * c + i]))
        copies[-1].start()

    for c in range(3):
        for i in (0, 3, 1, 2):
            for z in range(i * part, (i + 1) * part):
                merge(c, z)
            if i == 3:
                near_q = near_open * far[c, near_from]
                near_f = sign * (near_w * near_q)
                far_f = sign * (far_w * (far_open * far[c, far_from]))
                out_ref[c, near_to] = out_ref[c, near_to] + near_gain * (6.0 * near_q + 8.0 * near_f - far_f)
                out_ref[c, far_to] = out_ref[c, far_to] - far_gain * near_f
                send(c, 0)
            if i > 0:
                send(c, i)
    for copy in copies:
        copy.wait()


def bed_kernel(tall, lanes, bed_in, mine, theirs, *rest):
    out_ref = rest[-1]
    rows = (tall - 1) * SUB
    wide = (lanes + 1) * LANE
    span = lax.axis_index("span")
    wall = lax.axis_index("wall")
    plane = lax.axis_index("plane")

    def sheared(c):
        whole = []
        for t in range(tall):
            first = (c * tall + t) * (lanes + 1)
            whole.append(
                jnp.concatenate([mine[first + k] + theirs[first + k] for k in range(lanes + 1)], axis=1)
            )
        return jnp.concatenate(whole, axis=0)

    shear_x, shear_y = sheared(0), sheared(1)
    if bed_in:
        used = 2 * tall * (lanes + 1)

        def tile_of(s, w, which):
            pieces = []
            for k in range(lanes + 1):
                own = used + 3 * which + k
                from_mine = jnp.where(span == s, mine[own], mine[own + 6])
                from_theirs = jnp.where(span == s, theirs[own], theirs[own + 6])
                pieces.append(jnp.where(wall == w, from_mine, from_theirs))
            return pieces

        def window(pieces):
            return jnp.concatenate(pieces, axis=1)

        sub = iota((SUB, LANE), 0)
        whole = [window(tile_of(s, w, 0)) for s in range(2) for w in range(2)]
        after = tile_of(0, 0, 1)
        before = tile_of(1, 1, 1)
        whole.append(window([jnp.where(sub < EDGE, a, b) for a, b in zip(after, before)]))
        bed = jnp.concatenate(whole, axis=0)
    else:
        bed = rest[0][...]
    square = shear_x * shear_x + shear_y * shear_y
    factor = jnp.maximum(square - threshold_sq, 0.0) / (square + threshold_sq)
    load_x = shear_x * factor
    load_y = shear_y * factor
    divergence = 0.5 * (ahead(load_x, 1, 1) - ahead(load_x, -1, 1)) + 0.5 * (
        ahead(load_y, 1, 0) - ahead(load_y, -1, 0)
    )
    row = iota((tall * SUB, wide), 0)
    col = iota((tall * SUB, wide), 1)
    last_plane = plane == lax.axis_size("plane") - 1
    last_span = span == lax.axis_size("span") - 1
    row_low = jnp.where(last_plane, rows, rows + EDGE)
    row_high = jnp.where(plane == 0, rows + SUB, rows + EDGE)
    col_low = jnp.where(last_span, wide - LANE, wide - LANE // 2)
    col_high = jnp.where(span == 0, wide, wide - LANE // 2)
    valid = ((row < row_low) | (row >= row_high)) & ((col < col_low) | (col >= col_high))

    def step(height):
        around = ahead(height, 1, 0) + ahead(height, -1, 0) + ahead(height, 1, 1) + ahead(height, -1, 1)
        return height - bed_step * divergence + bed_step * slope_rate * (around - 4.0 * height)

    first = jnp.where(valid, step(bed), 0.0)
    out_ref[...] = step(first)[:rows, : lanes * LANE]


def pairings(axis):
    size = lax.axis_size(axis)
    lists = []
    for start in (0, 1):
        found = []
        for i in range(start, size - 1, 2):
            found += [(i, i + 1), (i + 1, i)]
        lists.append(found)
    return lists


def everyone(axis, lists):
    walls = lax.axis_size("wall")
    full = []
    for pairs in lists:
        target = dict(pairs)
        found = []
        for i in range(lax.axis_size(axis)):
            for w in range(walls):
                to = target[i] * walls + w if i in target else i * walls + walls - 1 - w
                found.append((i * walls + w, to))
        full.append(found)
    return full


def bed_around(bed_height, rows, cols):
    spans = lax.axis_size("span")
    whole = lax.all_gather(bed_height, ("span", "wall"), axis=0, tiled=True)
    padded = jnp.pad(whole, ((0, 0), (EDGE, EDGE)))
    piece = lax.dynamic_slice_in_dim(padded, lax.axis_index("span") * cols, cols + 2 * EDGE, axis=1)
    size = lax.axis_size("plane")
    up = [(i, i + 1) for i in range(size - 1)]
    before = lax.ppermute(piece[-EDGE:], "plane", up)
    after = lax.ppermute(piece[:EDGE], "plane", [(j, i) for i, j in up])
    tall = jnp.concatenate([piece, after, before], axis=0)
    gap = jnp.zeros((tall.shape[0], LANE - 2 * EDGE), jnp.float32)
    return jnp.concatenate([tall[:, EDGE:], gap, tall[:, :EDGE]], axis=1)


def body(velocity, levels, fraction, bed_height):
    _, layers, rows, cols = velocity.shape
    tiles = rows // SUB
    tall = tiles + 1
    lanes = cols // LANE
    spans = lax.axis_size("span")
    walls = lax.axis_size("wall")
    assert walls == 2 and layers * 2 * EDGE == LANE
    bed_in = spans == 2 and lanes == 2 and bed_height.shape == (SUB, 2 * cols)
    count = 3 * layers // 4 + (2 if bed_in else 1)
    dma = pltpu.SemaphoreType.DMA
    sheet = (3, layers, SUB, cols)
    send_a, send_b, vel, flat, bed, band = call(
        functools.partial(pack_kernel, layers, bed_in),
        [(count, SUB, cols), (count, SUB, cols), velocity.shape, (2, rows, cols), bed_height.shape]
        + [jax.ShapeDtypeStruct((4 * cols, cols), jnp.bfloat16)],
        [pltpu.with_memory_space_constraint(x, pltpu.HBM) for x in (velocity, levels, fraction, bed_height)],
        [pltpu.VMEM(levels.shape, jnp.int32), dma((6,))],
        any_inputs=(0, 1, 2, 3),
        moved=1_000_000,
        limit=10,
    )
    plane_a, plane_b = everyone("plane", pairings("plane"))
    got_b = lax.ppermute(send_b, ("plane", "wall"), plane_b)
    got_a = lax.ppermute(send_a, ("plane", "wall"), plane_a)

    deep = (layers + 4, rows, cols)
    flat_rows = (layers * rows, cols)
    new, shear, edge, third_q, third_f, third_x = call(
        functools.partial(inner_kernel, layers),
        [(2, layers, rows, cols), (2, rows, cols), (2, 5, tiles, SUB, LANE), deep, deep, flat_rows],
        [vel, flat, band],
        [pltpu.VMEM((2,) + deep, jnp.float32)] * 2
        + [pltpu.VMEM((3, layers * rows, 4 * cols), jnp.bfloat16), pltpu.VMEM((2,) + flat_rows, jnp.float32)],
        flops=20_000_000,
        moved=3_000_000,
    )
    span_lists = [p for p in pairings("span") if p]
    message = (2 * tall + 1 + (3 if bed_in else 0), SUB, LANE)
    unpacked = call(
        functools.partial(unpack_kernel, layers, bed_in),
        [sheet, (4, SUB, cols), (2, 5 * tall, SUB, LANE), (2, SUB, LANE), (6, SUB, LANE)]
        + [message] * len(span_lists),
        [got_a, got_b, edge, bed],
        moved=1_000_000,
        limit=10,
    )
    halo, beside, full, far, own_bed = unpacked[:5]
    messages = unpacked[5:]
    got = [lax.ppermute(m, "span", pairs) for m, pairs in zip(messages, span_lists)]
    shallow = pltpu.VMEM((2, layers + 4, SUB, cols), jnp.float32)
    (new_z,) = call(
        functools.partial(third_kernel, layers),
        [(1, layers, rows, cols)],
        [vel, flat, third_q, third_f, third_x],
        flops=5_000_000,
        moved=2_000_000,
    )
    fix, strip_shear, send_z = call(
        functools.partial(strip_kernel, layers),
        [sheet, (2, 2, SUB, cols), (3, 2, rows, cols)],
        [vel, flat, halo, beside, new_z],
        [shallow, shallow],
        any_inputs=(4,),
        flops=10_000_000,
        moved=2_000_000,
    )
    got_z = lax.ppermute(send_z, "wall", pairings("wall")[0])
    shear_count = 2 * tall * (lanes + 1)
    out_count = shear_count + (12 if bed_in else 0)
    fresh, mine = call(
        functools.partial(side_kernel, layers, len(got), bed_in),
        [(3, rows, LANE), (out_count, SUB, LANE)],
        [full, far, shear, strip_shear] + got + [own_bed, new_z],
        any_inputs=(5 + len(got),),
        moved=1_000_000,
        limit=10,
    )
    theirs = lax.ppermute(mine, "wall", pairings("wall")[0])
    (velocity_next,) = call(
        functools.partial(merge_kernel, layers),
        [velocity.shape],
        [new, new_z, fix, fresh, got_z, flat],
        [pltpu.VMEM(velocity.shape, jnp.float32), dma((12,))],
        any_outputs=(0,),
        flops=2_000_000,
        moved=4_000_000,
    )
    extra = [] if bed_in else [bed_around(bed_height, rows, cols)]
    (bed_next,) = call(
        functools.partial(bed_kernel, tall, lanes, bed_in),
        [(rows, cols)],
        [mine, theirs] + extra,
        moved=1_000_000,
        limit=10,
    )
    return velocity_next, bed_next


def solution(mesh):
    return jax.shard_map(
        body,
        mesh=mesh,
        in_specs=(
            P("groups", "wall", "plane", "span"),
            P(("groups", "plane"), "span"),
            P(("groups", "plane"), "span"),
            P(("groups", "plane", "span", "wall"), None),
        ),
        out_specs=(P("groups", "wall", "plane", "span"), P(("groups", "plane"), "span")),
        check_vma=False,
    )
```

```python
import functools

import jax
import jax.numpy as jnp
from jax import lax
from jax.experimental import pallas as pl
from jax.experimental.pallas import tpu as pltpu
from jax.sharding import PartitionSpec as P

time_step = 0.1
bed_step = 0.4
slope_rate = 0.25
threshold_sq = 0.25
gain = time_step / 12.0
EDGE = 4
SUB = 8
LANE = 128
VMEM = pltpu.VMEM
MIB = 1024 * 1024


def call(kernel, outs, ins, scratch=(), any_inputs=(), any_outputs=(), flops=0, moved=0, limit=20, aliases=None):
    specs = [pl.BlockSpec(memory_space=pl.ANY if i in any_inputs else VMEM) for i in range(len(ins))]
    shapes = [s if isinstance(s, jax.ShapeDtypeStruct) else jax.ShapeDtypeStruct(s, jnp.float32) for s in outs]
    return pl.pallas_call(
        kernel,
        out_shape=shapes,
        in_specs=specs,
        out_specs=[pl.BlockSpec(memory_space=pl.ANY if i in any_outputs else VMEM) for i in range(len(outs))],
        scratch_shapes=list(scratch),
        input_output_aliases=aliases or {},
        cost_estimate=pl.CostEstimate(flops=flops, bytes_accessed=moved, transcendentals=0),
        compiler_params=pltpu.CompilerParams(vmem_limit_bytes=limit * MIB),
    )(*ins)


def iota(shape, dim):
    return lax.broadcasted_iota(jnp.int32, shape, dim)


def ahead(x, step, axis):
    return pltpu.roll(x, (-step) % x.shape[axis], axis)


def sweep(flux, b, axis):
    a = 8.0 * flux
    return ahead((b - a) + ahead(flux, 1, axis), 1, axis) + ahead((b + a) - ahead(flux, -1, axis), -1, axis)


def opened_at(level, fraction, layer):
    return jnp.where(level == layer, fraction, jnp.where(layer > level, 1.0, 0.0))


def even(axis):
    return lax.rem(lax.axis_index(axis), 2) == 0


def beyond_terms(tile, level, fraction, base, layers, forward):
    near = pltpu.roll(level, SUB - 1, 0) if forward else pltpu.roll(level, 1, 0)
    far = pltpu.roll(level, SUB - 2, 0) if forward else pltpu.roll(level, 2, 0)
    sign = 1.0 if forward else -1.0
    one = [jnp.zeros(level.shape, jnp.float32)] * 2
    two = list(one)
    for z in range(layers):
        layer = (base + z).astype(jnp.float32)
        opened = opened_at(level, fraction, layer)
        near_hit, far_hit = near == layer, far == layer
        for c in range(2):
            q = opened * tile[c, z]
            flux = sign * (tile[1, z] * q)
            one[c] = one[c] + jnp.where(near_hit, 6.0 * q + 8.0 * flux, 0.0)
            two[c] = two[c] - jnp.where(far_hit, flux, 0.0)
    sub = iota(level.shape, 0)
    source = SUB - 3 if forward else 2
    past = source - 1 if forward else source + 1
    shift = 1 if forward else SUB - 1
    shift_two = 2 if forward else SUB - 2
    found = []
    for c in range(2):
        a = pltpu.roll(jnp.where(sub == source, one[c], 0.0), shift, 0)
        b = pltpu.roll(jnp.where((sub == source) | (sub == past), two[c], 0.0), shift_two, 0)
        found.append(a + b)
    return found


def pack_kernel(layers, bed_in, vel_in, lev_in, frac_in, bed_from, a_ref, b_ref, vel, flat, bed, band_ref, lev, sems):
    _, rows, cols = flat.shape
    wall = lax.axis_index("wall")
    base = wall * layers
    small = [
        pltpu.make_async_copy(lev_in, lev, sems.at[0]),
        pltpu.make_async_copy(frac_in, flat.at[1], sems.at[1]),
        pltpu.make_async_copy(bed_from, bed, sems.at[2]),
    ]
    pieces = []
    for i, (start, size) in enumerate(((0, SUB), (rows - SUB, SUB), (SUB, rows - 2 * SUB))):
        at = pl.ds(start, size)
        pieces.append(pltpu.make_async_copy(vel_in.at[:, :, at, :], vel.at[:, :, at, :], sems.at[3 + i]))
    for copy in small + pieces:
        copy.start()
    tall = iota((cols, cols), 0) - iota((cols, cols), 1)
    flux_band = jnp.where(tall == 1, -8.0, jnp.where(tall == -1, 8.0, 0.0))
    flux_band = flux_band + jnp.where(tall == 2, 1.0, jnp.where(tall == -2, -1.0, 0.0))
    field_band = jnp.where(jnp.abs(tall) == 1, 6.0, jnp.where(tall == 0, -36.0, 0.0))
    for i, band in enumerate((flux_band, flux_band, field_band, field_band)):
        band_ref[i * cols : (i + 1) * cols] = band.astype(jnp.bfloat16)
    sub = iota((SUB, cols), 0)
    pair = sub // 2
    is_even = even("plane")

    def put(n, low, high):
        a_ref[n] = jnp.where(is_even, low, high)
        b_ref[n] = jnp.where(is_even, high, low)

    def stack(fields, place):
        tile = jnp.zeros((SUB, cols), jnp.float32)
        for i, field in enumerate(fields):
            tile = jnp.where(pair == i, pltpu.roll(field, (2 * i + place) % SUB, 0), tile)
        return tile

    for copy in small:
        copy.wait()
    flat[0] = lev[...].astype(jnp.float32)
    low_lev, low_frac = flat[0, rows - SUB :], flat[1, rows - SUB :]
    high_lev, high_frac = flat[0, :SUB], flat[1, :SUB]
    count = 3 * layers // 4
    if bed_in:
        halves = [bed[:, i * cols : (i + 1) * cols] for i in range(bed.shape[1] // cols)]
        put(count + 1, stack(halves, 2), stack(halves, 0))
    top = vel.at[:, :, pl.ds(0, SUB), :]
    bottom = vel.at[:, :, pl.ds(rows - SUB, SUB), :]
    quads = [(c, k) for c in range(3) for k in range(layers // 4)]
    pieces[0].wait()
    high = [stack([top[c, 4 * k + i] for i in range(4)], 0) for c, k in quads]
    high_far = beyond_terms(top, high_lev, high_frac, base, layers, False)
    pieces[1].wait()
    for n, (c, k) in enumerate(quads):
        put(n, stack([bottom[c, 4 * k + i] for i in range(4)], 2), high[n])
    low_far = beyond_terms(bottom, low_lev, low_frac, base, layers, True)
    put(count, stack([low_lev, low_frac] + low_far, 2), stack([high_lev, high_frac] + high_far, 0))
    pieces[2].wait()


def gather_edges(read, layers, rows, cols, put):
    lane = iota((rows, LANE), 1)
    column = lax.rem(lane, 2 * EDGE)
    for c in range(3):
        right = jnp.zeros((rows, LANE), jnp.float32)
        left = right
        for z in range(layers):
            group = (lane // (2 * EDGE)) == z
            field = read(c, z)
            last = field[:, cols - LANE :]
            first = field[:, :LANE]
            at = 2 * EDGE * z
            right = jnp.where(group, pltpu.roll(last, (at - (LANE - EDGE)) % LANE, 1), right)
            left = jnp.where(group, pltpu.roll(first, (at + EDGE) % LANE, 1), left)
        put(0, c, jnp.where(column < EDGE, right, 0.0))
        put(1, c, jnp.where(column >= EDGE, left, 0.0))


def over_groups(x):
    step = 2 * EDGE
    while step < LANE:
        x = x + pltpu.roll(x, step, 1) + (pltpu.roll(x, 2 * step, 1) + pltpu.roll(x, 3 * step, 1))
        step *= 4
    return x


def repeat_edges(field, rows, cols):
    lane = iota((rows, LANE), 1)
    right = jnp.where(lane < EDGE, pltpu.roll(field[:, cols - LANE :], EDGE, 1), 0.0)
    left = pltpu.roll(jnp.where(lane < EDGE, field[:, :LANE], 0.0), EDGE, 1)
    return over_groups(right), over_groups(left)


def inner_change(z, cut, vel_y, q_ref, f_ref, x_ref):
    q = q_ref[z + 2, :, cut]
    rows = q.shape[0]
    total = x_ref[pl.ds(pl.multiple_of(z * rows, rows), rows), cut] + sweep(vel_y * q, 6.0 * q, 0)
    near = f_ref[z + 3, :, cut] - f_ref[z + 1, :, cut]
    both = q_ref[z + 3, :, cut] + q_ref[z + 1, :, cut]
    return total + (6.0 * both - 8.0 * near + (f_ref[z + 4, :, cut] - f_ref[z, :, cut]))


def third_kernel(layers, vel, flat, q_ref, f_ref, x_ref, new_ref):
    _, rows, cols = flat.shape
    base = lax.axis_index("wall") * layers

    def update(z, carry):
        layer = (base + z).astype(jnp.float32)
        for k in range(cols // LANE):
            cut = slice(k * LANE, (k + 1) * LANE)
            weight = gain * opened_at(flat[0, :, cut], flat[1, :, cut], layer)
            change = inner_change(z, cut, vel[1, z, :, cut], q_ref, f_ref, x_ref)
            new_ref[0, z, :, cut] = vel[2, z, :, cut] + weight * change
        return carry

    lax.fori_loop(0, layers, update, 0, unroll=2)


def inner_kernel(layers, vel, flat, band_ref, new_ref, shear_ref, edge_ref, third_q, third_f, third_x, *scratch):
    q_pair, f_pair, split_ref, x_pair = scratch
    q_ref = [q_pair.at[0], q_pair.at[1], third_q]
    f_ref = [f_pair.at[0], f_pair.at[1], third_f]
    x_ref = [x_pair.at[0], x_pair.at[1], third_x]
    _, rows, cols = flat.shape
    base = lax.axis_index("wall") * layers
    lanes = cols // LANE
    blank = jnp.zeros((rows, cols), jnp.float32)
    for c in range(3):
        for z in (0, 1, layers + 2, layers + 3):
            q_ref[c][z] = blank
            f_ref[c][z] = blank

    def halves(x):
        high = x.astype(jnp.bfloat16)
        return high, (x - high.astype(jnp.float32)).astype(jnp.bfloat16)

    def prepare(z, carry):
        layer = (base + z).astype(jnp.float32)
        at = pl.ds(pl.multiple_of(z * rows, rows), rows)
        for k in range(lanes):
            cut = slice(k * LANE, (k + 1) * LANE)
            opened = opened_at(flat[0, :, cut], flat[1, :, cut], layer)
            vel_x, vel_z = vel[0, z, :, cut], vel[2, z, :, cut]
            for c in range(3):
                q = opened * vel[c, z, :, cut]
                q_ref[c][z + 2, :, cut] = q
                f_ref[c][z + 2, :, cut] = vel_z * q
                parts = halves(vel_x * q) + halves(q)
                for i, part in enumerate(parts):
                    split_ref[c, at, i * cols + k * LANE : i * cols + (k + 1) * LANE] = part
        return carry

    lax.fori_loop(0, layers, prepare, 0, unroll=2)
    for c in range(3):
        x_ref[c][...] = jnp.dot(split_ref[c], band_ref[...], preferred_element_type=jnp.float32)

    def put(side, n, value):
        edge_ref[side, n] = value.reshape(rows // SUB, SUB, LANE)

    gather_edges(lambda c, z: vel[c, z], layers, rows, cols, put)
    for n in range(2):
        right, left = repeat_edges(flat[n], rows, cols)
        put(0, 3 + n, right)
        put(1, 3 + n, left)

    def outside(z, c, cut):
        total = jnp.zeros((rows, LANE), jnp.float32)
        for offset, weight in ((1, -8.0), (-1, 8.0), (2, 1.0), (-2, -1.0)):
            at = z + offset
            if 0 <= at < layers:
                total = total + weight * f_ref[c][at + 2, :, cut]
                if abs(offset) == 1:
                    total = total + 6.0 * q_ref[c][at + 2, :, cut]
        hit = flat[0, :, cut] == (base + z).astype(jnp.float32)
        return jnp.where(hit, gain * flat[1, :, cut] * total, 0.0)

    sums = []
    for k in range(lanes):
        cut = slice(k * LANE, (k + 1) * LANE)
        for c in range(2):
            sums.append(sum(outside(z, c, cut) for z in (-2, -1, layers, layers + 1)))

    def update(z, sums):
        sums = list(sums)
        layer = (base + z).astype(jnp.float32)
        for k in range(lanes):
            cut = slice(k * LANE, (k + 1) * LANE)
            level = flat[0, :, cut]
            weight = gain * opened_at(level, flat[1, :, cut], layer)
            hit = level == layer
            vel_y = vel[1, z, :, cut]
            for c in range(2):
                change = inner_change(z, cut, vel_y, q_ref[c], f_ref[c], x_ref[c])
                fresh = vel[c, z, :, cut] + weight * change
                new_ref[c, z, :, cut] = fresh
                sums[2 * k + c] = sums[2 * k + c] + jnp.where(hit, fresh, 0.0)
        return tuple(sums)

    sums = lax.fori_loop(0, layers, update, tuple(sums))
    for k in range(lanes):
        cut = slice(k * LANE, (k + 1) * LANE)
        scale = 1.0 / (0.5 + flat[1, :, cut])
        for c in range(2):
            shear_ref[c, :, cut] = sums[2 * k + c] * scale


def bed_window(tiles, first):
    lane = iota((SUB, LANE), 1)
    inside = [jnp.where(first, tiles[k], tiles[2 + k]) for k in range(2)]
    after = jnp.where(lane < 2, tiles[2], 0.0)
    before = jnp.where(lane >= LANE - 2, tiles[1], 0.0)
    return inside + [jnp.where(first, after, before)]


def unpack_kernel(layers, bed_in, got_a, got_b, edge, bed, vel, halo_ref, beside_ref, full_ref, far_ref, bed_ref, z_ref, *messages):
    start = jnp.where(lax.axis_index("wall") == 0, layers - 2, 0)
    for c in range(3):
        for z in range(2):
            z_ref[c, z] = vel[c, start + z]
    cols = halo_ref.shape[3]
    tiles = edge.shape[2]
    tall = tiles + 1
    sub = iota((SUB, cols), 0)
    is_even = even("plane")

    plane = lax.axis_index("plane")
    has_after, has_before = plane < lax.axis_size("plane") - 1, plane > 0

    def sides(n):
        one, two = got_a[n], got_b[n]
        after, before = jnp.where(is_even, one, two), jnp.where(is_even, two, one)
        return jnp.where(has_after, after, 0.0), jnp.where(has_before, before, 0.0)

    def spread(n, fields):
        low, high = sides(n)
        found = []
        for i in range(fields):
            above = pltpu.roll(high, (SUB - 2 - 2 * i) % SUB, 0)
            below = pltpu.roll(low, (-2 * i) % SUB, 0)
            found.append(jnp.where(sub < 2, below, jnp.where(sub >= SUB - 2, above, 0.0)))
        return found

    for c in range(3):
        for k in range(layers // 4):
            for i, tile in enumerate(spread(c * (layers // 4) + k, 4)):
                halo_ref[c, 4 * k + i] = tile
    count = 3 * layers // 4
    beside = spread(count, 4)
    for i, tile in enumerate(beside):
        beside_ref[i] = tile

    def put(side, n, value):
        full_ref[side, n * tall + tiles] = value

    gather_edges(lambda c, z: halo_ref[c, z], layers, SUB, cols, put)
    for n in range(2):
        right, left = repeat_edges(beside[n], SUB, cols)
        put(0, 3 + n, right)
        put(1, 3 + n, left)
    for side in range(2):
        for n in range(5):
            for t in range(tiles):
                full_ref[side, n * tall + t] = edge[side, n, t]
    lane = iota((SUB, LANE), 1)
    group = lane // (2 * EDGE)
    far_right = [repeat_edges(tile, SUB, cols) for tile in beside[2:]]
    for side in range(2):
        far_ref[side] = jnp.where(group == 0, far_right[0][side], jnp.where(group == 1, far_right[1][side], 0.0))
    right_first = even("span")
    packed = []
    for side, shift in ((0, EDGE), (1, LANE - EDGE)):
        for t in range(tall):
            u, v, w, level, fraction = [full_ref[side, n * tall + t] for n in range(5)]
            last = jnp.where(lax.rem(group, 2) == 0, level, fraction)
            packed.append(u + pltpu.roll(v, shift, 1))
            packed.append(w + pltpu.roll(last, shift, 1))
    for i, message in enumerate(messages):
        is_right = right_first if i == 0 else jnp.logical_not(right_first)
        for n in range(2 * tall):
            message[n] = jnp.where(is_right, packed[n], packed[2 * tall + n])
        message[2 * tall] = jnp.where(is_right, far_ref[0], far_ref[1])
    if bed_in:
        used = 2 * tall + 1
        first = lax.axis_index("span") == 0
        own = [bed[:, i * LANE : (i + 1) * LANE] for i in range(4)]
        past = [tile[:, k * LANE : (k + 1) * LANE] for tile in spread(count + 1, 2) for k in range(2)]
        for i, tile in enumerate(bed_window(own, first) + bed_window(past, first)):
            bed_ref[i] = tile
        there = jnp.logical_not(first)
        one, two, three = bed_window(own, there)
        four, five, six = bed_window(past, there)
        row = iota((SUB, LANE), 0)
        messages[0][used] = one
        messages[0][used + 1] = two
        moved = jnp.where(row < EDGE, pltpu.roll(five, 2, 0), pltpu.roll(five, SUB - 2, 0))
        messages[0][used + 2] = jnp.where((row < 2) | (row >= SUB - 2), four, moved)
        rest = pltpu.roll(three, LANE // 4, 1) + pltpu.roll(six, LANE // 2, 1)
        messages[0][used - 1] = jnp.where(first, far_ref[0], far_ref[1]) + rest
    else:
        bed_ref[0] = jnp.zeros((SUB, LANE), jnp.float32)


def strip_kernel(layers, spans, vel, flat, halo, beside, full, far, new_z, fix_ref, shear_ref, face_ref, q_ref, f_ref):
    _, rows, cols = flat.shape
    base = lax.axis_index("wall") * layers
    shape = (SUB, cols)
    sub = iota(shape, 0)
    low, high = sub < 2, sub >= SUB - 2
    blank = jnp.zeros(shape, jnp.float32)

    def faces(first, last):
        return jnp.where(low, first, jnp.where(high, last, 0.0))

    level, fraction = beside[0], beside[1]
    own_level = faces(flat[0, :SUB], flat[0, rows - SUB :])
    own_fraction = faces(flat[1, :SUB], flat[1, rows - SUB :])
    for c in range(2):
        for z in (0, 1, layers + 2, layers + 3):
            q_ref[c, z] = blank
            f_ref[c, z] = blank

    def prepare(z, carry):
        opened = opened_at(level, fraction, (base + z).astype(jnp.float32))
        for c in range(2):
            q = opened * halo[c, z]
            q_ref[c, z + 2] = q
            f_ref[c, z + 2] = halo[2, z] * q
        return carry

    lax.fori_loop(0, layers, prepare, 0, unroll=4)
    sums = []
    for c in range(2):
        found = gain * fraction * beside[2 + c]
        for z in (-2, -1, layers, layers + 1):
            total = blank
            for offset, weight in ((1, -8.0), (-1, 8.0), (2, 1.0), (-2, -1.0)):
                at = z + offset
                if 0 <= at < layers:
                    total = total + weight * f_ref[c, at + 2]
                    if abs(offset) == 1:
                        total = total + 6.0 * q_ref[c, at + 2]
            found = found + jnp.where(level == (base + z).astype(jnp.float32), gain * fraction * total, 0.0)
        sums.append(found)

    def update(z, sums):
        sums = list(sums)
        layer = (base + z).astype(jnp.float32)
        opened = opened_at(level, fraction, layer)
        own_opened = opened_at(own_level, own_fraction, layer)
        weight, own_weight = gain * opened, gain * own_opened
        hit, own_hit = level == layer, own_level == layer
        own_y = faces(vel[1, z, :SUB], vel[1, z, rows - SUB :])
        for c in range(3):
            q = q_ref[c, z + 2] if c < 2 else opened * halo[2, z]
            flux = halo[1, z] * q
            own = own_y if c == 1 else faces(vel[c, z, :SUB], vel[c, z, rows - SUB :])
            own_q = own_opened * own
            own_flux = own_y * own_q
            a, b = 8.0 * flux, 6.0 * q
            own_a, own_b = 8.0 * own_flux, 6.0 * own_q
            less_a, less_b, less = a - own_a, b - own_b, flux - own_flux
            after = jnp.where(sub == 0, less_b - less_a, 0.0) + ahead(jnp.where(low, less, 0.0), 1, 0)
            before = jnp.where(sub == SUB - 1, less_b + less_a, 0.0) - ahead(jnp.where(high, less, 0.0), -1, 0)
            fix = own_weight * faces(ahead(before, -1, 0), ahead(after, 1, 0))
            fix_ref[c, z] = fix
            if c == 2:
                continue
            after = jnp.where(sub == 0, own_b - own_a, b - a) + ahead(jnp.where(low, own_flux, 0.0), 1, 0)
            before = jnp.where(sub == SUB - 1, own_b + own_a, b + a) - ahead(jnp.where(high, own_flux, 0.0), -1, 0)
            total = ahead(after, 1, 0) + ahead(before, -1, 0) + sweep(halo[0, z] * q, b, 1) - 6.0 * b
            near = f_ref[c, z + 3] - f_ref[c, z + 1]
            both = q_ref[c, z + 3] + q_ref[c, z + 1]
            total = total + (6.0 * both - 8.0 * near + (f_ref[c, z + 4] - f_ref[c, z]))
            sums[c] = sums[c] + jnp.where(hit, halo[c, z] + weight * total, 0.0)
            sums[2 + c] = sums[2 + c] + jnp.where(own_hit, fix, 0.0)
        return tuple(sums)

    sums = lax.fori_loop(0, layers, update, (sums[0], sums[1], blank, blank), unroll=8)
    scale = 1.0 / (0.5 + fraction)
    own_scale = 1.0 / (0.5 + own_fraction)
    for c in range(2):
        shear_ref[0, c] = jnp.where(low | high, sums[c] * scale, 0.0)
        shear_ref[1, c] = sums[2 + c] * own_scale
    if spans == 1:
        fresh, shear = face_strip(full, far, jnp.logical_not(even("span")), None, base, layers)
        for n, value in enumerate(fresh + shear):
            face_ref[n] = value
    else:
        face_ref[...] = jnp.zeros(face_ref.shape, jnp.float32)


def column_strip(vel, levels, fraction, extra, base, layers):
    shape = levels.shape
    width = 2 * EDGE
    here = iota(shape, 1) // width
    layer = (here + base).astype(jnp.float32)
    opened = opened_at(levels, fraction, layer)
    hit = levels == layer
    hit_down = levels == layer - layers
    hit_up = levels == layer + layers
    scale = 1.0 / (0.5 + fraction)
    fresh, shear = [], []
    for c in range(3):
        q = opened * vel[c]
        b = 6.0 * q
        total = sweep(vel[0] * q, b, 1) + sweep(vel[1] * q, b, 0) - 6.0 * b
        flux = vel[2] * q
        plus = ahead(b - 8.0 * flux, width, 1)
        minus = ahead(b + 8.0 * flux, -width, 1)
        plus_far = ahead(flux, 2 * width, 1)
        minus_far = ahead(flux, -2 * width, 1)
        total = total + jnp.where(here <= layers - 2, plus, 0.0) + jnp.where(here <= layers - 3, plus_far, 0.0)
        total = total + jnp.where(here >= 1, minus, 0.0) - jnp.where(here >= 2, minus_far, 0.0)
        value = vel[c] + gain * opened * total
        fresh.append(value)
        if c < 2:
            down = jnp.where(here > layers - 2, plus, 0.0) + jnp.where(here > layers - 3, plus_far, 0.0)
            up = jnp.where(here < 1, minus, 0.0) - jnp.where(here < 2, minus_far, 0.0)
            part = jnp.where(hit, value, 0.0)
            part = part + gain * fraction * (jnp.where(hit_down, down, 0.0) + jnp.where(hit_up, up, 0.0))
            part = over_groups(part)
            more = extra if c == 0 else ahead(extra, width, 1)
            more = jnp.concatenate([jnp.zeros((shape[0] - SUB, LANE), jnp.float32), more], axis=0)
            shear.append((part + gain * fraction * more) * scale)
    return fresh, shear


def side_columns(shape, right):
    column = lax.rem(iota(shape, 1), 2 * EDGE)
    return jnp.where(right, column, 2 * EDGE - 1 - column)


def face_strip(full, far, right, got, base, layers):
    tall = full.shape[1] // 5
    shape = (tall * SUB, LANE)

    def own(n):
        return jnp.where(right, full[0, n], full[1, n])

    fields = [jnp.concatenate([own(n * tall + t) for t in range(tall)], axis=0) for n in range(5)]
    extra = jnp.where(right, far[0], far[1])
    if got is not None:
        given = side_columns(shape, right) >= EDGE
        alternate = lax.rem(iota(shape, 1) // (2 * EDGE), 2)
        both = [jnp.concatenate([got[2 * t + i] for t in range(tall)], axis=0) for i in range(2)]
        turned = [jnp.where(right, pltpu.roll(b, EDGE, 1), pltpu.roll(b, LANE - EDGE, 1)) for b in both]
        turned = [jnp.where(given, b, 0.0) for b in turned]
        theirs = [jnp.where(given, both[0], 0.0), turned[0], jnp.where(given, both[1], 0.0)]
        theirs.append(jnp.where(alternate == 0, turned[1], pltpu.roll(turned[1], 2 * EDGE, 1)))
        theirs.append(jnp.where(alternate == 1, turned[1], ahead(turned[1], 2 * EDGE, 1)))
        fields = [a + b for a, b in zip(fields, theirs)]
        extra = extra + got[2 * tall]
    return column_strip(fields[:3], fields[3], fields[4], extra, base, layers)


def side_kernel(layers, spans, bed_in, full, far, shear, strips, face, *rest):
    got = rest[:spans]
    rest = rest[spans:]
    own_bed = rest[0]
    fresh_ref, out_ref = rest[2:]
    _, rows, cols = shear.shape
    tiles = rows // SUB
    tall = tiles + 1
    base = lax.axis_index("wall") * layers
    right_first = even("span")
    fresh, first = face_strip(full, far, right_first, got[0], base, layers)
    if spans > 1:
        other_fresh, second = face_strip(full, far, jnp.logical_not(right_first), got[1], base, layers)
    else:
        other_fresh, second = [face[n] for n in range(3)], [face[3], face[4]]
    is_first = side_columns((tall * SUB, LANE), right_first) < EDGE
    for c in range(3):
        fresh_ref[c] = jnp.where(is_first, fresh[c], other_fresh[c])[:rows]
    results = [
        [jnp.where(right_first, a, b) for a, b in zip(first, second)],
        [jnp.where(right_first, b, a) for a, b in zip(first, second)],
    ]
    lane = iota((SUB, LANE), 1)
    sub = iota((SUB, LANE), 0)
    lanes = cols // LANE
    for c in range(2):
        right, left = results[0][c], results[1][c]
        for t in range(tall):
            at = slice(t * SUB, (t + 1) * SUB)
            for k in range(lanes):
                cut = slice(k * LANE, (k + 1) * LANE)
                if t == tiles:
                    piece = strips[0, c, :, cut]
                else:
                    piece = shear[c, at, cut]
                    if t == 0:
                        piece = piece + jnp.where(sub < 2, strips[1, c, :, cut], 0.0)
                    if t == tiles - 1:
                        piece = piece + jnp.where(sub >= SUB - 2, strips[1, c, :, cut], 0.0)
                if k == 0:
                    piece = jnp.where(lane < 2, pltpu.roll(left[at], LANE - EDGE, 1), piece)
                if k == lanes - 1:
                    piece = jnp.where(lane >= LANE - 2, pltpu.roll(right[at], LANE - EDGE, 1), piece)
                out_ref[(c * tall + t) * (lanes + 1) + k] = piece
            beyond = jnp.where(lane < 2, pltpu.roll(right[at], LANE - EDGE, 1), 0.0)
            beyond = jnp.where(lane >= LANE - 2, pltpu.roll(left[at], LANE - EDGE, 1), beyond)
            out_ref[(c * tall + t) * (lanes + 1) + lanes] = beyond
    if bed_in:
        used = 2 * tall * (lanes + 1)
        start = 2 * tall + 1
        beyond = (lane < 2) | (lane >= LANE - 2)
        outer = (sub < 2) | (sub >= SUB - 2)
        rest, pack = got[0][start - 1], got[0][start + 2]
        moved = jnp.where(sub < EDGE, pltpu.roll(pack, SUB - 2, 0), pltpu.roll(pack, 2, 0))
        theirs = [got[0][start], got[0][start + 1], jnp.where(beyond, pltpu.roll(rest, LANE - LANE // 4, 1), 0.0)]
        theirs += [jnp.where(outer, pack, 0.0), jnp.where(outer, moved, 0.0)]
        theirs.append(jnp.where(beyond, pltpu.roll(rest, LANE // 2, 1), 0.0))
        for i in range(6):
            out_ref[used + i] = own_bed[i]
            out_ref[used + 6 + i] = theirs[i]


def merge_kernel(layers, new, new_z, fix, fresh, far, flat, final, out_ref, sems):
    _, rows, cols = flat.shape
    lanes = cols // LANE
    wall = lax.axis_index("wall")
    lower = wall == 0
    sub = iota((SUB, LANE), 0)
    lane = iota((SUB, LANE), 1)
    levels = flat[0]
    fraction = flat[1]
    base = wall * layers
    near_from = jnp.where(lower, 0, 1)
    far_from = 1 - near_from
    near_to = jnp.where(lower, layers - 1, 0)
    far_to = jnp.where(lower, layers - 2, 1)
    sign = jnp.where(lower, -1.0, 1.0)
    other = jnp.where(lower, layers, 0)
    near_open = opened_at(levels, fraction, (other + jnp.where(lower, 0, layers - 1)).astype(jnp.float32))
    far_open = opened_at(levels, fraction, (other + jnp.where(lower, 1, layers - 2)).astype(jnp.float32))
    near_gain = gain * opened_at(levels, fraction, (base + near_to).astype(jnp.float32))
    far_gain = gain * opened_at(levels, fraction, (base + far_to).astype(jnp.float32))
    near_w, far_w = far[2, near_from], far[2, far_from]
    copies = []
    part = layers // 4

    def merge(c, z):
        for t in range(rows // SUB):
            at = slice(t * SUB, (t + 1) * SUB)
            side = pltpu.roll(fresh[c, at], (LANE - EDGE - 2 * EDGE * z) % LANE, 1)
            for k in range(lanes):
                cut = slice(k * LANE, (k + 1) * LANE)
                piece = new[c, z, at, cut] if c < 2 else new_z[0, z, at, cut]
                if t == 0:
                    piece = piece + jnp.where(sub < 2, fix[c, z, :, cut], 0.0)
                if t == rows // SUB - 1:
                    piece = piece + jnp.where(sub >= SUB - 2, fix[c, z, :, cut], 0.0)
                if k == 0:
                    piece = jnp.where(lane < 2, side, piece)
                if k == lanes - 1:
                    piece = jnp.where(lane >= LANE - 2, side, piece)
                out_ref[c, z, at, cut] = piece

    def send(c, i):
        at = pl.ds(i * part, part)
        copies.append(pltpu.make_async_copy(out_ref.at[c, at], final.at[c, at], sems.at[4 * c + i]))
        copies[-1].start()

    for c in range(3):
        for i in (0, 3, 1, 2):
            for z in range(i * part, (i + 1) * part):
                merge(c, z)
            if i == 3:
                near_q = near_open * far[c, near_from]
                near_f = sign * (near_w * near_q)
                far_f = sign * (far_w * (far_open * far[c, far_from]))
                out_ref[c, near_to] = out_ref[c, near_to] + near_gain * (6.0 * near_q + 8.0 * near_f - far_f)
                out_ref[c, far_to] = out_ref[c, far_to] - far_gain * near_f
                send(c, 0)
            if i > 0:
                send(c, i)
    for copy in copies:
        copy.wait()


def bed_kernel(tall, lanes, bed_in, mine, theirs, *rest):
    out_ref = rest[-1]
    rows = (tall - 1) * SUB
    wide = (lanes + 1) * LANE
    span = lax.axis_index("span")
    wall = lax.axis_index("wall")
    plane = lax.axis_index("plane")

    def sheared(c):
        whole = []
        for t in range(tall):
            first = (c * tall + t) * (lanes + 1)
            whole.append(
                jnp.concatenate([mine[first + k] + theirs[first + k] for k in range(lanes + 1)], axis=1)
            )
        return jnp.concatenate(whole, axis=0)

    shear_x, shear_y = sheared(0), sheared(1)
    if bed_in:
        used = 2 * tall * (lanes + 1)

        def tile_of(s, w, which):
            pieces = []
            for k in range(lanes + 1):
                own = used + 3 * which + k
                from_mine = jnp.where(span == s, mine[own], mine[own + 6])
                from_theirs = jnp.where(span == s, theirs[own], theirs[own + 6])
                pieces.append(jnp.where(wall == w, from_mine, from_theirs))
            return pieces

        def window(pieces):
            return jnp.concatenate(pieces, axis=1)

        sub = iota((SUB, LANE), 0)
        whole = [window(tile_of(s, w, 0)) for s in range(2) for w in range(2)]
        after = tile_of(0, 0, 1)
        before = tile_of(1, 1, 1)
        whole.append(window([jnp.where(sub < EDGE, a, b) for a, b in zip(after, before)]))
        bed = jnp.concatenate(whole, axis=0)
    else:
        bed = rest[0][...]
    square = shear_x * shear_x + shear_y * shear_y
    factor = jnp.maximum(square - threshold_sq, 0.0) / (square + threshold_sq)
    load_x = shear_x * factor
    load_y = shear_y * factor
    divergence = 0.5 * (ahead(load_x, 1, 1) - ahead(load_x, -1, 1)) + 0.5 * (
        ahead(load_y, 1, 0) - ahead(load_y, -1, 0)
    )
    row = iota((tall * SUB, wide), 0)
    col = iota((tall * SUB, wide), 1)
    last_plane = plane == lax.axis_size("plane") - 1
    last_span = span == lax.axis_size("span") - 1
    row_low = jnp.where(last_plane, rows, rows + EDGE)
    row_high = jnp.where(plane == 0, rows + SUB, rows + EDGE)
    col_low = jnp.where(last_span, wide - LANE, wide - LANE // 2)
    col_high = jnp.where(span == 0, wide, wide - LANE // 2)
    valid = ((row < row_low) | (row >= row_high)) & ((col < col_low) | (col >= col_high))

    def step(height):
        around = ahead(height, 1, 0) + ahead(height, -1, 0) + ahead(height, 1, 1) + ahead(height, -1, 1)
        return height - bed_step * divergence + bed_step * slope_rate * (around - 4.0 * height)

    first = jnp.where(valid, step(bed), 0.0)
    out_ref[...] = step(first)[:rows, : lanes * LANE]


def pairings(axis):
    size = lax.axis_size(axis)
    lists = []
    for start in (0, 1):
        found = []
        for i in range(start, size - 1, 2):
            found += [(i, i + 1), (i + 1, i)]
        lists.append(found)
    return lists


def everyone(axis, lists):
    walls = lax.axis_size("wall")
    full = []
    for pairs in lists:
        target = dict(pairs)
        found = []
        for i in range(lax.axis_size(axis)):
            for w in range(walls):
                to = target[i] * walls + w if i in target else i * walls + walls - 1 - w
                found.append((i * walls + w, to))
        full.append(found)
    return full


def bed_around(bed_height, rows, cols):
    spans = lax.axis_size("span")
    whole = lax.all_gather(bed_height, ("span", "wall"), axis=0, tiled=True)
    padded = jnp.pad(whole, ((0, 0), (EDGE, EDGE)))
    piece = lax.dynamic_slice_in_dim(padded, lax.axis_index("span") * cols, cols + 2 * EDGE, axis=1)
    size = lax.axis_size("plane")
    up = [(i, i + 1) for i in range(size - 1)]
    before = lax.ppermute(piece[-EDGE:], "plane", up)
    after = lax.ppermute(piece[:EDGE], "plane", [(j, i) for i, j in up])
    tall = jnp.concatenate([piece, after, before], axis=0)
    gap = jnp.zeros((tall.shape[0], LANE - 2 * EDGE), jnp.float32)
    return jnp.concatenate([tall[:, EDGE:], gap, tall[:, :EDGE]], axis=1)


def body(velocity, levels, fraction, bed_height):
    _, layers, rows, cols = velocity.shape
    tiles = rows // SUB
    tall = tiles + 1
    lanes = cols // LANE
    spans = lax.axis_size("span")
    walls = lax.axis_size("wall")
    assert walls == 2 and layers * 2 * EDGE == LANE
    bed_in = spans == 2 and lanes == 2 and bed_height.shape == (SUB, 2 * cols)
    count = 3 * layers // 4 + (2 if bed_in else 1)
    dma = pltpu.SemaphoreType.DMA
    sheet = (3, layers, SUB, cols)
    send_a, send_b, vel, flat, bed, band = call(
        functools.partial(pack_kernel, layers, bed_in),
        [(count, SUB, cols), (count, SUB, cols), velocity.shape, (2, rows, cols), bed_height.shape]
        + [jax.ShapeDtypeStruct((4 * cols, cols), jnp.bfloat16)],
        [pltpu.with_memory_space_constraint(x, pltpu.HBM) for x in (velocity, levels, fraction, bed_height)],
        [pltpu.VMEM(levels.shape, jnp.int32), dma((6,))],
        any_inputs=(0, 1, 2, 3),
        moved=1_000_000,
        limit=10,
    )
    plane_a, plane_b = everyone("plane", pairings("plane"))
    got_b = lax.ppermute(send_b, ("plane", "wall"), plane_b)
    got_a = lax.ppermute(send_a, ("plane", "wall"), plane_a)

    deep = (layers + 4, rows, cols)
    flat_rows = (layers * rows, cols)
    new, shear, edge, third_q, third_f, third_x = call(
        functools.partial(inner_kernel, layers),
        [(2, layers, rows, cols), (2, rows, cols), (2, 5, tiles, SUB, LANE), deep, deep, flat_rows],
        [vel, flat, band],
        [pltpu.VMEM((2,) + deep, jnp.float32)] * 2
        + [pltpu.VMEM((3, layers * rows, 4 * cols), jnp.bfloat16), pltpu.VMEM((2,) + flat_rows, jnp.float32)],
        flops=20_000_000,
        moved=3_000_000,
    )
    span_lists = [p for p in pairings("span") if p]
    message = (2 * tall + 1 + (3 if bed_in else 0), SUB, LANE)
    unpacked = call(
        functools.partial(unpack_kernel, layers, bed_in),
        [sheet, (4, SUB, cols), (2, 5 * tall, SUB, LANE), (2, SUB, LANE), (6, SUB, LANE), (3, 2, rows, cols)]
        + [message] * len(span_lists),
        [got_a, got_b, edge, bed, vel],
        moved=1_000_000,
        limit=10,
    )
    halo, beside, full, far, own_bed, send_z = unpacked[:6]
    messages = unpacked[6:]
    got = [lax.ppermute(m, "span", pairs) for m, pairs in zip(messages, span_lists)]
    shallow = pltpu.VMEM((2, layers + 4, SUB, cols), jnp.float32)
    (new_z,) = call(
        functools.partial(third_kernel, layers),
        [(1, layers, rows, cols)],
        [vel, flat, third_q, third_f, third_x],
        flops=5_000_000,
        moved=2_000_000,
    )
    fix, strip_shear, face = call(
        functools.partial(strip_kernel, layers, len(span_lists)),
        [sheet, (2, 2, SUB, cols), (5, tall * SUB, LANE)],
        [vel, flat, halo, beside, full, far, new_z],
        [shallow, shallow],
        any_inputs=(6,),
        flops=10_000_000,
        moved=2_000_000,
    )
    got_z = lax.ppermute(send_z, "wall", pairings("wall")[0])
    shear_count = 2 * tall * (lanes + 1)
    out_count = shear_count + (12 if bed_in else 0)
    fresh, mine = call(
        functools.partial(side_kernel, layers, len(got), bed_in),
        [(3, rows, LANE), (out_count, SUB, LANE)],
        [full, far, shear, strip_shear, face] + got + [own_bed, new_z],
        any_inputs=(6 + len(got),),
        moved=1_000_000,
        limit=10,
    )
    theirs = lax.ppermute(mine, "wall", pairings("wall")[0])
    (velocity_next,) = call(
        functools.partial(merge_kernel, layers),
        [velocity.shape],
        [new, new_z, fix, fresh, got_z, flat],
        [pltpu.VMEM(velocity.shape, jnp.float32), dma((12,))],
        any_outputs=(0,),
        flops=2_000_000,
        moved=4_000_000,
    )
    extra = [] if bed_in else [bed_around(bed_height, rows, cols)]
    (bed_next,) = call(
        functools.partial(bed_kernel, tall, lanes, bed_in),
        [(rows, cols)],
        [mine, theirs] + extra,
        moved=1_000_000,
        limit=10,
    )
    return velocity_next, bed_next


def solution(mesh):
    return jax.shard_map(
        body,
        mesh=mesh,
        in_specs=(
            P("groups", "wall", "plane", "span"),
            P(("groups", "plane"), "span"),
            P(("groups", "plane"), "span"),
            P(("groups", "plane", "span", "wall"), None),
        ),
        out_specs=(P("groups", "wall", "plane", "span"), P(("groups", "plane"), "span")),
        check_vma=False,
    )
```

```python
import functools

import jax
import jax.numpy as jnp
from jax import lax
from jax.experimental import pallas as pl
from jax.experimental.pallas import tpu as pltpu
from jax.sharding import PartitionSpec as P

time_step = 0.1
bed_step = 0.4
slope_rate = 0.25
threshold_sq = 0.25
gain = time_step / 12.0
EDGE = 4
SUB = 8
LANE = 128
VMEM = pltpu.VMEM
MIB = 1024 * 1024


def call(kernel, outs, ins, scratch=(), any_inputs=(), any_outputs=(), flops=0, moved=0, limit=20, aliases=None):
    specs = [pl.BlockSpec(memory_space=pl.ANY if i in any_inputs else VMEM) for i in range(len(ins))]
    shapes = [s if isinstance(s, jax.ShapeDtypeStruct) else jax.ShapeDtypeStruct(s, jnp.float32) for s in outs]
    return pl.pallas_call(
        kernel,
        out_shape=shapes,
        in_specs=specs,
        out_specs=[pl.BlockSpec(memory_space=pl.ANY if i in any_outputs else VMEM) for i in range(len(outs))],
        scratch_shapes=list(scratch),
        input_output_aliases=aliases or {},
        cost_estimate=pl.CostEstimate(flops=flops, bytes_accessed=moved, transcendentals=0),
        compiler_params=pltpu.CompilerParams(vmem_limit_bytes=limit * MIB),
    )(*ins)


def iota(shape, dim):
    return lax.broadcasted_iota(jnp.int32, shape, dim)


def ahead(x, step, axis):
    return pltpu.roll(x, (-step) % x.shape[axis], axis)


def sweep(flux, b, axis):
    a = 8.0 * flux
    return ahead((b - a) + ahead(flux, 1, axis), 1, axis) + ahead((b + a) - ahead(flux, -1, axis), -1, axis)


def opened_at(level, fraction, layer):
    return jnp.where(level == layer, fraction, jnp.where(layer > level, 1.0, 0.0))


def even(axis):
    return lax.rem(lax.axis_index(axis), 2) == 0


def beyond_terms(tile, level, fraction, base, layers, forward):
    near = pltpu.roll(level, SUB - 1, 0) if forward else pltpu.roll(level, 1, 0)
    far = pltpu.roll(level, SUB - 2, 0) if forward else pltpu.roll(level, 2, 0)
    sign = 1.0 if forward else -1.0
    blank = jnp.zeros(level.shape, jnp.float32)

    def add(z, sums):
        sums = list(sums)
        layer = (base + z).astype(jnp.float32)
        opened = opened_at(level, fraction, layer)
        near_hit, far_hit = near == layer, far == layer
        for c in range(2):
            q = opened * tile[c, z]
            flux = sign * (tile[1, z] * q)
            sums[c] = sums[c] + jnp.where(near_hit, 6.0 * q + 8.0 * flux, 0.0)
            sums[2 + c] = sums[2 + c] - jnp.where(far_hit, flux, 0.0)
        return tuple(sums)

    sums = lax.fori_loop(0, layers, add, (blank,) * 4, unroll=4)
    one, two = sums[:2], sums[2:]
    sub = iota(level.shape, 0)
    source = SUB - 3 if forward else 2
    past = source - 1 if forward else source + 1
    shift = 1 if forward else SUB - 1
    shift_two = 2 if forward else SUB - 2
    found = []
    for c in range(2):
        a = pltpu.roll(jnp.where(sub == source, one[c], 0.0), shift, 0)
        b = pltpu.roll(jnp.where((sub == source) | (sub == past), two[c], 0.0), shift_two, 0)
        found.append(a + b)
    return found


def pack_kernel(layers, bed_in, vel_in, lev_in, frac_in, bed_from, a_ref, b_ref, vel, flat, bed, band_ref, lev, sems):
    _, rows, cols = flat.shape
    wall = lax.axis_index("wall")
    base = wall * layers
    small = [
        pltpu.make_async_copy(lev_in, lev, sems.at[0]),
        pltpu.make_async_copy(frac_in, flat.at[1], sems.at[1]),
        pltpu.make_async_copy(bed_from, bed, sems.at[2]),
    ]
    pieces = []
    for i, (start, size) in enumerate(((0, SUB), (rows - SUB, SUB), (SUB, rows - 2 * SUB))):
        at = pl.ds(start, size)
        pieces.append(pltpu.make_async_copy(vel_in.at[:, :, at, :], vel.at[:, :, at, :], sems.at[3 + i]))
    for copy in small + pieces:
        copy.start()
    tall = iota((cols, cols), 0) - iota((cols, cols), 1)
    flux_band = jnp.where(tall == 1, -8.0, jnp.where(tall == -1, 8.0, 0.0))
    flux_band = flux_band + jnp.where(tall == 2, 1.0, jnp.where(tall == -2, -1.0, 0.0))
    field_band = jnp.where(jnp.abs(tall) == 1, 6.0, jnp.where(tall == 0, -36.0, 0.0))
    for i, band in enumerate((flux_band, flux_band, field_band, field_band)):
        band_ref[i * cols : (i + 1) * cols] = band.astype(jnp.bfloat16)
    sub = iota((SUB, cols), 0)
    pair = sub // 2
    is_even = even("plane")

    def put(n, low, high):
        a_ref[n] = jnp.where(is_even, low, high)
        b_ref[n] = jnp.where(is_even, high, low)

    def stack(fields, place):
        tile = jnp.zeros((SUB, cols), jnp.float32)
        for i, field in enumerate(fields):
            tile = jnp.where(pair == i, pltpu.roll(field, (2 * i + place) % SUB, 0), tile)
        return tile

    for copy in small:
        copy.wait()
    flat[0] = lev[...].astype(jnp.float32)
    low_lev, low_frac = flat[0, rows - SUB :], flat[1, rows - SUB :]
    high_lev, high_frac = flat[0, :SUB], flat[1, :SUB]
    count = 3 * layers // 4
    if bed_in:
        halves = [bed[:, i * cols : (i + 1) * cols] for i in range(bed.shape[1] // cols)]
        put(count + 1, stack(halves, 2), stack(halves, 0))
    top = vel.at[:, :, pl.ds(0, SUB), :]
    bottom = vel.at[:, :, pl.ds(rows - SUB, SUB), :]
    quads = [(c, k) for c in range(3) for k in range(layers // 4)]
    pieces[0].wait()
    high = [stack([top[c, 4 * k + i] for i in range(4)], 0) for c, k in quads]
    high_far = beyond_terms(top, high_lev, high_frac, base, layers, False)
    pieces[1].wait()
    for n, (c, k) in enumerate(quads):
        put(n, stack([bottom[c, 4 * k + i] for i in range(4)], 2), high[n])
    low_far = beyond_terms(bottom, low_lev, low_frac, base, layers, True)
    put(count, stack([low_lev, low_frac] + low_far, 2), stack([high_lev, high_frac] + high_far, 0))
    pieces[2].wait()


def gather_edges(read, layers, rows, cols, put):
    lane = iota((rows, LANE), 1)
    column = lax.rem(lane, 2 * EDGE)
    for c in range(3):
        right = jnp.zeros((rows, LANE), jnp.float32)
        left = right
        for z in range(layers):
            group = (lane // (2 * EDGE)) == z
            field = read(c, z)
            last = field[:, cols - LANE :]
            first = field[:, :LANE]
            at = 2 * EDGE * z
            right = jnp.where(group, pltpu.roll(last, (at - (LANE - EDGE)) % LANE, 1), right)
            left = jnp.where(group, pltpu.roll(first, (at + EDGE) % LANE, 1), left)
        put(0, c, jnp.where(column < EDGE, right, 0.0))
        put(1, c, jnp.where(column >= EDGE, left, 0.0))


def over_groups(x):
    step = 2 * EDGE
    while step < LANE:
        x = x + pltpu.roll(x, step, 1) + (pltpu.roll(x, 2 * step, 1) + pltpu.roll(x, 3 * step, 1))
        step *= 4
    return x


def repeat_edges(field, rows, cols):
    lane = iota((rows, LANE), 1)
    right = jnp.where(lane < EDGE, pltpu.roll(field[:, cols - LANE :], EDGE, 1), 0.0)
    left = pltpu.roll(jnp.where(lane < EDGE, field[:, :LANE], 0.0), EDGE, 1)
    return over_groups(right), over_groups(left)


def inner_change(z, cut, vel_y, q_ref, f_ref, x_ref):
    q = q_ref[z + 2, :, cut]
    rows = q.shape[0]
    total = x_ref[pl.ds(pl.multiple_of(z * rows, rows), rows), cut] + sweep(vel_y * q, 6.0 * q, 0)
    near = f_ref[z + 3, :, cut] - f_ref[z + 1, :, cut]
    both = q_ref[z + 3, :, cut] + q_ref[z + 1, :, cut]
    return total + (6.0 * both - 8.0 * near + (f_ref[z + 4, :, cut] - f_ref[z, :, cut]))


def third_kernel(layers, vel, flat, q_ref, f_ref, x_ref, new_ref, z_ref):
    start = jnp.where(lax.axis_index("wall") == 0, layers - 2, 0)
    for c in range(3):
        for z in range(2):
            z_ref[c, z] = vel[c, start + z]
    _, rows, cols = flat.shape
    base = lax.axis_index("wall") * layers

    def update(z, carry):
        layer = (base + z).astype(jnp.float32)
        for k in range(cols // LANE):
            cut = slice(k * LANE, (k + 1) * LANE)
            weight = gain * opened_at(flat[0, :, cut], flat[1, :, cut], layer)
            change = inner_change(z, cut, vel[1, z, :, cut], q_ref, f_ref, x_ref)
            new_ref[0, z, :, cut] = vel[2, z, :, cut] + weight * change
        return carry

    lax.fori_loop(0, layers, update, 0, unroll=2)


def inner_kernel(layers, vel, flat, band_ref, new_ref, shear_ref, edge_ref, third_q, third_f, third_x, *scratch):
    q_pair, f_pair, split_ref, x_pair = scratch
    q_ref = [q_pair.at[0], q_pair.at[1], third_q]
    f_ref = [f_pair.at[0], f_pair.at[1], third_f]
    x_ref = [x_pair.at[0], x_pair.at[1], third_x]
    _, rows, cols = flat.shape
    base = lax.axis_index("wall") * layers
    lanes = cols // LANE
    blank = jnp.zeros((rows, cols), jnp.float32)
    for c in range(3):
        for z in (0, 1, layers + 2, layers + 3):
            q_ref[c][z] = blank
            f_ref[c][z] = blank

    def halves(x):
        high = x.astype(jnp.bfloat16)
        return high, (x - high.astype(jnp.float32)).astype(jnp.bfloat16)

    def prepare(z, carry):
        layer = (base + z).astype(jnp.float32)
        at = pl.ds(pl.multiple_of(z * rows, rows), rows)
        for k in range(lanes):
            cut = slice(k * LANE, (k + 1) * LANE)
            opened = opened_at(flat[0, :, cut], flat[1, :, cut], layer)
            vel_x, vel_z = vel[0, z, :, cut], vel[2, z, :, cut]
            for c in range(3):
                q = opened * vel[c, z, :, cut]
                q_ref[c][z + 2, :, cut] = q
                f_ref[c][z + 2, :, cut] = vel_z * q
                parts = halves(vel_x * q) + halves(q)
                for i, part in enumerate(parts):
                    split_ref[c, at, i * cols + k * LANE : i * cols + (k + 1) * LANE] = part
        return carry

    lax.fori_loop(0, layers, prepare, 0, unroll=2)
    for c in range(3):
        x_ref[c][...] = jnp.dot(split_ref[c], band_ref[...], preferred_element_type=jnp.float32)

    def put(side, n, value):
        edge_ref[side, n] = value.reshape(rows // SUB, SUB, LANE)

    gather_edges(lambda c, z: vel[c, z], layers, rows, cols, put)
    for n in range(2):
        right, left = repeat_edges(flat[n], rows, cols)
        put(0, 3 + n, right)
        put(1, 3 + n, left)

    def outside(z, c, cut):
        total = jnp.zeros((rows, LANE), jnp.float32)
        for offset, weight in ((1, -8.0), (-1, 8.0), (2, 1.0), (-2, -1.0)):
            at = z + offset
            if 0 <= at < layers:
                total = total + weight * f_ref[c][at + 2, :, cut]
                if abs(offset) == 1:
                    total = total + 6.0 * q_ref[c][at + 2, :, cut]
        hit = flat[0, :, cut] == (base + z).astype(jnp.float32)
        return jnp.where(hit, gain * flat[1, :, cut] * total, 0.0)

    sums = []
    for k in range(lanes):
        cut = slice(k * LANE, (k + 1) * LANE)
        for c in range(2):
            sums.append(sum(outside(z, c, cut) for z in (-2, -1, layers, layers + 1)))

    def update(z, sums):
        sums = list(sums)
        layer = (base + z).astype(jnp.float32)
        for k in range(lanes):
            cut = slice(k * LANE, (k + 1) * LANE)
            level = flat[0, :, cut]
            weight = gain * opened_at(level, flat[1, :, cut], layer)
            hit = level == layer
            vel_y = vel[1, z, :, cut]
            for c in range(2):
                change = inner_change(z, cut, vel_y, q_ref[c], f_ref[c], x_ref[c])
                fresh = vel[c, z, :, cut] + weight * change
                new_ref[c, z, :, cut] = fresh
                sums[2 * k + c] = sums[2 * k + c] + jnp.where(hit, fresh, 0.0)
        return tuple(sums)

    sums = lax.fori_loop(0, layers, update, tuple(sums))
    for k in range(lanes):
        cut = slice(k * LANE, (k + 1) * LANE)
        scale = 1.0 / (0.5 + flat[1, :, cut])
        for c in range(2):
            shear_ref[c, :, cut] = sums[2 * k + c] * scale


def bed_window(tiles, first):
    lane = iota((SUB, LANE), 1)
    inside = [jnp.where(first, tiles[k], tiles[2 + k]) for k in range(2)]
    after = jnp.where(lane < 2, tiles[2], 0.0)
    before = jnp.where(lane >= LANE - 2, tiles[1], 0.0)
    return inside + [jnp.where(first, after, before)]


def unpack_kernel(layers, bed_in, got_a, got_b, edge, bed, halo_ref, beside_ref, full_ref, far_ref, bed_ref, *messages):
    cols = halo_ref.shape[3]
    tiles = edge.shape[2]
    tall = tiles + 1
    sub = iota((SUB, cols), 0)
    is_even = even("plane")

    plane = lax.axis_index("plane")
    has_after, has_before = plane < lax.axis_size("plane") - 1, plane > 0

    def sides(n):
        one, two = got_a[n], got_b[n]
        after, before = jnp.where(is_even, one, two), jnp.where(is_even, two, one)
        return jnp.where(has_after, after, 0.0), jnp.where(has_before, before, 0.0)

    def spread(n, fields):
        low, high = sides(n)
        found = []
        for i in range(fields):
            above = pltpu.roll(high, (SUB - 2 - 2 * i) % SUB, 0)
            below = pltpu.roll(low, (-2 * i) % SUB, 0)
            found.append(jnp.where(sub < 2, below, jnp.where(sub >= SUB - 2, above, 0.0)))
        return found

    for c in range(3):
        for k in range(layers // 4):
            for i, tile in enumerate(spread(c * (layers // 4) + k, 4)):
                halo_ref[c, 4 * k + i] = tile
    count = 3 * layers // 4
    beside = spread(count, 4)
    for i, tile in enumerate(beside):
        beside_ref[i] = tile

    def put(side, n, value):
        full_ref[side, n * tall + tiles] = value

    gather_edges(lambda c, z: halo_ref[c, z], layers, SUB, cols, put)
    for n in range(2):
        right, left = repeat_edges(beside[n], SUB, cols)
        put(0, 3 + n, right)
        put(1, 3 + n, left)
    for side in range(2):
        for n in range(5):
            for t in range(tiles):
                full_ref[side, n * tall + t] = edge[side, n, t]
    lane = iota((SUB, LANE), 1)
    group = lane // (2 * EDGE)
    far_right = [repeat_edges(tile, SUB, cols) for tile in beside[2:]]
    for side in range(2):
        far_ref[side] = jnp.where(group == 0, far_right[0][side], jnp.where(group == 1, far_right[1][side], 0.0))
    right_first = even("span")
    packed = []
    for side, shift in ((0, EDGE), (1, LANE - EDGE)):
        for t in range(tall):
            u, v, w, level, fraction = [full_ref[side, n * tall + t] for n in range(5)]
            last = jnp.where(lax.rem(group, 2) == 0, level, fraction)
            packed.append(u + pltpu.roll(v, shift, 1))
            packed.append(w + pltpu.roll(last, shift, 1))
    for i, message in enumerate(messages):
        is_right = right_first if i == 0 else jnp.logical_not(right_first)
        for n in range(2 * tall):
            message[n] = jnp.where(is_right, packed[n], packed[2 * tall + n])
        message[2 * tall] = jnp.where(is_right, far_ref[0], far_ref[1])
    if bed_in:
        used = 2 * tall + 1
        first = lax.axis_index("span") == 0
        own = [bed[:, i * LANE : (i + 1) * LANE] for i in range(4)]
        past = [tile[:, k * LANE : (k + 1) * LANE] for tile in spread(count + 1, 2) for k in range(2)]
        for i, tile in enumerate(bed_window(own, first) + bed_window(past, first)):
            bed_ref[i] = tile
        there = jnp.logical_not(first)
        one, two, three = bed_window(own, there)
        four, five, six = bed_window(past, there)
        row = iota((SUB, LANE), 0)
        messages[0][used] = one
        messages[0][used + 1] = two
        moved = jnp.where(row < EDGE, pltpu.roll(five, 2, 0), pltpu.roll(five, SUB - 2, 0))
        messages[0][used + 2] = jnp.where((row < 2) | (row >= SUB - 2), four, moved)
        rest = pltpu.roll(three, LANE // 4, 1) + pltpu.roll(six, LANE // 2, 1)
        messages[0][used - 1] = jnp.where(first, far_ref[0], far_ref[1]) + rest
    else:
        bed_ref[0] = jnp.zeros((SUB, LANE), jnp.float32)


def strip_kernel(layers, spans, vel, flat, halo, beside, full, far, new_z, fix_ref, shear_ref, face_ref, q_ref, f_ref):
    _, rows, cols = flat.shape
    base = lax.axis_index("wall") * layers
    shape = (SUB, cols)
    sub = iota(shape, 0)
    low, high = sub < 2, sub >= SUB - 2
    blank = jnp.zeros(shape, jnp.float32)

    def faces(first, last):
        return jnp.where(low, first, jnp.where(high, last, 0.0))

    level, fraction = beside[0], beside[1]
    own_level = faces(flat[0, :SUB], flat[0, rows - SUB :])
    own_fraction = faces(flat[1, :SUB], flat[1, rows - SUB :])
    for c in range(2):
        for z in (0, 1, layers + 2, layers + 3):
            q_ref[c, z] = blank
            f_ref[c, z] = blank

    def prepare(z, carry):
        opened = opened_at(level, fraction, (base + z).astype(jnp.float32))
        for c in range(2):
            q = opened * halo[c, z]
            q_ref[c, z + 2] = q
            f_ref[c, z + 2] = halo[2, z] * q
        return carry

    lax.fori_loop(0, layers, prepare, 0, unroll=4)
    sums = []
    for c in range(2):
        found = gain * fraction * beside[2 + c]
        for z in (-2, -1, layers, layers + 1):
            total = blank
            for offset, weight in ((1, -8.0), (-1, 8.0), (2, 1.0), (-2, -1.0)):
                at = z + offset
                if 0 <= at < layers:
                    total = total + weight * f_ref[c, at + 2]
                    if abs(offset) == 1:
                        total = total + 6.0 * q_ref[c, at + 2]
            found = found + jnp.where(level == (base + z).astype(jnp.float32), gain * fraction * total, 0.0)
        sums.append(found)

    def update(z, sums):
        sums = list(sums)
        layer = (base + z).astype(jnp.float32)
        opened = opened_at(level, fraction, layer)
        own_opened = opened_at(own_level, own_fraction, layer)
        weight, own_weight = gain * opened, gain * own_opened
        hit, own_hit = level == layer, own_level == layer
        own_y = faces(vel[1, z, :SUB], vel[1, z, rows - SUB :])
        for c in range(3):
            q = q_ref[c, z + 2] if c < 2 else opened * halo[2, z]
            flux = halo[1, z] * q
            own = own_y if c == 1 else faces(vel[c, z, :SUB], vel[c, z, rows - SUB :])
            own_q = own_opened * own
            own_flux = own_y * own_q
            a, b = 8.0 * flux, 6.0 * q
            own_a, own_b = 8.0 * own_flux, 6.0 * own_q
            less_a, less_b, less = a - own_a, b - own_b, flux - own_flux
            after = jnp.where(sub == 0, less_b - less_a, 0.0) + ahead(jnp.where(low, less, 0.0), 1, 0)
            before = jnp.where(sub == SUB - 1, less_b + less_a, 0.0) - ahead(jnp.where(high, less, 0.0), -1, 0)
            fix = own_weight * faces(ahead(before, -1, 0), ahead(after, 1, 0))
            fix_ref[c, z] = fix
            if c == 2:
                continue
            after = jnp.where(sub == 0, own_b - own_a, b - a) + ahead(jnp.where(low, own_flux, 0.0), 1, 0)
            before = jnp.where(sub == SUB - 1, own_b + own_a, b + a) - ahead(jnp.where(high, own_flux, 0.0), -1, 0)
            total = ahead(after, 1, 0) + ahead(before, -1, 0) + sweep(halo[0, z] * q, b, 1) - 6.0 * b
            near = f_ref[c, z + 3] - f_ref[c, z + 1]
            both = q_ref[c, z + 3] + q_ref[c, z + 1]
            total = total + (6.0 * both - 8.0 * near + (f_ref[c, z + 4] - f_ref[c, z]))
            sums[c] = sums[c] + jnp.where(hit, halo[c, z] + weight * total, 0.0)
            sums[2 + c] = sums[2 + c] + jnp.where(own_hit, fix, 0.0)
        return tuple(sums)

    sums = lax.fori_loop(0, layers, update, (sums[0], sums[1], blank, blank), unroll=8)
    scale = 1.0 / (0.5 + fraction)
    own_scale = 1.0 / (0.5 + own_fraction)
    for c in range(2):
        shear_ref[0, c] = jnp.where(low | high, sums[c] * scale, 0.0)
        shear_ref[1, c] = sums[2 + c] * own_scale
    if spans == 1:
        fresh, shear = face_strip(full, far, jnp.logical_not(even("span")), None, base, layers)
        for n, value in enumerate(fresh + shear):
            face_ref[n] = value
    else:
        face_ref[...] = jnp.zeros(face_ref.shape, jnp.float32)


def column_strip(vel, levels, fraction, extra, base, layers):
    shape = levels.shape
    width = 2 * EDGE
    here = iota(shape, 1) // width
    layer = (here + base).astype(jnp.float32)
    opened = opened_at(levels, fraction, layer)
    hit = levels == layer
    hit_down = levels == layer - layers
    hit_up = levels == layer + layers
    scale = 1.0 / (0.5 + fraction)
    fresh, shear = [], []
    for c in range(3):
        q = opened * vel[c]
        b = 6.0 * q
        total = sweep(vel[0] * q, b, 1) + sweep(vel[1] * q, b, 0) - 6.0 * b
        flux = vel[2] * q
        plus = ahead(b - 8.0 * flux, width, 1)
        minus = ahead(b + 8.0 * flux, -width, 1)
        plus_far = ahead(flux, 2 * width, 1)
        minus_far = ahead(flux, -2 * width, 1)
        total = total + jnp.where(here <= layers - 2, plus, 0.0) + jnp.where(here <= layers - 3, plus_far, 0.0)
        total = total + jnp.where(here >= 1, minus, 0.0) - jnp.where(here >= 2, minus_far, 0.0)
        value = vel[c] + gain * opened * total
        fresh.append(value)
        if c < 2:
            down = jnp.where(here > layers - 2, plus, 0.0) + jnp.where(here > layers - 3, plus_far, 0.0)
            up = jnp.where(here < 1, minus, 0.0) - jnp.where(here < 2, minus_far, 0.0)
            part = jnp.where(hit, value, 0.0)
            part = part + gain * fraction * (jnp.where(hit_down, down, 0.0) + jnp.where(hit_up, up, 0.0))
            part = over_groups(part)
            more = extra if c == 0 else ahead(extra, width, 1)
            more = jnp.concatenate([jnp.zeros((shape[0] - SUB, LANE), jnp.float32), more], axis=0)
            shear.append((part + gain * fraction * more) * scale)
    return fresh, shear


def side_columns(shape, right):
    column = lax.rem(iota(shape, 1), 2 * EDGE)
    return jnp.where(right, column, 2 * EDGE - 1 - column)


def face_strip(full, far, right, got, base, layers):
    tall = full.shape[1] // 5
    shape = (tall * SUB, LANE)

    def own(n):
        return jnp.where(right, full[0, n], full[1, n])

    fields = [jnp.concatenate([own(n * tall + t) for t in range(tall)], axis=0) for n in range(5)]
    extra = jnp.where(right, far[0], far[1])
    if got is not None:
        given = side_columns(shape, right) >= EDGE
        alternate = lax.rem(iota(shape, 1) // (2 * EDGE), 2)
        both = [jnp.concatenate([got[2 * t + i] for t in range(tall)], axis=0) for i in range(2)]
        turned = [jnp.where(right, pltpu.roll(b, EDGE, 1), pltpu.roll(b, LANE - EDGE, 1)) for b in both]
        turned = [jnp.where(given, b, 0.0) for b in turned]
        theirs = [jnp.where(given, both[0], 0.0), turned[0], jnp.where(given, both[1], 0.0)]
        theirs.append(jnp.where(alternate == 0, turned[1], pltpu.roll(turned[1], 2 * EDGE, 1)))
        theirs.append(jnp.where(alternate == 1, turned[1], ahead(turned[1], 2 * EDGE, 1)))
        fields = [a + b for a, b in zip(fields, theirs)]
        extra = extra + got[2 * tall]
    return column_strip(fields[:3], fields[3], fields[4], extra, base, layers)


def side_kernel(layers, spans, bed_in, full, far, shear, strips, face, *rest):
    got = rest[:spans]
    rest = rest[spans:]
    own_bed = rest[0]
    fresh_ref, out_ref = rest[2:]
    _, rows, cols = shear.shape
    tiles = rows // SUB
    tall = tiles + 1
    base = lax.axis_index("wall") * layers
    right_first = even("span")
    fresh, first = face_strip(full, far, right_first, got[0], base, layers)
    if spans > 1:
        other_fresh, second = face_strip(full, far, jnp.logical_not(right_first), got[1], base, layers)
    else:
        other_fresh, second = [face[n] for n in range(3)], [face[3], face[4]]
    is_first = side_columns((tall * SUB, LANE), right_first) < EDGE
    for c in range(3):
        fresh_ref[c] = jnp.where(is_first, fresh[c], other_fresh[c])[:rows]
    results = [
        [jnp.where(right_first, a, b) for a, b in zip(first, second)],
        [jnp.where(right_first, b, a) for a, b in zip(first, second)],
    ]
    lane = iota((SUB, LANE), 1)
    sub = iota((SUB, LANE), 0)
    lanes = cols // LANE
    for c in range(2):
        right, left = results[0][c], results[1][c]
        for t in range(tall):
            at = slice(t * SUB, (t + 1) * SUB)
            for k in range(lanes):
                cut = slice(k * LANE, (k + 1) * LANE)
                if t == tiles:
                    piece = strips[0, c, :, cut]
                else:
                    piece = shear[c, at, cut]
                    if t == 0:
                        piece = piece + jnp.where(sub < 2, strips[1, c, :, cut], 0.0)
                    if t == tiles - 1:
                        piece = piece + jnp.where(sub >= SUB - 2, strips[1, c, :, cut], 0.0)
                if k == 0:
                    piece = jnp.where(lane < 2, pltpu.roll(left[at], LANE - EDGE, 1), piece)
                if k == lanes - 1:
                    piece = jnp.where(lane >= LANE - 2, pltpu.roll(right[at], LANE - EDGE, 1), piece)
                out_ref[(c * tall + t) * (lanes + 1) + k] = piece
            beyond = jnp.where(lane < 2, pltpu.roll(right[at], LANE - EDGE, 1), 0.0)
            beyond = jnp.where(lane >= LANE - 2, pltpu.roll(left[at], LANE - EDGE, 1), beyond)
            out_ref[(c * tall + t) * (lanes + 1) + lanes] = beyond
    if bed_in:
        used = 2 * tall * (lanes + 1)
        start = 2 * tall + 1
        beyond = (lane < 2) | (lane >= LANE - 2)
        outer = (sub < 2) | (sub >= SUB - 2)
        rest, pack = got[0][start - 1], got[0][start + 2]
        moved = jnp.where(sub < EDGE, pltpu.roll(pack, SUB - 2, 0), pltpu.roll(pack, 2, 0))
        theirs = [got[0][start], got[0][start + 1], jnp.where(beyond, pltpu.roll(rest, LANE - LANE // 4, 1), 0.0)]
        theirs += [jnp.where(outer, pack, 0.0), jnp.where(outer, moved, 0.0)]
        theirs.append(jnp.where(beyond, pltpu.roll(rest, LANE // 2, 1), 0.0))
        for i in range(6):
            out_ref[used + i] = own_bed[i]
            out_ref[used + 6 + i] = theirs[i]


def merge_kernel(layers, new, new_z, fix, fresh, far, flat, final, out_ref, sems):
    _, rows, cols = flat.shape
    lanes = cols // LANE
    wall = lax.axis_index("wall")
    lower = wall == 0
    sub = iota((SUB, LANE), 0)
    lane = iota((SUB, LANE), 1)
    levels = flat[0]
    fraction = flat[1]
    base = wall * layers
    near_from = jnp.where(lower, 0, 1)
    far_from = 1 - near_from
    near_to = jnp.where(lower, layers - 1, 0)
    far_to = jnp.where(lower, layers - 2, 1)
    sign = jnp.where(lower, -1.0, 1.0)
    other = jnp.where(lower, layers, 0)
    near_open = opened_at(levels, fraction, (other + jnp.where(lower, 0, layers - 1)).astype(jnp.float32))
    far_open = opened_at(levels, fraction, (other + jnp.where(lower, 1, layers - 2)).astype(jnp.float32))
    near_gain = gain * opened_at(levels, fraction, (base + near_to).astype(jnp.float32))
    far_gain = gain * opened_at(levels, fraction, (base + far_to).astype(jnp.float32))
    near_w, far_w = far[2, near_from], far[2, far_from]
    copies = []
    part = layers // 4

    def merge(c, z):
        for t in range(rows // SUB):
            at = slice(t * SUB, (t + 1) * SUB)
            side = pltpu.roll(fresh[c, at], (LANE - EDGE - 2 * EDGE * z) % LANE, 1)
            for k in range(lanes):
                cut = slice(k * LANE, (k + 1) * LANE)
                piece = new[c, z, at, cut] if c < 2 else new_z[0, z, at, cut]
                if t == 0:
                    piece = piece + jnp.where(sub < 2, fix[c, z, :, cut], 0.0)
                if t == rows // SUB - 1:
                    piece = piece + jnp.where(sub >= SUB - 2, fix[c, z, :, cut], 0.0)
                if k == 0:
                    piece = jnp.where(lane < 2, side, piece)
                if k == lanes - 1:
                    piece = jnp.where(lane >= LANE - 2, side, piece)
                out_ref[c, z, at, cut] = piece

    def send(c, i):
        at = pl.ds(i * part, part)
        copies.append(pltpu.make_async_copy(out_ref.at[c, at], final.at[c, at], sems.at[4 * c + i]))
        copies[-1].start()

    for c in range(3):
        for i in (1, 2, 0, 3):
            for z in range(i * part, (i + 1) * part):
                merge(c, z)
            if i == 3:
                near_q = near_open * far[c, near_from]
                near_f = sign * (near_w * near_q)
                far_f = sign * (far_w * (far_open * far[c, far_from]))
                out_ref[c, near_to] = out_ref[c, near_to] + near_gain * (6.0 * near_q + 8.0 * near_f - far_f)
                out_ref[c, far_to] = out_ref[c, far_to] - far_gain * near_f
                send(c, 0)
            if i > 0:
                send(c, i)
    for copy in copies:
        copy.wait()


def bed_kernel(tall, lanes, bed_in, mine, theirs, *rest):
    out_ref = rest[-1]
    rows = (tall - 1) * SUB
    wide = (lanes + 1) * LANE
    span = lax.axis_index("span")
    wall = lax.axis_index("wall")
    plane = lax.axis_index("plane")

    def sheared(c):
        whole = []
        for t in range(tall):
            first = (c * tall + t) * (lanes + 1)
            whole.append(
                jnp.concatenate([mine[first + k] + theirs[first + k] for k in range(lanes + 1)], axis=1)
            )
        return jnp.concatenate(whole, axis=0)

    shear_x, shear_y = sheared(0), sheared(1)
    if bed_in:
        used = 2 * tall * (lanes + 1)

        def tile_of(s, w, which):
            pieces = []
            for k in range(lanes + 1):
                own = used + 3 * which + k
                from_mine = jnp.where(span == s, mine[own], mine[own + 6])
                from_theirs = jnp.where(span == s, theirs[own], theirs[own + 6])
                pieces.append(jnp.where(wall == w, from_mine, from_theirs))
            return pieces

        def window(pieces):
            return jnp.concatenate(pieces, axis=1)

        sub = iota((SUB, LANE), 0)
        whole = [window(tile_of(s, w, 0)) for s in range(2) for w in range(2)]
        after = tile_of(0, 0, 1)
        before = tile_of(1, 1, 1)
        whole.append(window([jnp.where(sub < EDGE, a, b) for a, b in zip(after, before)]))
        bed = jnp.concatenate(whole, axis=0)
    else:
        bed = rest[0][...]
    square = shear_x * shear_x + shear_y * shear_y
    factor = jnp.maximum(square - threshold_sq, 0.0) / (square + threshold_sq)
    load_x = shear_x * factor
    load_y = shear_y * factor
    divergence = 0.5 * (ahead(load_x, 1, 1) - ahead(load_x, -1, 1)) + 0.5 * (
        ahead(load_y, 1, 0) - ahead(load_y, -1, 0)
    )
    row = iota((tall * SUB, wide), 0)
    col = iota((tall * SUB, wide), 1)
    last_plane = plane == lax.axis_size("plane") - 1
    last_span = span == lax.axis_size("span") - 1
    row_low = jnp.where(last_plane, rows, rows + EDGE)
    row_high = jnp.where(plane == 0, rows + SUB, rows + EDGE)
    col_low = jnp.where(last_span, wide - LANE, wide - LANE // 2)
    col_high = jnp.where(span == 0, wide, wide - LANE // 2)
    valid = ((row < row_low) | (row >= row_high)) & ((col < col_low) | (col >= col_high))

    def step(height):
        around = ahead(height, 1, 0) + ahead(height, -1, 0) + ahead(height, 1, 1) + ahead(height, -1, 1)
        return height - bed_step * divergence + bed_step * slope_rate * (around - 4.0 * height)

    first = jnp.where(valid, step(bed), 0.0)
    out_ref[...] = step(first)[:rows, : lanes * LANE]


def pairings(axis):
    size = lax.axis_size(axis)
    lists = []
    for start in (0, 1):
        found = []
        for i in range(start, size - 1, 2):
            found += [(i, i + 1), (i + 1, i)]
        lists.append(found)
    return lists


def everyone(axis, lists):
    walls = lax.axis_size("wall")
    full = []
    for pairs in lists:
        target = dict(pairs)
        found = []
        for i in range(lax.axis_size(axis)):
            for w in range(walls):
                to = target[i] * walls + w if i in target else i * walls + walls - 1 - w
                found.append((i * walls + w, to))
        full.append(found)
    return full


def bed_around(bed_height, rows, cols):
    spans = lax.axis_size("span")
    whole = lax.all_gather(bed_height, ("span", "wall"), axis=0, tiled=True)
    padded = jnp.pad(whole, ((0, 0), (EDGE, EDGE)))
    piece = lax.dynamic_slice_in_dim(padded, lax.axis_index("span") * cols, cols + 2 * EDGE, axis=1)
    size = lax.axis_size("plane")
    up = [(i, i + 1) for i in range(size - 1)]
    before = lax.ppermute(piece[-EDGE:], "plane", up)
    after = lax.ppermute(piece[:EDGE], "plane", [(j, i) for i, j in up])
    tall = jnp.concatenate([piece, after, before], axis=0)
    gap = jnp.zeros((tall.shape[0], LANE - 2 * EDGE), jnp.float32)
    return jnp.concatenate([tall[:, EDGE:], gap, tall[:, :EDGE]], axis=1)


def body(velocity, levels, fraction, bed_height):
    _, layers, rows, cols = velocity.shape
    tiles = rows // SUB
    tall = tiles + 1
    lanes = cols // LANE
    spans = lax.axis_size("span")
    walls = lax.axis_size("wall")
    assert walls == 2 and layers * 2 * EDGE == LANE
    bed_in = spans == 2 and lanes == 2 and bed_height.shape == (SUB, 2 * cols)
    count = 3 * layers // 4 + (2 if bed_in else 1)
    dma = pltpu.SemaphoreType.DMA
    sheet = (3, layers, SUB, cols)
    send_a, send_b, vel, flat, bed, band = call(
        functools.partial(pack_kernel, layers, bed_in),
        [(count, SUB, cols), (count, SUB, cols), velocity.shape, (2, rows, cols), bed_height.shape]
        + [jax.ShapeDtypeStruct((4 * cols, cols), jnp.bfloat16)],
        [pltpu.with_memory_space_constraint(x, pltpu.HBM) for x in (velocity, levels, fraction, bed_height)],
        [pltpu.VMEM(levels.shape, jnp.int32), dma((6,))],
        any_inputs=(0, 1, 2, 3),
        moved=1_000_000,
        limit=10,
    )
    plane_a, plane_b = everyone("plane", pairings("plane"))
    got_b = lax.ppermute(send_b, ("plane", "wall"), plane_b)
    got_a = lax.ppermute(send_a, ("plane", "wall"), plane_a)

    deep = (layers + 4, rows, cols)
    flat_rows = (layers * rows, cols)
    new, shear, edge, third_q, third_f, third_x = call(
        functools.partial(inner_kernel, layers),
        [(2, layers, rows, cols), (2, rows, cols), (2, 5, tiles, SUB, LANE), deep, deep, flat_rows],
        [vel, flat, band],
        [pltpu.VMEM((2,) + deep, jnp.float32)] * 2
        + [pltpu.VMEM((3, layers * rows, 4 * cols), jnp.bfloat16), pltpu.VMEM((2,) + flat_rows, jnp.float32)],
        flops=20_000_000,
        moved=3_000_000,
    )
    span_lists = [p for p in pairings("span") if p]
    message = (2 * tall + 1 + (3 if bed_in else 0), SUB, LANE)
    unpacked = call(
        functools.partial(unpack_kernel, layers, bed_in),
        [sheet, (4, SUB, cols), (2, 5 * tall, SUB, LANE), (2, SUB, LANE), (6, SUB, LANE)]
        + [message] * len(span_lists),
        [got_a, got_b, edge, bed],
        moved=1_000_000,
        limit=10,
    )
    halo, beside, full, far, own_bed = unpacked[:5]
    messages = unpacked[5:]
    got = [lax.ppermute(m, "span", pairs) for m, pairs in zip(messages, span_lists)]
    shallow = pltpu.VMEM((2, layers + 4, SUB, cols), jnp.float32)
    new_z, send_z = call(
        functools.partial(third_kernel, layers),
        [(1, layers, rows, cols), (3, 2, rows, cols)],
        [vel, flat, third_q, third_f, third_x],
        flops=5_000_000,
        moved=2_000_000,
    )
    fix, strip_shear, face = call(
        functools.partial(strip_kernel, layers, len(span_lists)),
        [sheet, (2, 2, SUB, cols), (5, tall * SUB, LANE)],
        [vel, flat, halo, beside, full, far, new_z],
        [shallow, shallow],
        any_inputs=(6,),
        flops=10_000_000,
        moved=2_000_000,
    )
    got_z = lax.ppermute(send_z, "wall", pairings("wall")[0])
    shear_count = 2 * tall * (lanes + 1)
    out_count = shear_count + (12 if bed_in else 0)
    fresh, mine = call(
        functools.partial(side_kernel, layers, len(got), bed_in),
        [(3, rows, LANE), (out_count, SUB, LANE)],
        [full, far, shear, strip_shear, face] + got + [own_bed, new_z],
        any_inputs=(6 + len(got),),
        moved=1_000_000,
        limit=10,
    )
    theirs = lax.ppermute(mine, "wall", pairings("wall")[0])
    (velocity_next,) = call(
        functools.partial(merge_kernel, layers),
        [velocity.shape],
        [new, new_z, fix, fresh, got_z, flat],
        [pltpu.VMEM(velocity.shape, jnp.float32), dma((12,))],
        any_outputs=(0,),
        flops=2_000_000,
        moved=4_000_000,
    )
    extra = [] if bed_in else [bed_around(bed_height, rows, cols)]
    (bed_next,) = call(
        functools.partial(bed_kernel, tall, lanes, bed_in),
        [(rows, cols)],
        [mine, theirs] + extra,
        moved=1_000_000,
        limit=10,
    )
    return velocity_next, bed_next


def solution(mesh):
    return jax.shard_map(
        body,
        mesh=mesh,
        in_specs=(
            P("groups", "wall", "plane", "span"),
            P(("groups", "plane"), "span"),
            P(("groups", "plane"), "span"),
            P(("groups", "plane", "span", "wall"), None),
        ),
        out_specs=(P("groups", "wall", "plane", "span"), P(("groups", "plane"), "span")),
        check_vma=False,
    )
```

```python
import functools

import jax
import jax.numpy as jnp
from jax import lax
from jax.experimental import pallas as pl
from jax.experimental.pallas import tpu as pltpu
from jax.sharding import PartitionSpec as P

time_step = 0.1
bed_step = 0.4
slope_rate = 0.25
threshold_sq = 0.25
gain = time_step / 12.0
EDGE = 4
SUB = 8
LANE = 128
VMEM = pltpu.VMEM
MIB = 1024 * 1024


def call(kernel, outs, ins, scratch=(), any_inputs=(), any_outputs=(), flops=0, moved=0, limit=20, aliases=None):
    specs = [pl.BlockSpec(memory_space=pl.ANY if i in any_inputs else VMEM) for i in range(len(ins))]
    shapes = [s if isinstance(s, jax.ShapeDtypeStruct) else jax.ShapeDtypeStruct(s, jnp.float32) for s in outs]
    return pl.pallas_call(
        kernel,
        out_shape=shapes,
        in_specs=specs,
        out_specs=[pl.BlockSpec(memory_space=pl.ANY if i in any_outputs else VMEM) for i in range(len(outs))],
        scratch_shapes=list(scratch),
        input_output_aliases=aliases or {},
        cost_estimate=pl.CostEstimate(flops=flops, bytes_accessed=moved, transcendentals=0),
        compiler_params=pltpu.CompilerParams(vmem_limit_bytes=limit * MIB),
    )(*ins)


def iota(shape, dim):
    return lax.broadcasted_iota(jnp.int32, shape, dim)


def ahead(x, step, axis):
    return pltpu.roll(x, (-step) % x.shape[axis], axis)


def sweep(flux, b, axis):
    a = 8.0 * flux
    return ahead((b - a) + ahead(flux, 1, axis), 1, axis) + ahead((b + a) - ahead(flux, -1, axis), -1, axis)


def opened_at(level, fraction, layer):
    return jnp.where(level == layer, fraction, jnp.where(layer > level, 1.0, 0.0))


def even(axis):
    return lax.rem(lax.axis_index(axis), 2) == 0


def beyond_terms(tile, level, fraction, base, layers, forward):
    near = pltpu.roll(level, SUB - 1, 0) if forward else pltpu.roll(level, 1, 0)
    far = pltpu.roll(level, SUB - 2, 0) if forward else pltpu.roll(level, 2, 0)
    sign = 1.0 if forward else -1.0
    blank = jnp.zeros(level.shape, jnp.float32)

    def add(z, sums):
        sums = list(sums)
        layer = (base + z).astype(jnp.float32)
        opened = opened_at(level, fraction, layer)
        near_hit, far_hit = near == layer, far == layer
        for c in range(2):
            q = opened * tile[c, z]
            flux = sign * (tile[1, z] * q)
            sums[c] = sums[c] + jnp.where(near_hit, 6.0 * q + 8.0 * flux, 0.0)
            sums[2 + c] = sums[2 + c] - jnp.where(far_hit, flux, 0.0)
        return tuple(sums)

    sums = lax.fori_loop(0, layers, add, (blank,) * 4, unroll=4)
    one, two = sums[:2], sums[2:]
    sub = iota(level.shape, 0)
    source = SUB - 3 if forward else 2
    past = source - 1 if forward else source + 1
    shift = 1 if forward else SUB - 1
    shift_two = 2 if forward else SUB - 2
    found = []
    for c in range(2):
        a = pltpu.roll(jnp.where(sub == source, one[c], 0.0), shift, 0)
        b = pltpu.roll(jnp.where((sub == source) | (sub == past), two[c], 0.0), shift_two, 0)
        found.append(a + b)
    return found


def pack_kernel(layers, bed_in, vel_in, lev_in, frac_in, bed_from, a_ref, b_ref, vel, flat, bed, band_ref, lev, sems):
    _, rows, cols = flat.shape
    wall = lax.axis_index("wall")
    base = wall * layers
    small = [
        pltpu.make_async_copy(lev_in, lev, sems.at[0]),
        pltpu.make_async_copy(frac_in, flat.at[1], sems.at[1]),
        pltpu.make_async_copy(bed_from, bed, sems.at[2]),
    ]
    pieces = []
    for i, (start, size) in enumerate(((0, SUB), (rows - SUB, SUB), (SUB, rows - 2 * SUB))):
        at = pl.ds(start, size)
        pieces.append(pltpu.make_async_copy(vel_in.at[:, :, at, :], vel.at[:, :, at, :], sems.at[3 + i]))
    for copy in small + pieces:
        copy.start()
    tall = iota((cols, cols), 0) - iota((cols, cols), 1)
    flux_band = jnp.where(tall == 1, -8.0, jnp.where(tall == -1, 8.0, 0.0))
    flux_band = flux_band + jnp.where(tall == 2, 1.0, jnp.where(tall == -2, -1.0, 0.0))
    field_band = jnp.where(jnp.abs(tall) == 1, 6.0, jnp.where(tall == 0, -36.0, 0.0))
    for i, band in enumerate((flux_band, flux_band, field_band, field_band)):
        band_ref[i * cols : (i + 1) * cols] = band.astype(jnp.bfloat16)
    sub = iota((SUB, cols), 0)
    pair = sub // 2
    is_even = even("plane")

    def put(n, low, high):
        a_ref[n] = jnp.where(is_even, low, high)
        b_ref[n] = jnp.where(is_even, high, low)

    def stack(fields, place):
        tile = jnp.zeros((SUB, cols), jnp.float32)
        for i, field in enumerate(fields):
            tile = jnp.where(pair == i, pltpu.roll(field, (2 * i + place) % SUB, 0), tile)
        return tile

    for copy in small:
        copy.wait()
    flat[0] = lev[...].astype(jnp.float32)
    low_lev, low_frac = flat[0, rows - SUB :], flat[1, rows - SUB :]
    high_lev, high_frac = flat[0, :SUB], flat[1, :SUB]
    count = 3 * layers // 4
    if bed_in:
        halves = [bed[:, i * cols : (i + 1) * cols] for i in range(bed.shape[1] // cols)]
        put(count + 1, stack(halves, 2), stack(halves, 0))
    top = vel.at[:, :, pl.ds(0, SUB), :]
    bottom = vel.at[:, :, pl.ds(rows - SUB, SUB), :]
    quads = [(c, k) for c in range(3) for k in range(layers // 4)]
    pieces[0].wait()
    high = [stack([top[c, 4 * k + i] for i in range(4)], 0) for c, k in quads]
    high_far = beyond_terms(top, high_lev, high_frac, base, layers, False)
    pieces[1].wait()
    for n, (c, k) in enumerate(quads):
        put(n, stack([bottom[c, 4 * k + i] for i in range(4)], 2), high[n])
    low_far = beyond_terms(bottom, low_lev, low_frac, base, layers, True)
    put(count, stack([low_lev, low_frac] + low_far, 2), stack([high_lev, high_frac] + high_far, 0))
    pieces[2].wait()


def gather_edges(read, layers, rows, cols, put):
    lane = iota((rows, LANE), 1)
    column = lax.rem(lane, 2 * EDGE)
    for c in range(3):
        right = jnp.zeros((rows, LANE), jnp.float32)
        left = right
        for z in range(layers):
            group = (lane // (2 * EDGE)) == z
            field = read(c, z)
            last = field[:, cols - LANE :]
            first = field[:, :LANE]
            at = 2 * EDGE * z
            right = jnp.where(group, pltpu.roll(last, (at - (LANE - EDGE)) % LANE, 1), right)
            left = jnp.where(group, pltpu.roll(first, (at + EDGE) % LANE, 1), left)
        put(0, c, jnp.where(column < EDGE, right, 0.0))
        put(1, c, jnp.where(column >= EDGE, left, 0.0))


def over_groups(x):
    step = 2 * EDGE
    while step < LANE:
        x = x + pltpu.roll(x, step, 1) + (pltpu.roll(x, 2 * step, 1) + pltpu.roll(x, 3 * step, 1))
        step *= 4
    return x


def repeat_edges(field, rows, cols):
    lane = iota((rows, LANE), 1)
    right = jnp.where(lane < EDGE, pltpu.roll(field[:, cols - LANE :], EDGE, 1), 0.0)
    left = pltpu.roll(jnp.where(lane < EDGE, field[:, :LANE], 0.0), EDGE, 1)
    return over_groups(right), over_groups(left)


def inner_change(z, cut, vel_y, q_ref, f_ref, x_ref):
    q = q_ref[z + 2, :, cut]
    rows = q.shape[0]
    total = x_ref[pl.ds(pl.multiple_of(z * rows, rows), rows), cut] + sweep(vel_y * q, 6.0 * q, 0)
    near = f_ref[z + 3, :, cut] - f_ref[z + 1, :, cut]
    both = q_ref[z + 3, :, cut] + q_ref[z + 1, :, cut]
    return total + (6.0 * both - 8.0 * near + (f_ref[z + 4, :, cut] - f_ref[z, :, cut]))


def third_kernel(layers, vel, flat, q_ref, f_ref, x_ref, new_ref, z_ref):
    start = jnp.where(lax.axis_index("wall") == 0, layers - 2, 0)
    for c in range(3):
        for z in range(2):
            z_ref[c, z] = vel[c, start + z]
    _, rows, cols = flat.shape
    base = lax.axis_index("wall") * layers

    def update(z, carry):
        layer = (base + z).astype(jnp.float32)
        for k in range(cols // LANE):
            cut = slice(k * LANE, (k + 1) * LANE)
            weight = gain * opened_at(flat[0, :, cut], flat[1, :, cut], layer)
            change = inner_change(z, cut, vel[1, z, :, cut], q_ref, f_ref, x_ref)
            new_ref[0, z, :, cut] = vel[2, z, :, cut] + weight * change
        return carry

    lax.fori_loop(0, layers, update, 0, unroll=2)


def inner_kernel(layers, vel, flat, band_ref, new_ref, shear_ref, edge_ref, third_q, third_f, third_x, *scratch):
    q_pair, f_pair, split_ref, x_pair = scratch
    q_ref = [q_pair.at[0], q_pair.at[1], third_q]
    f_ref = [f_pair.at[0], f_pair.at[1], third_f]
    x_ref = [x_pair.at[0], x_pair.at[1], third_x]
    _, rows, cols = flat.shape
    base = lax.axis_index("wall") * layers
    lanes = cols // LANE
    blank = jnp.zeros((rows, cols), jnp.float32)
    for c in range(3):
        for z in (0, 1, layers + 2, layers + 3):
            q_ref[c][z] = blank
            f_ref[c][z] = blank

    def halves(x):
        high = x.astype(jnp.bfloat16)
        return high, (x - high.astype(jnp.float32)).astype(jnp.bfloat16)

    def prepare(z, carry):
        layer = (base + z).astype(jnp.float32)
        at = pl.ds(pl.multiple_of(z * rows, rows), rows)
        for k in range(lanes):
            cut = slice(k * LANE, (k + 1) * LANE)
            opened = opened_at(flat[0, :, cut], flat[1, :, cut], layer)
            vel_x, vel_z = vel[0, z, :, cut], vel[2, z, :, cut]
            for c in range(3):
                q = opened * vel[c, z, :, cut]
                q_ref[c][z + 2, :, cut] = q
                f_ref[c][z + 2, :, cut] = vel_z * q
                parts = halves(vel_x * q) + halves(q)
                for i, part in enumerate(parts):
                    split_ref[c, at, i * cols + k * LANE : i * cols + (k + 1) * LANE] = part
        return carry

    lax.fori_loop(0, layers, prepare, 0, unroll=4)
    for c in range(3):
        x_ref[c][...] = jnp.dot(split_ref[c], band_ref[...], preferred_element_type=jnp.float32)

    def put(side, n, value):
        edge_ref[side, n] = value.reshape(rows // SUB, SUB, LANE)

    gather_edges(lambda c, z: vel[c, z], layers, rows, cols, put)
    for n in range(2):
        right, left = repeat_edges(flat[n], rows, cols)
        put(0, 3 + n, right)
        put(1, 3 + n, left)

    def outside(z, c, cut):
        total = jnp.zeros((rows, LANE), jnp.float32)
        for offset, weight in ((1, -8.0), (-1, 8.0), (2, 1.0), (-2, -1.0)):
            at = z + offset
            if 0 <= at < layers:
                total = total + weight * f_ref[c][at + 2, :, cut]
                if abs(offset) == 1:
                    total = total + 6.0 * q_ref[c][at + 2, :, cut]
        hit = flat[0, :, cut] == (base + z).astype(jnp.float32)
        return jnp.where(hit, gain * flat[1, :, cut] * total, 0.0)

    sums = []
    for k in range(lanes):
        cut = slice(k * LANE, (k + 1) * LANE)
        for c in range(2):
            sums.append(sum(outside(z, c, cut) for z in (-2, -1, layers, layers + 1)))

    def update(z, sums):
        sums = list(sums)
        layer = (base + z).astype(jnp.float32)
        for k in range(lanes):
            cut = slice(k * LANE, (k + 1) * LANE)
            level = flat[0, :, cut]
            weight = gain * opened_at(level, flat[1, :, cut], layer)
            hit = level == layer
            vel_y = vel[1, z, :, cut]
            for c in range(2):
                change = inner_change(z, cut, vel_y, q_ref[c], f_ref[c], x_ref[c])
                fresh = vel[c, z, :, cut] + weight * change
                new_ref[c, z, :, cut] = fresh
                sums[2 * k + c] = sums[2 * k + c] + jnp.where(hit, fresh, 0.0)
        return tuple(sums)

    sums = lax.fori_loop(0, layers, update, tuple(sums))
    for k in range(lanes):
        cut = slice(k * LANE, (k + 1) * LANE)
        scale = 1.0 / (0.5 + flat[1, :, cut])
        for c in range(2):
            shear_ref[c, :, cut] = sums[2 * k + c] * scale


def bed_window(tiles, first):
    lane = iota((SUB, LANE), 1)
    inside = [jnp.where(first, tiles[k], tiles[2 + k]) for k in range(2)]
    after = jnp.where(lane < 2, tiles[2], 0.0)
    before = jnp.where(lane >= LANE - 2, tiles[1], 0.0)
    return inside + [jnp.where(first, after, before)]


def unpack_kernel(layers, bed_in, got_a, got_b, edge, bed, halo_ref, beside_ref, full_ref, far_ref, bed_ref, *messages):
    cols = halo_ref.shape[3]
    tiles = edge.shape[2]
    tall = tiles + 1
    sub = iota((SUB, cols), 0)
    is_even = even("plane")

    plane = lax.axis_index("plane")
    has_after, has_before = plane < lax.axis_size("plane") - 1, plane > 0

    def sides(n):
        one, two = got_a[n], got_b[n]
        after, before = jnp.where(is_even, one, two), jnp.where(is_even, two, one)
        return jnp.where(has_after, after, 0.0), jnp.where(has_before, before, 0.0)

    def spread(n, fields):
        low, high = sides(n)
        found = []
        for i in range(fields):
            above = pltpu.roll(high, (SUB - 2 - 2 * i) % SUB, 0)
            below = pltpu.roll(low, (-2 * i) % SUB, 0)
            found.append(jnp.where(sub < 2, below, jnp.where(sub >= SUB - 2, above, 0.0)))
        return found

    for c in range(3):
        for k in range(layers // 4):
            for i, tile in enumerate(spread(c * (layers // 4) + k, 4)):
                halo_ref[c, 4 * k + i] = tile
    count = 3 * layers // 4
    beside = spread(count, 4)
    for i, tile in enumerate(beside):
        beside_ref[i] = tile

    def put(side, n, value):
        full_ref[side, n * tall + tiles] = value

    gather_edges(lambda c, z: halo_ref[c, z], layers, SUB, cols, put)
    for n in range(2):
        right, left = repeat_edges(beside[n], SUB, cols)
        put(0, 3 + n, right)
        put(1, 3 + n, left)
    for side in range(2):
        for n in range(5):
            for t in range(tiles):
                full_ref[side, n * tall + t] = edge[side, n, t]
    lane = iota((SUB, LANE), 1)
    group = lane // (2 * EDGE)
    far_right = [repeat_edges(tile, SUB, cols) for tile in beside[2:]]
    for side in range(2):
        far_ref[side] = jnp.where(group == 0, far_right[0][side], jnp.where(group == 1, far_right[1][side], 0.0))
    right_first = even("span")
    packed = []
    for side, shift in ((0, EDGE), (1, LANE - EDGE)):
        for t in range(tall):
            u, v, w, level, fraction = [full_ref[side, n * tall + t] for n in range(5)]
            last = jnp.where(lax.rem(group, 2) == 0, level, fraction)
            packed.append(u + pltpu.roll(v, shift, 1))
            packed.append(w + pltpu.roll(last, shift, 1))
    for i, message in enumerate(messages):
        is_right = right_first if i == 0 else jnp.logical_not(right_first)
        for n in range(2 * tall):
            message[n] = jnp.where(is_right, packed[n], packed[2 * tall + n])
        message[2 * tall] = jnp.where(is_right, far_ref[0], far_ref[1])
    if bed_in:
        used = 2 * tall + 1
        first = lax.axis_index("span") == 0
        own = [bed[:, i * LANE : (i + 1) * LANE] for i in range(4)]
        past = [tile[:, k * LANE : (k + 1) * LANE] for tile in spread(count + 1, 2) for k in range(2)]
        for i, tile in enumerate(bed_window(own, first) + bed_window(past, first)):
            bed_ref[i] = tile
        there = jnp.logical_not(first)
        one, two, three = bed_window(own, there)
        four, five, six = bed_window(past, there)
        row = iota((SUB, LANE), 0)
        messages[0][used] = one
        messages[0][used + 1] = two
        moved = jnp.where(row < EDGE, pltpu.roll(five, 2, 0), pltpu.roll(five, SUB - 2, 0))
        messages[0][used + 2] = jnp.where((row < 2) | (row >= SUB - 2), four, moved)
        rest = pltpu.roll(three, LANE // 4, 1) + pltpu.roll(six, LANE // 2, 1)
        messages[0][used - 1] = jnp.where(first, far_ref[0], far_ref[1]) + rest
    else:
        bed_ref[0] = jnp.zeros((SUB, LANE), jnp.float32)


def strip_kernel(layers, spans, vel, flat, halo, beside, full, far, new_z, fix_ref, shear_ref, face_ref, q_ref, f_ref):
    _, rows, cols = flat.shape
    base = lax.axis_index("wall") * layers
    shape = (SUB, cols)
    sub = iota(shape, 0)
    low, high = sub < 2, sub >= SUB - 2
    blank = jnp.zeros(shape, jnp.float32)

    def faces(first, last):
        return jnp.where(low, first, jnp.where(high, last, 0.0))

    level, fraction = beside[0], beside[1]
    own_level = faces(flat[0, :SUB], flat[0, rows - SUB :])
    own_fraction = faces(flat[1, :SUB], flat[1, rows - SUB :])
    for c in range(2):
        for z in (0, 1, layers + 2, layers + 3):
            q_ref[c, z] = blank
            f_ref[c, z] = blank

    def prepare(z, carry):
        opened = opened_at(level, fraction, (base + z).astype(jnp.float32))
        for c in range(2):
            q = opened * halo[c, z]
            q_ref[c, z + 2] = q
            f_ref[c, z + 2] = halo[2, z] * q
        return carry

    lax.fori_loop(0, layers, prepare, 0, unroll=4)
    sums = []
    for c in range(2):
        found = gain * fraction * beside[2 + c]
        for z in (-2, -1, layers, layers + 1):
            total = blank
            for offset, weight in ((1, -8.0), (-1, 8.0), (2, 1.0), (-2, -1.0)):
                at = z + offset
                if 0 <= at < layers:
                    total = total + weight * f_ref[c, at + 2]
                    if abs(offset) == 1:
                        total = total + 6.0 * q_ref[c, at + 2]
            found = found + jnp.where(level == (base + z).astype(jnp.float32), gain * fraction * total, 0.0)
        sums.append(found)

    def update(z, sums):
        sums = list(sums)
        layer = (base + z).astype(jnp.float32)
        opened = opened_at(level, fraction, layer)
        own_opened = opened_at(own_level, own_fraction, layer)
        weight, own_weight = gain * opened, gain * own_opened
        hit, own_hit = level == layer, own_level == layer
        own_y = faces(vel[1, z, :SUB], vel[1, z, rows - SUB :])
        for c in range(3):
            q = q_ref[c, z + 2] if c < 2 else opened * halo[2, z]
            flux = halo[1, z] * q
            own = own_y if c == 1 else faces(vel[c, z, :SUB], vel[c, z, rows - SUB :])
            own_q = own_opened * own
            own_flux = own_y * own_q
            a, b = 8.0 * flux, 6.0 * q
            own_a, own_b = 8.0 * own_flux, 6.0 * own_q
            less_a, less_b, less = a - own_a, b - own_b, flux - own_flux
            after = jnp.where(sub == 0, less_b - less_a, 0.0) + ahead(jnp.where(low, less, 0.0), 1, 0)
            before = jnp.where(sub == SUB - 1, less_b + less_a, 0.0) - ahead(jnp.where(high, less, 0.0), -1, 0)
            fix = own_weight * faces(ahead(before, -1, 0), ahead(after, 1, 0))
            fix_ref[c, z] = fix
            if c == 2:
                continue
            after = jnp.where(sub == 0, own_b - own_a, b - a) + ahead(jnp.where(low, own_flux, 0.0), 1, 0)
            before = jnp.where(sub == SUB - 1, own_b + own_a, b + a) - ahead(jnp.where(high, own_flux, 0.0), -1, 0)
            total = ahead(after, 1, 0) + ahead(before, -1, 0) + sweep(halo[0, z] * q, b, 1) - 6.0 * b
            near = f_ref[c, z + 3] - f_ref[c, z + 1]
            both = q_ref[c, z + 3] + q_ref[c, z + 1]
            total = total + (6.0 * both - 8.0 * near + (f_ref[c, z + 4] - f_ref[c, z]))
            sums[c] = sums[c] + jnp.where(hit, halo[c, z] + weight * total, 0.0)
            sums[2 + c] = sums[2 + c] + jnp.where(own_hit, fix, 0.0)
        return tuple(sums)

    sums = lax.fori_loop(0, layers, update, (sums[0], sums[1], blank, blank), unroll=8)
    scale = 1.0 / (0.5 + fraction)
    own_scale = 1.0 / (0.5 + own_fraction)
    for c in range(2):
        shear_ref[0, c] = jnp.where(low | high, sums[c] * scale, 0.0)
        shear_ref[1, c] = sums[2 + c] * own_scale
    if spans == 1:
        fresh, shear = face_strip(full, far, jnp.logical_not(even("span")), None, base, layers)
        for n, value in enumerate(fresh + shear):
            face_ref[n] = value
    else:
        face_ref[...] = jnp.zeros(face_ref.shape, jnp.float32)


def column_strip(vel, levels, fraction, extra, base, layers):
    shape = levels.shape
    width = 2 * EDGE
    here = iota(shape, 1) // width
    layer = (here + base).astype(jnp.float32)
    opened = opened_at(levels, fraction, layer)
    hit = levels == layer
    hit_down = levels == layer - layers
    hit_up = levels == layer + layers
    scale = 1.0 / (0.5 + fraction)
    fresh, shear = [], []
    for c in range(3):
        q = opened * vel[c]
        b = 6.0 * q
        total = sweep(vel[0] * q, b, 1) + sweep(vel[1] * q, b, 0) - 6.0 * b
        flux = vel[2] * q
        plus = ahead(b - 8.0 * flux, width, 1)
        minus = ahead(b + 8.0 * flux, -width, 1)
        plus_far = ahead(flux, 2 * width, 1)
        minus_far = ahead(flux, -2 * width, 1)
        total = total + jnp.where(here <= layers - 2, plus, 0.0) + jnp.where(here <= layers - 3, plus_far, 0.0)
        total = total + jnp.where(here >= 1, minus, 0.0) - jnp.where(here >= 2, minus_far, 0.0)
        value = vel[c] + gain * opened * total
        fresh.append(value)
        if c < 2:
            down = jnp.where(here > layers - 2, plus, 0.0) + jnp.where(here > layers - 3, plus_far, 0.0)
            up = jnp.where(here < 1, minus, 0.0) - jnp.where(here < 2, minus_far, 0.0)
            part = jnp.where(hit, value, 0.0)
            part = part + gain * fraction * (jnp.where(hit_down, down, 0.0) + jnp.where(hit_up, up, 0.0))
            part = over_groups(part)
            more = extra if c == 0 else ahead(extra, width, 1)
            more = jnp.concatenate([jnp.zeros((shape[0] - SUB, LANE), jnp.float32), more], axis=0)
            shear.append((part + gain * fraction * more) * scale)
    return fresh, shear


def side_columns(shape, right):
    column = lax.rem(iota(shape, 1), 2 * EDGE)
    return jnp.where(right, column, 2 * EDGE - 1 - column)


def face_strip(full, far, right, got, base, layers):
    tall = full.shape[1] // 5
    shape = (tall * SUB, LANE)

    def own(n):
        return jnp.where(right, full[0, n], full[1, n])

    fields = [jnp.concatenate([own(n * tall + t) for t in range(tall)], axis=0) for n in range(5)]
    extra = jnp.where(right, far[0], far[1])
    if got is not None:
        given = side_columns(shape, right) >= EDGE
        alternate = lax.rem(iota(shape, 1) // (2 * EDGE), 2)
        both = [jnp.concatenate([got[2 * t + i] for t in range(tall)], axis=0) for i in range(2)]
        turned = [jnp.where(right, pltpu.roll(b, EDGE, 1), pltpu.roll(b, LANE - EDGE, 1)) for b in both]
        turned = [jnp.where(given, b, 0.0) for b in turned]
        theirs = [jnp.where(given, both[0], 0.0), turned[0], jnp.where(given, both[1], 0.0)]
        theirs.append(jnp.where(alternate == 0, turned[1], pltpu.roll(turned[1], 2 * EDGE, 1)))
        theirs.append(jnp.where(alternate == 1, turned[1], ahead(turned[1], 2 * EDGE, 1)))
        fields = [a + b for a, b in zip(fields, theirs)]
        extra = extra + got[2 * tall]
    return column_strip(fields[:3], fields[3], fields[4], extra, base, layers)


def side_kernel(layers, spans, bed_in, full, far, shear, strips, face, *rest):
    got = rest[:spans]
    rest = rest[spans:]
    own_bed = rest[0]
    fresh_ref, out_ref = rest[2:]
    _, rows, cols = shear.shape
    tiles = rows // SUB
    tall = tiles + 1
    base = lax.axis_index("wall") * layers
    right_first = even("span")
    fresh, first = face_strip(full, far, right_first, got[0], base, layers)
    if spans > 1:
        other_fresh, second = face_strip(full, far, jnp.logical_not(right_first), got[1], base, layers)
    else:
        other_fresh, second = [face[n] for n in range(3)], [face[3], face[4]]
    is_first = side_columns((tall * SUB, LANE), right_first) < EDGE
    for c in range(3):
        fresh_ref[c] = jnp.where(is_first, fresh[c], other_fresh[c])[:rows]
    results = [
        [jnp.where(right_first, a, b) for a, b in zip(first, second)],
        [jnp.where(right_first, b, a) for a, b in zip(first, second)],
    ]
    lane = iota((SUB, LANE), 1)
    sub = iota((SUB, LANE), 0)
    lanes = cols // LANE
    for c in range(2):
        right, left = results[0][c], results[1][c]
        for t in range(tall):
            at = slice(t * SUB, (t + 1) * SUB)
            for k in range(lanes):
                cut = slice(k * LANE, (k + 1) * LANE)
                if t == tiles:
                    piece = strips[0, c, :, cut]
                else:
                    piece = shear[c, at, cut]
                    if t == 0:
                        piece = piece + jnp.where(sub < 2, strips[1, c, :, cut], 0.0)
                    if t == tiles - 1:
                        piece = piece + jnp.where(sub >= SUB - 2, strips[1, c, :, cut], 0.0)
                if k == 0:
                    piece = jnp.where(lane < 2, pltpu.roll(left[at], LANE - EDGE, 1), piece)
                if k == lanes - 1:
                    piece = jnp.where(lane >= LANE - 2, pltpu.roll(right[at], LANE - EDGE, 1), piece)
                out_ref[(c * tall + t) * (lanes + 1) + k] = piece
            beyond = jnp.where(lane < 2, pltpu.roll(right[at], LANE - EDGE, 1), 0.0)
            beyond = jnp.where(lane >= LANE - 2, pltpu.roll(left[at], LANE - EDGE, 1), beyond)
            out_ref[(c * tall + t) * (lanes + 1) + lanes] = beyond
    if bed_in:
        used = 2 * tall * (lanes + 1)
        start = 2 * tall + 1
        beyond = (lane < 2) | (lane >= LANE - 2)
        outer = (sub < 2) | (sub >= SUB - 2)
        rest, pack = got[0][start - 1], got[0][start + 2]
        moved = jnp.where(sub < EDGE, pltpu.roll(pack, SUB - 2, 0), pltpu.roll(pack, 2, 0))
        theirs = [got[0][start], got[0][start + 1], jnp.where(beyond, pltpu.roll(rest, LANE - LANE // 4, 1), 0.0)]
        theirs += [jnp.where(outer, pack, 0.0), jnp.where(outer, moved, 0.0)]
        theirs.append(jnp.where(beyond, pltpu.roll(rest, LANE // 2, 1), 0.0))
        for i in range(6):
            out_ref[used + i] = own_bed[i]
            out_ref[used + 6 + i] = theirs[i]


def merge_kernel(layers, new, new_z, fix, fresh, far, flat, final, out_ref, sems):
    _, rows, cols = flat.shape
    lanes = cols // LANE
    wall = lax.axis_index("wall")
    lower = wall == 0
    sub = iota((SUB, LANE), 0)
    lane = iota((SUB, LANE), 1)
    levels = flat[0]
    fraction = flat[1]
    base = wall * layers
    near_from = jnp.where(lower, 0, 1)
    far_from = 1 - near_from
    near_to = jnp.where(lower, layers - 1, 0)
    far_to = jnp.where(lower, layers - 2, 1)
    sign = jnp.where(lower, -1.0, 1.0)
    other = jnp.where(lower, layers, 0)
    near_open = opened_at(levels, fraction, (other + jnp.where(lower, 0, layers - 1)).astype(jnp.float32))
    far_open = opened_at(levels, fraction, (other + jnp.where(lower, 1, layers - 2)).astype(jnp.float32))
    near_gain = gain * opened_at(levels, fraction, (base + near_to).astype(jnp.float32))
    far_gain = gain * opened_at(levels, fraction, (base + far_to).astype(jnp.float32))
    near_w, far_w = far[2, near_from], far[2, far_from]
    copies = []
    part = layers // 4

    def merge(c, z):
        for t in range(rows // SUB):
            at = slice(t * SUB, (t + 1) * SUB)
            side = pltpu.roll(fresh[c, at], (LANE - EDGE - 2 * EDGE * z) % LANE, 1)
            for k in range(lanes):
                cut = slice(k * LANE, (k + 1) * LANE)
                piece = new[c, z, at, cut] if c < 2 else new_z[0, z, at, cut]
                if t == 0:
                    piece = piece + jnp.where(sub < 2, fix[c, z, :, cut], 0.0)
                if t == rows // SUB - 1:
                    piece = piece + jnp.where(sub >= SUB - 2, fix[c, z, :, cut], 0.0)
                if k == 0:
                    piece = jnp.where(lane < 2, side, piece)
                if k == lanes - 1:
                    piece = jnp.where(lane >= LANE - 2, side, piece)
                out_ref[c, z, at, cut] = piece

    def send(c, i):
        at = pl.ds(i * part, part)
        copies.append(pltpu.make_async_copy(out_ref.at[c, at], final.at[c, at], sems.at[4 * c + i]))
        copies[-1].start()

    for c in range(3):
        for i in (1, 2, 0, 3):
            for z in range(i * part, (i + 1) * part):
                merge(c, z)
            if i == 3:
                near_q = near_open * far[c, near_from]
                near_f = sign * (near_w * near_q)
                far_f = sign * (far_w * (far_open * far[c, far_from]))
                out_ref[c, near_to] = out_ref[c, near_to] + near_gain * (6.0 * near_q + 8.0 * near_f - far_f)
                out_ref[c, far_to] = out_ref[c, far_to] - far_gain * near_f
                send(c, 0)
            if i > 0:
                send(c, i)
    for copy in copies:
        copy.wait()


def bed_kernel(tall, lanes, bed_in, mine, theirs, *rest):
    out_ref = rest[-1]
    rows = (tall - 1) * SUB
    wide = (lanes + 1) * LANE
    span = lax.axis_index("span")
    wall = lax.axis_index("wall")
    plane = lax.axis_index("plane")

    def sheared(c):
        whole = []
        for t in range(tall):
            first = (c * tall + t) * (lanes + 1)
            whole.append(
                jnp.concatenate([mine[first + k] + theirs[first + k] for k in range(lanes + 1)], axis=1)
            )
        return jnp.concatenate(whole, axis=0)

    shear_x, shear_y = sheared(0), sheared(1)
    if bed_in:
        used = 2 * tall * (lanes + 1)

        def tile_of(s, w, which):
            pieces = []
            for k in range(lanes + 1):
                own = used + 3 * which + k
                from_mine = jnp.where(span == s, mine[own], mine[own + 6])
                from_theirs = jnp.where(span == s, theirs[own], theirs[own + 6])
                pieces.append(jnp.where(wall == w, from_mine, from_theirs))
            return pieces

        def window(pieces):
            return jnp.concatenate(pieces, axis=1)

        sub = iota((SUB, LANE), 0)
        whole = [window(tile_of(s, w, 0)) for s in range(2) for w in range(2)]
        after = tile_of(0, 0, 1)
        before = tile_of(1, 1, 1)
        whole.append(window([jnp.where(sub < EDGE, a, b) for a, b in zip(after, before)]))
        bed = jnp.concatenate(whole, axis=0)
    else:
        bed = rest[0][...]
    square = shear_x * shear_x + shear_y * shear_y
    factor = jnp.maximum(square - threshold_sq, 0.0) / (square + threshold_sq)
    load_x = shear_x * factor
    load_y = shear_y * factor
    divergence = 0.5 * (ahead(load_x, 1, 1) - ahead(load_x, -1, 1)) + 0.5 * (
        ahead(load_y, 1, 0) - ahead(load_y, -1, 0)
    )
    row = iota((tall * SUB, wide), 0)
    col = iota((tall * SUB, wide), 1)
    last_plane = plane == lax.axis_size("plane") - 1
    last_span = span == lax.axis_size("span") - 1
    row_low = jnp.where(last_plane, rows, rows + EDGE)
    row_high = jnp.where(plane == 0, rows + SUB, rows + EDGE)
    col_low = jnp.where(last_span, wide - LANE, wide - LANE // 2)
    col_high = jnp.where(span == 0, wide, wide - LANE // 2)
    valid = ((row < row_low) | (row >= row_high)) & ((col < col_low) | (col >= col_high))

    def step(height):
        around = ahead(height, 1, 0) + ahead(height, -1, 0) + ahead(height, 1, 1) + ahead(height, -1, 1)
        return height - bed_step * divergence + bed_step * slope_rate * (around - 4.0 * height)

    first = jnp.where(valid, step(bed), 0.0)
    out_ref[...] = step(first)[:rows, : lanes * LANE]


def pairings(axis):
    size = lax.axis_size(axis)
    lists = []
    for start in (0, 1):
        found = []
        for i in range(start, size - 1, 2):
            found += [(i, i + 1), (i + 1, i)]
        lists.append(found)
    return lists


def everyone(axis, lists):
    walls = lax.axis_size("wall")
    full = []
    for pairs in lists:
        target = dict(pairs)
        found = []
        for i in range(lax.axis_size(axis)):
            for w in range(walls):
                to = target[i] * walls + w if i in target else i * walls + walls - 1 - w
                found.append((i * walls + w, to))
        full.append(found)
    return full


def bed_around(bed_height, rows, cols):
    spans = lax.axis_size("span")
    whole = lax.all_gather(bed_height, ("span", "wall"), axis=0, tiled=True)
    padded = jnp.pad(whole, ((0, 0), (EDGE, EDGE)))
    piece = lax.dynamic_slice_in_dim(padded, lax.axis_index("span") * cols, cols + 2 * EDGE, axis=1)
    size = lax.axis_size("plane")
    up = [(i, i + 1) for i in range(size - 1)]
    before = lax.ppermute(piece[-EDGE:], "plane", up)
    after = lax.ppermute(piece[:EDGE], "plane", [(j, i) for i, j in up])
    tall = jnp.concatenate([piece, after, before], axis=0)
    gap = jnp.zeros((tall.shape[0], LANE - 2 * EDGE), jnp.float32)
    return jnp.concatenate([tall[:, EDGE:], gap, tall[:, :EDGE]], axis=1)


def body(velocity, levels, fraction, bed_height):
    _, layers, rows, cols = velocity.shape
    tiles = rows // SUB
    tall = tiles + 1
    lanes = cols // LANE
    spans = lax.axis_size("span")
    walls = lax.axis_size("wall")
    assert walls == 2 and layers * 2 * EDGE == LANE
    bed_in = spans == 2 and lanes == 2 and bed_height.shape == (SUB, 2 * cols)
    count = 3 * layers // 4 + (2 if bed_in else 1)
    dma = pltpu.SemaphoreType.DMA
    sheet = (3, layers, SUB, cols)
    send_a, send_b, vel, flat, bed, band = call(
        functools.partial(pack_kernel, layers, bed_in),
        [(count, SUB, cols), (count, SUB, cols), velocity.shape, (2, rows, cols), bed_height.shape]
        + [jax.ShapeDtypeStruct((4 * cols, cols), jnp.bfloat16)],
        [pltpu.with_memory_space_constraint(x, pltpu.HBM) for x in (velocity, levels, fraction, bed_height)],
        [pltpu.VMEM(levels.shape, jnp.int32), dma((6,))],
        any_inputs=(0, 1, 2, 3),
        moved=1_000_000,
        limit=10,
    )
    plane_a, plane_b = everyone("plane", pairings("plane"))
    got_b = lax.ppermute(send_b, ("plane", "wall"), plane_b)
    got_a = lax.ppermute(send_a, ("plane", "wall"), plane_a)

    deep = (layers + 4, rows, cols)
    flat_rows = (layers * rows, cols)
    new, shear, edge, third_q, third_f, third_x = call(
        functools.partial(inner_kernel, layers),
        [(2, layers, rows, cols), (2, rows, cols), (2, 5, tiles, SUB, LANE), deep, deep, flat_rows],
        [vel, flat, band],
        [pltpu.VMEM((2,) + deep, jnp.float32)] * 2
        + [pltpu.VMEM((3, layers * rows, 4 * cols), jnp.bfloat16), pltpu.VMEM((2,) + flat_rows, jnp.float32)],
        flops=20_000_000,
        moved=3_000_000,
    )
    span_lists = [p for p in pairings("span") if p]
    message = (2 * tall + 1 + (3 if bed_in else 0), SUB, LANE)
    unpacked = call(
        functools.partial(unpack_kernel, layers, bed_in),
        [sheet, (4, SUB, cols), (2, 5 * tall, SUB, LANE), (2, SUB, LANE), (6, SUB, LANE)]
        + [message] * len(span_lists),
        [got_a, got_b, edge, bed],
        moved=1_000_000,
        limit=10,
    )
    halo, beside, full, far, own_bed = unpacked[:5]
    messages = unpacked[5:]
    got = [lax.ppermute(m, "span", pairs) for m, pairs in zip(messages, span_lists)]
    shallow = pltpu.VMEM((2, layers + 4, SUB, cols), jnp.float32)
    new_z, send_z = call(
        functools.partial(third_kernel, layers),
        [(1, layers, rows, cols), (3, 2, rows, cols)],
        [vel, flat, third_q, third_f, third_x],
        flops=5_000_000,
        moved=2_000_000,
    )
    fix, strip_shear, face = call(
        functools.partial(strip_kernel, layers, len(span_lists)),
        [sheet, (2, 2, SUB, cols), (5, tall * SUB, LANE)],
        [vel, flat, halo, beside, full, far, new_z],
        [shallow, shallow],
        any_inputs=(6,),
        flops=10_000_000,
        moved=2_000_000,
    )
    got_z = lax.ppermute(send_z, "wall", pairings("wall")[0])
    shear_count = 2 * tall * (lanes + 1)
    out_count = shear_count + (12 if bed_in else 0)
    fresh, mine = call(
        functools.partial(side_kernel, layers, len(got), bed_in),
        [(3, rows, LANE), (out_count, SUB, LANE)],
        [full, far, shear, strip_shear, face] + got + [own_bed, new_z],
        any_inputs=(6 + len(got),),
        moved=1_000_000,
        limit=10,
    )
    theirs = lax.ppermute(mine, "wall", pairings("wall")[0])
    (velocity_next,) = call(
        functools.partial(merge_kernel, layers),
        [velocity.shape],
        [new, new_z, fix, fresh, got_z, flat],
        [pltpu.VMEM(velocity.shape, jnp.float32), dma((12,))],
        any_outputs=(0,),
        flops=2_000_000,
        moved=4_000_000,
    )
    extra = [] if bed_in else [bed_around(bed_height, rows, cols)]
    (bed_next,) = call(
        functools.partial(bed_kernel, tall, lanes, bed_in),
        [(rows, cols)],
        [mine, theirs] + extra,
        moved=1_000_000,
        limit=10,
    )
    return velocity_next, bed_next


def solution(mesh):
    return jax.shard_map(
        body,
        mesh=mesh,
        in_specs=(
            P("groups", "wall", "plane", "span"),
            P(("groups", "plane"), "span"),
            P(("groups", "plane"), "span"),
            P(("groups", "plane", "span", "wall"), None),
        ),
        out_specs=(P("groups", "wall", "plane", "span"), P(("groups", "plane"), "span")),
        check_vma=False,
    )
```
